32 devices in a mesh: section: 2 (over x), expert: 16 (over z, y, core).
Axes of the slice: x: 2, y: 2, z: 4, core: 2. Of those that a mesh axis runs over, the one named last changes fastest.
Arguments:
- rows: bfloat16 [2, 512, 3584], P('section', 'expert'), may hold values from -6 to 6
- route_ids: int32 [2, 512, 2], P('section', 'expert'), may hold values from 0 to 7, all different within a row; in each aligned block of 32 rows (0 to 31, 32 to 63, ..., all dimensions but the last counted through in order) at most 16 rows name the same one
- route_weights: float32 [2, 512, 2], P('section', 'expert'), may hold values from 0.1 to 1
- w_gate_up: bfloat16 [2, 3584, 16384], P('section', None, 'expert'), may hold values from -0.09375 to 0.09375
- w_down: bfloat16 [2, 8192, 3584], P('section', 'expert'), may hold values from -0.1875 to 0.1875
Outputs:
- next_rows: bfloat16 [2, 512, 3584], P('section', 'expert')
The draws below stay inside these ranges and needn't reach their ends.
Inputs may be any that keep to these rules, and one draw needn't show every extreme that they name: `route_ids`: within each section, the 32 rows of one device name any one expert at most 16 times, a bound that some block reaches; the choices of one token differ.
All inputs are finite; a program needn't handle non-finite values.
Results may differ from the reference program's by a relative error of at most 0.0065.
Values may be sent and summed in bfloat16 or wider, within the bound.
No kernel may reach another device: no remote copies, remote signals or barrier semaphores. Data moves between devices by JAX's collectives and lax.ppermute only.
A program may use at most 64 MiB of HBM per device.

```python
import math
import jax
import jax.numpy as jnp
import numpy as np
from jax import lax

D = 3584
FF = 1024
SHARDS = 2
TOP = 2
TOK_DEV = 32
SECTIONS = 2
EXPERTS = 8
FH = 512
CAP = 16
TOKENS = 512
N_EXPERT = 16


def levels(own_key, shape, split, least, largest):
    def one(axis_at, blocks):
        draws = jax.random.uniform(jax.random.fold_in(jax.random.fold_in(own_key, 6), axis_at), (blocks,), jnp.float32, least / len(split), largest / len(split))
        return jnp.repeat(jnp.exp(draws), shape[axis_at] // blocks).reshape((-1,) + (1,) * (len(shape) - axis_at - 1))

    loudness = one(*split[0])
    for cut in split[1:]:
        loudness = loudness * one(*cut)
    return loudness


def routed_block(stream_key, own, number, rows, number_of, top, bound, slope):
    ranking = jax.random.permutation(stream_key, number_of)
    crowded, ordinary = shares(number_of, rows * top, bound, slope, True), shares(number_of, rows * top, bound, slope, False)
    places = jnp.arange(number_of)

    def named(tallies, offset_by):
        used = int((tallies > 0).sum())
        fixed = max(1, used // 4)
        shifted = fixed + (places - fixed + offset_by * (used - fixed)) % max(1, number_of - fixed)
        return jnp.zeros((number_of,), jnp.int32).at[ranking[jnp.where(places < fixed, places, shifted)]].set(jnp.asarray(tallies, jnp.int32))

    tallies = jnp.where(number % 4 == 0, named(crowded, number // 4), named(ordinary, number - number // 4 - 1))
    mixed = jax.random.permutation(jax.random.fold_in(own, 3), number_of)
    giver, taker = mixed[0:number_of // 2 * 2:2], mixed[1:number_of // 2 * 2:2]
    margin = jnp.minimum(tallies[giver] - 1, bound - tallies[taker]) // 2
    margin = jnp.where((giver == ranking[0]) | (taker == ranking[0]) | (tallies[taker] == 0), 0, jnp.maximum(margin, 0))
    shifted = jax.random.randint(jax.random.fold_in(own, 4), (number_of // 2,), 0, 1 << 20) % (margin + 1)
    tallies = tallies.at[giver].add(-shifted).at[taker].add(shifted)
    labels = jnp.searchsorted(jnp.cumsum(tallies), jnp.arange(rows * top), side="right").astype(jnp.int32)
    grid = labels.reshape(top, rows).T
    grid = grid[jax.random.permutation(jax.random.fold_in(own, 1), rows)]
    offset_by = jax.random.randint(jax.random.fold_in(own, 2), (rows, 1), 0, top)
    return jnp.take_along_axis(grid, (jnp.arange(top)[None, :] + offset_by) % top, axis=1)


def shares(number_of, total, reach, slope, full):
    weights = [(1 << 20) // math.isqrt(grade ** slope) + 1 for grade in range(1, number_of + 1)]
    largest = reach if full else min(reach, max(-(-total // number_of), total * weights[0] // sum(weights)))
    least = 1 if total - largest >= number_of - 1 else 0
    counts, spare = [largest] + [least] * (number_of - 1), total - largest - least * (number_of - 1)
    while spare > 0:
        free = [i for i in range(1, number_of) if counts[i] < largest] or [i for i in range(1, number_of) if counts[i] < reach]
        mass, left = sum([weights[i] for i in free]), spare
        for i in free:
            more = min(reach - counts[i], max(1, left * weights[i] // mass), spare)
            counts[i] = counts[i] + more
            spare = spare - more
    return np.array(counts)


def scatter_about(own_key, shape, scale, bound, split=(), held_as=jnp.bfloat16):
    level = levels(own_key, shape, split, -0.22, 0.18) if split else 1.0
    entries = jax.random.normal(own_key, shape, jnp.float32) * scale * level
    return jnp.minimum(jnp.maximum(entries, -bound), bound).astype(held_as)


def setup_inputs(seed: int = 0) -> dict:
    splits = jax.random.split(jax.random.key(seed), 6)
    rows = scatter_about(splits[0], (SECTIONS, TOKENS, D), 1.0, 6.0, ((0, 2), (1, 16)))
    route_ids_keys = jax.random.split(jax.random.fold_in(splits[1], 1), SECTIONS * TOKENS // TOK_DEV)
    route_ids_turns = jax.random.permutation(jax.random.fold_in(splits[1], 3), SECTIONS * TOKENS // TOK_DEV)
    route_ids = jax.vmap(lambda own, number: routed_block(jax.random.fold_in(splits[1], 2), own, number, TOK_DEV, EXPERTS, TOP, CAP, 2))(route_ids_keys, route_ids_turns).reshape((SECTIONS, TOKENS, TOP))
    route_weights = jnp.clip(jnp.exp(math.log(1.0) - 2.3025851 * jax.random.uniform(splits[2], (SECTIONS, TOKENS, TOP), jnp.float32) ** levels(splits[2], (SECTIONS, TOKENS, TOP), ((0, 2), (1, 16)), -0.2, 0.2)), 0.1, 1.0)
    w_gate_up = scatter_about(splits[3], (SECTIONS, D, 2 * EXPERTS * FF), D ** -0.5, 0.09375, ((0, 2), (2, 16)))
    w_down = scatter_about(splits[4], (SECTIONS, EXPERTS * FF, D), FF ** -0.5, 0.1875, ((0, 2), (1, 16)))
    return dict(rows=rows, route_ids=route_ids, route_weights=route_weights, w_gate_up=w_gate_up, w_down=w_down)


def slots_of(ids_block):
    onehot = (ids_block[..., None] == jnp.arange(EXPERTS, dtype=jnp.int32)).astype(jnp.int32)
    before = jnp.cumsum(onehot, axis=1) - onehot
    return jnp.sum(before * onehot, axis=2).astype(jnp.int32)


def section_layer(tokens, ids, weights, gate_up, down):
    sources = N_EXPERT
    pairs = TOK_DEV * TOP
    ids_block = ids.reshape(sources, pairs).astype(jnp.int32)
    slot = slots_of(ids_block)
    source = jnp.arange(sources, dtype=jnp.int32)[:, None]
    pair_index = jnp.arange(sources * pairs, dtype=jnp.int32).reshape(sources, pairs)
    place = ((ids_block * sources + source) * CAP + slot).reshape(-1).astype(jnp.int32)
    table = jnp.zeros((EXPERTS * sources * CAP,), jnp.int32).at[place].set(pair_index.reshape(-1))
    table = table.reshape(EXPERTS, sources * CAP)
    gate_up_all = jnp.moveaxis(gate_up.reshape(D, EXPERTS, SHARDS, 2, FH), 1, 0)
    down_all = down.reshape(EXPERTS, SHARDS, FH, D)

    def one_expert(packed):
        index_rows, w_in, w_out = packed
        picked = tokens[(index_rows // TOP).astype(jnp.int32)]
        total = jnp.zeros((picked.shape[0], D), jnp.float32)
        for shard in range(SHARDS):
            gate = jnp.dot(picked, w_in[:, shard, 0], preferred_element_type=jnp.float32)
            upper = jnp.dot(picked, w_in[:, shard, 1], preferred_element_type=jnp.float32)
            active = (jax.nn.silu(gate) * upper).astype(jnp.bfloat16)
            part = jnp.dot(active, w_out[shard], preferred_element_type=jnp.float32).astype(jnp.bfloat16)
            part = lax.optimization_barrier(part)
            total = total + part.astype(jnp.float32)
        return lax.optimization_barrier(total.astype(jnp.bfloat16))

    outputs = lax.map(one_expert, (table, gate_up_all, down_all))
    pair_out = outputs.reshape(-1, D)[place].astype(jnp.float32)
    pair_out = pair_out * weights.reshape(-1)[:, None].astype(jnp.float32)
    return jnp.sum(pair_out.reshape(TOKENS, TOP, D), axis=1).astype(jnp.bfloat16)


def reference(rows, route_ids, route_weights, w_gate_up, w_down):
    layers = [section_layer(rows[s], route_ids[s], route_weights[s], w_gate_up[s], w_down[s]) for s in range(SECTIONS)]
    return jnp.stack([layers[(s - 1) % SECTIONS] for s in range(SECTIONS)])
```

```python
import jax
import jax.numpy as jnp
from jax import lax
from jax.sharding import PartitionSpec as P


def passed_along(shard, axis, by):
    length = lax.axis_size(axis)
    return lax.ppermute(shard, axis, [(i, (i + by) % length) for i in range(length)])


def by_slots(rows, route_ids, route_weights, w_gate_up, w_down):
    devices = lax.axis_size("expert")
    experts = devices // 2
    tokens = rows[0]
    tok_count, width = tokens.shape
    top_count = route_ids.shape[2]
    choices_flat = route_ids[0].reshape(-1)
    capacity = max(2, 2 * tok_count * top_count // experts)
    onehot = (choices_flat[:, None] == jnp.arange(experts, dtype=jnp.int32)[None, :]).astype(
        jnp.int32
    )
    before = jnp.cumsum(onehot, axis=0) - onehot
    slot = jnp.sum(before * onehot, axis=1)
    place = slot * experts + choices_flat
    slot_total = experts * capacity
    picker = (place[None, :] == jnp.arange(slot_total, dtype=jnp.int32)[:, None]).astype(
        jnp.bfloat16
    )
    token_pairs = jnp.repeat(tokens, top_count, axis=0)
    packed = jnp.dot(picker, token_pairs, preferred_element_type=jnp.float32).astype(jnp.bfloat16)
    w_in = w_gate_up[0]
    w_out = w_down[0]
    hidden = w_out.shape[0]
    outgoing = jnp.broadcast_to(
        packed.reshape(capacity, experts, 1, width), (capacity, experts, 2, width)
    )
    outgoing = outgoing.reshape(capacity, devices, width)
    block = lax.all_to_all(outgoing, "expert", split_axis=1, concat_axis=1, tiled=True)
    flat = block.reshape(-1, width)
    both = jnp.dot(flat, w_in, preferred_element_type=jnp.float32)
    active = (jax.nn.silu(both[:, :hidden]) * both[:, hidden:]).astype(jnp.bfloat16)
    result = jnp.dot(active, w_out, preferred_element_type=jnp.float32)
    partial_out = result.reshape(block.shape[0], block.shape[1], width).astype(jnp.bfloat16)
    returned = lax.all_to_all(partial_out, "expert", split_axis=1, concat_axis=1, tiled=True)
    returned = returned.reshape(capacity, experts, 2, width).astype(jnp.float32)
    expert_out = jnp.sum(returned, axis=2).astype(jnp.bfloat16).reshape(slot_total, width)
    pair_out = expert_out[place].astype(jnp.float32) * route_weights[0].reshape(-1)[:, None]
    layer_out = jnp.sum(pair_out.reshape(tok_count, top_count, width), axis=1).astype(jnp.bfloat16)
    return passed_along(layer_out, "section", 1)[None]


def by_gather(rows, route_ids, route_weights, w_gate_up, w_down):
    devices = lax.axis_size("expert")
    experts = devices // 2
    mine = lax.axis_index("expert") // 2
    tokens = rows[0]
    w_in = w_gate_up[0]
    w_out = w_down[0]
    hidden = w_out.shape[0]
    chosen = route_ids[0][:, :, None] == jnp.arange(experts, dtype=jnp.int32)
    scale = jnp.sum(jnp.where(chosen, route_weights[0][:, :, None], 0.0), axis=1)
    every_scale = lax.all_gather(scale, "expert", axis=0, tiled=True)
    own_scale = lax.dynamic_index_in_dim(every_scale, mine, axis=1, keepdims=True)
    every = lax.all_gather(tokens, "expert", axis=0, tiled=True)
    both = jnp.dot(every, w_in, preferred_element_type=jnp.float32)
    active = (jax.nn.silu(both[:, :hidden]) * both[:, hidden:]).astype(jnp.bfloat16)
    result = jnp.dot(active, w_out, preferred_element_type=jnp.float32)
    part = (result * own_scale).astype(jnp.bfloat16)
    layer_out = lax.psum_scatter(part, "expert", scatter_dimension=0, tiled=True)
    return passed_along(layer_out, "section", 1)[None]


def per_device(rows, route_ids, route_weights, w_gate_up, w_down):
    experts = lax.axis_size("expert") // 2
    tok_count = rows.shape[1]
    capacity = max(2, 2 * tok_count * route_ids.shape[2] // experts)
    plan = by_gather if tok_count <= 2 * capacity else by_slots
    return plan(rows, route_ids, route_weights, w_gate_up, w_down)


def solution(mesh):
    in_specs = (
        P("section", "expert", None),
        P("section", "expert", None),
        P("section", "expert", None),
        P("section", None, "expert"),
        P("section", "expert", None),
    )
    out_specs = P("section", "expert", None)
    return jax.shard_map(
        per_device, mesh=mesh, in_specs=in_specs, out_specs=out_specs, check_vma=False
    )
```

```python
import jax
import jax.numpy as jnp
from jax import lax
from jax.experimental import pallas as pl
from jax.experimental.pallas import tpu as pltpu
from jax.sharding import PartitionSpec as P


def passed_along(shard, axis, by):
    length = lax.axis_size(axis)
    return lax.ppermute(shard, axis, [(i, (i + by) % length) for i in range(length)])


def by_slots(rows, route_ids, route_weights, w_gate_up, w_down):
    devices = lax.axis_size("expert")
    experts = devices // 2
    tokens = rows[0]
    tok_count, width = tokens.shape
    top_count = route_ids.shape[2]
    choices_flat = route_ids[0].reshape(-1)
    capacity = max(2, 2 * tok_count * top_count // experts)
    onehot = (choices_flat[:, None] == jnp.arange(experts, dtype=jnp.int32)[None, :]).astype(
        jnp.int32
    )
    before = jnp.cumsum(onehot, axis=0) - onehot
    slot = jnp.sum(before * onehot, axis=1)
    place = slot * experts + choices_flat
    slot_total = experts * capacity
    picker = (place[None, :] == jnp.arange(slot_total, dtype=jnp.int32)[:, None]).astype(
        jnp.bfloat16
    )
    token_pairs = jnp.repeat(tokens, top_count, axis=0)
    packed = jnp.dot(picker, token_pairs, preferred_element_type=jnp.float32).astype(jnp.bfloat16)
    w_in = w_gate_up[0]
    w_out = w_down[0]
    hidden = w_out.shape[0]
    outgoing = jnp.broadcast_to(
        packed.reshape(capacity, experts, 1, width), (capacity, experts, 2, width)
    )
    outgoing = outgoing.reshape(capacity, devices, width)
    block = lax.all_to_all(outgoing, "expert", split_axis=1, concat_axis=1, tiled=True)
    flat = block.reshape(-1, width)
    both = jnp.dot(flat, w_in, preferred_element_type=jnp.float32)
    active = (jax.nn.silu(both[:, :hidden]) * both[:, hidden:]).astype(jnp.bfloat16)
    result = jnp.dot(active, w_out, preferred_element_type=jnp.float32)
    partial_out = result.reshape(block.shape[0], block.shape[1], width).astype(jnp.bfloat16)
    returned = lax.all_to_all(partial_out, "expert", split_axis=1, concat_axis=1, tiled=True)
    returned = returned.reshape(capacity, experts, 2, width).astype(jnp.float32)
    expert_out = jnp.sum(returned, axis=2).astype(jnp.bfloat16).reshape(slot_total, width)
    pair_out = expert_out[place].astype(jnp.float32) * route_weights[0].reshape(-1)[:, None]
    layer_out = jnp.sum(pair_out.reshape(tok_count, top_count, width), axis=1).astype(jnp.bfloat16)
    return passed_along(layer_out, "section", 1)[None]


def pack_kernel(chip, ids, weights, tokens, *outs):
    blocks, mixing = outs[:-1], outs[-1]
    experts = len(blocks)
    capacity, _ = blocks[0].shape
    top_count, tok_count = ids.shape
    away = ids[...] ^ chip[0]
    partner = lax.broadcasted_iota(jnp.int32, (experts, tok_count), 0)
    named = jnp.zeros((experts, tok_count), jnp.float32)
    scale = jnp.zeros((experts, tok_count), jnp.float32)
    for k in range(top_count):
        hit = away[k : k + 1, :] == partner
        named = named + jnp.where(hit, 1.0, 0.0)
        scale = scale + jnp.where(hit, weights[k : k + 1, :], 0.0)
    square = (tok_count, tok_count)
    earlier = lax.broadcasted_iota(jnp.int32, square, 0) < lax.broadcasted_iota(jnp.int32, square, 1)
    rank = jnp.dot(
        named.astype(jnp.bfloat16),
        jnp.where(earlier, 1.0, 0.0).astype(jnp.bfloat16),
        preferred_element_type=jnp.float32,
    )
    rank = jnp.where(named > 0.5, rank, -1.0)
    slot = lax.broadcasted_iota(jnp.int32, (capacity, tok_count), 0).astype(jnp.float32)
    picks, scales = [], []
    for r in range(experts):
        hit = rank[r : r + 1, :] == slot
        picks.append(jnp.where(hit, 1.0, 0.0))
        scales.append(jnp.where(hit, scale[r : r + 1, :], 0.0))
    pick = jnp.concatenate(picks, axis=0).astype(jnp.bfloat16)
    packed = jnp.dot(pick, tokens[...], preferred_element_type=jnp.float32).astype(jnp.bfloat16)
    for r in range(experts):
        blocks[r][...] = packed[r * capacity : (r + 1) * capacity]
    left = jnp.concatenate(scales, axis=0)
    slots = experts * capacity
    same = lax.broadcasted_iota(jnp.int32, (slots, slots), 0) == lax.broadcasted_iota(
        jnp.int32, (slots, slots), 1
    )
    unit = jnp.where(same, 1.0, 0.0).astype(jnp.bfloat16)
    for part in range(3):
        piece = left.astype(jnp.bfloat16)
        left = left - piece.astype(jnp.float32)
        turned = lax.dot_general(
            piece, unit, (((0,), (0,)), ((), ())), preferred_element_type=jnp.float32
        )
        mixing[part * tok_count : (part + 1) * tok_count, :] = turned.astype(jnp.bfloat16)


def pack(chip, ids, weights, tokens, experts, capacity):
    tok_count, width = tokens.shape
    vmem = pl.BlockSpec(memory_space=pltpu.VMEM)
    return pl.pallas_call(
        pack_kernel,
        out_shape=[jax.ShapeDtypeStruct((capacity, width), jnp.bfloat16)] * experts
        + [jax.ShapeDtypeStruct((3 * tok_count, experts * capacity), jnp.bfloat16)],
        in_specs=[pl.BlockSpec(memory_space=pltpu.SMEM), vmem, vmem, vmem],
        out_specs=[vmem] * (experts + 1),
        compiler_params=pltpu.CompilerParams(vmem_limit_bytes=12 << 20),
        name="pack",
    )(chip, ids, weights, tokens)


def combine_kernel(mixing, *refs):
    blocks, out = refs[:-1], refs[-1]
    tok_count = out.shape[0]
    slots = jnp.concatenate([block[...] for block in blocks], axis=0)
    mixed = jnp.dot(mixing[...], slots, preferred_element_type=jnp.float32)
    total = mixed[2 * tok_count :] + mixed[tok_count : 2 * tok_count] + mixed[:tok_count]
    out[...] = total.astype(out.dtype)


def combine(mixing, blocks):
    tok_count = mixing.shape[0] // 3
    vmem = pl.BlockSpec(memory_space=pltpu.VMEM)
    return pl.pallas_call(
        combine_kernel,
        out_shape=jax.ShapeDtypeStruct((tok_count, blocks[0].shape[1]), jnp.bfloat16),
        in_specs=[vmem] * (1 + len(blocks)),
        out_specs=vmem,
        compiler_params=pltpu.CompilerParams(vmem_limit_bytes=12 << 20),
        name="combine",
    )(mixing, *blocks)


def sent(shard, sections, experts, section_step, chip_xor):
    pairs = []
    for s in range(sections):
        for e in range(experts):
            for core in range(2):
                target = ((s + section_step) % sections) * experts + (e ^ chip_xor)
                pairs.append(((s * experts + e) * 2 + core, target * 2 + core))
    return lax.ppermute(shard, ("section", "expert"), pairs)


def by_direct(rows, route_ids, route_weights, w_gate_up, w_down):
    sections = lax.axis_size("section")
    devices = lax.axis_size("expert")
    experts = devices // 2
    tokens = rows[0]
    tok_count, width = tokens.shape
    top_count = route_ids.shape[2]
    capacity = max(2, 2 * tok_count * top_count // experts)
    chip = lax.axis_index("expert") // 2
    swap = [(i, i ^ 1) for i in range(devices)]
    halves = [(w_gate_up[0], w_down[0])]
    halves.append(tuple(lax.ppermute(w, "expert", swap) for w in halves[0]))
    hidden = w_down.shape[1]
    packed = pack(
        chip.reshape(1).astype(jnp.int32), route_ids[0].T, route_weights[0].T, tokens, experts, capacity
    )
    blocks, mixing = packed[:-1], packed[-1]
    half = experts // 2
    first = [r for r in range(experts) if (r & half) and not (r & (half // 2))]
    second = [r for r in range(experts) if (r & half) and (r & (half // 2))]
    near = [r for r in range(half)]
    groups = [first + near[: half // 2], second + near[half // 2 :]]
    arrived = {0: blocks[0]}
    for r in first + second + near[half // 2 :] + near[1 : half // 2]:
        arrived[r] = sent(blocks[r], sections, experts, 0, r)
    mixing = sent(mixing, sections, experts, 1, 0)
    back = {}
    for group in groups:
        held = jnp.concatenate([arrived[r] for r in group], axis=0)
        total = jnp.zeros((held.shape[0], width), jnp.float32)
        for w_in, w_out in halves:
            both = jnp.dot(held, w_in, preferred_element_type=jnp.float32)
            active = (jax.nn.silu(both[:, :hidden]) * both[:, hidden:]).astype(jnp.bfloat16)
            total = total + jnp.dot(active, w_out, preferred_element_type=jnp.float32)
        total = total.astype(jnp.bfloat16)
        for at, r in enumerate(group):
            piece = total[at * capacity : (at + 1) * capacity]
            back[r] = sent(piece, sections, experts, 1, r)
    return combine(mixing, [back[r] for r in range(experts)])[None]


def per_device(rows, route_ids, route_weights, w_gate_up, w_down):
    experts = lax.axis_size("expert") // 2
    plan = by_direct if experts in (4, 8) else by_slots
    return plan(rows, route_ids, route_weights, w_gate_up, w_down)


def solution(mesh):
    in_specs = (
        P("section", "expert", None),
        P("section", "expert", None),
        P("section", "expert", None),
        P("section", None, "expert"),
        P("section", "expert", None),
    )
    out_specs = P("section", "expert", None)
    return jax.shard_map(
        per_device, mesh=mesh, in_specs=in_specs, out_specs=out_specs, check_vma=False
    )
```

```python
import jax
import jax.numpy as jnp
from jax import lax
from jax.experimental import pallas as pl
from jax.experimental.pallas import tpu as pltpu
from jax.sharding import PartitionSpec as P


def passed_along(shard, axis, by):
    length = lax.axis_size(axis)
    return lax.ppermute(shard, axis, [(i, (i + by) % length) for i in range(length)])


def by_slots(rows, route_ids, route_weights, w_gate_up, w_down):
    devices = lax.axis_size("expert")
    experts = devices // 2
    tokens = rows[0]
    tok_count, width = tokens.shape
    top_count = route_ids.shape[2]
    choices_flat = route_ids[0].reshape(-1)
    capacity = max(2, 2 * tok_count * top_count // experts)
    onehot = (choices_flat[:, None] == jnp.arange(experts, dtype=jnp.int32)[None, :]).astype(
        jnp.int32
    )
    before = jnp.cumsum(onehot, axis=0) - onehot
    slot = jnp.sum(before * onehot, axis=1)
    place = slot * experts + choices_flat
    slot_total = experts * capacity
    picker = (place[None, :] == jnp.arange(slot_total, dtype=jnp.int32)[:, None]).astype(
        jnp.bfloat16
    )
    token_pairs = jnp.repeat(tokens, top_count, axis=0)
    packed = jnp.dot(picker, token_pairs, preferred_element_type=jnp.float32).astype(jnp.bfloat16)
    w_in = w_gate_up[0]
    w_out = w_down[0]
    hidden = w_out.shape[0]
    outgoing = jnp.broadcast_to(
        packed.reshape(capacity, experts, 1, width), (capacity, experts, 2, width)
    )
    outgoing = outgoing.reshape(capacity, devices, width)
    block = lax.all_to_all(outgoing, "expert", split_axis=1, concat_axis=1, tiled=True)
    flat = block.reshape(-1, width)
    both = jnp.dot(flat, w_in, preferred_element_type=jnp.float32)
    active = (jax.nn.silu(both[:, :hidden]) * both[:, hidden:]).astype(jnp.bfloat16)
    result = jnp.dot(active, w_out, preferred_element_type=jnp.float32)
    partial_out = result.reshape(block.shape[0], block.shape[1], width).astype(jnp.bfloat16)
    returned = lax.all_to_all(partial_out, "expert", split_axis=1, concat_axis=1, tiled=True)
    returned = returned.reshape(capacity, experts, 2, width).astype(jnp.float32)
    expert_out = jnp.sum(returned, axis=2).astype(jnp.bfloat16).reshape(slot_total, width)
    pair_out = expert_out[place].astype(jnp.float32) * route_weights[0].reshape(-1)[:, None]
    layer_out = jnp.sum(pair_out.reshape(tok_count, top_count, width), axis=1).astype(jnp.bfloat16)
    return passed_along(layer_out, "section", 1)[None]


RING = (0, 1, 3, 2)


def on_ring(place):
    return place ^ (place >> 1)


def chosen_rows(codes, source, chip, capacity):
    tok_count = codes.shape[0]
    lane = lax.broadcasted_iota(jnp.int32, codes.shape, 1)
    wanted = [
        jnp.sum(jnp.where(lane == expert, codes, 0.0), axis=1, keepdims=True)
        for expert in (chip, chip ^ 1)
    ]
    slot = lax.broadcasted_iota(jnp.int32, (tok_count, 2 * capacity), 1)
    code = jnp.where(slot < capacity, slot + 1, slot + 1 - capacity).astype(jnp.float32)
    hit = jnp.where(slot < capacity, wanted[0], wanted[1]) == code
    pick = jnp.where(hit, 1.0, 0.0).astype(jnp.bfloat16)
    rows = lax.dot_general(
        pick, source, (((0,), (0,)), ((), ())), preferred_element_type=jnp.float32
    )
    return rows.astype(jnp.bfloat16)


def prepare_kernel(chip, ids_in, weights_in, rows_in, block, own, other, mixing, ids, weights, sems):
    tok_count, width = rows_in.shape
    top_count = ids.shape[0]
    capacity = own.shape[0]
    experts = mixing.shape[1] // capacity
    copies = [
        pltpu.make_async_copy(ids_in, ids, sems.at[0]),
        pltpu.make_async_copy(weights_in, weights, sems.at[1]),
        pltpu.make_async_copy(rows_in, block.at[:, pl.ds(0, width)], sems.at[2]),
    ]
    for copy in copies:
        copy.start()
    copies[0].wait()
    copies[1].wait()
    here = chip[0]
    expert = lax.broadcasted_iota(jnp.int32, (experts, tok_count), 0)
    square = (tok_count, tok_count)
    earlier = lax.broadcasted_iota(jnp.int32, square, 0) < lax.broadcasted_iota(jnp.int32, square, 1)
    named = jnp.zeros((experts, tok_count), jnp.float32)
    for k in range(top_count):
        named = named + jnp.where(ids[k : k + 1, :] == expert, 1.0, 0.0)
    rank = jnp.dot(
        named.astype(jnp.bfloat16),
        jnp.where(earlier, 1.0, 0.0).astype(jnp.bfloat16),
        preferred_element_type=jnp.float32,
    )
    code = jnp.where(named > 0.5, rank + 1.0, 0.0)
    lanes = block.shape[1] - width
    unit = jnp.where(
        lax.broadcasted_iota(jnp.int32, (experts, lanes), 0)
        == lax.broadcasted_iota(jnp.int32, (experts, lanes), 1),
        1.0,
        0.0,
    ).astype(jnp.bfloat16)
    codes = lax.dot_general(
        code.astype(jnp.bfloat16), unit, (((0,), (0,)), ((), ())), preferred_element_type=jnp.float32
    )
    block[:, width:] = codes.astype(jnp.bfloat16)
    slot = lax.broadcasted_iota(jnp.int32, (capacity, tok_count), 0).astype(jnp.float32)
    scales = []
    for at in range(experts):
        plane = on_ring((on_ring(here >> 1) + (at >> 1)) & 3)
        which = (plane << 1) | ((here & 1) ^ (at & 1))
        scale = jnp.zeros((1, tok_count), jnp.float32)
        for k in range(top_count):
            scale = scale + jnp.where(ids[k : k + 1, :] == which, weights[k : k + 1, :], 0.0)
        place = jnp.sum(jnp.where(expert == which, code, 0.0), axis=0, keepdims=True) - 1.0
        scales.append(jnp.where(place == slot, scale, 0.0))
    left = jnp.concatenate(scales, axis=0)
    slots = experts * capacity
    unit = jnp.where(
        lax.broadcasted_iota(jnp.int32, (slots, slots), 0)
        == lax.broadcasted_iota(jnp.int32, (slots, slots), 1),
        1.0,
        0.0,
    ).astype(jnp.bfloat16)
    for part in range(3):
        piece = left.astype(jnp.bfloat16)
        left = left - piece.astype(jnp.float32)
        turned = lax.dot_general(
            piece, unit, (((0,), (0,)), ((), ())), preferred_element_type=jnp.float32
        )
        mixing[part * tok_count : (part + 1) * tok_count, :] = turned.astype(jnp.bfloat16)
    copies[2].wait()
    rows = chosen_rows(codes, block[:, :width], here, capacity)
    own[...] = rows[:capacity]
    other[...] = rows[capacity:]


def prepare(chip, ids, weights, tokens, experts, capacity, lanes):
    tok_count, width = tokens.shape
    vmem = pl.BlockSpec(memory_space=pltpu.VMEM)
    anywhere = pl.BlockSpec(memory_space=pl.ANY)
    half = jax.ShapeDtypeStruct((capacity, width), jnp.bfloat16)
    return pl.pallas_call(
        prepare_kernel,
        out_shape=[
            jax.ShapeDtypeStruct((tok_count, width + lanes), jnp.bfloat16),
            half,
            half,
            jax.ShapeDtypeStruct((3 * tok_count, experts * capacity), jnp.bfloat16),
        ],
        in_specs=[pl.BlockSpec(memory_space=pltpu.SMEM), anywhere, anywhere, anywhere],
        out_specs=[vmem] * 4,
        scratch_shapes=[
            pltpu.VMEM(ids.shape, ids.dtype),
            pltpu.VMEM(weights.shape, weights.dtype),
            pltpu.SemaphoreType.DMA((3,)),
        ],
        compiler_params=pltpu.CompilerParams(vmem_limit_bytes=60 << 20),
        name="prepare",
    )(chip, ids, weights, tokens)


def choose_kernel(chip, block, own, other):
    capacity, width = own.shape
    codes = block[:, width:].astype(jnp.float32)
    rows = chosen_rows(codes, block[:, :width], chip[0], capacity)
    own[...] = rows[:capacity]
    other[...] = rows[capacity:]


def choose(chip, block, capacity, width):
    vmem = pl.BlockSpec(memory_space=pltpu.VMEM)
    half = jax.ShapeDtypeStruct((capacity, width), jnp.bfloat16)
    return pl.pallas_call(
        choose_kernel,
        out_shape=[half, half],
        in_specs=[pl.BlockSpec(memory_space=pltpu.SMEM), vmem],
        out_specs=[vmem] * 2,
        compiler_params=pltpu.CompilerParams(vmem_limit_bytes=12 << 20),
        name="choose",
    )(chip, block)


def load_kernel(source, target, sem):
    copy = pltpu.make_async_copy(source, target, sem)
    copy.start()
    copy.wait()


def loaded(weights):
    return pl.pallas_call(
        load_kernel,
        out_shape=pltpu.VMEM(weights.shape, weights.dtype),
        in_specs=[pl.BlockSpec(memory_space=pltpu.HBM)],
        out_specs=pl.BlockSpec(memory_space=pltpu.VMEM),
        scratch_shapes=[pltpu.SemaphoreType.DMA],
        compiler_params=pltpu.CompilerParams(vmem_limit_bytes=9 << 20),
        cost_estimate=pl.CostEstimate(
            flops=0, bytes_accessed=2 * weights.size * weights.dtype.itemsize, transcendentals=0
        ),
        name="loaded",
    )(weights)


def combine_kernel(mixing, *refs):
    blocks, out = refs[:-1], refs[-1]
    tok_count = out.shape[0]
    slots = jnp.concatenate([block[...] for block in blocks], axis=0)
    mixed = jnp.dot(mixing[...], slots, preferred_element_type=jnp.float32)
    total = mixed[2 * tok_count :] + mixed[tok_count : 2 * tok_count] + mixed[:tok_count]
    out[...] = total.astype(out.dtype)


def combine(mixing, blocks):
    tok_count = mixing.shape[0] // 3
    vmem = pl.BlockSpec(memory_space=pltpu.VMEM)
    return pl.pallas_call(
        combine_kernel,
        out_shape=jax.ShapeDtypeStruct((tok_count, blocks[0].shape[1]), jnp.bfloat16),
        in_specs=[vmem] * (1 + len(blocks)),
        out_specs=vmem,
        compiler_params=pltpu.CompilerParams(vmem_limit_bytes=12 << 20),
        name="combine",
    )(mixing, *blocks)


def sent(shard, sections, section_step, ring_step, flip):
    planes = len(RING)
    pairs = []
    for s in range(sections):
        for z in range(planes):
            for y in range(2):
                for core in range(2):
                    plane = RING[(RING.index(z) + ring_step) % planes]
                    target = (((s + section_step) % sections) * planes + plane) * 2 + (y ^ flip)
                    pairs.append((((s * planes + z) * 2 + y) * 2 + core, target * 2 + core))
    return lax.ppermute(shard, ("section", "expert"), pairs)


def after(value, other):
    return lax.optimization_barrier((value, other))[0]


def by_ring(rows, route_ids, route_weights, w_gate_up, w_down):
    sections = lax.axis_size("section")
    devices = lax.axis_size("expert")
    experts = devices // 2
    planes = len(RING)
    tokens = rows[0]
    tok_count, width = tokens.shape
    top_count = route_ids.shape[2]
    capacity = max(2, 2 * tok_count * top_count // experts)
    chip = (lax.axis_index("expert") // 2).reshape(1).astype(jnp.int32)
    swap = [(i, i ^ 1) for i in range(devices)]
    w_in, w_out = w_gate_up[0], w_down[0]
    hidden = w_out.shape[0]
    far_in = lax.ppermute(w_in, "expert", swap)
    far_out = lax.ppermute(w_out, "expert", swap)
    block, own, other, mixing = prepare(
        chip, route_ids[0].T, route_weights[0].T, tokens, experts, capacity, 128
    )
    held = [(own, sent(other, sections, 0, 0, 1))]
    near = (loaded(after(w_in, mixing)), loaded(after(w_out, mixing)))
    mixing = sent(mixing, sections, 1, 0, 0)

    def start(group):
        slots = jnp.concatenate([part for step in group for part in held[step]], axis=0)
        return slots, one_half(slots, *near)

    def finish(group, slots, total):
        total = (total + one_half(slots, *far)).astype(jnp.bfloat16)
        pieces = total.reshape(-1, capacity, width)
        back = [
            sent(pieces[2 * at + flip], sections, 1, -step, flip)
            for at, step in enumerate(group)
            for flip in range(2)
        ]
        return total, back

    def one_half(slots, first, second):
        both = jnp.dot(slots, first, preferred_element_type=jnp.float32)
        active = (jax.nn.silu(both[:, :hidden]) * both[:, hidden:]).astype(jnp.bfloat16)
        return jnp.dot(active, second, preferred_element_type=jnp.float32)

    block = sent(block, sections, 0, 1, 0)
    own, other = choose(chip, block, capacity, width)
    held.append((own, sent(other, sections, 0, 0, 1)))
    slots, total = start((0, 1))
    block = sent(block, sections, 0, 1, 0)
    own, other = choose(chip, block, capacity, width)
    held.append((own, sent(other, sections, 0, 0, 1)))
    far = (loaded(after(far_in, own)), loaded(after(far_out, own)))
    block = sent(block, sections, 0, 1, 0)
    total, back = finish((0, 1), slots, total)
    own, other = choose(chip, after(block, total), capacity, width)
    held[2] = after(held[2], own)
    held.append((own, sent(other, sections, 0, 0, 1)))
    total, more = finish((2,), *start((2,)))
    held[3], back = lax.optimization_barrier((held[3], back))
    back = back + more + finish((3,), *start((3,)))[1]
    return combine(mixing, back)[None]


def per_device(rows, route_ids, route_weights, w_gate_up, w_down):
    experts = lax.axis_size("expert") // 2
    plan = by_ring if experts == 2 * len(RING) else by_slots
    return plan(rows, route_ids, route_weights, w_gate_up, w_down)


def solution(mesh):
    in_specs = (
        P("section", "expert", None),
        P("section", "expert", None),
        P("section", "expert", None),
        P("section", None, "expert"),
        P("section", "expert", None),
    )
    out_specs = P("section", "expert", None)
    return jax.shard_map(
        per_device, mesh=mesh, in_specs=in_specs, out_specs=out_specs, check_vma=False
    )
```

```python
import functools

import jax
import jax.numpy as jnp
from jax import lax
from jax.experimental import pallas as pl
from jax.experimental.pallas import tpu as pltpu
from jax.sharding import PartitionSpec as P


def passed_along(shard, axis, by):
    length = lax.axis_size(axis)
    return lax.ppermute(shard, axis, [(i, (i + by) % length) for i in range(length)])


def by_slots(rows, route_ids, route_weights, w_gate_up, w_down):
    devices = lax.axis_size("expert")
    experts = devices // 2
    tokens = rows[0]
    tok_count, width = tokens.shape
    top_count = route_ids.shape[2]
    choices_flat = route_ids[0].reshape(-1)
    capacity = max(2, 2 * tok_count * top_count // experts)
    onehot = (choices_flat[:, None] == jnp.arange(experts, dtype=jnp.int32)[None, :]).astype(
        jnp.int32
    )
    before = jnp.cumsum(onehot, axis=0) - onehot
    slot = jnp.sum(before * onehot, axis=1)
    place = slot * experts + choices_flat
    slot_total = experts * capacity
    picker = (place[None, :] == jnp.arange(slot_total, dtype=jnp.int32)[:, None]).astype(
        jnp.bfloat16
    )
    token_pairs = jnp.repeat(tokens, top_count, axis=0)
    packed = jnp.dot(picker, token_pairs, preferred_element_type=jnp.float32).astype(jnp.bfloat16)
    w_in = w_gate_up[0]
    w_out = w_down[0]
    hidden = w_out.shape[0]
    outgoing = jnp.broadcast_to(
        packed.reshape(capacity, experts, 1, width), (capacity, experts, 2, width)
    )
    outgoing = outgoing.reshape(capacity, devices, width)
    block = lax.all_to_all(outgoing, "expert", split_axis=1, concat_axis=1, tiled=True)
    flat = block.reshape(-1, width)
    both = jnp.dot(flat, w_in, preferred_element_type=jnp.float32)
    active = (jax.nn.silu(both[:, :hidden]) * both[:, hidden:]).astype(jnp.bfloat16)
    result = jnp.dot(active, w_out, preferred_element_type=jnp.float32)
    partial_out = result.reshape(block.shape[0], block.shape[1], width).astype(jnp.bfloat16)
    returned = lax.all_to_all(partial_out, "expert", split_axis=1, concat_axis=1, tiled=True)
    returned = returned.reshape(capacity, experts, 2, width).astype(jnp.float32)
    expert_out = jnp.sum(returned, axis=2).astype(jnp.bfloat16).reshape(slot_total, width)
    pair_out = expert_out[place].astype(jnp.float32) * route_weights[0].reshape(-1)[:, None]
    layer_out = jnp.sum(pair_out.reshape(tok_count, top_count, width), axis=1).astype(jnp.bfloat16)
    return passed_along(layer_out, "section", 1)[None]


RING = (0, 1, 3, 2)
LANES = 128
TOKEN_LANE = 64


def on_ring(place):
    return place ^ (place >> 1)


def chip_at(chip, steps, flip):
    return (on_ring((on_ring(chip >> 1) + steps) & 3) << 1) | ((chip & 1) ^ flip)


def iota(shape, axis):
    return lax.broadcasted_iota(jnp.int32, shape, axis)


def ones_where(condition):
    return jnp.where(condition, 1.0, 0.0).astype(jnp.bfloat16)


def across(left, right):
    return lax.dot_general(left, right, (((0,), (0,)), ((), ())), preferred_element_type=jnp.float32)


def local_call(kernel, name, out_shape, in_specs, operands, scratch=(), limit=12, flops=0, moved=0):
    vmem = pl.BlockSpec(memory_space=pltpu.VMEM)
    return pl.pallas_call(
        kernel,
        out_shape=out_shape,
        in_specs=[vmem if spec is None else pl.BlockSpec(memory_space=spec) for spec in in_specs],
        out_specs=jax.tree.map(lambda _: vmem, out_shape),
        scratch_shapes=list(scratch),
        compiler_params=pltpu.CompilerParams(vmem_limit_bytes=limit << 20),
        cost_estimate=pl.CostEstimate(flops=flops, bytes_accessed=moved, transcendentals=0),
        name=name,
    )(*operands)


def prepare_kernel(ids_in, weights_in, rows_in, block, ids, weights, sems):
    tok_count, width = rows_in.shape
    top_count = ids.shape[0]
    experts = 2 * len(RING)
    copies = [
        pltpu.make_async_copy(ids_in, ids, sems.at[0]),
        pltpu.make_async_copy(weights_in, weights, sems.at[1]),
        pltpu.make_async_copy(rows_in, block.at[:, pl.ds(0, width)], sems.at[2]),
    ]
    for copy in copies:
        copy.start()
    square = (tok_count, tok_count)
    earlier = ones_where(iota(square, 0) < iota(square, 1))
    expert = iota((experts, tok_count), 0)
    unit = ones_where(iota((4 * experts, LANES), 0) == iota((4 * experts, LANES), 1))
    token = ones_where(iota((tok_count, LANES), 0) + TOKEN_LANE == iota((tok_count, LANES), 1))
    copies[0].wait()
    copies[1].wait()
    named = jnp.zeros((experts, tok_count), jnp.float32)
    scale = jnp.zeros((experts, tok_count), jnp.float32)
    for k in range(top_count):
        hit = ids[k : k + 1, :] == expert
        named = named + jnp.where(hit, 1.0, 0.0)
        scale = scale + jnp.where(hit, weights[k : k + 1, :], 0.0)
    rank = jnp.dot(named.astype(jnp.bfloat16), earlier, preferred_element_type=jnp.float32)
    notes = [jnp.where(named > 0.5, rank + 1.0, 0.0)]
    for _ in range(3):
        piece = scale.astype(jnp.bfloat16).astype(jnp.float32)
        scale = scale - piece
        notes.append(piece)
    notes = across(jnp.concatenate(notes, axis=0).astype(jnp.bfloat16), unit)
    block[:, width:] = notes.astype(jnp.bfloat16) + token
    copies[2].wait()


def prepare(ids, weights, tokens):
    tok_count, width = tokens.shape
    return local_call(
        prepare_kernel,
        "prepare",
        jax.ShapeDtypeStruct((tok_count, width + LANES), jnp.bfloat16),
        [pl.ANY] * 3,
        (ids, weights, tokens),
        [
            pltpu.VMEM(ids.shape, ids.dtype),
            pltpu.VMEM(weights.shape, weights.dtype),
            pltpu.SemaphoreType.DMA((3,)),
        ],
        limit=60,
    )


def choose_kernel(places, capacity, chip, block, *refs):
    refs = list(refs)
    first = refs.pop(0) if refs[-1].shape[0] == 2 * capacity else None
    tok_count = block.shape[0]
    notes = block[:, -LANES:].astype(jnp.float32)
    lane = iota(notes.shape, 1)
    slot = iota((tok_count, len(places) * capacity), 1)
    code = jnp.zeros(slot.shape, jnp.float32)
    order = jnp.zeros(slot.shape, jnp.int32)
    for at, (steps, flip) in enumerate(places):
        wanted = chip_at(chip[0], steps, flip)
        column = jnp.sum(jnp.where(lane == wanted, notes, 0.0), axis=1, keepdims=True)
        code = jnp.where(slot >= at * capacity, column, code)
        order = jnp.where(slot >= at * capacity, slot + 1 - at * capacity, order)
    rows = across(ones_where(code == order.astype(jnp.float32)), block[...]).astype(jnp.bfloat16)
    for at in range(len(places)):
        piece = rows[at * capacity : (at + 1) * capacity]
        if first is not None and at == len(places) - 1:
            refs[at][:capacity] = first[...]
            refs[at][capacity:] = piece
        else:
            refs[at][...] = piece


def choose(chip, block, capacity, places, first=None):
    out_shape = [jax.ShapeDtypeStruct((capacity, block.shape[1]), jnp.bfloat16) for _ in places]
    operands = (chip, block)
    if first is not None:
        out_shape[-1] = jax.ShapeDtypeStruct((2 * capacity, block.shape[1]), jnp.bfloat16)
        operands = operands + (first,)
    return local_call(
        functools.partial(choose_kernel, places, capacity),
        "choose",
        out_shape,
        [pltpu.SMEM] + [None] * (len(operands) - 1),
        operands,
    )


def load_kernel(source, target, sem):
    copy = pltpu.make_async_copy(source, target, sem)
    copy.start()
    copy.wait()


def loaded(weights):
    return local_call(
        load_kernel,
        "loaded",
        pltpu.VMEM(weights.shape, weights.dtype),
        [pl.ANY],
        (weights,),
        [pltpu.SemaphoreType.DMA],
        limit=9,
        moved=2 * weights.size * weights.dtype.itemsize,
    )


def gated(both):
    hidden = both.shape[1] // 2
    gate = both[:, :hidden]
    return (gate / (1.0 + jnp.exp(-gate)) * both[:, hidden:]).astype(jnp.bfloat16)


def near_kernel(*refs):
    pieces, (first, second, slots, total) = refs[:-4], refs[-4:]
    start = 0
    for piece in pieces:
        slots[start : start + piece.shape[0]] = piece[...]
        start += piece.shape[0]
    width = total.shape[1]
    both = jnp.dot(slots[:, :width], first[...], preferred_element_type=jnp.float32)
    total[...] = jnp.dot(gated(both), second[...], preferred_element_type=jnp.float32)


def near_pass(pieces, weights):
    count = sum(piece.shape[0] for piece in pieces)
    full = pieces[0].shape[1]
    width = full - LANES
    return local_call(
        near_kernel,
        "near_pass",
        [
            jax.ShapeDtypeStruct((count, full), jnp.bfloat16),
            jax.ShapeDtypeStruct((count, width), jnp.float32),
        ],
        [None] * (len(pieces) + 2),
        (*pieces, *weights),
        moved=2 * sum(w.size for w in weights),
    )


def write_pieces(chip, slots, total, outs):
    width = total.shape[1]
    experts = 2 * len(RING)
    notes = slots[:, width:].astype(jnp.float32)
    lane = iota(notes.shape, 1)
    mine = (lane >= experts) & (lane < 4 * experts) & ((lane & (experts - 1)) == chip[0])
    scale = jnp.sum(jnp.where(mine, notes, 0.0), axis=1, keepdims=True)
    start = 0
    for out in outs:
        stop = start + out.shape[0]
        out[:, :width] = (total[start:stop] * scale[start:stop]).astype(jnp.bfloat16)
        out[:, width:] = slots[start:stop, width:]
        start = stop


def far_kernel(parts, chip, slots, total, first_in, second_in, *refs):
    outs, (first, second, both, sems) = refs[:-4], refs[-4:]
    width = total.shape[1]
    step = width // parts
    hidden = second.shape[0]
    copies = []
    for at in range(parts):
        place = pl.ds(at * step, step)
        copies.append(pltpu.make_async_copy(first_in.at[place], first.at[place], sems.at[at]))
    for at in range(2):
        place = pl.ds(at * (hidden // 2), hidden // 2)
        copies.append(
            pltpu.make_async_copy(second_in.at[place], second.at[place], sems.at[parts + at])
        )
    for copy in copies:
        copy.start()
    for at in range(parts):
        copies[at].wait()
        place = slice(at * step, (at + 1) * step)
        term = jnp.dot(slots[:, place], first[place], preferred_element_type=jnp.float32)
        both[...] = term if at == 0 else both[...] + term
    active = gated(both[...])
    for at in range(2):
        copies[parts + at].wait()
        place = slice(at * (hidden // 2), (at + 1) * (hidden // 2))
        total[...] += jnp.dot(active[:, place], second[place], preferred_element_type=jnp.float32)
    write_pieces(chip, slots, total, outs)


def far_body(parts, chip, slots, total_in, first_in, second_in, *refs):
    outs, (first, second, both, total, sems) = refs[:-5], refs[-5:]
    total[...] = total_in[...]
    far_kernel(parts, chip, slots, total, first_in, second_in, *outs, first, second, both, sems)


def far_pass(chip, slots, total, weights, capacity):
    count, full = slots.shape
    hidden = weights[1].shape[0]
    parts = 7
    piece = jax.ShapeDtypeStruct((capacity, full), jnp.bfloat16)
    outs = local_call(
        functools.partial(far_body, parts),
        "far_pass",
        [piece] * (count // capacity) + [pltpu.VMEM(w.shape, w.dtype) for w in weights],
        [pltpu.SMEM, None, None, pl.ANY, pl.ANY],
        (chip, slots, total, *weights),
        [
            pltpu.VMEM((count, 2 * hidden), jnp.float32),
            pltpu.VMEM(total.shape, jnp.float32),
            pltpu.SemaphoreType.DMA((parts + 2,)),
        ],
        limit=20,
        moved=2 * sum(w.size for w in weights),
    )
    return outs[:-2], outs[-2:]


def last_kernel(chip, *refs):
    pieces, weights, outs, (slots, total) = refs[:2], refs[2:6], refs[6:-2], refs[-2:]
    start = 0
    for piece in pieces:
        slots[start : start + piece.shape[0]] = piece[...]
        start += piece.shape[0]
    width = total.shape[1]
    for half in range(2):
        first, second = weights[2 * half : 2 * half + 2]
        both = jnp.dot(slots[:, :width], first[...], preferred_element_type=jnp.float32)
        term = jnp.dot(gated(both), second[...], preferred_element_type=jnp.float32)
        total[...] = term if half == 0 else total[...] + term
    write_pieces(chip, slots, total, outs)


def last_pass(chip, pieces, near, far):
    capacity, full = pieces[0].shape
    count = capacity * len(pieces)
    return local_call(
        last_kernel,
        "last_pass",
        [jax.ShapeDtypeStruct((capacity, full), jnp.bfloat16)] * len(pieces),
        [pltpu.SMEM] + [None] * (len(pieces) + 4),
        (chip, *pieces, *near, *far),
        [pltpu.VMEM((count, full), jnp.bfloat16), pltpu.VMEM((count, full - LANES), jnp.float32)],
        moved=2 * sum(w.size for w in (*near, *far)),
    )


def combine_kernel(*refs):
    blocks, out, slots = refs[:-2], refs[-2], refs[-1]
    tok_count, width = out.shape
    start = 0
    for block in blocks:
        slots[start : start + block.shape[0]] = block[...]
        start += block.shape[0]
    token = slots[:, width:]
    part = width // 7
    for at in range(7):
        place = slice(at * part, (at + 1) * part)
        mixed = across(token, slots[:, place])
        out[:, place] = mixed[TOKEN_LANE : TOKEN_LANE + tok_count].astype(out.dtype)


def combine(blocks, tok_count):
    capacity, full = blocks[0].shape
    return local_call(
        combine_kernel,
        "combine",
        jax.ShapeDtypeStruct((tok_count, full - LANES), jnp.bfloat16),
        [None] * len(blocks),
        tuple(blocks),
        [pltpu.VMEM((capacity * len(blocks), full), jnp.bfloat16)],
    )


def sent(shard, sections, section_step, ring_step, flip):
    planes = len(RING)
    pairs = []
    for s in range(sections):
        for z in range(planes):
            for y in range(2):
                for core in range(2):
                    plane = RING[(RING.index(z) + ring_step) % planes]
                    target = (((s + section_step) % sections) * planes + plane) * 2 + (y ^ flip)
                    pairs.append((((s * planes + z) * 2 + y) * 2 + core, target * 2 + core))
    return lax.ppermute(shard, ("section", "expert"), pairs)


def after(value, other):
    return lax.optimization_barrier((value, other))[0]


def by_ring(rows, route_ids, route_weights, w_gate_up, w_down):
    sections = lax.axis_size("section")
    devices = lax.axis_size("expert")
    experts = devices // 2
    tokens = rows[0]
    tok_count = tokens.shape[0]
    top_count = route_ids.shape[2]
    capacity = max(2, 2 * tok_count * top_count // experts)
    chip = (lax.axis_index("expert") // 2).reshape(1).astype(jnp.int32)
    swap = [(i, i ^ 1) for i in range(devices)]
    w_in, w_out = w_gate_up[0], w_down[0]
    far = (lax.ppermute(w_in, "expert", swap), lax.ppermute(w_out, "expert", swap))
    block = prepare(route_ids[0].T, route_weights[0].T, tokens)
    block1 = sent(block, sections, 0, 1, 0)
    own0, other0, back0, back1 = choose(chip, block, capacity, ((0, 0), (0, 1), (3, 0), (3, 1)))
    own3 = sent(back0, sections, 0, 3, 0)
    other3 = sent(back1, sections, 0, 3, 1)
    near = (loaded(after(w_in, back1)), loaded(after(w_out, back1)))
    block2 = sent(after(block1, near), sections, 0, 1, 0)
    own1, other = choose(chip, block1, capacity, ((0, 0), (0, 1)), other0)
    other01 = sent(after(other, (own3, other3)), sections, 0, 0, 1)
    own2, other = choose(chip, block2, capacity, ((0, 0), (0, 1)))
    other2 = sent(other, sections, 0, 0, 1)
    slots, total = near_pass((own1, own3, other3, own0, other01), near)
    pieces, far = far_pass(chip, slots, total, far, capacity)
    places = ((1, 0), (3, 0), (3, 1), (0, 0), (0, 1), (1, 1))
    back = [
        sent(piece, sections, 1, -steps, flip) for piece, (steps, flip) in zip(pieces, places)
    ]
    pieces = last_pass(chip, (own2, other2), near, far)
    back += [sent(piece, sections, 1, -2, flip) for flip, piece in enumerate(pieces)]
    return combine(back, tok_count)[None]


def per_device(rows, route_ids, route_weights, w_gate_up, w_down):
    experts = lax.axis_size("expert") // 2
    fits = experts == 2 * len(RING) and rows.shape[1] <= LANES - TOKEN_LANE
    plan = by_ring if fits else by_slots
    return plan(rows, route_ids, route_weights, w_gate_up, w_down)


def solution(mesh):
    in_specs = (
        P("section", "expert", None),
        P("section", "expert", None),
        P("section", "expert", None),
        P("section", None, "expert"),
        P("section", "expert", None),
    )
    out_specs = P("section", "expert", None)
    return jax.shard_map(
        per_device, mesh=mesh, in_specs=in_specs, out_specs=out_specs, check_vma=False
    )
```

```python
import functools

import jax
import jax.numpy as jnp
from jax import lax
from jax.experimental import pallas as pl
from jax.experimental.pallas import tpu as pltpu
from jax.sharding import PartitionSpec as P


def passed_along(shard, axis, by):
    length = lax.axis_size(axis)
    return lax.ppermute(shard, axis, [(i, (i + by) % length) for i in range(length)])


def by_slots(rows, route_ids, route_weights, w_gate_up, w_down):
    devices = lax.axis_size("expert")
    experts = devices // 2
    tokens = rows[0]
    tok_count, width = tokens.shape
    top_count = route_ids.shape[2]
    choices_flat = route_ids[0].reshape(-1)
    capacity = max(2, 2 * tok_count * top_count // experts)
    onehot = (choices_flat[:, None] == jnp.arange(experts, dtype=jnp.int32)[None, :]).astype(
        jnp.int32
    )
    before = jnp.cumsum(onehot, axis=0) - onehot
    slot = jnp.sum(before * onehot, axis=1)
    place = slot * experts + choices_flat
    slot_total = experts * capacity
    picker = (place[None, :] == jnp.arange(slot_total, dtype=jnp.int32)[:, None]).astype(
        jnp.bfloat16
    )
    token_pairs = jnp.repeat(tokens, top_count, axis=0)
    packed = jnp.dot(picker, token_pairs, preferred_element_type=jnp.float32).astype(jnp.bfloat16)
    w_in = w_gate_up[0]
    w_out = w_down[0]
    hidden = w_out.shape[0]
    outgoing = jnp.broadcast_to(
        packed.reshape(capacity, experts, 1, width), (capacity, experts, 2, width)
    )
    outgoing = outgoing.reshape(capacity, devices, width)
    block = lax.all_to_all(outgoing, "expert", split_axis=1, concat_axis=1, tiled=True)
    flat = block.reshape(-1, width)
    both = jnp.dot(flat, w_in, preferred_element_type=jnp.float32)
    active = (jax.nn.silu(both[:, :hidden]) * both[:, hidden:]).astype(jnp.bfloat16)
    result = jnp.dot(active, w_out, preferred_element_type=jnp.float32)
    partial_out = result.reshape(block.shape[0], block.shape[1], width).astype(jnp.bfloat16)
    returned = lax.all_to_all(partial_out, "expert", split_axis=1, concat_axis=1, tiled=True)
    returned = returned.reshape(capacity, experts, 2, width).astype(jnp.float32)
    expert_out = jnp.sum(returned, axis=2).astype(jnp.bfloat16).reshape(slot_total, width)
    pair_out = expert_out[place].astype(jnp.float32) * route_weights[0].reshape(-1)[:, None]
    layer_out = jnp.sum(pair_out.reshape(tok_count, top_count, width), axis=1).astype(jnp.bfloat16)
    return passed_along(layer_out, "section", 1)[None]


RING = (0, 1, 3, 2)
LANES = 128
TOKEN_LANE = 64


def on_ring(place):
    return place ^ (place >> 1)


def chip_at(chip, steps, flip):
    return (on_ring((on_ring(chip >> 1) + steps) & 3) << 1) | ((chip & 1) ^ flip)


def iota(shape, axis):
    return lax.broadcasted_iota(jnp.int32, shape, axis)


def ones_where(condition):
    return jnp.where(condition, 1.0, 0.0).astype(jnp.bfloat16)


def across(left, right):
    return lax.dot_general(left, right, (((0,), (0,)), ((), ())), preferred_element_type=jnp.float32)


def local_call(kernel, name, out_shape, in_specs, operands, scratch=(), limit=12, flops=0, moved=0):
    vmem = pl.BlockSpec(memory_space=pltpu.VMEM)
    return pl.pallas_call(
        kernel,
        out_shape=out_shape,
        in_specs=[vmem if spec is None else pl.BlockSpec(memory_space=spec) for spec in in_specs],
        out_specs=jax.tree.map(lambda _: vmem, out_shape),
        scratch_shapes=list(scratch),
        compiler_params=pltpu.CompilerParams(vmem_limit_bytes=limit << 20),
        cost_estimate=pl.CostEstimate(flops=flops, bytes_accessed=moved, transcendentals=0),
        name=name,
    )(*operands)


def prepare_kernel(ids_in, weights_in, rows_in, block, ids, weights, sems):
    tok_count, width = rows_in.shape
    top_count = ids.shape[0]
    experts = 2 * len(RING)
    copies = [
        pltpu.make_async_copy(ids_in, ids, sems.at[0]),
        pltpu.make_async_copy(weights_in, weights, sems.at[1]),
        pltpu.make_async_copy(rows_in, block.at[:, pl.ds(0, width)], sems.at[2]),
    ]
    for copy in copies:
        copy.start()
    square = (tok_count, tok_count)
    earlier = ones_where(iota(square, 0) < iota(square, 1))
    expert = iota((experts, tok_count), 0)
    unit = ones_where(iota((4 * experts, LANES), 0) == iota((4 * experts, LANES), 1))
    token = ones_where(iota((tok_count, LANES), 0) + TOKEN_LANE == iota((tok_count, LANES), 1))
    copies[0].wait()
    copies[1].wait()
    named = jnp.zeros((experts, tok_count), jnp.float32)
    scale = jnp.zeros((experts, tok_count), jnp.float32)
    for k in range(top_count):
        hit = ids[k : k + 1, :] == expert
        named = named + jnp.where(hit, 1.0, 0.0)
        scale = scale + jnp.where(hit, weights[k : k + 1, :], 0.0)
    rank = jnp.dot(named.astype(jnp.bfloat16), earlier, preferred_element_type=jnp.float32)
    notes = [jnp.where(named > 0.5, rank + 1.0, 0.0)]
    for _ in range(3):
        piece = scale.astype(jnp.bfloat16).astype(jnp.float32)
        scale = scale - piece
        notes.append(piece)
    notes = across(jnp.concatenate(notes, axis=0).astype(jnp.bfloat16), unit)
    block[:, width:] = notes.astype(jnp.bfloat16) + token
    copies[2].wait()


def prepare(ids, weights, tokens):
    tok_count, width = tokens.shape
    return local_call(
        prepare_kernel,
        "prepare",
        pltpu.VMEM((tok_count, width + LANES), jnp.bfloat16),
        [pl.ANY] * 3,
        (ids, weights, tokens),
        [
            pltpu.VMEM(ids.shape, ids.dtype),
            pltpu.VMEM(weights.shape, weights.dtype),
            pltpu.SemaphoreType.DMA((3,)),
        ],
        limit=60,
    )


def choose_kernel(places, capacity, chip, block, *refs):
    refs = list(refs)
    first = refs.pop(0) if refs[-1].shape[0] == 2 * capacity else None
    tok_count = block.shape[0]
    notes = block[:, -LANES:].astype(jnp.float32)
    lane = iota(notes.shape, 1)
    slot = iota((tok_count, len(places) * capacity), 1)
    code = jnp.zeros(slot.shape, jnp.float32)
    order = jnp.zeros(slot.shape, jnp.int32)
    for at, (steps, flip) in enumerate(places):
        wanted = chip_at(chip[0], steps, flip)
        column = jnp.sum(jnp.where(lane == wanted, notes, 0.0), axis=1, keepdims=True)
        code = jnp.where(slot >= at * capacity, column, code)
        order = jnp.where(slot >= at * capacity, slot + 1 - at * capacity, order)
    rows = across(ones_where(code == order.astype(jnp.float32)), block[...]).astype(jnp.bfloat16)
    for at in range(len(places)):
        piece = rows[at * capacity : (at + 1) * capacity]
        if first is not None and at == len(places) - 1:
            refs[at][:capacity] = first[...]
            refs[at][capacity:] = piece
        else:
            refs[at][...] = piece


def choose(chip, block, capacity, places, first=None):
    out_shape = [jax.ShapeDtypeStruct((capacity, block.shape[1]), jnp.bfloat16) for _ in places]
    operands = (chip, block)
    if first is not None:
        out_shape[-1] = jax.ShapeDtypeStruct((2 * capacity, block.shape[1]), jnp.bfloat16)
        operands = operands + (first,)
    return local_call(
        functools.partial(choose_kernel, places, capacity),
        "choose",
        out_shape,
        [pltpu.SMEM] + [None] * (len(operands) - 1),
        operands,
    )


def load_kernel(source, target, sem):
    copy = pltpu.make_async_copy(source, target, sem)
    copy.start()
    copy.wait()


def loaded(weights):
    return local_call(
        load_kernel,
        "loaded",
        pltpu.VMEM(weights.shape, weights.dtype),
        [pl.ANY],
        (weights,),
        [pltpu.SemaphoreType.DMA],
        limit=9,
        moved=2 * weights.size * weights.dtype.itemsize,
    )


def gated(both):
    hidden = both.shape[1] // 2
    gate = both[:, :hidden]
    return (gate / (1.0 + jnp.exp(-gate)) * both[:, hidden:]).astype(jnp.bfloat16)


def write_pieces(chip, slots, total, outs):
    width = total.shape[1]
    experts = 2 * len(RING)
    notes = slots[:, width:].astype(jnp.float32)
    lane = iota(notes.shape, 1)
    mine = (lane >= experts) & (lane < 4 * experts) & ((lane & (experts - 1)) == chip[0])
    scale = jnp.sum(jnp.where(mine, notes, 0.0), axis=1, keepdims=True)
    start = 0
    for out in outs:
        stop = start + out.shape[0]
        out[:, :width] = (total[start:stop] * scale[start:stop]).astype(jnp.bfloat16)
        out[:, width:] = slots[start:stop, width:]
        start = stop


def expert_kernel(chip, *refs):
    outs, (slots, total) = refs[-10:-2], refs[-2:]
    pieces, weights = refs[:-14], refs[-14:-10]
    start = 0
    for piece in pieces:
        slots[start : start + piece.shape[0]] = piece[...]
        start += piece.shape[0]
    width = total.shape[1]
    for half in range(2):
        first, second = weights[2 * half : 2 * half + 2]
        both = jnp.dot(slots[:, :width], first[...], preferred_element_type=jnp.float32)
        term = jnp.dot(gated(both), second[...], preferred_element_type=jnp.float32)
        total[...] = term if half == 0 else total[...] + term
    write_pieces(chip, slots, total, outs)


def expert_pass(chip, pieces, near, far, capacity):
    full = pieces[0].shape[1]
    count = capacity * 2 * len(RING)
    return local_call(
        expert_kernel,
        "expert_pass",
        [jax.ShapeDtypeStruct((capacity, full), jnp.bfloat16)] * (2 * len(RING)),
        [pltpu.SMEM] + [None] * (len(pieces) + 4),
        (chip, *pieces, *near, *far),
        [pltpu.VMEM((count, full), jnp.bfloat16), pltpu.VMEM((count, full - LANES), jnp.float32)],
        moved=2 * sum(w.size for w in (*near, *far)),
    )


def combine_kernel(*refs):
    blocks, out, slots = refs[:-2], refs[-2], refs[-1]
    tok_count, width = out.shape
    start = 0
    for block in blocks:
        slots[start : start + block.shape[0]] = block[...]
        start += block.shape[0]
    token = slots[:, width:]
    part = width // 7
    for at in range(7):
        place = slice(at * part, (at + 1) * part)
        mixed = across(token, slots[:, place])
        out[:, place] = mixed[TOKEN_LANE : TOKEN_LANE + tok_count].astype(out.dtype)


def combine(blocks, tok_count):
    capacity, full = blocks[0].shape
    return local_call(
        combine_kernel,
        "combine",
        jax.ShapeDtypeStruct((tok_count, full - LANES), jnp.bfloat16),
        [None] * len(blocks),
        tuple(blocks),
        [pltpu.VMEM((capacity * len(blocks), full), jnp.bfloat16)],
    )


def sent(shard, sections, section_step, ring_step, flip):
    planes = len(RING)
    pairs = []
    for s in range(sections):
        for z in range(planes):
            for y in range(2):
                for core in range(2):
                    plane = RING[(RING.index(z) + ring_step) % planes]
                    target = (((s + section_step) % sections) * planes + plane) * 2 + (y ^ flip)
                    pairs.append((((s * planes + z) * 2 + y) * 2 + core, target * 2 + core))
    return lax.ppermute(shard, ("section", "expert"), pairs)


def after(value, other):
    return lax.optimization_barrier((value, other))[0]


def by_ring(rows, route_ids, route_weights, w_gate_up, w_down):
    sections = lax.axis_size("section")
    devices = lax.axis_size("expert")
    experts = devices // 2
    tokens = rows[0]
    tok_count = tokens.shape[0]
    top_count = route_ids.shape[2]
    capacity = max(2, 2 * tok_count * top_count // experts)
    chip = (lax.axis_index("expert") // 2).reshape(1).astype(jnp.int32)
    swap = [(i, i ^ 1) for i in range(devices)]
    w_in, w_out = w_gate_up[0], w_down[0]
    far_out = lax.ppermute(w_out, "expert", swap)
    far_in = lax.ppermute(w_in, "expert", swap)
    block = prepare(route_ids[0].T, route_weights[0].T, tokens)
    block1 = sent(block, sections, 0, 1, 0)
    own0, other0, back0, back1 = choose(chip, block, capacity, ((0, 0), (0, 1), (3, 0), (3, 1)))
    own3 = sent(back0, sections, 0, 3, 0)
    other3 = sent(back1, sections, 0, 3, 1)
    near = (loaded(after(w_in, back1)), loaded(after(w_out, back1)))
    far_out = loaded(after(far_out, near))
    block1 = after(block1, far_out)
    own1, on0, on1, other = choose(chip, block1, capacity, ((0, 0), (1, 0), (1, 1), (0, 1)), other0)
    own2 = sent(on0, sections, 0, 1, 0)
    other2 = sent(on1, sections, 0, 1, 1)
    other01 = sent(other, sections, 0, 0, 1)
    far = (loaded(after(far_in, (own3, other3, other))), far_out)
    places = ((2, 0), (2, 1), (1, 0), (3, 0), (3, 1), (0, 0), (0, 1), (1, 1))
    pieces = (own2, other2, own1, own3, other3, own0, other01)
    pieces = expert_pass(chip, pieces, near, far, capacity)
    back = [
        sent(piece, sections, 1, -steps, flip) for piece, (steps, flip) in zip(pieces, places)
    ]
    return combine(back, tok_count)[None]


def per_device(rows, route_ids, route_weights, w_gate_up, w_down):
    experts = lax.axis_size("expert") // 2
    fits = experts == 2 * len(RING) and rows.shape[1] <= LANES - TOKEN_LANE
    plan = by_ring if fits else by_slots
    return plan(rows, route_ids, route_weights, w_gate_up, w_down)


def solution(mesh):
    in_specs = (
        P("section", "expert", None),
        P("section", "expert", None),
        P("section", "expert", None),
        P("section", None, "expert"),
        P("section", "expert", None),
    )
    out_specs = P("section", "expert", None)
    return jax.shard_map(
        per_device, mesh=mesh, in_specs=in_specs, out_specs=out_specs, check_vma=False
    )
```

```python
import functools

import jax
import jax.numpy as jnp
from jax import lax
from jax.experimental import pallas as pl
from jax.experimental.pallas import tpu as pltpu
from jax.sharding import PartitionSpec as P


def passed_along(shard, axis, by):
    length = lax.axis_size(axis)
    return lax.ppermute(shard, axis, [(i, (i + by) % length) for i in range(length)])


def by_slots(rows, route_ids, route_weights, w_gate_up, w_down):
    devices = lax.axis_size("expert")
    experts = devices // 2
    tokens = rows[0]
    tok_count, width = tokens.shape
    top_count = route_ids.shape[2]
    choices_flat = route_ids[0].reshape(-1)
    capacity = max(2, 2 * tok_count * top_count // experts)
    onehot = (choices_flat[:, None] == jnp.arange(experts, dtype=jnp.int32)[None, :]).astype(
        jnp.int32
    )
    before = jnp.cumsum(onehot, axis=0) - onehot
    slot = jnp.sum(before * onehot, axis=1)
    place = slot * experts + choices_flat
    slot_total = experts * capacity
    picker = (place[None, :] == jnp.arange(slot_total, dtype=jnp.int32)[:, None]).astype(
        jnp.bfloat16
    )
    token_pairs = jnp.repeat(tokens, top_count, axis=0)
    packed = jnp.dot(picker, token_pairs, preferred_element_type=jnp.float32).astype(jnp.bfloat16)
    w_in = w_gate_up[0]
    w_out = w_down[0]
    hidden = w_out.shape[0]
    outgoing = jnp.broadcast_to(
        packed.reshape(capacity, experts, 1, width), (capacity, experts, 2, width)
    )
    outgoing = outgoing.reshape(capacity, devices, width)
    block = lax.all_to_all(outgoing, "expert", split_axis=1, concat_axis=1, tiled=True)
    flat = block.reshape(-1, width)
    both = jnp.dot(flat, w_in, preferred_element_type=jnp.float32)
    active = (jax.nn.silu(both[:, :hidden]) * both[:, hidden:]).astype(jnp.bfloat16)
    result = jnp.dot(active, w_out, preferred_element_type=jnp.float32)
    partial_out = result.reshape(block.shape[0], block.shape[1], width).astype(jnp.bfloat16)
    returned = lax.all_to_all(partial_out, "expert", split_axis=1, concat_axis=1, tiled=True)
    returned = returned.reshape(capacity, experts, 2, width).astype(jnp.float32)
    expert_out = jnp.sum(returned, axis=2).astype(jnp.bfloat16).reshape(slot_total, width)
    pair_out = expert_out[place].astype(jnp.float32) * route_weights[0].reshape(-1)[:, None]
    layer_out = jnp.sum(pair_out.reshape(tok_count, top_count, width), axis=1).astype(jnp.bfloat16)
    return passed_along(layer_out, "section", 1)[None]


LANES = 128
TOKEN_LANE = 64


def iota(shape, axis):
    return lax.broadcasted_iota(jnp.int32, shape, axis)


def ones_where(condition):
    return jnp.where(condition, 1.0, 0.0).astype(jnp.bfloat16)


def across(left, right):
    return lax.dot_general(left, right, (((0,), (0,)), ((), ())), preferred_element_type=jnp.float32)


def local_call(kernel, name, out_shape, in_specs, operands, scratch=(), limit=12, flops=0, moved=0):
    vmem = pl.BlockSpec(memory_space=pltpu.VMEM)
    return pl.pallas_call(
        kernel,
        out_shape=out_shape,
        in_specs=[vmem if spec is None else pl.BlockSpec(memory_space=spec) for spec in in_specs],
        out_specs=jax.tree.map(lambda _: vmem, out_shape),
        scratch_shapes=list(scratch),
        compiler_params=pltpu.CompilerParams(vmem_limit_bytes=limit << 20),
        cost_estimate=pl.CostEstimate(flops=flops, bytes_accessed=moved, transcendentals=0),
        name=name,
    )(*operands)


def pack_kernel(experts, ids_in, weights_in, rows_in, packed, ids, weights, block, sems):
    tok_count, width = rows_in.shape
    top_count = ids.shape[0]
    capacity = packed.shape[0] // experts
    copies = [
        pltpu.make_async_copy(ids_in, ids, sems.at[0]),
        pltpu.make_async_copy(weights_in, weights, sems.at[1]),
        pltpu.make_async_copy(rows_in, block.at[:, pl.ds(0, width)], sems.at[2]),
    ]
    for copy in copies:
        copy.start()
    square = (tok_count, tok_count)
    earlier = ones_where(iota(square, 0) < iota(square, 1))
    expert = iota((experts, tok_count), 0)
    unit = ones_where(iota((4 * experts, LANES), 0) == iota((4 * experts, LANES), 1))
    token = ones_where(iota((tok_count, LANES), 0) + TOKEN_LANE == iota((tok_count, LANES), 1))
    slot = iota((capacity, tok_count), 0).astype(jnp.float32)
    copies[0].wait()
    copies[1].wait()
    named = jnp.zeros((experts, tok_count), jnp.float32)
    scale = jnp.zeros((experts, tok_count), jnp.float32)
    for k in range(top_count):
        hit = ids[k : k + 1, :] == expert
        named = named + jnp.where(hit, 1.0, 0.0)
        scale = scale + jnp.where(hit, weights[k : k + 1, :], 0.0)
    rank = jnp.dot(named.astype(jnp.bfloat16), earlier, preferred_element_type=jnp.float32)
    rank = jnp.where(named > 0.5, rank, -1.0)
    pick = [jnp.where(rank[e : e + 1, :] == slot, 1.0, 0.0) for e in range(experts)]
    pick = jnp.concatenate(pick, axis=0).astype(jnp.bfloat16)
    notes = [jnp.zeros_like(scale)]
    for _ in range(3):
        piece = scale.astype(jnp.bfloat16).astype(jnp.float32)
        scale = scale - piece
        notes.append(piece)
    notes = across(jnp.concatenate(notes, axis=0).astype(jnp.bfloat16), unit)
    block[:, width:] = notes.astype(jnp.bfloat16) + token
    copies[2].wait()
    rows = jnp.dot(pick, block[...], preferred_element_type=jnp.float32)
    packed[...] = rows.astype(jnp.bfloat16)


def pack(ids, weights, tokens, experts, capacity):
    tok_count, width = tokens.shape
    return local_call(
        functools.partial(pack_kernel, experts),
        "pack",
        pltpu.VMEM((experts * capacity, width + LANES), jnp.bfloat16),
        [pl.ANY] * 3,
        tuple(pltpu.with_memory_space_constraint(x, pltpu.HBM) for x in (ids, weights, tokens)),
        [
            pltpu.VMEM(ids.shape, ids.dtype),
            pltpu.VMEM(weights.shape, weights.dtype),
            pltpu.VMEM((tok_count, width + LANES), jnp.bfloat16),
            pltpu.SemaphoreType.DMA((3,)),
        ],
        limit=8,
    )


def gated(both):
    hidden = both.shape[1] // 2
    gate = both[:, :hidden]
    return (gate / (1.0 + jnp.exp(-gate)) * both[:, hidden:]).astype(jnp.bfloat16)


def expert_kernel(sections, slots, far_in, far_out, near_in, near_out, *refs):
    apart, (close, total, w_in, w_out, sems) = refs[:-5], refs[-5:]
    copies = [
        pltpu.make_async_copy(near_in, w_in, sems.at[0]),
        pltpu.make_async_copy(near_out, w_out, sems.at[1]),
    ]
    for copy in copies:
        copy.start()
    chip, section = lax.axis_index("expert") >> 1, lax.axis_index("section")
    width = total.shape[1]
    half = len(apart)
    experts = 2 * half
    capacity = slots.shape[0] // experts
    both = jnp.dot(slots[:, :width], far_in[...], preferred_element_type=jnp.float32)
    total[...] = jnp.dot(gated(both), far_out[...], preferred_element_type=jnp.float32)
    copies[0].wait()
    both = jnp.dot(slots[:, :width], w_in[...], preferred_element_type=jnp.float32)
    copies[1].wait()
    total[...] += jnp.dot(gated(both), w_out[...], preferred_element_type=jnp.float32)
    notes = slots[:, width:].astype(jnp.float32)
    lane = iota(notes.shape, 1)
    mine = (lane >= experts) & (lane < 4 * experts) & ((lane & (experts - 1)) == chip)
    total[...] = total[...] * jnp.sum(jnp.where(mine, notes, 0.0), axis=1, keepdims=True)

    def rows_of(source, count):
        return pl.ds(pl.multiple_of(source * capacity, capacity), count * capacity)

    for r, out in enumerate(apart):
        rows = rows_of(chip ^ (half + r), 1)
        out[:, :width] = total[rows, :].astype(jnp.bfloat16)
        out[:, width:] = slots[rows, width:]
    close[...] = jnp.zeros(close.shape, close.dtype)
    rows = rows_of(chip & half, half)
    target = jnp.where(section == sections - 1, 0, section + 1) * half
    to = rows_of(target, half)
    close[to, :width] = total[rows, :].astype(jnp.bfloat16)
    close[to, width:] = slots[rows, width:]


def expert_pass(slots, far, near, capacity, experts, sections):
    count, full = slots.shape
    half = experts // 2
    piece = jax.ShapeDtypeStruct((capacity, full), jnp.bfloat16)
    close = jax.ShapeDtypeStruct((sections * half * capacity, full), jnp.bfloat16)
    outs = local_call(
        functools.partial(expert_kernel, sections),
        "expert_pass",
        [piece] * half + [close],
        [None] * 3 + [pl.ANY] * 2,
        (slots, *far, *(pltpu.with_memory_space_constraint(w, pltpu.HBM) for w in near)),
        [
            pltpu.VMEM((count, full - LANES), jnp.float32),
            *(pltpu.VMEM(w.shape, w.dtype) for w in near),
            pltpu.SemaphoreType.DMA((2,)),
        ],
        limit=40,
        moved=2 * sum(w.size for w in (*far, *near)),
    )
    return outs[:-1], outs[-1]


def combine_kernel(*refs):
    blocks, out, slots = refs[:-2], refs[-2], refs[-1]
    tok_count, width = out.shape
    start = 0
    for block in blocks:
        slots[start : start + block.shape[0]] = block[...]
        start += block.shape[0]
    token = slots[:, width:]
    part = width // 7
    for at in range(7):
        place = slice(at * part, (at + 1) * part)
        mixed = across(token, slots[:, place])[TOKEN_LANE : TOKEN_LANE + tok_count]
        out[:, place] = mixed.astype(out.dtype)


def combine(blocks, tok_count):
    full = blocks[0].shape[1]
    count = sum(block.shape[0] for block in blocks)
    return local_call(
        combine_kernel,
        "combine",
        jax.ShapeDtypeStruct((tok_count, full - LANES), jnp.bfloat16),
        [None] * len(blocks),
        tuple(blocks),
        [pltpu.VMEM((count, full), jnp.bfloat16)],
    )


def by_chips(rows, route_ids, route_weights, w_gate_up, w_down):
    sections = lax.axis_size("section")
    devices = lax.axis_size("expert")
    experts = devices // 2
    half = experts // 2
    tokens = rows[0]
    tok_count = tokens.shape[0]
    top_count = route_ids.shape[2]
    capacity = max(2, 2 * tok_count * top_count // experts)
    swap = [(i, i ^ 1) for i in range(devices)]
    w_in, w_out = w_gate_up[0], w_down[0]
    far = [lax.ppermute(w, "expert", swap) for w in (w_out, w_in)]
    packed = pack(route_ids[0].T, route_weights[0].T, tokens, experts, capacity)
    groups = [[2 * e + core for e in range(experts)] for core in range(2)]
    slots = lax.all_to_all(packed, "expert", 0, 0, axis_index_groups=groups, tiled=True)
    pieces, close = expert_pass(
        slots, (far[1], far[0]), (w_in, w_out), capacity, experts, sections
    )
    axes = ("section", "expert")
    back = []
    for r, piece in enumerate(pieces):
        pairs = [
            (
                (s * experts + e) * 2 + core,
                ((s + 1) % sections * experts + (e ^ (half + r))) * 2 + core,
            )
            for s in range(sections)
            for e in range(experts)
            for core in range(2)
        ]
        back.append(lax.ppermute(piece, axes, pairs))
    groups = [
        [(s * experts + e) * 2 + core for s in range(sections) for e in range(at, at + half)]
        for at in (0, half)
        for core in range(2)
    ]
    back.append(lax.all_to_all(close, axes, 0, 0, axis_index_groups=groups, tiled=True))
    return combine(back, tok_count)[None]


def per_device(rows, route_ids, route_weights, w_gate_up, w_down):
    experts = lax.axis_size("expert") // 2
    fits = experts in (4, 8) and rows.shape[1] <= LANES - TOKEN_LANE
    plan = by_chips if fits else by_slots
    return plan(rows, route_ids, route_weights, w_gate_up, w_down)


def solution(mesh):
    in_specs = (
        P("section", "expert", None),
        P("section", "expert", None),
        P("section", "expert", None),
        P("section", None, "expert"),
        P("section", "expert", None),
    )
    out_specs = P("section", "expert", None)
    return jax.shard_map(
        per_device, mesh=mesh, in_specs=in_specs, out_specs=out_specs, check_vma=False
    )
```

```python
import functools

import jax
import jax.numpy as jnp
from jax import lax
from jax.experimental import pallas as pl
from jax.experimental.pallas import tpu as pltpu
from jax.sharding import PartitionSpec as P


def passed_along(shard, axis, by):
    length = lax.axis_size(axis)
    return lax.ppermute(shard, axis, [(i, (i + by) % length) for i in range(length)])


def by_slots(rows, route_ids, route_weights, w_gate_up, w_down):
    devices = lax.axis_size("expert")
    experts = devices // 2
    tokens = rows[0]
    tok_count, width = tokens.shape
    top_count = route_ids.shape[2]
    choices_flat = route_ids[0].reshape(-1)
    capacity = max(2, 2 * tok_count * top_count // experts)
    onehot = (choices_flat[:, None] == jnp.arange(experts, dtype=jnp.int32)[None, :]).astype(
        jnp.int32
    )
    before = jnp.cumsum(onehot, axis=0) - onehot
    slot = jnp.sum(before * onehot, axis=1)
    place = slot * experts + choices_flat
    slot_total = experts * capacity
    picker = (place[None, :] == jnp.arange(slot_total, dtype=jnp.int32)[:, None]).astype(
        jnp.bfloat16
    )
    token_pairs = jnp.repeat(tokens, top_count, axis=0)
    packed = jnp.dot(picker, token_pairs, preferred_element_type=jnp.float32).astype(jnp.bfloat16)
    w_in = w_gate_up[0]
    w_out = w_down[0]
    hidden = w_out.shape[0]
    outgoing = jnp.broadcast_to(
        packed.reshape(capacity, experts, 1, width), (capacity, experts, 2, width)
    )
    outgoing = outgoing.reshape(capacity, devices, width)
    block = lax.all_to_all(outgoing, "expert", split_axis=1, concat_axis=1, tiled=True)
    flat = block.reshape(-1, width)
    both = jnp.dot(flat, w_in, preferred_element_type=jnp.float32)
    active = (jax.nn.silu(both[:, :hidden]) * both[:, hidden:]).astype(jnp.bfloat16)
    result = jnp.dot(active, w_out, preferred_element_type=jnp.float32)
    partial_out = result.reshape(block.shape[0], block.shape[1], width).astype(jnp.bfloat16)
    returned = lax.all_to_all(partial_out, "expert", split_axis=1, concat_axis=1, tiled=True)
    returned = returned.reshape(capacity, experts, 2, width).astype(jnp.float32)
    expert_out = jnp.sum(returned, axis=2).astype(jnp.bfloat16).reshape(slot_total, width)
    pair_out = expert_out[place].astype(jnp.float32) * route_weights[0].reshape(-1)[:, None]
    layer_out = jnp.sum(pair_out.reshape(tok_count, top_count, width), axis=1).astype(jnp.bfloat16)
    return passed_along(layer_out, "section", 1)[None]


RING = (0, 1, 3, 2)
LANES = 128
TOKEN_LANE = 64


def on_ring(place):
    return place ^ (place >> 1)


def chip_at(chip, steps, flip):
    return (on_ring((on_ring(chip >> 1) + steps) & 3) << 1) | ((chip & 1) ^ flip)


def iota(shape, axis):
    return lax.broadcasted_iota(jnp.int32, shape, axis)


def ones_where(condition):
    return jnp.where(condition, 1.0, 0.0).astype(jnp.bfloat16)


def across(left, right):
    return lax.dot_general(left, right, (((0,), (0,)), ((), ())), preferred_element_type=jnp.float32)


def local_call(kernel, name, out_shape, in_specs, operands, scratch=(), limit=12, flops=0, moved=0):
    vmem = pl.BlockSpec(memory_space=pltpu.VMEM)
    return pl.pallas_call(
        kernel,
        out_shape=out_shape,
        in_specs=[vmem if spec is None else pl.BlockSpec(memory_space=spec) for spec in in_specs],
        out_specs=jax.tree.map(lambda _: vmem, out_shape),
        scratch_shapes=list(scratch),
        compiler_params=pltpu.CompilerParams(vmem_limit_bytes=limit << 20),
        cost_estimate=pl.CostEstimate(flops=flops, bytes_accessed=moved, transcendentals=0),
        name=name,
    )(*operands)


def prepare_kernel(ids_in, weights_in, rows_in, block, ids, weights, sems):
    tok_count, width = rows_in.shape
    top_count = ids.shape[0]
    experts = 2 * len(RING)
    copies = [
        pltpu.make_async_copy(ids_in, ids, sems.at[0]),
        pltpu.make_async_copy(weights_in, weights, sems.at[1]),
        pltpu.make_async_copy(rows_in, block.at[:, pl.ds(0, width)], sems.at[2]),
    ]
    for copy in copies:
        copy.start()
    square = (tok_count, tok_count)
    earlier = ones_where(iota(square, 0) < iota(square, 1))
    expert = iota((experts, tok_count), 0)
    unit = ones_where(iota((4 * experts, LANES), 0) == iota((4 * experts, LANES), 1))
    token = ones_where(iota((tok_count, LANES), 0) + TOKEN_LANE == iota((tok_count, LANES), 1))
    copies[0].wait()
    copies[1].wait()
    named = jnp.zeros((experts, tok_count), jnp.float32)
    scale = jnp.zeros((experts, tok_count), jnp.float32)
    for k in range(top_count):
        hit = ids[k : k + 1, :] == expert
        named = named + jnp.where(hit, 1.0, 0.0)
        scale = scale + jnp.where(hit, weights[k : k + 1, :], 0.0)
    rank = jnp.dot(named.astype(jnp.bfloat16), earlier, preferred_element_type=jnp.float32)
    notes = [jnp.where(named > 0.5, rank + 1.0, 0.0)]
    for _ in range(3):
        piece = scale.astype(jnp.bfloat16).astype(jnp.float32)
        scale = scale - piece
        notes.append(piece)
    notes = across(jnp.concatenate(notes, axis=0).astype(jnp.bfloat16), unit)
    block[:, width:] = notes.astype(jnp.bfloat16) + token
    copies[2].wait()


def prepare(ids, weights, tokens):
    tok_count, width = tokens.shape
    return local_call(
        prepare_kernel,
        "prepare",
        pltpu.VMEM((tok_count, width + LANES), jnp.bfloat16),
        [pl.ANY] * 3,
        tuple(pltpu.with_memory_space_constraint(x, pltpu.HBM) for x in (ids, weights, tokens)),
        [
            pltpu.VMEM(ids.shape, ids.dtype),
            pltpu.VMEM(weights.shape, weights.dtype),
            pltpu.SemaphoreType.DMA((3,)),
        ],
        limit=8,
    )


def choose_kernel(places, capacity, block, *refs):
    chip = lax.axis_index("expert") >> 1
    refs = list(refs)
    first = refs.pop(0) if refs[-1].shape[0] == 2 * capacity else None
    tok_count = block.shape[0]
    notes = block[:, -LANES:].astype(jnp.float32)
    lane = iota(notes.shape, 1)
    slot = iota((tok_count, len(places) * capacity), 1)
    code = jnp.zeros(slot.shape, jnp.float32)
    order = jnp.zeros(slot.shape, jnp.int32)
    for at, (steps, flip) in enumerate(places):
        wanted = chip_at(chip, steps, flip)
        column = jnp.sum(jnp.where(lane == wanted, notes, 0.0), axis=1, keepdims=True)
        code = jnp.where(slot >= at * capacity, column, code)
        order = jnp.where(slot >= at * capacity, slot + 1 - at * capacity, order)
    rows = across(ones_where(code == order.astype(jnp.float32)), block[...]).astype(jnp.bfloat16)
    for at in range(len(places)):
        piece = rows[at * capacity : (at + 1) * capacity]
        if first is not None and at == len(places) - 1:
            refs[at][:capacity] = first[...]
            refs[at][capacity:] = piece
        else:
            refs[at][...] = piece


def choose(block, capacity, places, first=None):
    out_shape = [jax.ShapeDtypeStruct((capacity, block.shape[1]), jnp.bfloat16) for _ in places]
    operands = (block,)
    if first is not None:
        out_shape[-1] = jax.ShapeDtypeStruct((2 * capacity, block.shape[1]), jnp.bfloat16)
        operands = operands + (first,)
    return local_call(
        functools.partial(choose_kernel, places, capacity),
        "choose",
        out_shape,
        [None] * len(operands),
        operands,
    )


def load_kernel(source, target, sem):
    copy = pltpu.make_async_copy(source, target, sem)
    copy.start()
    copy.wait()


def loaded(weights):
    return local_call(
        load_kernel,
        "loaded",
        pltpu.VMEM(weights.shape, weights.dtype),
        [pl.ANY],
        (weights,),
        [pltpu.SemaphoreType.DMA],
        limit=9,
        moved=2 * weights.size * weights.dtype.itemsize,
    )


def gated(both):
    hidden = both.shape[1] // 2
    gate = both[:, :hidden]
    return (gate / (1.0 + jnp.exp(-gate)) * both[:, hidden:]).astype(jnp.bfloat16)


def write_pieces(slots, total, outs):
    chip = lax.axis_index("expert") >> 1
    width = total.shape[1]
    experts = 2 * len(RING)
    notes = slots[:, width:].astype(jnp.float32)
    lane = iota(notes.shape, 1)
    mine = (lane >= experts) & (lane < 4 * experts) & ((lane & (experts - 1)) == chip)
    scale = jnp.sum(jnp.where(mine, notes, 0.0), axis=1, keepdims=True)
    start = 0
    for out in outs:
        stop = start + out.shape[0]
        out[:, :width] = (total[start:stop] * scale[start:stop]).astype(jnp.bfloat16)
        out[:, width:] = slots[start:stop, width:]
        start = stop


def expert_kernel(*refs):
    outs, (slots, total) = refs[-10:-2], refs[-2:]
    pieces, weights = refs[:-14], refs[-14:-10]
    start = 0
    for piece in pieces:
        slots[start : start + piece.shape[0]] = piece[...]
        start += piece.shape[0]
    width = total.shape[1]
    for half in range(2):
        first, second = weights[2 * half : 2 * half + 2]
        both = jnp.dot(slots[:, :width], first[...], preferred_element_type=jnp.float32)
        term = jnp.dot(gated(both), second[...], preferred_element_type=jnp.float32)
        total[...] = term if half == 0 else total[...] + term
    write_pieces(slots, total, outs)


def expert_pass(pieces, near, far, capacity):
    full = pieces[0].shape[1]
    count = capacity * 2 * len(RING)
    return local_call(
        expert_kernel,
        "expert_pass",
        [jax.ShapeDtypeStruct((capacity, full), jnp.bfloat16)] * (2 * len(RING)),
        [None] * (len(pieces) + 4),
        (*pieces, *near, *far),
        [pltpu.VMEM((count, full), jnp.bfloat16), pltpu.VMEM((count, full - LANES), jnp.float32)],
        limit=24,
        moved=2 * sum(w.size for w in (*near, *far)),
    )


def combine_kernel(*refs):
    blocks, out, slots = refs[:-2], refs[-2], refs[-1]
    tok_count, width = out.shape
    start = 0
    for block in blocks:
        slots[start : start + block.shape[0]] = block[...]
        start += block.shape[0]
    token = slots[:, width:]
    part = width // 7
    for at in range(7):
        place = slice(at * part, (at + 1) * part)
        mixed = across(token, slots[:, place])
        out[:, place] = mixed[TOKEN_LANE : TOKEN_LANE + tok_count].astype(out.dtype)


def combine(blocks, tok_count):
    capacity, full = blocks[0].shape
    return local_call(
        combine_kernel,
        "combine",
        jax.ShapeDtypeStruct((tok_count, full - LANES), jnp.bfloat16),
        [None] * len(blocks),
        tuple(blocks),
        [pltpu.VMEM((capacity * len(blocks), full), jnp.bfloat16)],
    )


def sent(shard, sections, section_step, ring_step, flip):
    planes = len(RING)
    pairs = []
    for s in range(sections):
        for z in range(planes):
            for y in range(2):
                for core in range(2):
                    plane = RING[(RING.index(z) + ring_step) % planes]
                    target = (((s + section_step) % sections) * planes + plane) * 2 + (y ^ flip)
                    pairs.append((((s * planes + z) * 2 + y) * 2 + core, target * 2 + core))
    return lax.ppermute(shard, ("section", "expert"), pairs)


def after(value, other):
    return lax.optimization_barrier((value, other))[0]


def by_ring(rows, route_ids, route_weights, w_gate_up, w_down):
    sections = lax.axis_size("section")
    devices = lax.axis_size("expert")
    experts = devices // 2
    tokens = rows[0]
    tok_count = tokens.shape[0]
    top_count = route_ids.shape[2]
    capacity = max(2, 2 * tok_count * top_count // experts)
    swap = [(i, i ^ 1) for i in range(devices)]
    w_in, w_out = w_gate_up[0], w_down[0]
    far_out = lax.ppermute(w_out, "expert", swap)
    far_in = lax.ppermute(w_in, "expert", swap)
    block = prepare(route_ids[0].T, route_weights[0].T, tokens)
    block1 = sent(block, sections, 0, 1, 0)
    own0, other0, back0, back1 = choose(block, capacity, ((0, 0), (0, 1), (3, 0), (3, 1)))
    own3 = sent(back0, sections, 0, 3, 0)
    other3 = sent(back1, sections, 0, 3, 1)
    near = (loaded(after(w_in, back1)), loaded(after(w_out, back1)))
    block1 = after(block1, near)
    own1, on0, on1, other = choose(block1, capacity, ((0, 0), (1, 0), (1, 1), (0, 1)), other0)
    own2 = sent(on0, sections, 0, 1, 0)
    other2 = sent(on1, sections, 0, 1, 1)
    other01 = sent(other, sections, 0, 0, 1)
    places = ((0, 0), (2, 0), (2, 1), (0, 1), (1, 1), (1, 0), (3, 0), (3, 1))
    pieces = (own0, own2, other2, other01, own1, own3, other3)
    pieces = expert_pass(pieces, near, (far_in, far_out), capacity)
    back = [
        sent(piece, sections, 1, -steps, flip) for piece, (steps, flip) in zip(pieces, places)
    ]
    return combine(back, tok_count)[None]


def per_device(rows, route_ids, route_weights, w_gate_up, w_down):
    experts = lax.axis_size("expert") // 2
    fits = experts == 2 * len(RING) and rows.shape[1] <= LANES - TOKEN_LANE
    plan = by_ring if fits else by_slots
    return plan(rows, route_ids, route_weights, w_gate_up, w_down)


def solution(mesh):
    in_specs = (
        P("section", "expert", None),
        P("section", "expert", None),
        P("section", "expert", None),
        P("section", None, "expert"),
        P("section", "expert", None),
    )
    out_specs = P("section", "expert", None)
    return jax.shard_map(
        per_device, mesh=mesh, in_specs=in_specs, out_specs=out_specs, check_vma=False
    )
```

```python
import functools

import jax
import jax.numpy as jnp
from jax import lax
from jax.experimental import pallas as pl
from jax.experimental.pallas import tpu as pltpu
from jax.sharding import PartitionSpec as P


def passed_along(shard, axis, by):
    length = lax.axis_size(axis)
    return lax.ppermute(shard, axis, [(i, (i + by) % length) for i in range(length)])


def by_slots(rows, route_ids, route_weights, w_gate_up, w_down):
    devices = lax.axis_size("expert")
    experts = devices // 2
    tokens = rows[0]
    tok_count, width = tokens.shape
    top_count = route_ids.shape[2]
    choices_flat = route_ids[0].reshape(-1)
    capacity = max(2, 2 * tok_count * top_count // experts)
    onehot = (choices_flat[:, None] == jnp.arange(experts, dtype=jnp.int32)[None, :]).astype(
        jnp.int32
    )
    before = jnp.cumsum(onehot, axis=0) - onehot
    slot = jnp.sum(before * onehot, axis=1)
    place = slot * experts + choices_flat
    slot_total = experts * capacity
    picker = (place[None, :] == jnp.arange(slot_total, dtype=jnp.int32)[:, None]).astype(
        jnp.bfloat16
    )
    token_pairs = jnp.repeat(tokens, top_count, axis=0)
    packed = jnp.dot(picker, token_pairs, preferred_element_type=jnp.float32).astype(jnp.bfloat16)
    w_in = w_gate_up[0]
    w_out = w_down[0]
    hidden = w_out.shape[0]
    outgoing = jnp.broadcast_to(
        packed.reshape(capacity, experts, 1, width), (capacity, experts, 2, width)
    )
    outgoing = outgoing.reshape(capacity, devices, width)
    block = lax.all_to_all(outgoing, "expert", split_axis=1, concat_axis=1, tiled=True)
    flat = block.reshape(-1, width)
    both = jnp.dot(flat, w_in, preferred_element_type=jnp.float32)
    active = (jax.nn.silu(both[:, :hidden]) * both[:, hidden:]).astype(jnp.bfloat16)
    result = jnp.dot(active, w_out, preferred_element_type=jnp.float32)
    partial_out = result.reshape(block.shape[0], block.shape[1], width).astype(jnp.bfloat16)
    returned = lax.all_to_all(partial_out, "expert", split_axis=1, concat_axis=1, tiled=True)
    returned = returned.reshape(capacity, experts, 2, width).astype(jnp.float32)
    expert_out = jnp.sum(returned, axis=2).astype(jnp.bfloat16).reshape(slot_total, width)
    pair_out = expert_out[place].astype(jnp.float32) * route_weights[0].reshape(-1)[:, None]
    layer_out = jnp.sum(pair_out.reshape(tok_count, top_count, width), axis=1).astype(jnp.bfloat16)
    return passed_along(layer_out, "section", 1)[None]


RING = (0, 1, 3, 2)
LANES = 128
TOKEN_LANE = 64


def on_ring(place):
    return place ^ (place >> 1)


def chip_at(chip, steps, flip):
    return (on_ring((on_ring(chip >> 1) + steps) & 3) << 1) | ((chip & 1) ^ flip)


def iota(shape, axis):
    return lax.broadcasted_iota(jnp.int32, shape, axis)


def ones_where(condition):
    return jnp.where(condition, 1.0, 0.0).astype(jnp.bfloat16)


def across(left, right):
    return lax.dot_general(left, right, (((0,), (0,)), ((), ())), preferred_element_type=jnp.float32)


def local_call(kernel, name, out_shape, in_specs, operands, scratch=(), limit=12, flops=0, moved=0):
    vmem = pl.BlockSpec(memory_space=pltpu.VMEM)
    return pl.pallas_call(
        kernel,
        out_shape=out_shape,
        in_specs=[vmem if spec is None else pl.BlockSpec(memory_space=spec) for spec in in_specs],
        out_specs=jax.tree.map(lambda _: vmem, out_shape),
        scratch_shapes=list(scratch),
        compiler_params=pltpu.CompilerParams(vmem_limit_bytes=limit << 20),
        cost_estimate=pl.CostEstimate(flops=flops, bytes_accessed=moved, transcendentals=0),
        name=name,
    )(*operands)


def prepare_kernel(ids_in, weights_in, rows_in, block, ids, weights, sems):
    tok_count, width = rows_in.shape
    top_count = ids.shape[0]
    experts = 2 * len(RING)
    copies = [
        pltpu.make_async_copy(ids_in, ids, sems.at[0]),
        pltpu.make_async_copy(weights_in, weights, sems.at[1]),
        pltpu.make_async_copy(rows_in, block.at[:, pl.ds(0, width)], sems.at[2]),
    ]
    for copy in copies:
        copy.start()
    square = (tok_count, tok_count)
    earlier = ones_where(iota(square, 0) < iota(square, 1))
    expert = iota((experts, tok_count), 0)
    unit = ones_where(iota((4 * experts, LANES), 0) == iota((4 * experts, LANES), 1))
    token = ones_where(iota((tok_count, LANES), 0) + TOKEN_LANE == iota((tok_count, LANES), 1))
    copies[0].wait()
    copies[1].wait()
    named = jnp.zeros((experts, tok_count), jnp.float32)
    scale = jnp.zeros((experts, tok_count), jnp.float32)
    for k in range(top_count):
        hit = ids[k : k + 1, :] == expert
        named = named + jnp.where(hit, 1.0, 0.0)
        scale = scale + jnp.where(hit, weights[k : k + 1, :], 0.0)
    rank = jnp.dot(named.astype(jnp.bfloat16), earlier, preferred_element_type=jnp.float32)
    notes = [jnp.where(named > 0.5, rank + 1.0, 0.0)]
    for _ in range(3):
        piece = scale.astype(jnp.bfloat16).astype(jnp.float32)
        scale = scale - piece
        notes.append(piece)
    notes = across(jnp.concatenate(notes, axis=0).astype(jnp.bfloat16), unit)
    block[:, width:] = notes.astype(jnp.bfloat16) + token
    copies[2].wait()


def prepare(ids, weights, tokens):
    tok_count, width = tokens.shape
    return local_call(
        prepare_kernel,
        "prepare",
        pltpu.VMEM((tok_count, width + LANES), jnp.bfloat16),
        [pl.ANY] * 3,
        tuple(pltpu.with_memory_space_constraint(x, pltpu.HBM) for x in (ids, weights, tokens)),
        [
            pltpu.VMEM(ids.shape, ids.dtype),
            pltpu.VMEM(weights.shape, weights.dtype),
            pltpu.SemaphoreType.DMA((3,)),
        ],
        limit=8,
    )


def choose_kernel(places, capacity, block, *refs):
    chip = lax.axis_index("expert") >> 1
    refs = list(refs)
    first = refs.pop(0) if refs[-1].shape[0] == 2 * capacity else None
    tok_count = block.shape[0]
    notes = block[:, -LANES:].astype(jnp.float32)
    lane = iota(notes.shape, 1)
    slot = iota((tok_count, len(places) * capacity), 1)
    code = jnp.zeros(slot.shape, jnp.float32)
    order = jnp.zeros(slot.shape, jnp.int32)
    for at, (steps, flip) in enumerate(places):
        wanted = chip_at(chip, steps, flip)
        column = jnp.sum(jnp.where(lane == wanted, notes, 0.0), axis=1, keepdims=True)
        code = jnp.where(slot >= at * capacity, column, code)
        order = jnp.where(slot >= at * capacity, slot + 1 - at * capacity, order)
    rows = across(ones_where(code == order.astype(jnp.float32)), block[...]).astype(jnp.bfloat16)
    for at in range(len(places)):
        piece = rows[at * capacity : (at + 1) * capacity]
        if first is not None and at == len(places) - 1:
            refs[at][:capacity] = first[...]
            refs[at][capacity:] = piece
        else:
            refs[at][...] = piece


def choose(block, capacity, places, first=None):
    out_shape = [jax.ShapeDtypeStruct((capacity, block.shape[1]), jnp.bfloat16) for _ in places]
    operands = (block,)
    if first is not None:
        out_shape[-1] = jax.ShapeDtypeStruct((2 * capacity, block.shape[1]), jnp.bfloat16)
        operands = operands + (first,)
    return local_call(
        functools.partial(choose_kernel, places, capacity),
        "choose",
        out_shape,
        [None] * len(operands),
        operands,
    )


def load_kernel(source, target, sem):
    copy = pltpu.make_async_copy(source, target, sem)
    copy.start()
    copy.wait()


def loaded(weights):
    return local_call(
        load_kernel,
        "loaded",
        pltpu.VMEM(weights.shape, weights.dtype),
        [pl.ANY],
        (weights,),
        [pltpu.SemaphoreType.DMA],
        limit=9,
        moved=2 * weights.size * weights.dtype.itemsize,
    )


def gated(both):
    hidden = both.shape[1] // 2
    gate = both[:, :hidden]
    return (gate / (1.0 + jnp.exp(-gate)) * both[:, hidden:]).astype(jnp.bfloat16)


def write_pieces(slots, total, outs):
    chip = lax.axis_index("expert") >> 1
    width = total.shape[1]
    experts = 2 * len(RING)
    notes = slots[:, width:].astype(jnp.float32)
    lane = iota(notes.shape, 1)
    mine = (lane >= experts) & (lane < 4 * experts) & ((lane & (experts - 1)) == chip)
    scale = jnp.sum(jnp.where(mine, notes, 0.0), axis=1, keepdims=True)
    start = 0
    for out in outs:
        stop = start + out.shape[0]
        out[:, :width] = (total[start:stop] * scale[start:stop]).astype(jnp.bfloat16)
        out[:, width:] = slots[start:stop, width:]
        start = stop


def expert_kernel(*refs):
    outs, (slots, total) = refs[-10:-2], refs[-2:]
    pieces, weights = refs[:-14], refs[-14:-10]
    start = 0
    for piece in pieces:
        slots[start : start + piece.shape[0]] = piece[...]
        start += piece.shape[0]
    width = total.shape[1]
    for half in range(2):
        first, second = weights[2 * half : 2 * half + 2]
        both = jnp.dot(slots[:, :width], first[...], preferred_element_type=jnp.float32)
        term = jnp.dot(gated(both), second[...], preferred_element_type=jnp.float32)
        total[...] = term if half == 0 else total[...] + term
    write_pieces(slots, total, outs)


def expert_pass(pieces, near, far, capacity):
    full = pieces[0].shape[1]
    count = capacity * 2 * len(RING)
    return local_call(
        expert_kernel,
        "expert_pass",
        [jax.ShapeDtypeStruct((capacity, full), jnp.bfloat16)] * (2 * len(RING)),
        [None] * (len(pieces) + 4),
        (*pieces, *near, *far),
        [pltpu.VMEM((count, full), jnp.bfloat16), pltpu.VMEM((count, full - LANES), jnp.float32)],
        limit=24,
        moved=2 * sum(w.size for w in (*near, *far)),
    )


def combine_kernel(count, *refs):
    blocks, more, (out, slots) = refs[:count], refs[count:-2], refs[-2:]
    tok_count, width = out.shape
    start = 0
    for block in blocks:
        slots[start : start + block.shape[0]] = block[...]
        start += block.shape[0]
    token = slots[:, width:]
    part = width // 7
    for at in range(7):
        place = slice(at * part, (at + 1) * part)
        mixed = across(token, slots[:, place])[TOKEN_LANE : TOKEN_LANE + tok_count]
        for other in more:
            mixed = mixed + other[:, place].astype(jnp.float32)
        out[:, place] = mixed.astype(out.dtype)


def combine(blocks, tok_count, *more):
    capacity, full = blocks[0].shape
    return local_call(
        functools.partial(combine_kernel, len(blocks)),
        "combine",
        jax.ShapeDtypeStruct((tok_count, full - LANES), jnp.bfloat16),
        [None] * (len(blocks) + len(more)),
        (*blocks, *more),
        [pltpu.VMEM((capacity * len(blocks), full), jnp.bfloat16)],
    )


def sent(shard, sections, section_step, ring_step, flip):
    planes = len(RING)
    pairs = []
    for s in range(sections):
        for z in range(planes):
            for y in range(2):
                for core in range(2):
                    plane = RING[(RING.index(z) + ring_step) % planes]
                    target = (((s + section_step) % sections) * planes + plane) * 2 + (y ^ flip)
                    pairs.append((((s * planes + z) * 2 + y) * 2 + core, target * 2 + core))
    return lax.ppermute(shard, ("section", "expert"), pairs)


def after(value, other):
    return lax.optimization_barrier((value, other))[0]


def by_ring(rows, route_ids, route_weights, w_gate_up, w_down):
    sections = lax.axis_size("section")
    devices = lax.axis_size("expert")
    experts = devices // 2
    tokens = rows[0]
    tok_count = tokens.shape[0]
    top_count = route_ids.shape[2]
    capacity = max(2, 2 * tok_count * top_count // experts)
    swap = [(i, i ^ 1) for i in range(devices)]
    w_in, w_out = w_gate_up[0], w_down[0]
    far_out = lax.ppermute(w_out, "expert", swap)
    far_in = lax.ppermute(w_in, "expert", swap)
    block = prepare(route_ids[0].T, route_weights[0].T, tokens)
    block1 = sent(block, sections, 0, 1, 0)
    own0, other0, back0, back1 = choose(block, capacity, ((0, 0), (0, 1), (3, 0), (3, 1)))
    near = (loaded(after(w_in, block)), loaded(after(w_out, block)))
    back0, back1 = after((back0, back1), near)
    own3 = sent(back0, sections, 0, 3, 0)
    other3 = sent(back1, sections, 0, 3, 1)
    block1 = after(block1, near)
    own1, on0, on1, other = choose(block1, capacity, ((0, 0), (1, 0), (1, 1), (0, 1)), other0)
    own2 = sent(on0, sections, 0, 1, 0)
    other2 = sent(on1, sections, 0, 1, 1)
    other01 = sent(other, sections, 0, 0, 1)
    slots = (own0, own1, own3, other3, other01, own2, other2)
    places = ((0, 0), (1, 0), (3, 0), (3, 1), (0, 1), (1, 1), (2, 0), (2, 1))
    pieces = dict(zip(places, expert_pass(slots, near, (far_in, far_out), capacity)))
    here, straight = [pieces[0, 0]], []
    for steps, flip in ((1, 0), (1, 1), (3, 0), (3, 1), (0, 1)):
        here.append(sent(pieces[steps, flip], sections, 0, -steps, flip))
    for flip in range(2):
        straight.append(sent(pieces[2, flip], sections, 1, -2, flip))
    here = after(here, straight[0])
    most = sent(combine(here, tok_count), sections, 1, 0, 0)
    return combine(straight, tok_count, most)[None]


def per_device(rows, route_ids, route_weights, w_gate_up, w_down):
    experts = lax.axis_size("expert") // 2
    fits = experts == 2 * len(RING) and rows.shape[1] <= LANES - TOKEN_LANE
    plan = by_ring if fits else by_slots
    return plan(rows, route_ids, route_weights, w_gate_up, w_down)


def solution(mesh):
    in_specs = (
        P("section", "expert", None),
        P("section", "expert", None),
        P("section", "expert", None),
        P("section", None, "expert"),
        P("section", "expert", None),
    )
    out_specs = P("section", "expert", None)
    return jax.shard_map(
        per_device, mesh=mesh, in_specs=in_specs, out_specs=out_specs, check_vma=False
    )
```

```python
import functools

import jax
import jax.numpy as jnp
from jax import lax
from jax.experimental import pallas as pl
from jax.experimental.pallas import tpu as pltpu
from jax.sharding import PartitionSpec as P


def passed_along(shard, axis, by):
    length = lax.axis_size(axis)
    return lax.ppermute(shard, axis, [(i, (i + by) % length) for i in range(length)])


def by_slots(rows, route_ids, route_weights, w_gate_up, w_down):
    devices = lax.axis_size("expert")
    experts = devices // 2
    tokens = rows[0]
    tok_count, width = tokens.shape
    top_count = route_ids.shape[2]
    choices_flat = route_ids[0].reshape(-1)
    capacity = max(2, 2 * tok_count * top_count // experts)
    onehot = (choices_flat[:, None] == jnp.arange(experts, dtype=jnp.int32)[None, :]).astype(
        jnp.int32
    )
    before = jnp.cumsum(onehot, axis=0) - onehot
    slot = jnp.sum(before * onehot, axis=1)
    place = slot * experts + choices_flat
    slot_total = experts * capacity
    picker = (place[None, :] == jnp.arange(slot_total, dtype=jnp.int32)[:, None]).astype(
        jnp.bfloat16
    )
    token_pairs = jnp.repeat(tokens, top_count, axis=0)
    packed = jnp.dot(picker, token_pairs, preferred_element_type=jnp.float32).astype(jnp.bfloat16)
    w_in = w_gate_up[0]
    w_out = w_down[0]
    hidden = w_out.shape[0]
    outgoing = jnp.broadcast_to(
        packed.reshape(capacity, experts, 1, width), (capacity, experts, 2, width)
    )
    outgoing = outgoing.reshape(capacity, devices, width)
    block = lax.all_to_all(outgoing, "expert", split_axis=1, concat_axis=1, tiled=True)
    flat = block.reshape(-1, width)
    both = jnp.dot(flat, w_in, preferred_element_type=jnp.float32)
    active = (jax.nn.silu(both[:, :hidden]) * both[:, hidden:]).astype(jnp.bfloat16)
    result = jnp.dot(active, w_out, preferred_element_type=jnp.float32)
    partial_out = result.reshape(block.shape[0], block.shape[1], width).astype(jnp.bfloat16)
    returned = lax.all_to_all(partial_out, "expert", split_axis=1, concat_axis=1, tiled=True)
    returned = returned.reshape(capacity, experts, 2, width).astype(jnp.float32)
    expert_out = jnp.sum(returned, axis=2).astype(jnp.bfloat16).reshape(slot_total, width)
    pair_out = expert_out[place].astype(jnp.float32) * route_weights[0].reshape(-1)[:, None]
    layer_out = jnp.sum(pair_out.reshape(tok_count, top_count, width), axis=1).astype(jnp.bfloat16)
    return passed_along(layer_out, "section", 1)[None]


RING = (0, 1, 3, 2)
LANES = 128
TOKEN_LANE = 64


def on_ring(place):
    return place ^ (place >> 1)


def chip_at(chip, steps, flip):
    return (on_ring((on_ring(chip >> 1) + steps) & 3) << 1) | ((chip & 1) ^ flip)


def iota(shape, axis):
    return lax.broadcasted_iota(jnp.int32, shape, axis)


def ones_where(condition):
    return jnp.where(condition, 1.0, 0.0).astype(jnp.bfloat16)


def across(left, right):
    return lax.dot_general(left, right, (((0,), (0,)), ((), ())), preferred_element_type=jnp.float32)


def local_call(kernel, name, out_shape, in_specs, operands, scratch=(), limit=12, flops=0, moved=0):
    vmem = pl.BlockSpec(memory_space=pltpu.VMEM)
    return pl.pallas_call(
        kernel,
        out_shape=out_shape,
        in_specs=[vmem if spec is None else pl.BlockSpec(memory_space=spec) for spec in in_specs],
        out_specs=jax.tree.map(lambda _: vmem, out_shape),
        scratch_shapes=list(scratch),
        compiler_params=pltpu.CompilerParams(vmem_limit_bytes=limit << 20),
        cost_estimate=pl.CostEstimate(flops=flops, bytes_accessed=moved, transcendentals=0),
        name=name,
    )(*operands)


def prepare_kernel(ids_in, weights_in, rows_in, block, ids, weights, sems):
    tok_count, width = rows_in.shape
    top_count = ids.shape[0]
    experts = 2 * len(RING)
    copies = [
        pltpu.make_async_copy(ids_in, ids, sems.at[0]),
        pltpu.make_async_copy(weights_in, weights, sems.at[1]),
        pltpu.make_async_copy(rows_in, block.at[:, pl.ds(0, width)], sems.at[2]),
    ]
    for copy in copies:
        copy.start()
    square = (tok_count, tok_count)
    earlier = ones_where(iota(square, 0) < iota(square, 1))
    expert = iota((experts, tok_count), 0)
    unit = ones_where(iota((4 * experts, LANES), 0) == iota((4 * experts, LANES), 1))
    token = ones_where(iota((tok_count, LANES), 0) + TOKEN_LANE == iota((tok_count, LANES), 1))
    copies[0].wait()
    copies[1].wait()
    named = jnp.zeros((experts, tok_count), jnp.float32)
    scale = jnp.zeros((experts, tok_count), jnp.float32)
    for k in range(top_count):
        hit = ids[k : k + 1, :] == expert
        named = named + jnp.where(hit, 1.0, 0.0)
        scale = scale + jnp.where(hit, weights[k : k + 1, :], 0.0)
    rank = jnp.dot(named.astype(jnp.bfloat16), earlier, preferred_element_type=jnp.float32)
    notes = [jnp.where(named > 0.5, rank + 1.0, 0.0)]
    for _ in range(3):
        piece = scale.astype(jnp.bfloat16).astype(jnp.float32)
        scale = scale - piece
        notes.append(piece)
    notes = across(jnp.concatenate(notes, axis=0).astype(jnp.bfloat16), unit)
    block[:, width:] = notes.astype(jnp.bfloat16) + token
    copies[2].wait()


def prepare(ids, weights, tokens):
    tok_count, width = tokens.shape
    return local_call(
        prepare_kernel,
        "prepare",
        pltpu.VMEM((tok_count, width + LANES), jnp.bfloat16),
        [pl.ANY] * 3,
        tuple(pltpu.with_memory_space_constraint(x, pltpu.HBM) for x in (ids, weights, tokens)),
        [
            pltpu.VMEM(ids.shape, ids.dtype),
            pltpu.VMEM(weights.shape, weights.dtype),
            pltpu.SemaphoreType.DMA((3,)),
        ],
        limit=8,
    )


def choose_kernel(places, capacity, block, *refs):
    chip = lax.axis_index("expert") >> 1
    tok_count = block.shape[0]
    notes = block[:, -LANES:].astype(jnp.float32)
    lane = iota(notes.shape, 1)
    slot = iota((tok_count, len(places) * capacity), 1)
    code = jnp.zeros(slot.shape, jnp.float32)
    order = jnp.zeros(slot.shape, jnp.int32)
    for at, (steps, flip) in enumerate(places):
        wanted = chip_at(chip, steps, flip)
        column = jnp.sum(jnp.where(lane == wanted, notes, 0.0), axis=1, keepdims=True)
        code = jnp.where(slot >= at * capacity, column, code)
        order = jnp.where(slot >= at * capacity, slot + 1 - at * capacity, order)
    rows = across(ones_where(code == order.astype(jnp.float32)), block[...]).astype(jnp.bfloat16)
    for at in range(len(places)):
        refs[at][...] = rows[at * capacity : (at + 1) * capacity]


def choose(block, capacity, places):
    return local_call(
        functools.partial(choose_kernel, places, capacity),
        "choose",
        [jax.ShapeDtypeStruct((capacity, block.shape[1]), jnp.bfloat16) for _ in places],
        [None],
        (block,),
    )


def load_kernel(source, target, sem):
    copy = pltpu.make_async_copy(source, target, sem)
    copy.start()
    copy.wait()


def loaded(weights):
    return local_call(
        load_kernel,
        "loaded",
        pltpu.VMEM(weights.shape, weights.dtype),
        [pl.ANY],
        (weights,),
        [pltpu.SemaphoreType.DMA],
        limit=9,
        moved=2 * weights.size * weights.dtype.itemsize,
    )


def gated(both):
    hidden = both.shape[1] // 2
    gate = both[:, :hidden]
    return (gate / (1.0 + jnp.exp(-gate)) * both[:, hidden:]).astype(jnp.bfloat16)


def write_pieces(slots, total, outs):
    chip = lax.axis_index("expert") >> 1
    width = total.shape[1]
    experts = 2 * len(RING)
    notes = slots[:, width:].astype(jnp.float32)
    lane = iota(notes.shape, 1)
    mine = (lane >= experts) & (lane < 4 * experts) & ((lane & (experts - 1)) == chip)
    scale = jnp.sum(jnp.where(mine, notes, 0.0), axis=1, keepdims=True)
    start = 0
    for out in outs:
        stop = start + out.shape[0]
        out[:, :width] = (total[start:stop] * scale[start:stop]).astype(jnp.bfloat16)
        out[:, width:] = slots[start:stop, width:]
        start = stop


def near_kernel(*refs):
    pieces, (first, second, slots, total) = refs[:-4], refs[-4:]
    start = 0
    for piece in pieces:
        slots[start : start + piece.shape[0]] = piece[...]
        start += piece.shape[0]
    width = total.shape[1]
    both = jnp.dot(slots[:, :width], first[...], preferred_element_type=jnp.float32)
    total[...] = jnp.dot(gated(both), second[...], preferred_element_type=jnp.float32)


def near_pass(pieces, weights):
    count = sum(piece.shape[0] for piece in pieces)
    full = pieces[0].shape[1]
    return local_call(
        near_kernel,
        "near_pass",
        [
            jax.ShapeDtypeStruct((count, full), jnp.bfloat16),
            jax.ShapeDtypeStruct((count, full - LANES), jnp.float32),
        ],
        [None] * (len(pieces) + 2),
        (*pieces, *weights),
        moved=2 * sum(w.size for w in weights),
    )


def far_kernel(slots, before, first, second, *refs):
    outs, total = refs[:-1], refs[-1]
    width = total.shape[1]
    both = jnp.dot(slots[:, :width], first[...], preferred_element_type=jnp.float32)
    term = jnp.dot(gated(both), second[...], preferred_element_type=jnp.float32)
    total[...] = before[...] + term
    write_pieces(slots, total, outs)


def far_pass(slots, total, weights, capacity):
    count, full = slots.shape
    return local_call(
        far_kernel,
        "far_pass",
        [jax.ShapeDtypeStruct((capacity, full), jnp.bfloat16)] * (count // capacity),
        [None] * 4,
        (slots, total, *weights),
        [pltpu.VMEM(total.shape, jnp.float32)],
        limit=24,
        moved=2 * sum(w.size for w in weights),
    )


def combine_kernel(*refs):
    blocks, out, slots = refs[:-2], refs[-2], refs[-1]
    tok_count, width = out.shape
    start = 0
    for block in blocks:
        slots[start : start + block.shape[0]] = block[...]
        start += block.shape[0]
    token = slots[:, width:]
    part = width // 7
    for at in range(7):
        place = slice(at * part, (at + 1) * part)
        mixed = across(token, slots[:, place])
        out[:, place] = mixed[TOKEN_LANE : TOKEN_LANE + tok_count].astype(out.dtype)


def combine(blocks, tok_count):
    capacity, full = blocks[0].shape
    return local_call(
        combine_kernel,
        "combine",
        jax.ShapeDtypeStruct((tok_count, full - LANES), jnp.bfloat16),
        [None] * len(blocks),
        tuple(blocks),
        [pltpu.VMEM((capacity * len(blocks), full), jnp.bfloat16)],
    )


def sent(shard, sections, section_step, ring_step, flip):
    planes = len(RING)
    pairs = []
    for s in range(sections):
        for z in range(planes):
            for y in range(2):
                for core in range(2):
                    plane = RING[(RING.index(z) + ring_step) % planes]
                    target = (((s + section_step) % sections) * planes + plane) * 2 + (y ^ flip)
                    pairs.append((((s * planes + z) * 2 + y) * 2 + core, target * 2 + core))
    return lax.ppermute(shard, ("section", "expert"), pairs)


def after(value, other):
    return lax.optimization_barrier((value, other))[0]


def by_ring(rows, route_ids, route_weights, w_gate_up, w_down):
    sections = lax.axis_size("section")
    devices = lax.axis_size("expert")
    experts = devices // 2
    tokens = rows[0]
    tok_count = tokens.shape[0]
    top_count = route_ids.shape[2]
    capacity = max(2, 2 * tok_count * top_count // experts)
    swap = [(i, i ^ 1) for i in range(devices)]
    w_in, w_out = w_gate_up[0], w_down[0]
    far_out = lax.ppermute(w_out, "expert", swap)
    far_in = lax.ppermute(w_in, "expert", swap)
    block = prepare(route_ids[0].T, route_weights[0].T, tokens)
    block1 = sent(block, sections, 0, 1, 0)
    own0, other, back0, back1 = choose(block, capacity, ((0, 0), (0, 1), (3, 0), (3, 1)))
    other0 = sent(other, sections, 0, 0, 1)
    near = (loaded(after(w_in, own0)), loaded(after(w_out, own0)))
    block1 = after(block1, (near, other0))
    own1, other, on0, on1 = choose(block1, capacity, ((0, 0), (0, 1), (1, 0), (1, 1)))
    other1 = sent(other, sections, 0, 0, 1)
    own2 = sent(on0, sections, 0, 1, 0)
    other2 = sent(on1, sections, 0, 1, 1)
    back0, back1 = after((back0, back1), other1)
    own3 = sent(back0, sections, 0, 3, 0)
    other3 = sent(back1, sections, 0, 3, 1)
    pieces = (own0, other0, own1, own2, other2, other1, own3, other3)
    places = ((0, 0), (0, 1), (1, 0), (2, 0), (2, 1), (1, 1), (3, 0), (3, 1))
    slots, total = near_pass(pieces, near)
    pieces = far_pass(slots, total, (far_in, far_out), capacity)
    back = [
        sent(piece, sections, 1, -steps, flip) for piece, (steps, flip) in zip(pieces, places)
    ]
    return combine(back, tok_count)[None]


def per_device(rows, route_ids, route_weights, w_gate_up, w_down):
    experts = lax.axis_size("expert") // 2
    fits = experts == 2 * len(RING) and rows.shape[1] <= LANES - TOKEN_LANE
    plan = by_ring if fits else by_slots
    return plan(rows, route_ids, route_weights, w_gate_up, w_down)


def solution(mesh):
    in_specs = (
        P("section", "expert", None),
        P("section", "expert", None),
        P("section", "expert", None),
        P("section", None, "expert"),
        P("section", "expert", None),
    )
    out_specs = P("section", "expert", None)
    return jax.shard_map(
        per_device, mesh=mesh, in_specs=in_specs, out_specs=out_specs, check_vma=False
    )
```

```python
import functools

import jax
import jax.numpy as jnp
from jax import lax
from jax.experimental import pallas as pl
from jax.experimental.pallas import tpu as pltpu
from jax.sharding import PartitionSpec as P


def passed_along(shard, axis, by):
    length = lax.axis_size(axis)
    return lax.ppermute(shard, axis, [(i, (i + by) % length) for i in range(length)])


def by_slots(rows, route_ids, route_weights, w_gate_up, w_down):
    devices = lax.axis_size("expert")
    experts = devices // 2
    tokens = rows[0]
    tok_count, width = tokens.shape
    top_count = route_ids.shape[2]
    choices_flat = route_ids[0].reshape(-1)
    capacity = max(2, 2 * tok_count * top_count // experts)
    onehot = (choices_flat[:, None] == jnp.arange(experts, dtype=jnp.int32)[None, :]).astype(
        jnp.int32
    )
    before = jnp.cumsum(onehot, axis=0) - onehot
    slot = jnp.sum(before * onehot, axis=1)
    place = slot * experts + choices_flat
    slot_total = experts * capacity
    picker = (place[None, :] == jnp.arange(slot_total, dtype=jnp.int32)[:, None]).astype(
        jnp.bfloat16
    )
    token_pairs = jnp.repeat(tokens, top_count, axis=0)
    packed = jnp.dot(picker, token_pairs, preferred_element_type=jnp.float32).astype(jnp.bfloat16)
    w_in = w_gate_up[0]
    w_out = w_down[0]
    hidden = w_out.shape[0]
    outgoing = jnp.broadcast_to(
        packed.reshape(capacity, experts, 1, width), (capacity, experts, 2, width)
    )
    outgoing = outgoing.reshape(capacity, devices, width)
    block = lax.all_to_all(outgoing, "expert", split_axis=1, concat_axis=1, tiled=True)
    flat = block.reshape(-1, width)
    both = jnp.dot(flat, w_in, preferred_element_type=jnp.float32)
    active = (jax.nn.silu(both[:, :hidden]) * both[:, hidden:]).astype(jnp.bfloat16)
    result = jnp.dot(active, w_out, preferred_element_type=jnp.float32)
    partial_out = result.reshape(block.shape[0], block.shape[1], width).astype(jnp.bfloat16)
    returned = lax.all_to_all(partial_out, "expert", split_axis=1, concat_axis=1, tiled=True)
    returned = returned.reshape(capacity, experts, 2, width).astype(jnp.float32)
    expert_out = jnp.sum(returned, axis=2).astype(jnp.bfloat16).reshape(slot_total, width)
    pair_out = expert_out[place].astype(jnp.float32) * route_weights[0].reshape(-1)[:, None]
    layer_out = jnp.sum(pair_out.reshape(tok_count, top_count, width), axis=1).astype(jnp.bfloat16)
    return passed_along(layer_out, "section", 1)[None]


RING = (0, 1, 3, 2)
LANES = 128
TOKEN_LANE = 64


def on_ring(place):
    return place ^ (place >> 1)


def chip_at(chip, steps, flip):
    return (on_ring((on_ring(chip >> 1) + steps) & 3) << 1) | ((chip & 1) ^ flip)


def iota(shape, axis):
    return lax.broadcasted_iota(jnp.int32, shape, axis)


def ones_where(condition):
    return jnp.where(condition, 1.0, 0.0).astype(jnp.bfloat16)


def across(left, right):
    return lax.dot_general(left, right, (((0,), (0,)), ((), ())), preferred_element_type=jnp.float32)


def local_call(kernel, name, out_shape, in_specs, operands, scratch=(), limit=12, flops=0, moved=0):
    vmem = pl.BlockSpec(memory_space=pltpu.VMEM)
    return pl.pallas_call(
        kernel,
        out_shape=out_shape,
        in_specs=[vmem if spec is None else pl.BlockSpec(memory_space=spec) for spec in in_specs],
        out_specs=jax.tree.map(lambda _: vmem, out_shape),
        scratch_shapes=list(scratch),
        compiler_params=pltpu.CompilerParams(vmem_limit_bytes=limit << 20),
        cost_estimate=pl.CostEstimate(flops=flops, bytes_accessed=moved, transcendentals=0),
        name=name,
    )(*operands)


def prepare_kernel(ids_in, weights_in, rows_in, block, ids, weights, sems):
    tok_count, width = rows_in.shape
    top_count = ids.shape[0]
    experts = 2 * len(RING)
    copies = [
        pltpu.make_async_copy(ids_in, ids, sems.at[0]),
        pltpu.make_async_copy(weights_in, weights, sems.at[1]),
        pltpu.make_async_copy(rows_in, block.at[:, pl.ds(0, width)], sems.at[2]),
    ]
    for copy in copies:
        copy.start()
    square = (tok_count, tok_count)
    earlier = ones_where(iota(square, 0) < iota(square, 1))
    expert = iota((experts, tok_count), 0)
    unit = ones_where(iota((4 * experts, LANES), 0) == iota((4 * experts, LANES), 1))
    token = ones_where(iota((tok_count, LANES), 0) + TOKEN_LANE == iota((tok_count, LANES), 1))
    copies[0].wait()
    copies[1].wait()
    named = jnp.zeros((experts, tok_count), jnp.float32)
    scale = jnp.zeros((experts, tok_count), jnp.float32)
    for k in range(top_count):
        hit = ids[k : k + 1, :] == expert
        named = named + jnp.where(hit, 1.0, 0.0)
        scale = scale + jnp.where(hit, weights[k : k + 1, :], 0.0)
    rank = jnp.dot(named.astype(jnp.bfloat16), earlier, preferred_element_type=jnp.float32)
    notes = [jnp.where(named > 0.5, rank + 1.0, 0.0)]
    for _ in range(3):
        piece = scale.astype(jnp.bfloat16).astype(jnp.float32)
        scale = scale - piece
        notes.append(piece)
    notes = across(jnp.concatenate(notes, axis=0).astype(jnp.bfloat16), unit)
    block[:, width:] = notes.astype(jnp.bfloat16) + token
    copies[2].wait()


def prepare(ids, weights, tokens):
    tok_count, width = tokens.shape
    return local_call(
        prepare_kernel,
        "prepare",
        pltpu.VMEM((tok_count, width + LANES), jnp.bfloat16),
        [pl.ANY] * 3,
        tuple(pltpu.with_memory_space_constraint(x, pltpu.HBM) for x in (ids, weights, tokens)),
        [
            pltpu.VMEM(ids.shape, ids.dtype),
            pltpu.VMEM(weights.shape, weights.dtype),
            pltpu.SemaphoreType.DMA((3,)),
        ],
        limit=8,
    )


def choose_kernel(places, capacity, block, *refs):
    chip = lax.axis_index("expert") >> 1
    tok_count = block.shape[0]
    notes = block[:, -LANES:].astype(jnp.float32)
    lane = iota(notes.shape, 1)
    slot = iota((tok_count, len(places) * capacity), 1)
    code = jnp.zeros(slot.shape, jnp.float32)
    order = jnp.zeros(slot.shape, jnp.int32)
    for at, (steps, flip) in enumerate(places):
        wanted = chip_at(chip, steps, flip)
        column = jnp.sum(jnp.where(lane == wanted, notes, 0.0), axis=1, keepdims=True)
        code = jnp.where(slot >= at * capacity, column, code)
        order = jnp.where(slot >= at * capacity, slot + 1 - at * capacity, order)
    rows = across(ones_where(code == order.astype(jnp.float32)), block[...]).astype(jnp.bfloat16)
    for at in range(len(places)):
        refs[at][...] = rows[at * capacity : (at + 1) * capacity]


def choose(block, capacity, places):
    return local_call(
        functools.partial(choose_kernel, places, capacity),
        "choose",
        [jax.ShapeDtypeStruct((capacity, block.shape[1]), jnp.bfloat16) for _ in places],
        [None],
        (block,),
    )


def load_kernel(source, target, sem):
    copy = pltpu.make_async_copy(source, target, sem)
    copy.start()
    copy.wait()


def loaded(weights):
    return local_call(
        load_kernel,
        "loaded",
        pltpu.VMEM(weights.shape, weights.dtype),
        [pl.ANY],
        (weights,),
        [pltpu.SemaphoreType.DMA],
        limit=9,
        moved=2 * weights.size * weights.dtype.itemsize,
    )


def gated(both):
    hidden = both.shape[1] // 2
    gate = both[:, :hidden]
    return (gate / (1.0 + jnp.exp(-gate)) * both[:, hidden:]).astype(jnp.bfloat16)


def write_pieces(slots, total, outs):
    chip = lax.axis_index("expert") >> 1
    width = total.shape[1]
    experts = 2 * len(RING)
    notes = slots[:, width:].astype(jnp.float32)
    lane = iota(notes.shape, 1)
    mine = (lane >= experts) & (lane < 4 * experts) & ((lane & (experts - 1)) == chip)
    scale = jnp.sum(jnp.where(mine, notes, 0.0), axis=1, keepdims=True)
    start = 0
    for out in outs:
        stop = start + out.shape[0]
        out[:, :width] = (total[start:stop] * scale[start:stop]).astype(jnp.bfloat16)
        out[:, width:] = slots[start:stop, width:]
        start = stop


def near_kernel(*refs):
    pieces, (first, second, slots, total) = refs[:-4], refs[-4:]
    start = 0
    for piece in pieces:
        slots[start : start + piece.shape[0]] = piece[...]
        start += piece.shape[0]
    width = total.shape[1]
    both = jnp.dot(slots[:, :width], first[...], preferred_element_type=jnp.float32)
    total[...] = jnp.dot(gated(both), second[...], preferred_element_type=jnp.float32)


def near_pass(pieces, weights):
    count = sum(piece.shape[0] for piece in pieces)
    full = pieces[0].shape[1]
    return local_call(
        near_kernel,
        "near_pass",
        [
            jax.ShapeDtypeStruct((count, full), jnp.bfloat16),
            jax.ShapeDtypeStruct((count, full - LANES), jnp.float32),
        ],
        [None] * (len(pieces) + 2),
        (*pieces, *weights),
        moved=2 * sum(w.size for w in weights),
    )


def far_kernel(slots, before, first, second, *refs):
    outs, total = refs[:-1], refs[-1]
    width = total.shape[1]
    both = jnp.dot(slots[:, :width], first[...], preferred_element_type=jnp.float32)
    term = jnp.dot(gated(both), second[...], preferred_element_type=jnp.float32)
    total[...] = before[...] + term
    write_pieces(slots, total, outs)


def far_pass(slots, total, weights, capacity):
    count, full = slots.shape
    return local_call(
        far_kernel,
        "far_pass",
        [jax.ShapeDtypeStruct((capacity, full), jnp.bfloat16)] * (count // capacity),
        [None] * 4,
        (slots, total, *weights),
        [pltpu.VMEM(total.shape, jnp.float32)],
        limit=24,
        moved=2 * sum(w.size for w in weights),
    )


def combine_kernel(count, *refs):
    blocks, more, (out, slots) = refs[:count], refs[count:-2], refs[-2:]
    tok_count, width = out.shape
    start = 0
    for block in blocks:
        slots[start : start + block.shape[0]] = block[...]
        start += block.shape[0]
    token = slots[:, width:]
    part = width // 7
    for at in range(7):
        place = slice(at * part, (at + 1) * part)
        mixed = across(token, slots[:, place])[TOKEN_LANE : TOKEN_LANE + tok_count]
        for other in more:
            mixed = mixed + other[:, place].astype(jnp.float32)
        out[:, place] = mixed.astype(out.dtype)


def combine(blocks, tok_count, *more):
    capacity, full = blocks[0].shape
    return local_call(
        functools.partial(combine_kernel, len(blocks)),
        "combine",
        jax.ShapeDtypeStruct((tok_count, full - LANES), jnp.bfloat16),
        [None] * (len(blocks) + len(more)),
        (*blocks, *more),
        [pltpu.VMEM((capacity * len(blocks), full), jnp.bfloat16)],
    )


def sent(shard, sections, section_step, ring_step, flip):
    planes = len(RING)
    pairs = []
    for s in range(sections):
        for z in range(planes):
            for y in range(2):
                for core in range(2):
                    plane = RING[(RING.index(z) + ring_step) % planes]
                    target = (((s + section_step) % sections) * planes + plane) * 2 + (y ^ flip)
                    pairs.append((((s * planes + z) * 2 + y) * 2 + core, target * 2 + core))
    return lax.ppermute(shard, ("section", "expert"), pairs)


def after(value, other):
    return lax.optimization_barrier((value, other))[0]


def by_ring(rows, route_ids, route_weights, w_gate_up, w_down):
    sections = lax.axis_size("section")
    devices = lax.axis_size("expert")
    experts = devices // 2
    tokens = rows[0]
    tok_count = tokens.shape[0]
    top_count = route_ids.shape[2]
    capacity = max(2, 2 * tok_count * top_count // experts)
    swap = [(i, i ^ 1) for i in range(devices)]
    w_in, w_out = w_gate_up[0], w_down[0]
    far_out = lax.ppermute(w_out, "expert", swap)
    far_in = lax.ppermute(w_in, "expert", swap)
    block = prepare(route_ids[0].T, route_weights[0].T, tokens)
    block1 = sent(block, sections, 0, 1, 0)
    own0, other, back0, back1 = choose(block, capacity, ((0, 0), (0, 1), (3, 0), (3, 1)))
    other0 = sent(other, sections, 0, 0, 1)
    near = (loaded(after(w_in, own0)), loaded(after(w_out, own0)))
    block1 = after(block1, (near, other0))
    own1, other, on0, on1 = choose(block1, capacity, ((0, 0), (0, 1), (1, 0), (1, 1)))
    other1 = sent(other, sections, 0, 0, 1)
    own2 = sent(on0, sections, 0, 1, 0)
    other2 = sent(on1, sections, 0, 1, 1)
    back0, back1 = after((back0, back1), other1)
    own3 = sent(back0, sections, 0, 3, 0)
    other3 = sent(back1, sections, 0, 3, 1)
    pieces = (own0, other0, own1, own2, other2, other1, own3, other3)
    places = ((0, 0), (0, 1), (1, 0), (2, 0), (2, 1), (1, 1), (3, 0), (3, 1))
    slots, total = near_pass(pieces, near)
    pieces = far_pass(slots, total, (far_in, far_out), capacity)
    piece = dict(zip(places, pieces))
    merged = [
        piece[3, 0],
        sent(piece[2, 0], sections, 0, 1, 0),
        sent(piece[2, 1], sections, 0, 1, 1),
        sent(piece[3, 1], sections, 0, 0, 1),
    ]
    straight = [sent(piece[0, flip], sections, 1, 0, flip) for flip in range(2)]
    merged, straight = lax.optimization_barrier((merged, straight))
    straight += [sent(piece[1, flip], sections, 1, -1, flip) for flip in range(2)]
    merged = sent(combine(merged, tok_count), sections, 1, 1, 0)
    return combine(straight, tok_count, merged)[None]


def per_device(rows, route_ids, route_weights, w_gate_up, w_down):
    experts = lax.axis_size("expert") // 2
    fits = experts == 2 * len(RING) and rows.shape[1] <= LANES - TOKEN_LANE
    plan = by_ring if fits else by_slots
    return plan(rows, route_ids, route_weights, w_gate_up, w_down)


def solution(mesh):
    in_specs = (
        P("section", "expert", None),
        P("section", "expert", None),
        P("section", "expert", None),
        P("section", None, "expert"),
        P("section", "expert", None),
    )
    out_specs = P("section", "expert", None)
    return jax.shard_map(
        per_device, mesh=mesh, in_specs=in_specs, out_specs=out_specs, check_vma=False
    )
```

```python
import functools

import jax
import jax.numpy as jnp
from jax import lax
from jax.experimental import pallas as pl
from jax.experimental.pallas import tpu as pltpu
from jax.sharding import PartitionSpec as P


def passed_along(shard, axis, by):
    length = lax.axis_size(axis)
    return lax.ppermute(shard, axis, [(i, (i + by) % length) for i in range(length)])


def by_slots(rows, route_ids, route_weights, w_gate_up, w_down):
    devices = lax.axis_size("expert")
    experts = devices // 2
    tokens = rows[0]
    tok_count, width = tokens.shape
    top_count = route_ids.shape[2]
    choices_flat = route_ids[0].reshape(-1)
    capacity = max(2, 2 * tok_count * top_count // experts)
    onehot = (choices_flat[:, None] == jnp.arange(experts, dtype=jnp.int32)[None, :]).astype(
        jnp.int32
    )
    before = jnp.cumsum(onehot, axis=0) - onehot
    slot = jnp.sum(before * onehot, axis=1)
    place = slot * experts + choices_flat
    slot_total = experts * capacity
    picker = (place[None, :] == jnp.arange(slot_total, dtype=jnp.int32)[:, None]).astype(
        jnp.bfloat16
    )
    token_pairs = jnp.repeat(tokens, top_count, axis=0)
    packed = jnp.dot(picker, token_pairs, preferred_element_type=jnp.float32).astype(jnp.bfloat16)
    w_in = w_gate_up[0]
    w_out = w_down[0]
    hidden = w_out.shape[0]
    outgoing = jnp.broadcast_to(
        packed.reshape(capacity, experts, 1, width), (capacity, experts, 2, width)
    )
    outgoing = outgoing.reshape(capacity, devices, width)
    block = lax.all_to_all(outgoing, "expert", split_axis=1, concat_axis=1, tiled=True)
    flat = block.reshape(-1, width)
    both = jnp.dot(flat, w_in, preferred_element_type=jnp.float32)
    active = (jax.nn.silu(both[:, :hidden]) * both[:, hidden:]).astype(jnp.bfloat16)
    result = jnp.dot(active, w_out, preferred_element_type=jnp.float32)
    partial_out = result.reshape(block.shape[0], block.shape[1], width).astype(jnp.bfloat16)
    returned = lax.all_to_all(partial_out, "expert", split_axis=1, concat_axis=1, tiled=True)
    returned = returned.reshape(capacity, experts, 2, width).astype(jnp.float32)
    expert_out = jnp.sum(returned, axis=2).astype(jnp.bfloat16).reshape(slot_total, width)
    pair_out = expert_out[place].astype(jnp.float32) * route_weights[0].reshape(-1)[:, None]
    layer_out = jnp.sum(pair_out.reshape(tok_count, top_count, width), axis=1).astype(jnp.bfloat16)
    return passed_along(layer_out, "section", 1)[None]


RING = (0, 1, 3, 2)
LANES = 128
TOKEN_LANE = 64


def on_ring(place):
    return place ^ (place >> 1)


def chip_at(chip, steps, flip):
    return (on_ring((on_ring(chip >> 1) + steps) & 3) << 1) | ((chip & 1) ^ flip)


def iota(shape, axis):
    return lax.broadcasted_iota(jnp.int32, shape, axis)


def ones_where(condition):
    return jnp.where(condition, 1.0, 0.0).astype(jnp.bfloat16)


def across(left, right):
    return lax.dot_general(left, right, (((0,), (0,)), ((), ())), preferred_element_type=jnp.float32)


def local_call(kernel, name, out_shape, in_specs, operands, scratch=(), limit=12, flops=0, moved=0):
    vmem = pl.BlockSpec(memory_space=pltpu.VMEM)
    return pl.pallas_call(
        kernel,
        out_shape=out_shape,
        in_specs=[vmem if spec is None else pl.BlockSpec(memory_space=spec) for spec in in_specs],
        out_specs=jax.tree.map(lambda _: vmem, out_shape),
        scratch_shapes=list(scratch),
        compiler_params=pltpu.CompilerParams(vmem_limit_bytes=limit << 20),
        cost_estimate=pl.CostEstimate(flops=flops, bytes_accessed=moved, transcendentals=0),
        name=name,
    )(*operands)


def prepare_kernel(ids_in, weights_in, rows_in, block, ids, weights, sems):
    tok_count, width = rows_in.shape
    top_count = ids.shape[0]
    experts = 2 * len(RING)
    copies = [
        pltpu.make_async_copy(ids_in, ids, sems.at[0]),
        pltpu.make_async_copy(weights_in, weights, sems.at[1]),
        pltpu.make_async_copy(rows_in, block.at[:, pl.ds(0, width)], sems.at[2]),
    ]
    for copy in copies:
        copy.start()
    square = (tok_count, tok_count)
    earlier = ones_where(iota(square, 0) < iota(square, 1))
    expert = iota((experts, tok_count), 0)
    unit = ones_where(iota((4 * experts, LANES), 0) == iota((4 * experts, LANES), 1))
    token = ones_where(iota((tok_count, LANES), 0) + TOKEN_LANE == iota((tok_count, LANES), 1))
    copies[0].wait()
    copies[1].wait()
    named = jnp.zeros((experts, tok_count), jnp.float32)
    scale = jnp.zeros((experts, tok_count), jnp.float32)
    for k in range(top_count):
        hit = ids[k : k + 1, :] == expert
        named = named + jnp.where(hit, 1.0, 0.0)
        scale = scale + jnp.where(hit, weights[k : k + 1, :], 0.0)
    rank = jnp.dot(named.astype(jnp.bfloat16), earlier, preferred_element_type=jnp.float32)
    notes = [jnp.where(named > 0.5, rank + 1.0, 0.0)]
    for _ in range(3):
        piece = scale.astype(jnp.bfloat16).astype(jnp.float32)
        scale = scale - piece
        notes.append(piece)
    notes = across(jnp.concatenate(notes, axis=0).astype(jnp.bfloat16), unit)
    block[:, width:] = notes.astype(jnp.bfloat16) + token
    copies[2].wait()


def prepare(ids, weights, tokens):
    tok_count, width = tokens.shape
    return local_call(
        prepare_kernel,
        "prepare",
        pltpu.VMEM((tok_count, width + LANES), jnp.bfloat16),
        [pl.ANY] * 3,
        tuple(pltpu.with_memory_space_constraint(x, pltpu.HBM) for x in (ids, weights, tokens)),
        [
            pltpu.VMEM(ids.shape, ids.dtype),
            pltpu.VMEM(weights.shape, weights.dtype),
            pltpu.SemaphoreType.DMA((3,)),
        ],
        limit=8,
    )


def choose_kernel(places, capacity, block, *refs):
    chip = lax.axis_index("expert") >> 1
    tok_count = block.shape[0]
    notes = block[:, -LANES:].astype(jnp.float32)
    lane = iota(notes.shape, 1)
    slot = iota((tok_count, len(places) * capacity), 1)
    code = jnp.zeros(slot.shape, jnp.float32)
    order = jnp.zeros(slot.shape, jnp.int32)
    for at, (steps, flip) in enumerate(places):
        wanted = chip_at(chip, steps, flip)
        column = jnp.sum(jnp.where(lane == wanted, notes, 0.0), axis=1, keepdims=True)
        code = jnp.where(slot >= at * capacity, column, code)
        order = jnp.where(slot >= at * capacity, slot + 1 - at * capacity, order)
    rows = across(ones_where(code == order.astype(jnp.float32)), block[...]).astype(jnp.bfloat16)
    for at in range(len(places)):
        refs[at][...] = rows[at * capacity : (at + 1) * capacity]


def choose(block, capacity, places):
    return local_call(
        functools.partial(choose_kernel, places, capacity),
        "choose",
        [jax.ShapeDtypeStruct((capacity, block.shape[1]), jnp.bfloat16) for _ in places],
        [None],
        (block,),
    )


def load_kernel(source, target, sem):
    copy = pltpu.make_async_copy(source, target, sem)
    copy.start()
    copy.wait()


def loaded(weights):
    return local_call(
        load_kernel,
        "loaded",
        pltpu.VMEM(weights.shape, weights.dtype),
        [pl.ANY],
        (weights,),
        [pltpu.SemaphoreType.DMA],
        limit=9,
        moved=2 * weights.size * weights.dtype.itemsize,
    )


def gated(both):
    hidden = both.shape[1] // 2
    gate = both[:, :hidden]
    return (gate / (1.0 + jnp.exp(-gate)) * both[:, hidden:]).astype(jnp.bfloat16)


def write_pieces(slots, total, outs):
    chip = lax.axis_index("expert") >> 1
    width = total.shape[1]
    experts = 2 * len(RING)
    notes = slots[:, width:].astype(jnp.float32)
    lane = iota(notes.shape, 1)
    mine = (lane >= experts) & (lane < 4 * experts) & ((lane & (experts - 1)) == chip)
    scale = jnp.sum(jnp.where(mine, notes, 0.0), axis=1, keepdims=True)
    start = 0
    for out in outs:
        stop = start + out.shape[0]
        out[:, :width] = (total[start:stop] * scale[start:stop]).astype(jnp.bfloat16)
        out[:, width:] = slots[start:stop, width:]
        start = stop


def near_kernel(*refs):
    pieces, (first, second, slots, total) = refs[:-4], refs[-4:]
    start = 0
    for piece in pieces:
        slots[start : start + piece.shape[0]] = piece[...]
        start += piece.shape[0]
    width = total.shape[1]
    both = jnp.dot(slots[:, :width], first[...], preferred_element_type=jnp.float32)
    total[...] = jnp.dot(gated(both), second[...], preferred_element_type=jnp.float32)


def near_pass(pieces, weights):
    count = sum(piece.shape[0] for piece in pieces)
    full = pieces[0].shape[1]
    return local_call(
        near_kernel,
        "near_pass",
        [
            jax.ShapeDtypeStruct((count, full), jnp.bfloat16),
            jax.ShapeDtypeStruct((count, full - LANES), jnp.float32),
        ],
        [None] * (len(pieces) + 2),
        (*pieces, *weights),
        moved=2 * sum(w.size for w in weights),
    )


def far_kernel(slots, before, first, second, *refs):
    outs, total = refs[:-1], refs[-1]
    width = total.shape[1]
    both = jnp.dot(slots[:, :width], first[...], preferred_element_type=jnp.float32)
    term = jnp.dot(gated(both), second[...], preferred_element_type=jnp.float32)
    total[...] = before[...] + term
    write_pieces(slots, total, outs)


def far_pass(slots, total, weights, capacity):
    count, full = slots.shape
    return local_call(
        far_kernel,
        "far_pass",
        [jax.ShapeDtypeStruct((capacity, full), jnp.bfloat16)] * (count // capacity),
        [None] * 4,
        (slots, total, *weights),
        [pltpu.VMEM(total.shape, jnp.float32)],
        limit=24,
        moved=2 * sum(w.size for w in weights),
    )


def combine_kernel(count, *refs):
    blocks, more, (out, slots) = refs[:count], refs[count:-2], refs[-2:]
    tok_count, width = out.shape
    start = 0
    for block in blocks:
        slots[start : start + block.shape[0]] = block[...]
        start += block.shape[0]
    token = slots[:, width:]
    part = width // 7
    for at in range(7):
        place = slice(at * part, (at + 1) * part)
        mixed = across(token, slots[:, place])[TOKEN_LANE : TOKEN_LANE + tok_count]
        for other in more:
            mixed = mixed + other[:, place].astype(jnp.float32)
        out[:, place] = mixed.astype(out.dtype)


def combine(blocks, tok_count, *more):
    capacity, full = blocks[0].shape
    return local_call(
        functools.partial(combine_kernel, len(blocks)),
        "combine",
        jax.ShapeDtypeStruct((tok_count, full - LANES), jnp.bfloat16),
        [None] * (len(blocks) + len(more)),
        (*blocks, *more),
        [pltpu.VMEM((capacity * len(blocks), full), jnp.bfloat16)],
    )


def sent(shard, sections, section_step, ring_step, flip):
    planes = len(RING)
    pairs = []
    for s in range(sections):
        for z in range(planes):
            for y in range(2):
                for core in range(2):
                    plane = RING[(RING.index(z) + ring_step) % planes]
                    target = (((s + section_step) % sections) * planes + plane) * 2 + (y ^ flip)
                    pairs.append((((s * planes + z) * 2 + y) * 2 + core, target * 2 + core))
    return lax.ppermute(shard, ("section", "expert"), pairs)


def after(value, other):
    return lax.optimization_barrier((value, other))[0]


def by_ring(rows, route_ids, route_weights, w_gate_up, w_down):
    sections = lax.axis_size("section")
    devices = lax.axis_size("expert")
    experts = devices // 2
    tokens = rows[0]
    tok_count = tokens.shape[0]
    top_count = route_ids.shape[2]
    capacity = max(2, 2 * tok_count * top_count // experts)
    swap = [(i, i ^ 1) for i in range(devices)]
    w_in, w_out = w_gate_up[0], w_down[0]
    far_out = lax.ppermute(w_out, "expert", swap)
    far_in = lax.ppermute(w_in, "expert", swap)
    block = prepare(route_ids[0].T, route_weights[0].T, tokens)
    block1 = sent(block, sections, 0, 1, 0)
    own0, other, back0, back1 = choose(block, capacity, ((0, 0), (0, 1), (3, 0), (3, 1)))
    other0 = sent(other, sections, 0, 0, 1)
    near = (loaded(after(w_in, own0)), loaded(after(w_out, own0)))
    block1 = after(block1, (near, other0))
    own1, other, on0, on1 = choose(block1, capacity, ((0, 0), (0, 1), (1, 0), (1, 1)))
    own2 = sent(on0, sections, 0, 1, 0)
    other2 = sent(on1, sections, 0, 1, 1)
    own3 = sent(after(back0, own1), sections, 0, 3, 0)
    other1 = sent(after(other, own2), sections, 0, 0, 1)
    other3 = sent(after(back1, other2), sections, 0, 3, 1)
    pieces = (own0, other0, own1, own2, other2, other1, own3, other3)
    places = ((0, 0), (0, 1), (1, 0), (2, 0), (2, 1), (1, 1), (3, 0), (3, 1))
    slots, total = near_pass(pieces, near)
    pieces = far_pass(slots, total, (far_in, far_out), capacity)
    piece = dict(zip(places, pieces))
    straight = [sent(piece[1, 0], sections, 1, -1, 0)]
    merged = [
        piece[3, 0],
        sent(piece[2, 0], sections, 0, 1, 0),
        sent(piece[2, 1], sections, 0, 1, 1),
        sent(piece[3, 1], sections, 0, 0, 1),
    ]
    straight.append(sent(piece[1, 1], sections, 1, -1, 1))
    merged, straight = lax.optimization_barrier((merged, straight))
    straight += [sent(piece[0, flip], sections, 1, 0, flip) for flip in range(2)]
    merged = sent(combine(merged, tok_count), sections, 1, 1, 0)
    return combine(straight, tok_count, merged)[None]


def per_device(rows, route_ids, route_weights, w_gate_up, w_down):
    experts = lax.axis_size("expert") // 2
    fits = experts == 2 * len(RING) and rows.shape[1] <= LANES - TOKEN_LANE
    plan = by_ring if fits else by_slots
    return plan(rows, route_ids, route_weights, w_gate_up, w_down)


def solution(mesh):
    in_specs = (
        P("section", "expert", None),
        P("section", "expert", None),
        P("section", "expert", None),
        P("section", None, "expert"),
        P("section", "expert", None),
    )
    out_specs = P("section", "expert", None)
    return jax.shard_map(
        per_device, mesh=mesh, in_specs=in_specs, out_specs=out_specs, check_vma=False
    )
```

```python
import functools

import jax
import jax.numpy as jnp
from jax import lax
from jax.experimental import pallas as pl
from jax.experimental.pallas import tpu as pltpu
from jax.sharding import PartitionSpec as P


def passed_along(shard, axis, by):
    length = lax.axis_size(axis)
    return lax.ppermute(shard, axis, [(i, (i + by) % length) for i in range(length)])


def by_slots(rows, route_ids, route_weights, w_gate_up, w_down):
    devices = lax.axis_size("expert")
    experts = devices // 2
    tokens = rows[0]
    tok_count, width = tokens.shape
    top_count = route_ids.shape[2]
    choices_flat = route_ids[0].reshape(-1)
    capacity = max(2, 2 * tok_count * top_count // experts)
    onehot = (choices_flat[:, None] == jnp.arange(experts, dtype=jnp.int32)[None, :]).astype(
        jnp.int32
    )
    before = jnp.cumsum(onehot, axis=0) - onehot
    slot = jnp.sum(before * onehot, axis=1)
    place = slot * experts + choices_flat
    slot_total = experts * capacity
    picker = (place[None, :] == jnp.arange(slot_total, dtype=jnp.int32)[:, None]).astype(
        jnp.bfloat16
    )
    token_pairs = jnp.repeat(tokens, top_count, axis=0)
    packed = jnp.dot(picker, token_pairs, preferred_element_type=jnp.float32).astype(jnp.bfloat16)
    w_in = w_gate_up[0]
    w_out = w_down[0]
    hidden = w_out.shape[0]
    outgoing = jnp.broadcast_to(
        packed.reshape(capacity, experts, 1, width), (capacity, experts, 2, width)
    )
    outgoing = outgoing.reshape(capacity, devices, width)
    block = lax.all_to_all(outgoing, "expert", split_axis=1, concat_axis=1, tiled=True)
    flat = block.reshape(-1, width)
    both = jnp.dot(flat, w_in, preferred_element_type=jnp.float32)
    active = (jax.nn.silu(both[:, :hidden]) * both[:, hidden:]).astype(jnp.bfloat16)
    result = jnp.dot(active, w_out, preferred_element_type=jnp.float32)
    partial_out = result.reshape(block.shape[0], block.shape[1], width).astype(jnp.bfloat16)
    returned = lax.all_to_all(partial_out, "expert", split_axis=1, concat_axis=1, tiled=True)
    returned = returned.reshape(capacity, experts, 2, width).astype(jnp.float32)
    expert_out = jnp.sum(returned, axis=2).astype(jnp.bfloat16).reshape(slot_total, width)
    pair_out = expert_out[place].astype(jnp.float32) * route_weights[0].reshape(-1)[:, None]
    layer_out = jnp.sum(pair_out.reshape(tok_count, top_count, width), axis=1).astype(jnp.bfloat16)
    return passed_along(layer_out, "section", 1)[None]


RING = (0, 1, 3, 2)
LANES = 128
TOKEN_LANE = 64


def on_ring(place):
    return place ^ (place >> 1)


def chip_at(chip, steps, flip):
    return (on_ring((on_ring(chip >> 1) + steps) & 3) << 1) | ((chip & 1) ^ flip)


def iota(shape, axis):
    return lax.broadcasted_iota(jnp.int32, shape, axis)


def ones_where(condition):
    return jnp.where(condition, 1.0, 0.0).astype(jnp.bfloat16)


def across(left, right):
    return lax.dot_general(left, right, (((0,), (0,)), ((), ())), preferred_element_type=jnp.float32)


def local_call(kernel, name, out_shape, in_specs, operands, scratch=(), limit=12, flops=0, moved=0):
    vmem = pl.BlockSpec(memory_space=pltpu.VMEM)
    return pl.pallas_call(
        kernel,
        out_shape=out_shape,
        in_specs=[vmem if spec is None else pl.BlockSpec(memory_space=spec) for spec in in_specs],
        out_specs=jax.tree.map(lambda _: vmem, out_shape),
        scratch_shapes=list(scratch),
        compiler_params=pltpu.CompilerParams(vmem_limit_bytes=limit << 20),
        cost_estimate=pl.CostEstimate(flops=flops, bytes_accessed=moved, transcendentals=0),
        name=name,
    )(*operands)


def prepare_kernel(ids_in, weights_in, rows_in, block, ids, weights, sems):
    tok_count, width = rows_in.shape
    top_count = ids.shape[0]
    experts = 2 * len(RING)
    copies = [
        pltpu.make_async_copy(ids_in, ids, sems.at[0]),
        pltpu.make_async_copy(weights_in, weights, sems.at[1]),
        pltpu.make_async_copy(rows_in, block.at[:, pl.ds(0, width)], sems.at[2]),
    ]
    for copy in copies:
        copy.start()
    square = (tok_count, tok_count)
    earlier = ones_where(iota(square, 0) < iota(square, 1))
    expert = iota((experts, tok_count), 0)
    unit = ones_where(iota((4 * experts, LANES), 0) == iota((4 * experts, LANES), 1))
    token = ones_where(iota((tok_count, LANES), 0) + TOKEN_LANE == iota((tok_count, LANES), 1))
    copies[0].wait()
    copies[1].wait()
    named = jnp.zeros((experts, tok_count), jnp.float32)
    scale = jnp.zeros((experts, tok_count), jnp.float32)
    for k in range(top_count):
        hit = ids[k : k + 1, :] == expert
        named = named + jnp.where(hit, 1.0, 0.0)
        scale = scale + jnp.where(hit, weights[k : k + 1, :], 0.0)
    rank = jnp.dot(named.astype(jnp.bfloat16), earlier, preferred_element_type=jnp.float32)
    notes = [jnp.where(named > 0.5, rank + 1.0, 0.0)]
    for _ in range(3):
        piece = scale.astype(jnp.bfloat16).astype(jnp.float32)
        scale = scale - piece
        notes.append(piece)
    notes = across(jnp.concatenate(notes, axis=0).astype(jnp.bfloat16), unit)
    block[:, width:] = notes.astype(jnp.bfloat16) + token
    copies[2].wait()


def prepare(ids, weights, tokens):
    tok_count, width = tokens.shape
    return local_call(
        prepare_kernel,
        "prepare",
        pltpu.VMEM((tok_count, width + LANES), jnp.bfloat16),
        [pl.ANY] * 3,
        tuple(pltpu.with_memory_space_constraint(x, pltpu.HBM) for x in (ids, weights, tokens)),
        [
            pltpu.VMEM(ids.shape, ids.dtype),
            pltpu.VMEM(weights.shape, weights.dtype),
            pltpu.SemaphoreType.DMA((3,)),
        ],
        limit=8,
    )


def choose_kernel(places, capacity, block, *refs):
    chip = lax.axis_index("expert") >> 1
    tok_count = block.shape[0]
    notes = block[:, -LANES:].astype(jnp.float32)
    lane = iota(notes.shape, 1)
    slot = iota((tok_count, len(places) * capacity), 1)
    code = jnp.zeros(slot.shape, jnp.float32)
    order = jnp.zeros(slot.shape, jnp.int32)
    for at, (steps, flip) in enumerate(places):
        wanted = chip_at(chip, steps, flip)
        column = jnp.sum(jnp.where(lane == wanted, notes, 0.0), axis=1, keepdims=True)
        code = jnp.where(slot >= at * capacity, column, code)
        order = jnp.where(slot >= at * capacity, slot + 1 - at * capacity, order)
    rows = across(ones_where(code == order.astype(jnp.float32)), block[...]).astype(jnp.bfloat16)
    for at in range(len(places)):
        refs[at][...] = rows[at * capacity : (at + 1) * capacity]


def choose(block, capacity, places):
    return local_call(
        functools.partial(choose_kernel, places, capacity),
        "choose",
        [jax.ShapeDtypeStruct((capacity, block.shape[1]), jnp.bfloat16) for _ in places],
        [None],
        (block,),
    )


def load_kernel(source, target, sem):
    copy = pltpu.make_async_copy(source, target, sem)
    copy.start()
    copy.wait()


def loaded(weights):
    return local_call(
        load_kernel,
        "loaded",
        pltpu.VMEM(weights.shape, weights.dtype),
        [pl.ANY],
        (weights,),
        [pltpu.SemaphoreType.DMA],
        limit=9,
        moved=2 * weights.size * weights.dtype.itemsize,
    )


def gated(both):
    hidden = both.shape[1] // 2
    gate = both[:, :hidden]
    return (gate / (1.0 + jnp.exp(-gate)) * both[:, hidden:]).astype(jnp.bfloat16)


def write_pieces(slots, total, outs):
    chip = lax.axis_index("expert") >> 1
    width = total.shape[1]
    experts = 2 * len(RING)
    notes = slots[:, width:].astype(jnp.float32)
    lane = iota(notes.shape, 1)
    mine = (lane >= experts) & (lane < 4 * experts) & ((lane & (experts - 1)) == chip)
    scale = jnp.sum(jnp.where(mine, notes, 0.0), axis=1, keepdims=True)
    start = 0
    for out in outs:
        stop = start + out.shape[0]
        out[:, :width] = (total[start:stop] * scale[start:stop]).astype(jnp.bfloat16)
        out[:, width:] = slots[start:stop, width:]
        start = stop


def near_kernel(*refs):
    pieces, (first, second, slots, total) = refs[:-4], refs[-4:]
    start = 0
    for piece in pieces:
        slots[start : start + piece.shape[0]] = piece[...]
        start += piece.shape[0]
    width = total.shape[1]
    both = jnp.dot(slots[:, :width], first[...], preferred_element_type=jnp.float32)
    total[...] = jnp.dot(gated(both), second[...], preferred_element_type=jnp.float32)


def near_pass(pieces, weights):
    count = sum(piece.shape[0] for piece in pieces)
    full = pieces[0].shape[1]
    return local_call(
        near_kernel,
        "near_pass",
        [
            jax.ShapeDtypeStruct((count, full), jnp.bfloat16),
            jax.ShapeDtypeStruct((count, full - LANES), jnp.float32),
        ],
        [None] * (len(pieces) + 2),
        (*pieces, *weights),
        moved=2 * sum(w.size for w in weights),
    )


def far_kernel(slots, before, first, second, *refs):
    outs, total = refs[:-1], refs[-1]
    width = total.shape[1]
    both = jnp.dot(slots[:, :width], first[...], preferred_element_type=jnp.float32)
    term = jnp.dot(gated(both), second[...], preferred_element_type=jnp.float32)
    total[...] = before[...] + term
    write_pieces(slots, total, outs)


def far_pass(slots, total, weights, capacity):
    count, full = slots.shape
    return local_call(
        far_kernel,
        "far_pass",
        [jax.ShapeDtypeStruct((capacity, full), jnp.bfloat16)] * (count // capacity),
        [None] * 4,
        (slots, total, *weights),
        [pltpu.VMEM(total.shape, jnp.float32)],
        limit=24,
        moved=2 * sum(w.size for w in weights),
    )


PARTS = 7


def combine_kernel(count, *refs):
    blocks, more, (out, slots, mixed, sems) = refs[:count], refs[count:-4], refs[-4:]
    tok_count, width = out.shape
    start = 0
    for block in blocks:
        slots[start : start + block.shape[0]] = block[...]
        start += block.shape[0]
    token = slots[:, width:]
    part = width // PARTS
    copies = []
    for at in range(PARTS):
        place = pl.ds(at * part, part)
        total = across(token, slots[:, place])[TOKEN_LANE : TOKEN_LANE + tok_count]
        for other in more:
            total = total + other[:, place].astype(jnp.float32)
        mixed[:, place] = total.astype(out.dtype)
        copies.append(
            pltpu.make_async_copy(mixed.at[:, place], out.at[:, place], sems.at[at])
        )
        copies[-1].start()
    for copy in copies:
        copy.wait()


def combine(blocks, tok_count, *more):
    capacity, full = blocks[0].shape
    shape = (tok_count, full - LANES)
    return pl.pallas_call(
        functools.partial(combine_kernel, len(blocks)),
        out_shape=jax.ShapeDtypeStruct(shape, jnp.bfloat16),
        in_specs=[pl.BlockSpec(memory_space=pltpu.VMEM)] * (len(blocks) + len(more)),
        out_specs=pl.BlockSpec(memory_space=pl.ANY),
        scratch_shapes=[
            pltpu.VMEM((capacity * len(blocks), full), jnp.bfloat16),
            pltpu.VMEM(shape, jnp.bfloat16),
            pltpu.SemaphoreType.DMA((PARTS,)),
        ],
        compiler_params=pltpu.CompilerParams(vmem_limit_bytes=12 << 20),
        name="combine",
    )(*blocks, *more)


def merge_kernel(*refs):
    blocks, (out, slots) = refs[:-2], refs[-2:]
    tok_count, width = out.shape
    start = 0
    for block in blocks:
        slots[start : start + block.shape[0]] = block[...]
        start += block.shape[0]
    token = slots[:, width:]
    part = width // PARTS
    for at in range(PARTS):
        place = pl.ds(at * part, part)
        total = across(token, slots[:, place])[TOKEN_LANE : TOKEN_LANE + tok_count]
        out[:, place] = total.astype(out.dtype)


def merge(blocks, tok_count):
    capacity, full = blocks[0].shape
    return local_call(
        merge_kernel,
        "merge",
        jax.ShapeDtypeStruct((tok_count, full - LANES), jnp.bfloat16),
        [None] * len(blocks),
        tuple(blocks),
        [pltpu.VMEM((capacity * len(blocks), full), jnp.bfloat16)],
    )


def sent(shard, sections, section_step, ring_step, flip):
    planes = len(RING)
    pairs = []
    for s in range(sections):
        for z in range(planes):
            for y in range(2):
                for core in range(2):
                    plane = RING[(RING.index(z) + ring_step) % planes]
                    target = (((s + section_step) % sections) * planes + plane) * 2 + (y ^ flip)
                    pairs.append((((s * planes + z) * 2 + y) * 2 + core, target * 2 + core))
    return lax.ppermute(shard, ("section", "expert"), pairs)


def after(value, other):
    return lax.optimization_barrier((value, other))[0]


def by_ring(rows, route_ids, route_weights, w_gate_up, w_down):
    sections = lax.axis_size("section")
    devices = lax.axis_size("expert")
    experts = devices // 2
    tokens = rows[0]
    tok_count = tokens.shape[0]
    top_count = route_ids.shape[2]
    capacity = max(2, 2 * tok_count * top_count // experts)
    swap = [(i, i ^ 1) for i in range(devices)]
    w_in, w_out = w_gate_up[0], w_down[0]
    far_out = lax.ppermute(w_out, "expert", swap)
    far_in = lax.ppermute(w_in, "expert", swap)
    block = prepare(route_ids[0].T, route_weights[0].T, tokens)
    block1 = sent(block, sections, 0, 1, 0)
    own0, other, back0, back1 = choose(block, capacity, ((0, 0), (0, 1), (3, 0), (3, 1)))
    other0 = sent(other, sections, 0, 0, 1)
    near = (loaded(after(w_in, own0)), loaded(after(w_out, own0)))
    block1 = after(block1, (near, other0))
    own1, other, on0, on1 = choose(block1, capacity, ((0, 0), (0, 1), (1, 0), (1, 1)))
    other1 = sent(other, sections, 0, 0, 1)
    own2 = sent(on0, sections, 0, 1, 0)
    other2 = sent(on1, sections, 0, 1, 1)
    back0, back1 = after((back0, back1), other1)
    own3 = sent(back0, sections, 0, 3, 0)
    other3 = sent(back1, sections, 0, 3, 1)
    pieces = (own0, other0, own1, own2, other2, other1, own3, other3)
    places = ((0, 0), (0, 1), (1, 0), (2, 0), (2, 1), (1, 1), (3, 0), (3, 1))
    slots, total = near_pass(pieces, near)
    pieces = far_pass(slots, total, (far_in, far_out), capacity)
    piece = dict(zip(places, pieces))
    straight = [sent(piece[0, 0], sections, 1, 0, 0)]
    merged = [
        piece[3, 0],
        sent(piece[2, 0], sections, 0, 1, 0),
        sent(piece[2, 1], sections, 0, 1, 1),
        sent(piece[3, 1], sections, 0, 0, 1),
    ]
    straight.append(sent(piece[0, 1], sections, 1, 0, 1))
    first, *merged, last = lax.optimization_barrier([straight[0], *merged, straight[1]])
    straight = [first, last]
    straight += [sent(piece[1, flip], sections, 1, -1, flip) for flip in range(2)]
    merged = sent(merge(merged, tok_count), sections, 1, 1, 0)
    return combine(straight, tok_count, merged)[None]


def per_device(rows, route_ids, route_weights, w_gate_up, w_down):
    experts = lax.axis_size("expert") // 2
    fits = experts == 2 * len(RING) and rows.shape[1] <= LANES - TOKEN_LANE
    plan = by_ring if fits else by_slots
    return plan(rows, route_ids, route_weights, w_gate_up, w_down)


def solution(mesh):
    in_specs = (
        P("section", "expert", None),
        P("section", "expert", None),
        P("section", "expert", None),
        P("section", None, "expert"),
        P("section", "expert", None),
    )
    out_specs = P("section", "expert", None)
    return jax.shard_map(
        per_device, mesh=mesh, in_specs=in_specs, out_specs=out_specs, check_vma=False
    )
```

```python
import functools

import jax
import jax.numpy as jnp
from jax import lax
from jax.experimental import pallas as pl
from jax.experimental.pallas import tpu as pltpu
from jax.sharding import PartitionSpec as P


def passed_along(shard, axis, by):
    length = lax.axis_size(axis)
    return lax.ppermute(shard, axis, [(i, (i + by) % length) for i in range(length)])


def by_slots(rows, route_ids, route_weights, w_gate_up, w_down):
    devices = lax.axis_size("expert")
    experts = devices // 2
    tokens = rows[0]
    tok_count, width = tokens.shape
    top_count = route_ids.shape[2]
    choices_flat = route_ids[0].reshape(-1)
    capacity = max(2, 2 * tok_count * top_count // experts)
    onehot = (choices_flat[:, None] == jnp.arange(experts, dtype=jnp.int32)[None, :]).astype(
        jnp.int32
    )
    before = jnp.cumsum(onehot, axis=0) - onehot
    slot = jnp.sum(before * onehot, axis=1)
    place = slot * experts + choices_flat
    slot_total = experts * capacity
    picker = (place[None, :] == jnp.arange(slot_total, dtype=jnp.int32)[:, None]).astype(
        jnp.bfloat16
    )
    token_pairs = jnp.repeat(tokens, top_count, axis=0)
    packed = jnp.dot(picker, token_pairs, preferred_element_type=jnp.float32).astype(jnp.bfloat16)
    w_in = w_gate_up[0]
    w_out = w_down[0]
    hidden = w_out.shape[0]
    outgoing = jnp.broadcast_to(
        packed.reshape(capacity, experts, 1, width), (capacity, experts, 2, width)
    )
    outgoing = outgoing.reshape(capacity, devices, width)
    block = lax.all_to_all(outgoing, "expert", split_axis=1, concat_axis=1, tiled=True)
    flat = block.reshape(-1, width)
    both = jnp.dot(flat, w_in, preferred_element_type=jnp.float32)
    active = (jax.nn.silu(both[:, :hidden]) * both[:, hidden:]).astype(jnp.bfloat16)
    result = jnp.dot(active, w_out, preferred_element_type=jnp.float32)
    partial_out = result.reshape(block.shape[0], block.shape[1], width).astype(jnp.bfloat16)
    returned = lax.all_to_all(partial_out, "expert", split_axis=1, concat_axis=1, tiled=True)
    returned = returned.reshape(capacity, experts, 2, width).astype(jnp.float32)
    expert_out = jnp.sum(returned, axis=2).astype(jnp.bfloat16).reshape(slot_total, width)
    pair_out = expert_out[place].astype(jnp.float32) * route_weights[0].reshape(-1)[:, None]
    layer_out = jnp.sum(pair_out.reshape(tok_count, top_count, width), axis=1).astype(jnp.bfloat16)
    return passed_along(layer_out, "section", 1)[None]


RING = (0, 1, 3, 2)
LANES = 128
TOKEN_LANE = 64


def on_ring(place):
    return place ^ (place >> 1)


def chip_at(chip, steps, flip):
    return (on_ring((on_ring(chip >> 1) + steps) & 3) << 1) | ((chip & 1) ^ flip)


def iota(shape, axis):
    return lax.broadcasted_iota(jnp.int32, shape, axis)


def ones_where(condition):
    return jnp.where(condition, 1.0, 0.0).astype(jnp.bfloat16)


def across(left, right):
    return lax.dot_general(left, right, (((0,), (0,)), ((), ())), preferred_element_type=jnp.float32)


def local_call(kernel, name, out_shape, in_specs, operands, scratch=(), limit=12, flops=0, moved=0):
    vmem = pl.BlockSpec(memory_space=pltpu.VMEM)
    return pl.pallas_call(
        kernel,
        out_shape=out_shape,
        in_specs=[vmem if spec is None else pl.BlockSpec(memory_space=spec) for spec in in_specs],
        out_specs=jax.tree.map(lambda _: vmem, out_shape),
        scratch_shapes=list(scratch),
        compiler_params=pltpu.CompilerParams(vmem_limit_bytes=limit << 20),
        cost_estimate=pl.CostEstimate(flops=flops, bytes_accessed=moved, transcendentals=0),
        name=name,
    )(*operands)


def prepare_kernel(ids_in, weights_in, rows_in, block, ids, weights, sems):
    tok_count, width = rows_in.shape
    top_count = ids.shape[0]
    experts = 2 * len(RING)
    copies = [
        pltpu.make_async_copy(ids_in, ids, sems.at[0]),
        pltpu.make_async_copy(weights_in, weights, sems.at[1]),
        pltpu.make_async_copy(rows_in, block.at[:, pl.ds(0, width)], sems.at[2]),
    ]
    for copy in copies:
        copy.start()
    square = (tok_count, tok_count)
    earlier = ones_where(iota(square, 0) < iota(square, 1))
    expert = iota((experts, tok_count), 0)
    unit = ones_where(iota((4 * experts, LANES), 0) == iota((4 * experts, LANES), 1))
    token = ones_where(iota((tok_count, LANES), 0) + TOKEN_LANE == iota((tok_count, LANES), 1))
    copies[0].wait()
    copies[1].wait()
    named = jnp.zeros((experts, tok_count), jnp.float32)
    scale = jnp.zeros((experts, tok_count), jnp.float32)
    for k in range(top_count):
        hit = ids[k : k + 1, :] == expert
        named = named + jnp.where(hit, 1.0, 0.0)
        scale = scale + jnp.where(hit, weights[k : k + 1, :], 0.0)
    rank = jnp.dot(named.astype(jnp.bfloat16), earlier, preferred_element_type=jnp.float32)
    notes = [jnp.where(named > 0.5, rank + 1.0, 0.0)]
    for _ in range(3):
        piece = scale.astype(jnp.bfloat16).astype(jnp.float32)
        scale = scale - piece
        notes.append(piece)
    notes = across(jnp.concatenate(notes, axis=0).astype(jnp.bfloat16), unit)
    block[:, width:] = notes.astype(jnp.bfloat16) + token
    copies[2].wait()


def prepare(ids, weights, tokens):
    tok_count, width = tokens.shape
    return local_call(
        prepare_kernel,
        "prepare",
        pltpu.VMEM((tok_count, width + LANES), jnp.bfloat16),
        [pl.ANY] * 3,
        tuple(pltpu.with_memory_space_constraint(x, pltpu.HBM) for x in (ids, weights, tokens)),
        [
            pltpu.VMEM(ids.shape, ids.dtype),
            pltpu.VMEM(weights.shape, weights.dtype),
            pltpu.SemaphoreType.DMA((3,)),
        ],
        limit=8,
    )


def choose_kernel(places, capacity, block, *refs):
    chip = lax.axis_index("expert") >> 1
    tok_count = block.shape[0]
    notes = block[:, -LANES:].astype(jnp.float32)
    lane = iota(notes.shape, 1)
    slot = iota((tok_count, len(places) * capacity), 1)
    code = jnp.zeros(slot.shape, jnp.float32)
    order = jnp.zeros(slot.shape, jnp.int32)
    for at, (steps, flip) in enumerate(places):
        wanted = chip_at(chip, steps, flip)
        column = jnp.sum(jnp.where(lane == wanted, notes, 0.0), axis=1, keepdims=True)
        code = jnp.where(slot >= at * capacity, column, code)
        order = jnp.where(slot >= at * capacity, slot + 1 - at * capacity, order)
    rows = across(ones_where(code == order.astype(jnp.float32)), block[...]).astype(jnp.bfloat16)
    for at in range(len(places)):
        refs[at][...] = rows[at * capacity : (at + 1) * capacity]


def choose(block, capacity, places):
    return local_call(
        functools.partial(choose_kernel, places, capacity),
        "choose",
        [jax.ShapeDtypeStruct((capacity, block.shape[1]), jnp.bfloat16) for _ in places],
        [None],
        (block,),
    )


def load_kernel(source, target, sem):
    copy = pltpu.make_async_copy(source, target, sem)
    copy.start()
    copy.wait()


def loaded(weights):
    return local_call(
        load_kernel,
        "loaded",
        pltpu.VMEM(weights.shape, weights.dtype),
        [pl.ANY],
        (weights,),
        [pltpu.SemaphoreType.DMA],
        limit=9,
        moved=2 * weights.size * weights.dtype.itemsize,
    )


def gated(both):
    hidden = both.shape[1] // 2
    gate = both[:, :hidden]
    return (gate / (1.0 + jnp.exp(-gate)) * both[:, hidden:]).astype(jnp.bfloat16)


def write_pieces(slots, total, outs):
    chip = lax.axis_index("expert") >> 1
    width = total.shape[1]
    experts = 2 * len(RING)
    notes = slots[:, width:].astype(jnp.float32)
    lane = iota(notes.shape, 1)
    mine = (lane >= experts) & (lane < 4 * experts) & ((lane & (experts - 1)) == chip)
    scale = jnp.sum(jnp.where(mine, notes, 0.0), axis=1, keepdims=True)
    start = 0
    for out in outs:
        stop = start + out.shape[0]
        out[:, :width] = (total[start:stop] * scale[start:stop]).astype(jnp.bfloat16)
        out[:, width:] = slots[start:stop, width:]
        start = stop


def near_kernel(*refs):
    pieces, (first, second, slots, total) = refs[:-4], refs[-4:]
    start = 0
    for piece in pieces:
        slots[start : start + piece.shape[0]] = piece[...]
        start += piece.shape[0]
    width = total.shape[1]
    both = jnp.dot(slots[:, :width], first[...], preferred_element_type=jnp.float32)
    total[...] = jnp.dot(gated(both), second[...], preferred_element_type=jnp.float32)


def near_pass(pieces, weights):
    count = sum(piece.shape[0] for piece in pieces)
    full = pieces[0].shape[1]
    return local_call(
        near_kernel,
        "near_pass",
        [
            jax.ShapeDtypeStruct((count, full), jnp.bfloat16),
            jax.ShapeDtypeStruct((count, full - LANES), jnp.float32),
        ],
        [None] * (len(pieces) + 2),
        (*pieces, *weights),
        moved=2 * sum(w.size for w in weights),
    )


def far_kernel(slots, before, first, second, *refs):
    outs, total = refs[:-1], refs[-1]
    width = total.shape[1]
    both = jnp.dot(slots[:, :width], first[...], preferred_element_type=jnp.float32)
    term = jnp.dot(gated(both), second[...], preferred_element_type=jnp.float32)
    total[...] = before[...] + term
    write_pieces(slots, total, outs)


def far_pass(slots, total, weights, capacity):
    count, full = slots.shape
    return local_call(
        far_kernel,
        "far_pass",
        [jax.ShapeDtypeStruct((capacity, full), jnp.bfloat16)] * (count // capacity),
        [None] * 4,
        (slots, total, *weights),
        [pltpu.VMEM(total.shape, jnp.float32)],
        limit=24,
        moved=2 * sum(w.size for w in weights),
    )


def combine_kernel(count, *refs):
    blocks, more, (out, slots) = refs[:count], refs[count:-2], refs[-2:]
    tok_count, width = out.shape
    start = 0
    for block in blocks:
        slots[start : start + block.shape[0]] = block[...]
        start += block.shape[0]
    token = slots[:, width:]
    part = width // 7
    for at in range(7):
        place = slice(at * part, (at + 1) * part)
        mixed = across(token, slots[:, place])[TOKEN_LANE : TOKEN_LANE + tok_count]
        for other in more:
            mixed = mixed + other[:, place].astype(jnp.float32)
        out[:, place] = mixed.astype(out.dtype)


def combine(blocks, tok_count, *more):
    capacity, full = blocks[0].shape
    return local_call(
        functools.partial(combine_kernel, len(blocks)),
        "combine",
        jax.ShapeDtypeStruct((tok_count, full - LANES), jnp.bfloat16),
        [None] * (len(blocks) + len(more)),
        (*blocks, *more),
        [pltpu.VMEM((capacity * len(blocks), full), jnp.bfloat16)],
    )


def sent(shard, sections, section_step, ring_step, flip):
    planes = len(RING)
    pairs = []
    for s in range(sections):
        for z in range(planes):
            for y in range(2):
                for core in range(2):
                    plane = RING[(RING.index(z) + ring_step) % planes]
                    target = (((s + section_step) % sections) * planes + plane) * 2 + (y ^ flip)
                    pairs.append((((s * planes + z) * 2 + y) * 2 + core, target * 2 + core))
    return lax.ppermute(shard, ("section", "expert"), pairs)


def after(value, other):
    return lax.optimization_barrier((value, other))[0]


def by_ring(rows, route_ids, route_weights, w_gate_up, w_down):
    sections = lax.axis_size("section")
    devices = lax.axis_size("expert")
    experts = devices // 2
    tokens = rows[0]
    tok_count = tokens.shape[0]
    top_count = route_ids.shape[2]
    capacity = max(2, 2 * tok_count * top_count // experts)
    swap = [(i, i ^ 1) for i in range(devices)]
    w_in, w_out = w_gate_up[0], w_down[0]
    far_out = lax.ppermute(w_out, "expert", swap)
    far_in = lax.ppermute(w_in, "expert", swap)
    block = prepare(route_ids[0].T, route_weights[0].T, tokens)
    block1 = sent(block, sections, 0, 1, 0)
    own0, other, back0, back1 = choose(block, capacity, ((0, 0), (0, 1), (3, 0), (3, 1)))
    other0 = sent(other, sections, 0, 0, 1)
    near = (loaded(after(w_in, own0)), loaded(after(w_out, own0)))
    block1 = after(block1, (near, other0))
    own1, other, on0, on1 = choose(block1, capacity, ((0, 0), (0, 1), (1, 0), (1, 1)))
    other1 = sent(other, sections, 0, 0, 1)
    own2 = sent(on0, sections, 0, 1, 0)
    other2 = sent(on1, sections, 0, 1, 1)
    back0, back1 = after((back0, back1), other1)
    own3 = sent(back0, sections, 0, 3, 0)
    other3 = sent(back1, sections, 0, 3, 1)
    pieces = (own0, other0, own1, own2, other2, other1, own3, other3)
    places = ((0, 0), (0, 1), (1, 0), (2, 0), (2, 1), (1, 1), (3, 0), (3, 1))
    slots, total = near_pass(pieces, near)
    pieces = far_pass(slots, total, (far_in, far_out), capacity)
    piece = dict(zip(places, pieces))
    straight = {at: sent(piece[at, 0], sections, 1, -at, 0) for at in range(2)}
    first = [
        straight[1],
        sent(piece[2, 1], sections, 0, 1, 1),
        sent(piece[3, 1], sections, 0, 0, 1),
        sent(piece[2, 0], sections, 0, 1, 0),
        straight[0],
    ]
    one, *merged, zero = lax.optimization_barrier(first)
    merged.append(piece[3, 0])
    straight = [one, zero] + [sent(piece[at, 1], sections, 1, -at, 1) for at in range(2)]
    merged = sent(combine(merged, tok_count), sections, 1, 1, 0)
    return combine(straight, tok_count, merged)[None]


def per_device(rows, route_ids, route_weights, w_gate_up, w_down):
    experts = lax.axis_size("expert") // 2
    fits = experts == 2 * len(RING) and rows.shape[1] <= LANES - TOKEN_LANE
    plan = by_ring if fits else by_slots
    return plan(rows, route_ids, route_weights, w_gate_up, w_down)


def solution(mesh):
    in_specs = (
        P("section", "expert", None),
        P("section", "expert", None),
        P("section", "expert", None),
        P("section", None, "expert"),
        P("section", "expert", None),
    )
    out_specs = P("section", "expert", None)
    return jax.shard_map(
        per_device, mesh=mesh, in_specs=in_specs, out_specs=out_specs, check_vma=False
    )
```

```python
import functools

import jax
import jax.numpy as jnp
from jax import lax
from jax.experimental import pallas as pl
from jax.experimental.pallas import tpu as pltpu
from jax.sharding import PartitionSpec as P


def passed_along(shard, axis, by):
    length = lax.axis_size(axis)
    return lax.ppermute(shard, axis, [(i, (i + by) % length) for i in range(length)])


def by_slots(rows, route_ids, route_weights, w_gate_up, w_down):
    devices = lax.axis_size("expert")
    experts = devices // 2
    tokens = rows[0]
    tok_count, width = tokens.shape
    top_count = route_ids.shape[2]
    choices_flat = route_ids[0].reshape(-1)
    capacity = max(2, 2 * tok_count * top_count // experts)
    onehot = (choices_flat[:, None] == jnp.arange(experts, dtype=jnp.int32)[None, :]).astype(
        jnp.int32
    )
    before = jnp.cumsum(onehot, axis=0) - onehot
    slot = jnp.sum(before * onehot, axis=1)
    place = slot * experts + choices_flat
    slot_total = experts * capacity
    picker = (place[None, :] == jnp.arange(slot_total, dtype=jnp.int32)[:, None]).astype(
        jnp.bfloat16
    )
    token_pairs = jnp.repeat(tokens, top_count, axis=0)
    packed = jnp.dot(picker, token_pairs, preferred_element_type=jnp.float32).astype(jnp.bfloat16)
    w_in = w_gate_up[0]
    w_out = w_down[0]
    hidden = w_out.shape[0]
    outgoing = jnp.broadcast_to(
        packed.reshape(capacity, experts, 1, width), (capacity, experts, 2, width)
    )
    outgoing = outgoing.reshape(capacity, devices, width)
    block = lax.all_to_all(outgoing, "expert", split_axis=1, concat_axis=1, tiled=True)
    flat = block.reshape(-1, width)
    both = jnp.dot(flat, w_in, preferred_element_type=jnp.float32)
    active = (jax.nn.silu(both[:, :hidden]) * both[:, hidden:]).astype(jnp.bfloat16)
    result = jnp.dot(active, w_out, preferred_element_type=jnp.float32)
    partial_out = result.reshape(block.shape[0], block.shape[1], width).astype(jnp.bfloat16)
    returned = lax.all_to_all(partial_out, "expert", split_axis=1, concat_axis=1, tiled=True)
    returned = returned.reshape(capacity, experts, 2, width).astype(jnp.float32)
    expert_out = jnp.sum(returned, axis=2).astype(jnp.bfloat16).reshape(slot_total, width)
    pair_out = expert_out[place].astype(jnp.float32) * route_weights[0].reshape(-1)[:, None]
    layer_out = jnp.sum(pair_out.reshape(tok_count, top_count, width), axis=1).astype(jnp.bfloat16)
    return passed_along(layer_out, "section", 1)[None]


RING = (0, 1, 3, 2)
LANES = 128
TOKEN_LANE = 64


def on_ring(place):
    return place ^ (place >> 1)


def chip_at(chip, steps, flip):
    return (on_ring((on_ring(chip >> 1) + steps) & 3) << 1) | ((chip & 1) ^ flip)


def iota(shape, axis):
    return lax.broadcasted_iota(jnp.int32, shape, axis)


def ones_where(condition):
    return jnp.where(condition, 1.0, 0.0).astype(jnp.bfloat16)


def across(left, right):
    return lax.dot_general(left, right, (((0,), (0,)), ((), ())), preferred_element_type=jnp.float32)


def local_call(kernel, name, out_shape, in_specs, operands, scratch=(), limit=12, flops=0, moved=0):
    vmem = pl.BlockSpec(memory_space=pltpu.VMEM)
    return pl.pallas_call(
        kernel,
        out_shape=out_shape,
        in_specs=[vmem if spec is None else pl.BlockSpec(memory_space=spec) for spec in in_specs],
        out_specs=jax.tree.map(lambda _: vmem, out_shape),
        scratch_shapes=list(scratch),
        compiler_params=pltpu.CompilerParams(vmem_limit_bytes=limit << 20),
        cost_estimate=pl.CostEstimate(flops=flops, bytes_accessed=moved, transcendentals=0),
        name=name,
    )(*operands)


def prepare_kernel(ids_in, weights_in, rows_in, block, ids, weights, sems):
    tok_count, width = rows_in.shape
    top_count = ids.shape[0]
    experts = 2 * len(RING)
    copies = [
        pltpu.make_async_copy(ids_in, ids, sems.at[0]),
        pltpu.make_async_copy(weights_in, weights, sems.at[1]),
        pltpu.make_async_copy(rows_in, block.at[:, pl.ds(0, width)], sems.at[2]),
    ]
    for copy in copies:
        copy.start()
    square = (tok_count, tok_count)
    earlier = ones_where(iota(square, 0) < iota(square, 1))
    expert = iota((experts, tok_count), 0)
    unit = ones_where(iota((4 * experts, LANES), 0) == iota((4 * experts, LANES), 1))
    token = ones_where(iota((tok_count, LANES), 0) + TOKEN_LANE == iota((tok_count, LANES), 1))
    copies[0].wait()
    copies[1].wait()
    named = jnp.zeros((experts, tok_count), jnp.float32)
    scale = jnp.zeros((experts, tok_count), jnp.float32)
    for k in range(top_count):
        hit = ids[k : k + 1, :] == expert
        named = named + jnp.where(hit, 1.0, 0.0)
        scale = scale + jnp.where(hit, weights[k : k + 1, :], 0.0)
    rank = jnp.dot(named.astype(jnp.bfloat16), earlier, preferred_element_type=jnp.float32)
    notes = [jnp.where(named > 0.5, rank + 1.0, 0.0)]
    for _ in range(3):
        piece = scale.astype(jnp.bfloat16).astype(jnp.float32)
        scale = scale - piece
        notes.append(piece)
    notes = across(jnp.concatenate(notes, axis=0).astype(jnp.bfloat16), unit)
    block[:, width:] = notes.astype(jnp.bfloat16) + token
    copies[2].wait()


def prepare(ids, weights, tokens):
    tok_count, width = tokens.shape
    return local_call(
        prepare_kernel,
        "prepare",
        pltpu.VMEM((tok_count, width + LANES), jnp.bfloat16),
        [pl.ANY] * 3,
        tuple(pltpu.with_memory_space_constraint(x, pltpu.HBM) for x in (ids, weights, tokens)),
        [
            pltpu.VMEM(ids.shape, ids.dtype),
            pltpu.VMEM(weights.shape, weights.dtype),
            pltpu.SemaphoreType.DMA((3,)),
        ],
        limit=8,
    )


def choose_kernel(places, capacity, block, *refs):
    chip = lax.axis_index("expert") >> 1
    tok_count = block.shape[0]
    notes = block[:, -LANES:].astype(jnp.float32)
    lane = iota(notes.shape, 1)
    slot = iota((tok_count, len(places) * capacity), 1)
    code = jnp.zeros(slot.shape, jnp.float32)
    order = jnp.zeros(slot.shape, jnp.int32)
    for at, (steps, flip) in enumerate(places):
        wanted = chip_at(chip, steps, flip)
        column = jnp.sum(jnp.where(lane == wanted, notes, 0.0), axis=1, keepdims=True)
        code = jnp.where(slot >= at * capacity, column, code)
        order = jnp.where(slot >= at * capacity, slot + 1 - at * capacity, order)
    rows = across(ones_where(code == order.astype(jnp.float32)), block[...]).astype(jnp.bfloat16)
    for at in range(len(places)):
        refs[at][...] = rows[at * capacity : (at + 1) * capacity]


def choose(block, capacity, places):
    return local_call(
        functools.partial(choose_kernel, places, capacity),
        "choose",
        [jax.ShapeDtypeStruct((capacity, block.shape[1]), jnp.bfloat16) for _ in places],
        [None],
        (block,),
    )


def load_kernel(source, target, sem):
    copy = pltpu.make_async_copy(source, target, sem)
    copy.start()
    copy.wait()


def loaded(weights):
    return local_call(
        load_kernel,
        "loaded",
        pltpu.VMEM(weights.shape, weights.dtype),
        [pl.ANY],
        (weights,),
        [pltpu.SemaphoreType.DMA],
        limit=9,
        moved=2 * weights.size * weights.dtype.itemsize,
    )


def gated(both):
    hidden = both.shape[1] // 2
    gate = both[:, :hidden]
    return (gate / (1.0 + jnp.exp(-gate)) * both[:, hidden:]).astype(jnp.bfloat16)


def write_pieces(slots, total, outs):
    chip = lax.axis_index("expert") >> 1
    width = total.shape[1]
    experts = 2 * len(RING)
    notes = slots[:, width:].astype(jnp.float32)
    lane = iota(notes.shape, 1)
    mine = (lane >= experts) & (lane < 4 * experts) & ((lane & (experts - 1)) == chip)
    scale = jnp.sum(jnp.where(mine, notes, 0.0), axis=1, keepdims=True)
    start = 0
    for out in outs:
        stop = start + out.shape[0]
        out[:, :width] = (total[start:stop] * scale[start:stop]).astype(jnp.bfloat16)
        out[:, width:] = slots[start:stop, width:]
        start = stop


def near_kernel(*refs):
    pieces, (first, second, slots, total) = refs[:-4], refs[-4:]
    start = 0
    for piece in pieces:
        slots[start : start + piece.shape[0]] = piece[...]
        start += piece.shape[0]
    width = total.shape[1]
    both = jnp.dot(slots[:, :width], first[...], preferred_element_type=jnp.float32)
    total[...] = jnp.dot(gated(both), second[...], preferred_element_type=jnp.float32)


def near_pass(pieces, weights):
    count = sum(piece.shape[0] for piece in pieces)
    full = pieces[0].shape[1]
    return local_call(
        near_kernel,
        "near_pass",
        [
            jax.ShapeDtypeStruct((count, full), jnp.bfloat16),
            jax.ShapeDtypeStruct((count, full - LANES), jnp.float32),
        ],
        [None] * (len(pieces) + 2),
        (*pieces, *weights),
        moved=2 * sum(w.size for w in weights),
    )


def far_kernel(slots, before, first, second, *refs):
    outs, total = refs[:-1], refs[-1]
    width = total.shape[1]
    both = jnp.dot(slots[:, :width], first[...], preferred_element_type=jnp.float32)
    term = jnp.dot(gated(both), second[...], preferred_element_type=jnp.float32)
    total[...] = before[...] + term
    write_pieces(slots, total, outs)


def far_pass(slots, total, weights, capacity):
    count, full = slots.shape
    return local_call(
        far_kernel,
        "far_pass",
        [jax.ShapeDtypeStruct((capacity, full), jnp.bfloat16)] * (count // capacity),
        [None] * 4,
        (slots, total, *weights),
        [pltpu.VMEM(total.shape, jnp.float32)],
        limit=24,
        moved=2 * sum(w.size for w in weights),
    )


def combine_kernel(count, *refs):
    blocks, more, (out, slots) = refs[:count], refs[count:-2], refs[-2:]
    tok_count, width = out.shape
    start = 0
    for block in blocks:
        slots[start : start + block.shape[0]] = block[...]
        start += block.shape[0]
    token = slots[:, width:]
    part = width // 7
    for at in range(7):
        place = slice(at * part, (at + 1) * part)
        mixed = across(token, slots[:, place])[TOKEN_LANE : TOKEN_LANE + tok_count]
        for other in more:
            mixed = mixed + other[:, place].astype(jnp.float32)
        out[:, place] = mixed.astype(out.dtype)


def combine(blocks, tok_count, *more):
    capacity, full = blocks[0].shape
    return local_call(
        functools.partial(combine_kernel, len(blocks)),
        "combine",
        jax.ShapeDtypeStruct((tok_count, full - LANES), jnp.bfloat16),
        [None] * (len(blocks) + len(more)),
        (*blocks, *more),
        [pltpu.VMEM((capacity * len(blocks), full), jnp.bfloat16)],
    )


def sent(shard, sections, section_step, ring_step, flip):
    planes = len(RING)
    pairs = []
    for s in range(sections):
        for z in range(planes):
            for y in range(2):
                for core in range(2):
                    plane = RING[(RING.index(z) + ring_step) % planes]
                    target = (((s + section_step) % sections) * planes + plane) * 2 + (y ^ flip)
                    pairs.append((((s * planes + z) * 2 + y) * 2 + core, target * 2 + core))
    return lax.ppermute(shard, ("section", "expert"), pairs)


def after(value, other):
    return lax.optimization_barrier((value, other))[0]


def by_ring(rows, route_ids, route_weights, w_gate_up, w_down):
    sections = lax.axis_size("section")
    devices = lax.axis_size("expert")
    experts = devices // 2
    tokens = rows[0]
    tok_count = tokens.shape[0]
    top_count = route_ids.shape[2]
    capacity = max(2, 2 * tok_count * top_count // experts)
    swap = [(i, i ^ 1) for i in range(devices)]
    w_in, w_out = w_gate_up[0], w_down[0]
    far_out = lax.ppermute(w_out, "expert", swap)
    far_in = lax.ppermute(w_in, "expert", swap)
    block = prepare(route_ids[0].T, route_weights[0].T, tokens)
    block1 = sent(block, sections, 0, 1, 0)
    own0, other, back0, back1 = choose(block, capacity, ((0, 0), (0, 1), (3, 0), (3, 1)))
    other0 = sent(other, sections, 0, 0, 1)
    near = (loaded(after(w_in, own0)), loaded(after(w_out, own0)))
    block1 = after(block1, (near, other0))
    own1, other, on0, on1 = choose(block1, capacity, ((0, 0), (0, 1), (1, 0), (1, 1)))
    other1 = sent(other, sections, 0, 0, 1)
    own2 = sent(on0, sections, 0, 1, 0)
    other2 = sent(on1, sections, 0, 1, 1)
    back0, back1 = after((back0, back1), other1)
    own3 = sent(back0, sections, 0, 3, 0)
    other3 = sent(back1, sections, 0, 3, 1)
    pieces = (own0, other0, own1, own2, other2, other1, own3, other3)
    places = ((0, 0), (0, 1), (1, 0), (2, 0), (2, 1), (1, 1), (3, 0), (3, 1))
    slots, total = near_pass(pieces, near)
    pieces = far_pass(slots, total, (far_in, far_out), capacity)
    piece = dict(zip(places, pieces))
    first = [
        sent(piece[1, 0], sections, 1, -1, 0),
        sent(piece[2, 1], sections, 0, 1, 1),
        sent(piece[3, 1], sections, 0, 0, 1),
        sent(piece[2, 0], sections, 0, 1, 0),
        sent(piece[0, 0], sections, 1, 0, 0),
        sent(piece[0, 1], sections, 1, 0, 1),
    ]
    one, two, three, four, *straight = lax.optimization_barrier(first)
    merged = [piece[3, 0], two, three, four]
    straight += [one, sent(piece[1, 1], sections, 1, -1, 1)]
    merged = sent(combine(merged, tok_count), sections, 1, 1, 0)
    return combine(straight, tok_count, merged)[None]


def per_device(rows, route_ids, route_weights, w_gate_up, w_down):
    experts = lax.axis_size("expert") // 2
    fits = experts == 2 * len(RING) and rows.shape[1] <= LANES - TOKEN_LANE
    plan = by_ring if fits else by_slots
    return plan(rows, route_ids, route_weights, w_gate_up, w_down)


def solution(mesh):
    in_specs = (
        P("section", "expert", None),
        P("section", "expert", None),
        P("section", "expert", None),
        P("section", None, "expert"),
        P("section", "expert", None),
    )
    out_specs = P("section", "expert", None)
    return jax.shard_map(
        per_device, mesh=mesh, in_specs=in_specs, out_specs=out_specs, check_vma=False
    )
```

```python
import functools

import jax
import jax.numpy as jnp
from jax import lax
from jax.experimental import pallas as pl
from jax.experimental.pallas import tpu as pltpu
from jax.sharding import PartitionSpec as P


def passed_along(shard, axis, by):
    length = lax.axis_size(axis)
    return lax.ppermute(shard, axis, [(i, (i + by) % length) for i in range(length)])


def by_slots(rows, route_ids, route_weights, w_gate_up, w_down):
    devices = lax.axis_size("expert")
    experts = devices // 2
    tokens = rows[0]
    tok_count, width = tokens.shape
    top_count = route_ids.shape[2]
    choices_flat = route_ids[0].reshape(-1)
    capacity = max(2, 2 * tok_count * top_count // experts)
    onehot = (choices_flat[:, None] == jnp.arange(experts, dtype=jnp.int32)[None, :]).astype(
        jnp.int32
    )
    before = jnp.cumsum(onehot, axis=0) - onehot
    slot = jnp.sum(before * onehot, axis=1)
    place = slot * experts + choices_flat
    slot_total = experts * capacity
    picker = (place[None, :] == jnp.arange(slot_total, dtype=jnp.int32)[:, None]).astype(
        jnp.bfloat16
    )
    token_pairs = jnp.repeat(tokens, top_count, axis=0)
    packed = jnp.dot(picker, token_pairs, preferred_element_type=jnp.float32).astype(jnp.bfloat16)
    w_in = w_gate_up[0]
    w_out = w_down[0]
    hidden = w_out.shape[0]
    outgoing = jnp.broadcast_to(
        packed.reshape(capacity, experts, 1, width), (capacity, experts, 2, width)
    )
    outgoing = outgoing.reshape(capacity, devices, width)
    block = lax.all_to_all(outgoing, "expert", split_axis=1, concat_axis=1, tiled=True)
    flat = block.reshape(-1, width)
    both = jnp.dot(flat, w_in, preferred_element_type=jnp.float32)
    active = (jax.nn.silu(both[:, :hidden]) * both[:, hidden:]).astype(jnp.bfloat16)
    result = jnp.dot(active, w_out, preferred_element_type=jnp.float32)
    partial_out = result.reshape(block.shape[0], block.shape[1], width).astype(jnp.bfloat16)
    returned = lax.all_to_all(partial_out, "expert", split_axis=1, concat_axis=1, tiled=True)
    returned = returned.reshape(capacity, experts, 2, width).astype(jnp.float32)
    expert_out = jnp.sum(returned, axis=2).astype(jnp.bfloat16).reshape(slot_total, width)
    pair_out = expert_out[place].astype(jnp.float32) * route_weights[0].reshape(-1)[:, None]
    layer_out = jnp.sum(pair_out.reshape(tok_count, top_count, width), axis=1).astype(jnp.bfloat16)
    return passed_along(layer_out, "section", 1)[None]


RING = (0, 1, 3, 2)
LANES = 128
TOKEN_LANE = 64


def on_ring(place):
    return place ^ (place >> 1)


def chip_at(chip, steps, flip):
    return (on_ring((on_ring(chip >> 1) + steps) & 3) << 1) | ((chip & 1) ^ flip)


def iota(shape, axis):
    return lax.broadcasted_iota(jnp.int32, shape, axis)


def ones_where(condition):
    return jnp.where(condition, 1.0, 0.0).astype(jnp.bfloat16)


def across(left, right):
    return lax.dot_general(left, right, (((0,), (0,)), ((), ())), preferred_element_type=jnp.float32)


def local_call(kernel, name, out_shape, in_specs, operands, scratch=(), limit=12, flops=0, moved=0):
    vmem = pl.BlockSpec(memory_space=pltpu.VMEM)
    return pl.pallas_call(
        kernel,
        out_shape=out_shape,
        in_specs=[vmem if spec is None else pl.BlockSpec(memory_space=spec) for spec in in_specs],
        out_specs=jax.tree.map(lambda _: vmem, out_shape),
        scratch_shapes=list(scratch),
        compiler_params=pltpu.CompilerParams(vmem_limit_bytes=limit << 20),
        cost_estimate=pl.CostEstimate(flops=flops, bytes_accessed=moved, transcendentals=0),
        name=name,
    )(*operands)


def prepare_kernel(ids_in, weights_in, rows_in, block, ids, weights, sems):
    tok_count, width = rows_in.shape
    top_count = ids.shape[0]
    experts = 2 * len(RING)
    copies = [
        pltpu.make_async_copy(ids_in, ids, sems.at[0]),
        pltpu.make_async_copy(weights_in, weights, sems.at[1]),
        pltpu.make_async_copy(rows_in, block.at[:, pl.ds(0, width)], sems.at[2]),
    ]
    for copy in copies:
        copy.start()
    square = (tok_count, tok_count)
    earlier = ones_where(iota(square, 0) < iota(square, 1))
    expert = iota((experts, tok_count), 0)
    unit = ones_where(iota((4 * experts, LANES), 0) == iota((4 * experts, LANES), 1))
    token = ones_where(iota((tok_count, LANES), 0) + TOKEN_LANE == iota((tok_count, LANES), 1))
    copies[0].wait()
    copies[1].wait()
    named = jnp.zeros((experts, tok_count), jnp.float32)
    scale = jnp.zeros((experts, tok_count), jnp.float32)
    for k in range(top_count):
        hit = ids[k : k + 1, :] == expert
        named = named + jnp.where(hit, 1.0, 0.0)
        scale = scale + jnp.where(hit, weights[k : k + 1, :], 0.0)
    rank = jnp.dot(named.astype(jnp.bfloat16), earlier, preferred_element_type=jnp.float32)
    notes = [jnp.where(named > 0.5, rank + 1.0, 0.0)]
    for _ in range(3):
        piece = scale.astype(jnp.bfloat16).astype(jnp.float32)
        scale = scale - piece
        notes.append(piece)
    notes = across(jnp.concatenate(notes, axis=0).astype(jnp.bfloat16), unit)
    block[:, width:] = notes.astype(jnp.bfloat16) + token
    copies[2].wait()


def prepare(ids, weights, tokens):
    tok_count, width = tokens.shape
    return local_call(
        prepare_kernel,
        "prepare",
        pltpu.VMEM((tok_count, width + LANES), jnp.bfloat16),
        [pl.ANY] * 3,
        tuple(pltpu.with_memory_space_constraint(x, pltpu.HBM) for x in (ids, weights, tokens)),
        [
            pltpu.VMEM(ids.shape, ids.dtype),
            pltpu.VMEM(weights.shape, weights.dtype),
            pltpu.SemaphoreType.DMA((3,)),
        ],
        limit=8,
    )


def choose_kernel(places, capacity, block, *refs):
    chip = lax.axis_index("expert") >> 1
    tok_count = block.shape[0]
    notes = block[:, -LANES:].astype(jnp.float32)
    lane = iota(notes.shape, 1)
    slot = iota((tok_count, len(places) * capacity), 1)
    code = jnp.zeros(slot.shape, jnp.float32)
    order = jnp.zeros(slot.shape, jnp.int32)
    for at, (steps, flip) in enumerate(places):
        wanted = chip_at(chip, steps, flip)
        column = jnp.sum(jnp.where(lane == wanted, notes, 0.0), axis=1, keepdims=True)
        code = jnp.where(slot >= at * capacity, column, code)
        order = jnp.where(slot >= at * capacity, slot + 1 - at * capacity, order)
    rows = across(ones_where(code == order.astype(jnp.float32)), block[...]).astype(jnp.bfloat16)
    for at in range(len(places)):
        refs[at][...] = rows[at * capacity : (at + 1) * capacity]


def choose(block, capacity, places):
    return local_call(
        functools.partial(choose_kernel, places, capacity),
        "choose",
        [jax.ShapeDtypeStruct((capacity, block.shape[1]), jnp.bfloat16) for _ in places],
        [None],
        (block,),
    )


def load_kernel(source, target, sem):
    copy = pltpu.make_async_copy(source, target, sem)
    copy.start()
    copy.wait()


def loaded(weights):
    return local_call(
        load_kernel,
        "loaded",
        pltpu.VMEM(weights.shape, weights.dtype),
        [pl.ANY],
        (weights,),
        [pltpu.SemaphoreType.DMA],
        limit=9,
        moved=2 * weights.size * weights.dtype.itemsize,
    )


def gated(both):
    hidden = both.shape[1] // 2
    gate = both[:, :hidden]
    return (gate / (1.0 + jnp.exp(-gate)) * both[:, hidden:]).astype(jnp.bfloat16)


def write_pieces(slots, total, outs):
    chip = lax.axis_index("expert") >> 1
    width = total.shape[1]
    experts = 2 * len(RING)
    notes = slots[:, width:].astype(jnp.float32)
    lane = iota(notes.shape, 1)
    mine = (lane >= experts) & (lane < 4 * experts) & ((lane & (experts - 1)) == chip)
    scale = jnp.sum(jnp.where(mine, notes, 0.0), axis=1, keepdims=True)
    start = 0
    for out in outs:
        stop = start + out.shape[0]
        out[:, :width] = (total[start:stop] * scale[start:stop]).astype(jnp.bfloat16)
        out[:, width:] = slots[start:stop, width:]
        start = stop


def near_kernel(*refs):
    pieces, (first, second, slots, total) = refs[:-4], refs[-4:]
    start = 0
    for piece in pieces:
        slots[start : start + piece.shape[0]] = piece[...]
        start += piece.shape[0]
    width = total.shape[1]
    both = jnp.dot(slots[:, :width], first[...], preferred_element_type=jnp.float32)
    total[...] = jnp.dot(gated(both), second[...], preferred_element_type=jnp.float32)


def near_pass(pieces, weights):
    count = sum(piece.shape[0] for piece in pieces)
    full = pieces[0].shape[1]
    return local_call(
        near_kernel,
        "near_pass",
        [
            jax.ShapeDtypeStruct((count, full), jnp.bfloat16),
            jax.ShapeDtypeStruct((count, full - LANES), jnp.float32),
        ],
        [None] * (len(pieces) + 2),
        (*pieces, *weights),
        moved=2 * sum(w.size for w in weights),
    )


def far_kernel(slots, before, first, second, *refs):
    outs, total = refs[:-1], refs[-1]
    width = total.shape[1]
    both = jnp.dot(slots[:, :width], first[...], preferred_element_type=jnp.float32)
    term = jnp.dot(gated(both), second[...], preferred_element_type=jnp.float32)
    total[...] = before[...] + term
    write_pieces(slots, total, outs)


def far_pass(slots, total, weights, capacity):
    count, full = slots.shape
    return local_call(
        far_kernel,
        "far_pass",
        [jax.ShapeDtypeStruct((capacity, full), jnp.bfloat16)] * (count // capacity),
        [None] * 4,
        (slots, total, *weights),
        [pltpu.VMEM(total.shape, jnp.float32)],
        limit=24,
        moved=2 * sum(w.size for w in weights),
    )


def combine_kernel(count, *refs):
    blocks, more, (out, slots) = refs[:count], refs[count:-2], refs[-2:]
    tok_count, width = out.shape
    start = 0
    for block in blocks:
        slots[start : start + block.shape[0]] = block[...]
        start += block.shape[0]
    token = slots[:, width:]
    part = width // 7
    for at in range(7):
        place = slice(at * part, (at + 1) * part)
        mixed = across(token, slots[:, place])[TOKEN_LANE : TOKEN_LANE + tok_count]
        for other in more:
            mixed = mixed + other[:, place].astype(jnp.float32)
        out[:, place] = mixed.astype(out.dtype)


def combine(blocks, tok_count, *more):
    capacity, full = blocks[0].shape
    return local_call(
        functools.partial(combine_kernel, len(blocks)),
        "combine",
        jax.ShapeDtypeStruct((tok_count, full - LANES), jnp.bfloat16),
        [None] * (len(blocks) + len(more)),
        (*blocks, *more),
        [pltpu.VMEM((capacity * len(blocks), full), jnp.bfloat16)],
    )


def sent(shard, sections, section_step, ring_step, flip):
    planes = len(RING)
    pairs = []
    for s in range(sections):
        for z in range(planes):
            for y in range(2):
                for core in range(2):
                    plane = RING[(RING.index(z) + ring_step) % planes]
                    target = (((s + section_step) % sections) * planes + plane) * 2 + (y ^ flip)
                    pairs.append((((s * planes + z) * 2 + y) * 2 + core, target * 2 + core))
    return lax.ppermute(shard, ("section", "expert"), pairs)


def after(value, other):
    return lax.optimization_barrier((value, other))[0]


def by_ring(rows, route_ids, route_weights, w_gate_up, w_down):
    sections = lax.axis_size("section")
    devices = lax.axis_size("expert")
    experts = devices // 2
    tokens = rows[0]
    tok_count = tokens.shape[0]
    top_count = route_ids.shape[2]
    capacity = max(2, 2 * tok_count * top_count // experts)
    swap = [(i, i ^ 1) for i in range(devices)]
    w_in, w_out = w_gate_up[0], w_down[0]
    far_out = lax.ppermute(w_out, "expert", swap)
    far_in = lax.ppermute(w_in, "expert", swap)
    block = prepare(route_ids[0].T, route_weights[0].T, tokens)
    block1 = sent(block, sections, 0, 1, 0)
    own0, other, back0, back1 = choose(block, capacity, ((0, 0), (0, 1), (3, 0), (3, 1)))
    other0 = sent(other, sections, 0, 0, 1)
    near = (loaded(after(w_in, own0)), loaded(after(w_out, own0)))
    block1 = after(block1, (near, other0))
    own1, other, on0, on1 = choose(block1, capacity, ((0, 0), (0, 1), (1, 0), (1, 1)))
    other1 = sent(other, sections, 0, 0, 1)
    own2 = sent(on0, sections, 0, 1, 0)
    other2 = sent(on1, sections, 0, 1, 1)
    back0, back1 = after((back0, back1), other1)
    own3 = sent(back0, sections, 0, 3, 0)
    other3 = sent(back1, sections, 0, 3, 1)
    pieces = (own0, other0, own1, own2, other2, other1, own3, other3)
    places = ((0, 0), (0, 1), (1, 0), (2, 0), (2, 1), (1, 1), (3, 0), (3, 1))
    slots, total = near_pass(pieces, near)
    pieces = far_pass(slots, total, (far_in, far_out), capacity)
    piece = dict(zip(places, pieces))
    blocks = [
        sent(piece[2, 1], sections, 0, 0, 1),
        sent(piece[1, 0], sections, 0, 1, 0),
        sent(piece[1, 1], sections, 0, 1, 1),
        piece[2, 0],
    ]
    total = sent(combine(blocks, tok_count), sections, 0, 1, 0)
    side = sent(piece[3, 1], sections, 0, 0, 1)
    straight = [sent(piece[0, flip], sections, 1, 0, flip) for flip in range(2)]
    total, side, straight = lax.optimization_barrier((total, side, straight))
    total = sent(combine([side, piece[3, 0]], tok_count, total), sections, 1, 1, 0)
    return combine(straight, tok_count, total)[None]


def per_device(rows, route_ids, route_weights, w_gate_up, w_down):
    experts = lax.axis_size("expert") // 2
    fits = experts == 2 * len(RING) and rows.shape[1] <= LANES - TOKEN_LANE
    plan = by_ring if fits else by_slots
    return plan(rows, route_ids, route_weights, w_gate_up, w_down)


def solution(mesh):
    in_specs = (
        P("section", "expert", None),
        P("section", "expert", None),
        P("section", "expert", None),
        P("section", None, "expert"),
        P("section", "expert", None),
    )
    out_specs = P("section", "expert", None)
    return jax.shard_map(
        per_device, mesh=mesh, in_specs=in_specs, out_specs=out_specs, check_vma=False
    )
```

```python
import functools

import jax
import jax.numpy as jnp
from jax import lax
from jax.experimental import pallas as pl
from jax.experimental.pallas import tpu as pltpu
from jax.sharding import PartitionSpec as P


def passed_along(shard, axis, by):
    length = lax.axis_size(axis)
    return lax.ppermute(shard, axis, [(i, (i + by) % length) for i in range(length)])


def by_slots(rows, route_ids, route_weights, w_gate_up, w_down):
    devices = lax.axis_size("expert")
    experts = devices // 2
    tokens = rows[0]
    tok_count, width = tokens.shape
    top_count = route_ids.shape[2]
    choices_flat = route_ids[0].reshape(-1)
    capacity = max(2, 2 * tok_count * top_count // experts)
    onehot = (choices_flat[:, None] == jnp.arange(experts, dtype=jnp.int32)[None, :]).astype(
        jnp.int32
    )
    before = jnp.cumsum(onehot, axis=0) - onehot
    slot = jnp.sum(before * onehot, axis=1)
    place = slot * experts + choices_flat
    slot_total = experts * capacity
    picker = (place[None, :] == jnp.arange(slot_total, dtype=jnp.int32)[:, None]).astype(
        jnp.bfloat16
    )
    token_pairs = jnp.repeat(tokens, top_count, axis=0)
    packed = jnp.dot(picker, token_pairs, preferred_element_type=jnp.float32).astype(jnp.bfloat16)
    w_in = w_gate_up[0]
    w_out = w_down[0]
    hidden = w_out.shape[0]
    outgoing = jnp.broadcast_to(
        packed.reshape(capacity, experts, 1, width), (capacity, experts, 2, width)
    )
    outgoing = outgoing.reshape(capacity, devices, width)
    block = lax.all_to_all(outgoing, "expert", split_axis=1, concat_axis=1, tiled=True)
    flat = block.reshape(-1, width)
    both = jnp.dot(flat, w_in, preferred_element_type=jnp.float32)
    active = (jax.nn.silu(both[:, :hidden]) * both[:, hidden:]).astype(jnp.bfloat16)
    result = jnp.dot(active, w_out, preferred_element_type=jnp.float32)
    partial_out = result.reshape(block.shape[0], block.shape[1], width).astype(jnp.bfloat16)
    returned = lax.all_to_all(partial_out, "expert", split_axis=1, concat_axis=1, tiled=True)
    returned = returned.reshape(capacity, experts, 2, width).astype(jnp.float32)
    expert_out = jnp.sum(returned, axis=2).astype(jnp.bfloat16).reshape(slot_total, width)
    pair_out = expert_out[place].astype(jnp.float32) * route_weights[0].reshape(-1)[:, None]
    layer_out = jnp.sum(pair_out.reshape(tok_count, top_count, width), axis=1).astype(jnp.bfloat16)
    return passed_along(layer_out, "section", 1)[None]


RING = (0, 1, 3, 2)
LANES = 128
TOKEN_LANE = 64


def on_ring(place):
    return place ^ (place >> 1)


def chip_at(chip, steps, flip):
    return (on_ring((on_ring(chip >> 1) + steps) & 3) << 1) | ((chip & 1) ^ flip)


def iota(shape, axis):
    return lax.broadcasted_iota(jnp.int32, shape, axis)


def ones_where(condition):
    return jnp.where(condition, 1.0, 0.0).astype(jnp.bfloat16)


def across(left, right):
    return lax.dot_general(left, right, (((0,), (0,)), ((), ())), preferred_element_type=jnp.float32)


def local_call(kernel, name, out_shape, in_specs, operands, scratch=(), limit=12, flops=0, moved=0):
    vmem = pl.BlockSpec(memory_space=pltpu.VMEM)
    return pl.pallas_call(
        kernel,
        out_shape=out_shape,
        in_specs=[vmem if spec is None else pl.BlockSpec(memory_space=spec) for spec in in_specs],
        out_specs=jax.tree.map(lambda _: vmem, out_shape),
        scratch_shapes=list(scratch),
        compiler_params=pltpu.CompilerParams(vmem_limit_bytes=limit << 20),
        cost_estimate=pl.CostEstimate(flops=flops, bytes_accessed=moved, transcendentals=0),
        name=name,
    )(*operands)


def prepare_kernel(ids_in, weights_in, rows_in, block, ids, weights, sems):
    tok_count, width = rows_in.shape
    top_count = ids.shape[0]
    experts = 2 * len(RING)
    copies = [
        pltpu.make_async_copy(ids_in, ids, sems.at[0]),
        pltpu.make_async_copy(weights_in, weights, sems.at[1]),
        pltpu.make_async_copy(rows_in, block.at[:, pl.ds(0, width)], sems.at[2]),
    ]
    for copy in copies:
        copy.start()
    square = (tok_count, tok_count)
    earlier = ones_where(iota(square, 0) < iota(square, 1))
    expert = iota((experts, tok_count), 0)
    unit = ones_where(iota((4 * experts, LANES), 0) == iota((4 * experts, LANES), 1))
    token = ones_where(iota((tok_count, LANES), 0) + TOKEN_LANE == iota((tok_count, LANES), 1))
    copies[0].wait()
    copies[1].wait()
    named = jnp.zeros((experts, tok_count), jnp.float32)
    scale = jnp.zeros((experts, tok_count), jnp.float32)
    for k in range(top_count):
        hit = ids[k : k + 1, :] == expert
        named = named + jnp.where(hit, 1.0, 0.0)
        scale = scale + jnp.where(hit, weights[k : k + 1, :], 0.0)
    rank = jnp.dot(named.astype(jnp.bfloat16), earlier, preferred_element_type=jnp.float32)
    notes = [jnp.where(named > 0.5, rank + 1.0, 0.0)]
    for _ in range(3):
        piece = scale.astype(jnp.bfloat16).astype(jnp.float32)
        scale = scale - piece
        notes.append(piece)
    notes = across(jnp.concatenate(notes, axis=0).astype(jnp.bfloat16), unit)
    block[:, width:] = notes.astype(jnp.bfloat16) + token
    copies[2].wait()


def prepare(ids, weights, tokens):
    tok_count, width = tokens.shape
    return local_call(
        prepare_kernel,
        "prepare",
        pltpu.VMEM((tok_count, width + LANES), jnp.bfloat16),
        [pl.ANY] * 3,
        tuple(pltpu.with_memory_space_constraint(x, pltpu.HBM) for x in (ids, weights, tokens)),
        [
            pltpu.VMEM(ids.shape, ids.dtype),
            pltpu.VMEM(weights.shape, weights.dtype),
            pltpu.SemaphoreType.DMA((3,)),
        ],
        limit=8,
    )


def choose_kernel(places, capacity, block, *refs):
    chip = lax.axis_index("expert") >> 1
    tok_count = block.shape[0]
    notes = block[:, -LANES:].astype(jnp.float32)
    lane = iota(notes.shape, 1)
    slot = iota((tok_count, len(places) * capacity), 1)
    code = jnp.zeros(slot.shape, jnp.float32)
    order = jnp.zeros(slot.shape, jnp.int32)
    for at, (steps, flip) in enumerate(places):
        wanted = chip_at(chip, steps, flip)
        column = jnp.sum(jnp.where(lane == wanted, notes, 0.0), axis=1, keepdims=True)
        code = jnp.where(slot >= at * capacity, column, code)
        order = jnp.where(slot >= at * capacity, slot + 1 - at * capacity, order)
    rows = across(ones_where(code == order.astype(jnp.float32)), block[...]).astype(jnp.bfloat16)
    for at in range(len(places)):
        refs[at][...] = rows[at * capacity : (at + 1) * capacity]


def choose(block, capacity, places):
    return local_call(
        functools.partial(choose_kernel, places, capacity),
        "choose",
        [jax.ShapeDtypeStruct((capacity, block.shape[1]), jnp.bfloat16) for _ in places],
        [None],
        (block,),
    )


def load_kernel(source, target, sem):
    copy = pltpu.make_async_copy(source, target, sem)
    copy.start()
    copy.wait()


def loaded(weights):
    return local_call(
        load_kernel,
        "loaded",
        pltpu.VMEM(weights.shape, weights.dtype),
        [pl.ANY],
        (weights,),
        [pltpu.SemaphoreType.DMA],
        limit=9,
        moved=2 * weights.size * weights.dtype.itemsize,
    )


def gated(both):
    hidden = both.shape[1] // 2
    gate = both[:, :hidden]
    return (gate / (1.0 + jnp.exp(-gate)) * both[:, hidden:]).astype(jnp.bfloat16)


def write_pieces(slots, total, outs):
    chip = lax.axis_index("expert") >> 1
    width = total.shape[1]
    experts = 2 * len(RING)
    notes = slots[:, width:].astype(jnp.float32)
    lane = iota(notes.shape, 1)
    mine = (lane >= experts) & (lane < 4 * experts) & ((lane & (experts - 1)) == chip)
    scale = jnp.sum(jnp.where(mine, notes, 0.0), axis=1, keepdims=True)
    start = 0
    for out in outs:
        stop = start + out.shape[0]
        out[:, :width] = (total[start:stop] * scale[start:stop]).astype(jnp.bfloat16)
        out[:, width:] = slots[start:stop, width:]
        start = stop


def near_kernel(*refs):
    pieces, (first, second, slots, total) = refs[:-4], refs[-4:]
    start = 0
    for piece in pieces:
        slots[start : start + piece.shape[0]] = piece[...]
        start += piece.shape[0]
    width = total.shape[1]
    both = jnp.dot(slots[:, :width], first[...], preferred_element_type=jnp.float32)
    total[...] = jnp.dot(gated(both), second[...], preferred_element_type=jnp.float32)


def near_pass(pieces, weights):
    count = sum(piece.shape[0] for piece in pieces)
    full = pieces[0].shape[1]
    return local_call(
        near_kernel,
        "near_pass",
        [
            jax.ShapeDtypeStruct((count, full), jnp.bfloat16),
            jax.ShapeDtypeStruct((count, full - LANES), jnp.float32),
        ],
        [None] * (len(pieces) + 2),
        (*pieces, *weights),
        moved=2 * sum(w.size for w in weights),
    )


def far_kernel(slots, before, first, second, *refs):
    outs, total = refs[:-1], refs[-1]
    width = total.shape[1]
    both = jnp.dot(slots[:, :width], first[...], preferred_element_type=jnp.float32)
    term = jnp.dot(gated(both), second[...], preferred_element_type=jnp.float32)
    total[...] = before[...] + term
    write_pieces(slots, total, outs)


def far_pass(slots, total, weights, capacity):
    count, full = slots.shape
    return local_call(
        far_kernel,
        "far_pass",
        [jax.ShapeDtypeStruct((capacity, full), jnp.bfloat16)] * (count // capacity),
        [None] * 4,
        (slots, total, *weights),
        [pltpu.VMEM(total.shape, jnp.float32)],
        limit=24,
        moved=2 * sum(w.size for w in weights),
    )


def combine_kernel(count, *refs):
    blocks, more, (out, slots) = refs[:count], refs[count:-2], refs[-2:]
    tok_count, width = out.shape
    start = 0
    for block in blocks:
        slots[start : start + block.shape[0]] = block[...]
        start += block.shape[0]
    token = slots[:, width:]
    part = width // 7
    for at in range(7):
        place = slice(at * part, (at + 1) * part)
        mixed = across(token, slots[:, place])[TOKEN_LANE : TOKEN_LANE + tok_count]
        for other in more:
            mixed = mixed + other[:, place].astype(jnp.float32)
        out[:, place] = mixed.astype(out.dtype)


def combine(blocks, tok_count, *more):
    capacity, full = blocks[0].shape
    return local_call(
        functools.partial(combine_kernel, len(blocks)),
        "combine",
        jax.ShapeDtypeStruct((tok_count, full - LANES), jnp.bfloat16),
        [None] * (len(blocks) + len(more)),
        (*blocks, *more),
        [pltpu.VMEM((capacity * len(blocks), full), jnp.bfloat16)],
    )


def sent(shard, sections, section_step, ring_step, flip):
    planes = len(RING)
    pairs = []
    for s in range(sections):
        for z in range(planes):
            for y in range(2):
                for core in range(2):
                    plane = RING[(RING.index(z) + ring_step) % planes]
                    target = (((s + section_step) % sections) * planes + plane) * 2 + (y ^ flip)
                    pairs.append((((s * planes + z) * 2 + y) * 2 + core, target * 2 + core))
    return lax.ppermute(shard, ("section", "expert"), pairs)


def after(value, other):
    return lax.optimization_barrier((value, other))[0]


def by_ring(rows, route_ids, route_weights, w_gate_up, w_down):
    sections = lax.axis_size("section")
    devices = lax.axis_size("expert")
    experts = devices // 2
    tokens = rows[0]
    tok_count = tokens.shape[0]
    top_count = route_ids.shape[2]
    capacity = max(2, 2 * tok_count * top_count // experts)
    swap = [(i, i ^ 1) for i in range(devices)]
    w_in, w_out = w_gate_up[0], w_down[0]
    far_out = lax.ppermute(w_out, "expert", swap)
    far_in = lax.ppermute(w_in, "expert", swap)
    block = prepare(route_ids[0].T, route_weights[0].T, tokens)
    block1 = sent(block, sections, 0, 1, 0)
    own0, other, back0, back1 = choose(block, capacity, ((0, 0), (0, 1), (3, 0), (3, 1)))
    other0 = sent(other, sections, 0, 0, 1)
    near = (loaded(after(w_in, own0)), loaded(after(w_out, own0)))
    block1 = after(block1, (near, other0))
    own1, other, on0, on1 = choose(block1, capacity, ((0, 0), (0, 1), (1, 0), (1, 1)))
    other1 = sent(other, sections, 0, 0, 1)
    own2 = sent(on0, sections, 0, 1, 0)
    other2 = sent(on1, sections, 0, 1, 1)
    back0, back1 = after((back0, back1), other1)
    own3 = sent(back0, sections, 0, 3, 0)
    other3 = sent(back1, sections, 0, 3, 1)
    pieces = (own0, other0, own1, own2, other2, other1, own3, other3)
    places = ((0, 0), (0, 1), (1, 0), (2, 0), (2, 1), (1, 1), (3, 0), (3, 1))
    slots, total = near_pass(pieces, near)
    pieces = far_pass(slots, total, (far_in, far_out), capacity)
    piece = dict(zip(places, pieces))
    first = [
        sent(piece[0, 0], sections, 1, 0, 0),
        sent(piece[2, 1], sections, 0, 1, 1),
        sent(piece[3, 1], sections, 0, 0, 1),
        sent(piece[2, 0], sections, 0, 1, 0),
    ]
    zero, *merged = lax.optimization_barrier(first)
    merged.append(piece[3, 0])
    straight = [zero, sent(piece[0, 1], sections, 1, 0, 1)]
    straight += [sent(piece[1, flip], sections, 1, -1, flip) for flip in range(2)]
    merged = sent(combine(merged, tok_count), sections, 1, 1, 0)
    return combine(straight, tok_count, merged)[None]


def per_device(rows, route_ids, route_weights, w_gate_up, w_down):
    experts = lax.axis_size("expert") // 2
    fits = experts == 2 * len(RING) and rows.shape[1] <= LANES - TOKEN_LANE
    plan = by_ring if fits else by_slots
    return plan(rows, route_ids, route_weights, w_gate_up, w_down)


def solution(mesh):
    in_specs = (
        P("section", "expert", None),
        P("section", "expert", None),
        P("section", "expert", None),
        P("section", None, "expert"),
        P("section", "expert", None),
    )
    out_specs = P("section", "expert", None)
    return jax.shard_map(
        per_device, mesh=mesh, in_specs=in_specs, out_specs=out_specs, check_vma=False
    )
```

```python
import functools

import jax
import jax.numpy as jnp
from jax import lax
from jax.experimental import pallas as pl
from jax.experimental.pallas import tpu as pltpu
from jax.sharding import PartitionSpec as P


def passed_along(shard, axis, by):
    length = lax.axis_size(axis)
    return lax.ppermute(shard, axis, [(i, (i + by) % length) for i in range(length)])


def by_slots(rows, route_ids, route_weights, w_gate_up, w_down):
    devices = lax.axis_size("expert")
    experts = devices // 2
    tokens = rows[0]
    tok_count, width = tokens.shape
    top_count = route_ids.shape[2]
    choices_flat = route_ids[0].reshape(-1)
    capacity = max(2, 2 * tok_count * top_count // experts)
    onehot = (choices_flat[:, None] == jnp.arange(experts, dtype=jnp.int32)[None, :]).astype(
        jnp.int32
    )
    before = jnp.cumsum(onehot, axis=0) - onehot
    slot = jnp.sum(before * onehot, axis=1)
    place = slot * experts + choices_flat
    slot_total = experts * capacity
    picker = (place[None, :] == jnp.arange(slot_total, dtype=jnp.int32)[:, None]).astype(
        jnp.bfloat16
    )
    token_pairs = jnp.repeat(tokens, top_count, axis=0)
    packed = jnp.dot(picker, token_pairs, preferred_element_type=jnp.float32).astype(jnp.bfloat16)
    w_in = w_gate_up[0]
    w_out = w_down[0]
    hidden = w_out.shape[0]
    outgoing = jnp.broadcast_to(
        packed.reshape(capacity, experts, 1, width), (capacity, experts, 2, width)
    )
    outgoing = outgoing.reshape(capacity, devices, width)
    block = lax.all_to_all(outgoing, "expert", split_axis=1, concat_axis=1, tiled=True)
    flat = block.reshape(-1, width)
    both = jnp.dot(flat, w_in, preferred_element_type=jnp.float32)
    active = (jax.nn.silu(both[:, :hidden]) * both[:, hidden:]).astype(jnp.bfloat16)
    result = jnp.dot(active, w_out, preferred_element_type=jnp.float32)
    partial_out = result.reshape(block.shape[0], block.shape[1], width).astype(jnp.bfloat16)
    returned = lax.all_to_all(partial_out, "expert", split_axis=1, concat_axis=1, tiled=True)
    returned = returned.reshape(capacity, experts, 2, width).astype(jnp.float32)
    expert_out = jnp.sum(returned, axis=2).astype(jnp.bfloat16).reshape(slot_total, width)
    pair_out = expert_out[place].astype(jnp.float32) * route_weights[0].reshape(-1)[:, None]
    layer_out = jnp.sum(pair_out.reshape(tok_count, top_count, width), axis=1).astype(jnp.bfloat16)
    return passed_along(layer_out, "section", 1)[None]


RING = (0, 1, 3, 2)
LANES = 128
TOKEN_LANE = 64


def on_ring(place):
    return place ^ (place >> 1)


def chip_at(chip, steps, flip):
    return (on_ring((on_ring(chip >> 1) + steps) & 3) << 1) | ((chip & 1) ^ flip)


def iota(shape, axis):
    return lax.broadcasted_iota(jnp.int32, shape, axis)


def ones_where(condition):
    return jnp.where(condition, 1.0, 0.0).astype(jnp.bfloat16)


def across(left, right):
    return lax.dot_general(left, right, (((0,), (0,)), ((), ())), preferred_element_type=jnp.float32)


def local_call(kernel, name, out_shape, in_specs, operands, scratch=(), limit=12, flops=0, moved=0):
    vmem = pl.BlockSpec(memory_space=pltpu.VMEM)
    return pl.pallas_call(
        kernel,
        out_shape=out_shape,
        in_specs=[vmem if spec is None else pl.BlockSpec(memory_space=spec) for spec in in_specs],
        out_specs=jax.tree.map(lambda _: vmem, out_shape),
        scratch_shapes=list(scratch),
        compiler_params=pltpu.CompilerParams(vmem_limit_bytes=limit << 20),
        cost_estimate=pl.CostEstimate(flops=flops, bytes_accessed=moved, transcendentals=0),
        name=name,
    )(*operands)


def prepare_kernel(ids_in, weights_in, rows_in, block, ids, weights, sems):
    tok_count, width = rows_in.shape
    top_count = ids.shape[0]
    experts = 2 * len(RING)
    copies = [
        pltpu.make_async_copy(ids_in, ids, sems.at[0]),
        pltpu.make_async_copy(weights_in, weights, sems.at[1]),
        pltpu.make_async_copy(rows_in, block.at[:, pl.ds(0, width)], sems.at[2]),
    ]
    for copy in copies:
        copy.start()
    square = (tok_count, tok_count)
    earlier = ones_where(iota(square, 0) < iota(square, 1))
    expert = iota((experts, tok_count), 0)
    unit = ones_where(iota((4 * experts, LANES), 0) == iota((4 * experts, LANES), 1))
    token = ones_where(iota((tok_count, LANES), 0) + TOKEN_LANE == iota((tok_count, LANES), 1))
    copies[0].wait()
    copies[1].wait()
    named = jnp.zeros((experts, tok_count), jnp.float32)
    scale = jnp.zeros((experts, tok_count), jnp.float32)
    for k in range(top_count):
        hit = ids[k : k + 1, :] == expert
        named = named + jnp.where(hit, 1.0, 0.0)
        scale = scale + jnp.where(hit, weights[k : k + 1, :], 0.0)
    rank = jnp.dot(named.astype(jnp.bfloat16), earlier, preferred_element_type=jnp.float32)
    notes = [jnp.where(named > 0.5, rank + 1.0, 0.0)]
    for _ in range(3):
        piece = scale.astype(jnp.bfloat16).astype(jnp.float32)
        scale = scale - piece
        notes.append(piece)
    notes = across(jnp.concatenate(notes, axis=0).astype(jnp.bfloat16), unit)
    block[:, width:] = notes.astype(jnp.bfloat16) + token
    copies[2].wait()


def prepare(ids, weights, tokens):
    tok_count, width = tokens.shape
    return local_call(
        prepare_kernel,
        "prepare",
        pltpu.VMEM((tok_count, width + LANES), jnp.bfloat16),
        [pl.ANY] * 3,
        tuple(pltpu.with_memory_space_constraint(x, pltpu.HBM) for x in (ids, weights, tokens)),
        [
            pltpu.VMEM(ids.shape, ids.dtype),
            pltpu.VMEM(weights.shape, weights.dtype),
            pltpu.SemaphoreType.DMA((3,)),
        ],
        limit=8,
    )


def choose_kernel(places, capacity, block, *refs):
    chip = lax.axis_index("expert") >> 1
    tok_count = block.shape[0]
    notes = block[:, -LANES:].astype(jnp.float32)
    lane = iota(notes.shape, 1)
    slot = iota((tok_count, len(places) * capacity), 1)
    code = jnp.zeros(slot.shape, jnp.float32)
    order = jnp.zeros(slot.shape, jnp.int32)
    for at, (steps, flip) in enumerate(places):
        wanted = chip_at(chip, steps, flip)
        column = jnp.sum(jnp.where(lane == wanted, notes, 0.0), axis=1, keepdims=True)
        code = jnp.where(slot >= at * capacity, column, code)
        order = jnp.where(slot >= at * capacity, slot + 1 - at * capacity, order)
    rows = across(ones_where(code == order.astype(jnp.float32)), block[...]).astype(jnp.bfloat16)
    for at in range(len(places)):
        refs[at][...] = rows[at * capacity : (at + 1) * capacity]


def choose(block, capacity, places):
    return local_call(
        functools.partial(choose_kernel, places, capacity),
        "choose",
        [jax.ShapeDtypeStruct((capacity, block.shape[1]), jnp.bfloat16) for _ in places],
        [None],
        (block,),
    )


def load_kernel(source, target, sem):
    copy = pltpu.make_async_copy(source, target, sem)
    copy.start()
    copy.wait()


def loaded(weights):
    return local_call(
        load_kernel,
        "loaded",
        pltpu.VMEM(weights.shape, weights.dtype),
        [pl.ANY],
        (weights,),
        [pltpu.SemaphoreType.DMA],
        limit=9,
        moved=2 * weights.size * weights.dtype.itemsize,
    )


def gated(both):
    hidden = both.shape[1] // 2
    gate = both[:, :hidden]
    return (gate / (1.0 + jnp.exp(-gate)) * both[:, hidden:]).astype(jnp.bfloat16)


def write_pieces(slots, total, outs):
    chip = lax.axis_index("expert") >> 1
    width = total.shape[1]
    experts = 2 * len(RING)
    notes = slots[:, width:].astype(jnp.float32)
    lane = iota(notes.shape, 1)
    mine = (lane >= experts) & (lane < 4 * experts) & ((lane & (experts - 1)) == chip)
    scale = jnp.sum(jnp.where(mine, notes, 0.0), axis=1, keepdims=True)
    start = 0
    for out in outs:
        stop = start + out.shape[0]
        out[:, :width] = (total[start:stop] * scale[start:stop]).astype(jnp.bfloat16)
        out[:, width:] = slots[start:stop, width:]
        start = stop


def near_kernel(*refs):
    pieces, (first, second, slots, total) = refs[:-4], refs[-4:]
    start = 0
    for piece in pieces:
        slots[start : start + piece.shape[0]] = piece[...]
        start += piece.shape[0]
    width = total.shape[1]
    both = jnp.dot(slots[:, :width], first[...], preferred_element_type=jnp.float32)
    total[...] = jnp.dot(gated(both), second[...], preferred_element_type=jnp.float32)


def near_pass(pieces, weights):
    count = sum(piece.shape[0] for piece in pieces)
    full = pieces[0].shape[1]
    return local_call(
        near_kernel,
        "near_pass",
        [
            jax.ShapeDtypeStruct((count, full), jnp.bfloat16),
            jax.ShapeDtypeStruct((count, full - LANES), jnp.float32),
        ],
        [None] * (len(pieces) + 2),
        (*pieces, *weights),
        moved=2 * sum(w.size for w in weights),
    )


def far_kernel(slots, before, first, second, *refs):
    outs, total = refs[:-1], refs[-1]
    width = total.shape[1]
    both = jnp.dot(slots[:, :width], first[...], preferred_element_type=jnp.float32)
    term = jnp.dot(gated(both), second[...], preferred_element_type=jnp.float32)
    total[...] = before[...] + term
    write_pieces(slots, total, outs)


def far_pass(slots, total, weights, capacity):
    count, full = slots.shape
    return local_call(
        far_kernel,
        "far_pass",
        [jax.ShapeDtypeStruct((capacity, full), jnp.bfloat16)] * (count // capacity),
        [None] * 4,
        (slots, total, *weights),
        [pltpu.VMEM(total.shape, jnp.float32)],
        limit=24,
        moved=2 * sum(w.size for w in weights),
    )


def combine_kernel(count, *refs):
    blocks, more, (out, slots) = refs[:count], refs[count:-2], refs[-2:]
    tok_count, width = out.shape
    start = 0
    for block in blocks:
        slots[start : start + block.shape[0]] = block[...]
        start += block.shape[0]
    token = slots[:, width:]
    part = width // 7
    for at in range(7):
        place = slice(at * part, (at + 1) * part)
        mixed = across(token, slots[:, place])[TOKEN_LANE : TOKEN_LANE + tok_count]
        for other in more:
            mixed = mixed + other[:, place].astype(jnp.float32)
        out[:, place] = mixed.astype(out.dtype)


def combine(blocks, tok_count, *more):
    capacity, full = blocks[0].shape
    return local_call(
        functools.partial(combine_kernel, len(blocks)),
        "combine",
        jax.ShapeDtypeStruct((tok_count, full - LANES), jnp.bfloat16),
        [None] * (len(blocks) + len(more)),
        (*blocks, *more),
        [pltpu.VMEM((capacity * len(blocks), full), jnp.bfloat16)],
    )


def sent(shard, sections, section_step, ring_step, flip):
    planes = len(RING)
    pairs = []
    for s in range(sections):
        for z in range(planes):
            for y in range(2):
                for core in range(2):
                    plane = RING[(RING.index(z) + ring_step) % planes]
                    target = (((s + section_step) % sections) * planes + plane) * 2 + (y ^ flip)
                    pairs.append((((s * planes + z) * 2 + y) * 2 + core, target * 2 + core))
    return lax.ppermute(shard, ("section", "expert"), pairs)


def after(value, other):
    return lax.optimization_barrier((value, other))[0]


def by_ring(rows, route_ids, route_weights, w_gate_up, w_down):
    sections = lax.axis_size("section")
    devices = lax.axis_size("expert")
    experts = devices // 2
    tokens = rows[0]
    tok_count = tokens.shape[0]
    top_count = route_ids.shape[2]
    capacity = max(2, 2 * tok_count * top_count // experts)
    swap = [(i, i ^ 1) for i in range(devices)]
    w_in, w_out = w_gate_up[0], w_down[0]
    far_out = lax.ppermute(w_out, "expert", swap)
    far_in = lax.ppermute(w_in, "expert", swap)
    block = prepare(route_ids[0].T, route_weights[0].T, tokens)
    block1 = sent(block, sections, 0, 1, 0)
    own0, other, back0, back1 = choose(block, capacity, ((0, 0), (0, 1), (3, 0), (3, 1)))
    other0 = sent(other, sections, 0, 0, 1)
    near = (loaded(after(w_in, own0)), loaded(after(w_out, own0)))
    block1 = after(block1, (near, other0))
    own1, other, on0, on1 = choose(block1, capacity, ((0, 0), (0, 1), (1, 0), (1, 1)))
    other1 = sent(other, sections, 0, 0, 1)
    own2 = sent(on0, sections, 0, 1, 0)
    other2 = sent(on1, sections, 0, 1, 1)
    back1, back0 = after((back1, back0), other1)
    other3 = sent(back1, sections, 0, 3, 1)
    own3 = sent(back0, sections, 0, 3, 0)
    pieces = (own0, other0, own1, own2, other2, other1, other3, own3)
    places = ((0, 0), (0, 1), (1, 0), (2, 0), (2, 1), (1, 1), (3, 1), (3, 0))
    slots, total = near_pass(pieces, near)
    pieces = far_pass(slots, total, (far_in, far_out), capacity)
    piece = dict(zip(places, pieces))
    first = [
        sent(piece[0, 1], sections, 1, 0, 1),
        sent(piece[2, 1], sections, 0, 1, 1),
        sent(piece[3, 1], sections, 0, 0, 1),
        sent(piece[2, 0], sections, 0, 1, 0),
        sent(piece[0, 0], sections, 1, 0, 0),
    ]
    one, *merged, zero = lax.optimization_barrier(first)
    merged.append(piece[3, 0])
    straight = [zero, one]
    straight += [sent(piece[1, flip], sections, 1, -1, flip) for flip in range(2)]
    merged = sent(combine(merged, tok_count), sections, 1, 1, 0)
    return combine(straight, tok_count, merged)[None]


def per_device(rows, route_ids, route_weights, w_gate_up, w_down):
    experts = lax.axis_size("expert") // 2
    fits = experts == 2 * len(RING) and rows.shape[1] <= LANES - TOKEN_LANE
    plan = by_ring if fits else by_slots
    return plan(rows, route_ids, route_weights, w_gate_up, w_down)


def solution(mesh):
    in_specs = (
        P("section", "expert", None),
        P("section", "expert", None),
        P("section", "expert", None),
        P("section", None, "expert"),
        P("section", "expert", None),
    )
    out_specs = P("section", "expert", None)
    return jax.shard_map(
        per_device, mesh=mesh, in_specs=in_specs, out_specs=out_specs, check_vma=False
    )
```

```python
import functools

import jax
import jax.numpy as jnp
from jax import lax
from jax.experimental import pallas as pl
from jax.experimental.pallas import tpu as pltpu
from jax.sharding import PartitionSpec as P


def passed_along(shard, axis, by):
    length = lax.axis_size(axis)
    return lax.ppermute(shard, axis, [(i, (i + by) % length) for i in range(length)])


def by_slots(rows, route_ids, route_weights, w_gate_up, w_down):
    devices = lax.axis_size("expert")
    experts = devices // 2
    tokens = rows[0]
    tok_count, width = tokens.shape
    top_count = route_ids.shape[2]
    choices_flat = route_ids[0].reshape(-1)
    capacity = max(2, 2 * tok_count * top_count // experts)
    onehot = (choices_flat[:, None] == jnp.arange(experts, dtype=jnp.int32)[None, :]).astype(
        jnp.int32
    )
    before = jnp.cumsum(onehot, axis=0) - onehot
    slot = jnp.sum(before * onehot, axis=1)
    place = slot * experts + choices_flat
    slot_total = experts * capacity
    picker = (place[None, :] == jnp.arange(slot_total, dtype=jnp.int32)[:, None]).astype(
        jnp.bfloat16
    )
    token_pairs = jnp.repeat(tokens, top_count, axis=0)
    packed = jnp.dot(picker, token_pairs, preferred_element_type=jnp.float32).astype(jnp.bfloat16)
    w_in = w_gate_up[0]
    w_out = w_down[0]
    hidden = w_out.shape[0]
    outgoing = jnp.broadcast_to(
        packed.reshape(capacity, experts, 1, width), (capacity, experts, 2, width)
    )
    outgoing = outgoing.reshape(capacity, devices, width)
    block = lax.all_to_all(outgoing, "expert", split_axis=1, concat_axis=1, tiled=True)
    flat = block.reshape(-1, width)
    both = jnp.dot(flat, w_in, preferred_element_type=jnp.float32)
    active = (jax.nn.silu(both[:, :hidden]) * both[:, hidden:]).astype(jnp.bfloat16)
    result = jnp.dot(active, w_out, preferred_element_type=jnp.float32)
    partial_out = result.reshape(block.shape[0], block.shape[1], width).astype(jnp.bfloat16)
    returned = lax.all_to_all(partial_out, "expert", split_axis=1, concat_axis=1, tiled=True)
    returned = returned.reshape(capacity, experts, 2, width).astype(jnp.float32)
    expert_out = jnp.sum(returned, axis=2).astype(jnp.bfloat16).reshape(slot_total, width)
    pair_out = expert_out[place].astype(jnp.float32) * route_weights[0].reshape(-1)[:, None]
    layer_out = jnp.sum(pair_out.reshape(tok_count, top_count, width), axis=1).astype(jnp.bfloat16)
    return passed_along(layer_out, "section", 1)[None]


RING = (0, 1, 3, 2)
LANES = 128
TOKEN_LANE = 64


def on_ring(place):
    return place ^ (place >> 1)


def chip_at(chip, steps, flip):
    return (on_ring((on_ring(chip >> 1) + steps) & 3) << 1) | ((chip & 1) ^ flip)


def iota(shape, axis):
    return lax.broadcasted_iota(jnp.int32, shape, axis)


def ones_where(condition):
    return jnp.where(condition, 1.0, 0.0).astype(jnp.bfloat16)


def across(left, right):
    return lax.dot_general(left, right, (((0,), (0,)), ((), ())), preferred_element_type=jnp.float32)


def local_call(kernel, name, out_shape, in_specs, operands, scratch=(), limit=12, flops=0, moved=0):
    vmem = pl.BlockSpec(memory_space=pltpu.VMEM)
    return pl.pallas_call(
        kernel,
        out_shape=out_shape,
        in_specs=[vmem if spec is None else pl.BlockSpec(memory_space=spec) for spec in in_specs],
        out_specs=jax.tree.map(lambda _: vmem, out_shape),
        scratch_shapes=list(scratch),
        compiler_params=pltpu.CompilerParams(vmem_limit_bytes=limit << 20),
        cost_estimate=pl.CostEstimate(flops=flops, bytes_accessed=moved, transcendentals=0),
        name=name,
    )(*operands)


def prepare_kernel(ids_in, weights_in, rows_in, block, ids, weights, sems):
    tok_count, width = rows_in.shape
    top_count = ids.shape[0]
    experts = 2 * len(RING)
    copies = [
        pltpu.make_async_copy(ids_in, ids, sems.at[0]),
        pltpu.make_async_copy(weights_in, weights, sems.at[1]),
        pltpu.make_async_copy(rows_in, block.at[:, pl.ds(0, width)], sems.at[2]),
    ]
    for copy in copies:
        copy.start()
    square = (tok_count, tok_count)
    earlier = ones_where(iota(square, 0) < iota(square, 1))
    expert = iota((experts, tok_count), 0)
    unit = ones_where(iota((4 * experts, LANES), 0) == iota((4 * experts, LANES), 1))
    token = ones_where(iota((tok_count, LANES), 0) + TOKEN_LANE == iota((tok_count, LANES), 1))
    copies[0].wait()
    copies[1].wait()
    named = jnp.zeros((experts, tok_count), jnp.float32)
    scale = jnp.zeros((experts, tok_count), jnp.float32)
    for k in range(top_count):
        hit = ids[k : k + 1, :] == expert
        named = named + jnp.where(hit, 1.0, 0.0)
        scale = scale + jnp.where(hit, weights[k : k + 1, :], 0.0)
    rank = jnp.dot(named.astype(jnp.bfloat16), earlier, preferred_element_type=jnp.float32)
    notes = [jnp.where(named > 0.5, rank + 1.0, 0.0)]
    for _ in range(3):
        piece = scale.astype(jnp.bfloat16).astype(jnp.float32)
        scale = scale - piece
        notes.append(piece)
    notes = across(jnp.concatenate(notes, axis=0).astype(jnp.bfloat16), unit)
    block[:, width:] = notes.astype(jnp.bfloat16) + token
    copies[2].wait()


def prepare(ids, weights, tokens):
    tok_count, width = tokens.shape
    return local_call(
        prepare_kernel,
        "prepare",
        pltpu.VMEM((tok_count, width + LANES), jnp.bfloat16),
        [pl.ANY] * 3,
        tuple(pltpu.with_memory_space_constraint(x, pltpu.HBM) for x in (ids, weights, tokens)),
        [
            pltpu.VMEM(ids.shape, ids.dtype),
            pltpu.VMEM(weights.shape, weights.dtype),
            pltpu.SemaphoreType.DMA((3,)),
        ],
        limit=8,
    )


def choose_kernel(places, capacity, block, *refs):
    chip = lax.axis_index("expert") >> 1
    tok_count = block.shape[0]
    notes = block[:, -LANES:].astype(jnp.float32)
    lane = iota(notes.shape, 1)
    slot = iota((tok_count, len(places) * capacity), 1)
    code = jnp.zeros(slot.shape, jnp.float32)
    order = jnp.zeros(slot.shape, jnp.int32)
    for at, (steps, flip) in enumerate(places):
        wanted = chip_at(chip, steps, flip)
        column = jnp.sum(jnp.where(lane == wanted, notes, 0.0), axis=1, keepdims=True)
        code = jnp.where(slot >= at * capacity, column, code)
        order = jnp.where(slot >= at * capacity, slot + 1 - at * capacity, order)
    rows = across(ones_where(code == order.astype(jnp.float32)), block[...]).astype(jnp.bfloat16)
    for at in range(len(places)):
        refs[at][...] = rows[at * capacity : (at + 1) * capacity]


def choose(block, capacity, places):
    return local_call(
        functools.partial(choose_kernel, places, capacity),
        "choose",
        [jax.ShapeDtypeStruct((capacity, block.shape[1]), jnp.bfloat16) for _ in places],
        [None],
        (block,),
    )


def load_kernel(source, target, sem):
    copy = pltpu.make_async_copy(source, target, sem)
    copy.start()
    copy.wait()


def loaded(weights):
    return local_call(
        load_kernel,
        "loaded",
        pltpu.VMEM(weights.shape, weights.dtype),
        [pl.ANY],
        (weights,),
        [pltpu.SemaphoreType.DMA],
        limit=9,
        moved=2 * weights.size * weights.dtype.itemsize,
    )


def gated(both):
    hidden = both.shape[1] // 2
    gate = both[:, :hidden]
    return (gate / (1.0 + jnp.exp(-gate)) * both[:, hidden:]).astype(jnp.bfloat16)


def write_pieces(slots, total, outs):
    chip = lax.axis_index("expert") >> 1
    width = total.shape[1]
    experts = 2 * len(RING)
    notes = slots[:, width:].astype(jnp.float32)
    lane = iota(notes.shape, 1)
    mine = (lane >= experts) & (lane < 4 * experts) & ((lane & (experts - 1)) == chip)
    scale = jnp.sum(jnp.where(mine, notes, 0.0), axis=1, keepdims=True)
    start = 0
    for out in outs:
        stop = start + out.shape[0]
        out[:, :width] = (total[start:stop] * scale[start:stop]).astype(jnp.bfloat16)
        out[:, width:] = slots[start:stop, width:]
        start = stop


def near_kernel(*refs):
    pieces, (first, second, slots, total) = refs[:-4], refs[-4:]
    start = 0
    for piece in pieces:
        slots[start : start + piece.shape[0]] = piece[...]
        start += piece.shape[0]
    width = total.shape[1]
    both = jnp.dot(slots[:, :width], first[...], preferred_element_type=jnp.float32)
    total[...] = jnp.dot(gated(both), second[...], preferred_element_type=jnp.float32)


def near_pass(pieces, weights):
    count = sum(piece.shape[0] for piece in pieces)
    full = pieces[0].shape[1]
    return local_call(
        near_kernel,
        "near_pass",
        [
            jax.ShapeDtypeStruct((count, full), jnp.bfloat16),
            jax.ShapeDtypeStruct((count, full - LANES), jnp.float32),
        ],
        [None] * (len(pieces) + 2),
        (*pieces, *weights),
        moved=2 * sum(w.size for w in weights),
    )


def far_kernel(slots, before, first, second, *refs):
    outs, total = refs[:-1], refs[-1]
    width = total.shape[1]
    both = jnp.dot(slots[:, :width], first[...], preferred_element_type=jnp.float32)
    term = jnp.dot(gated(both), second[...], preferred_element_type=jnp.float32)
    total[...] = before[...] + term
    write_pieces(slots, total, outs)


def far_pass(slots, total, weights, capacity):
    count, full = slots.shape
    return local_call(
        far_kernel,
        "far_pass",
        [jax.ShapeDtypeStruct((capacity, full), jnp.bfloat16)] * (count // capacity),
        [None] * 4,
        (slots, total, *weights),
        [pltpu.VMEM(total.shape, jnp.float32)],
        limit=24,
        moved=2 * sum(w.size for w in weights),
    )


def combine_kernel(count, *refs):
    blocks, more, (out, slots) = refs[:count], refs[count:-2], refs[-2:]
    tok_count, width = out.shape
    start = 0
    for block in blocks:
        slots[start : start + block.shape[0]] = block[...]
        start += block.shape[0]
    token = slots[:, width:]
    part = width // 7
    for at in range(7):
        place = slice(at * part, (at + 1) * part)
        mixed = across(token, slots[:, place])[TOKEN_LANE : TOKEN_LANE + tok_count]
        for other in more:
            mixed = mixed + other[:, place].astype(jnp.float32)
        out[:, place] = mixed.astype(out.dtype)


def combine(blocks, tok_count, *more):
    capacity, full = blocks[0].shape
    return local_call(
        functools.partial(combine_kernel, len(blocks)),
        "combine",
        jax.ShapeDtypeStruct((tok_count, full - LANES), jnp.bfloat16),
        [None] * (len(blocks) + len(more)),
        (*blocks, *more),
        [pltpu.VMEM((capacity * len(blocks), full), jnp.bfloat16)],
    )


def sent(shard, sections, section_step, ring_step, flip):
    planes = len(RING)
    pairs = []
    for s in range(sections):
        for z in range(planes):
            for y in range(2):
                for core in range(2):
                    plane = RING[(RING.index(z) + ring_step) % planes]
                    target = (((s + section_step) % sections) * planes + plane) * 2 + (y ^ flip)
                    pairs.append((((s * planes + z) * 2 + y) * 2 + core, target * 2 + core))
    return lax.ppermute(shard, ("section", "expert"), pairs)


def after(value, other):
    return lax.optimization_barrier((value, other))[0]


def by_ring(rows, route_ids, route_weights, w_gate_up, w_down):
    sections = lax.axis_size("section")
    devices = lax.axis_size("expert")
    experts = devices // 2
    tokens = rows[0]
    tok_count = tokens.shape[0]
    top_count = route_ids.shape[2]
    capacity = max(2, 2 * tok_count * top_count // experts)
    swap = [(i, i ^ 1) for i in range(devices)]
    w_in, w_out = w_gate_up[0], w_down[0]
    far_out = lax.ppermute(w_out, "expert", swap)
    far_in = lax.ppermute(w_in, "expert", swap)
    block = prepare(route_ids[0].T, route_weights[0].T, tokens)
    block1 = sent(block, sections, 0, 1, 0)
    own0, other, back0, back1 = choose(block, capacity, ((0, 0), (0, 1), (3, 0), (3, 1)))
    other0 = sent(other, sections, 0, 0, 1)
    near = (loaded(after(w_in, own0)), loaded(after(w_out, own0)))
    block1 = after(block1, (near, other0))
    own1, other, on0, on1 = choose(block1, capacity, ((0, 0), (0, 1), (1, 0), (1, 1)))
    other1 = sent(other, sections, 0, 0, 1)
    own2 = sent(on0, sections, 0, 1, 0)
    other2 = sent(on1, sections, 0, 1, 1)
    back1, back0 = after((back1, back0), other1)
    other3 = sent(back1, sections, 0, 3, 1)
    own3 = sent(back0, sections, 0, 3, 0)
    pieces = (own0, other0, own1, own2, other2, other1, other3, own3)
    places = ((0, 0), (0, 1), (1, 0), (2, 0), (2, 1), (1, 1), (3, 1), (3, 0))
    slots, total = near_pass(pieces, near)
    pieces = far_pass(slots, total, (far_in, far_out), capacity)
    piece = dict(zip(places, pieces))
    first = [
        sent(piece[0, 0], sections, 1, 0, 0),
        sent(piece[2, 1], sections, 0, 1, 1),
        sent(piece[3, 1], sections, 0, 0, 1),
        sent(piece[0, 1], sections, 1, 0, 1),
        sent(piece[2, 0], sections, 0, 1, 0),
    ]
    zero, two, three, one, four = lax.optimization_barrier(first)
    merged = [piece[3, 0], two, three, four]
    straight = [zero, one]
    straight += [sent(piece[1, flip], sections, 1, -1, flip) for flip in range(2)]
    merged = sent(combine(merged, tok_count), sections, 1, 1, 0)
    return combine(straight, tok_count, merged)[None]


def per_device(rows, route_ids, route_weights, w_gate_up, w_down):
    experts = lax.axis_size("expert") // 2
    fits = experts == 2 * len(RING) and rows.shape[1] <= LANES - TOKEN_LANE
    plan = by_ring if fits else by_slots
    return plan(rows, route_ids, route_weights, w_gate_up, w_down)


def solution(mesh):
    in_specs = (
        P("section", "expert", None),
        P("section", "expert", None),
        P("section", "expert", None),
        P("section", None, "expert"),
        P("section", "expert", None),
    )
    out_specs = P("section", "expert", None)
    return jax.shard_map(
        per_device, mesh=mesh, in_specs=in_specs, out_specs=out_specs, check_vma=False
    )
```

```python
import functools

import jax
import jax.numpy as jnp
from jax import lax
from jax.experimental import pallas as pl
from jax.experimental.pallas import tpu as pltpu
from jax.sharding import PartitionSpec as P


def passed_along(shard, axis, by):
    length = lax.axis_size(axis)
    return lax.ppermute(shard, axis, [(i, (i + by) % length) for i in range(length)])


def by_slots(rows, route_ids, route_weights, w_gate_up, w_down):
    devices = lax.axis_size("expert")
    experts = devices // 2
    tokens = rows[0]
    tok_count, width = tokens.shape
    top_count = route_ids.shape[2]
    choices_flat = route_ids[0].reshape(-1)
    capacity = max(2, 2 * tok_count * top_count // experts)
    onehot = (choices_flat[:, None] == jnp.arange(experts, dtype=jnp.int32)[None, :]).astype(
        jnp.int32
    )
    before = jnp.cumsum(onehot, axis=0) - onehot
    slot = jnp.sum(before * onehot, axis=1)
    place = slot * experts + choices_flat
    slot_total = experts * capacity
    picker = (place[None, :] == jnp.arange(slot_total, dtype=jnp.int32)[:, None]).astype(
        jnp.bfloat16
    )
    token_pairs = jnp.repeat(tokens, top_count, axis=0)
    packed = jnp.dot(picker, token_pairs, preferred_element_type=jnp.float32).astype(jnp.bfloat16)
    w_in = w_gate_up[0]
    w_out = w_down[0]
    hidden = w_out.shape[0]
    outgoing = jnp.broadcast_to(
        packed.reshape(capacity, experts, 1, width), (capacity, experts, 2, width)
    )
    outgoing = outgoing.reshape(capacity, devices, width)
    block = lax.all_to_all(outgoing, "expert", split_axis=1, concat_axis=1, tiled=True)
    flat = block.reshape(-1, width)
    both = jnp.dot(flat, w_in, preferred_element_type=jnp.float32)
    active = (jax.nn.silu(both[:, :hidden]) * both[:, hidden:]).astype(jnp.bfloat16)
    result = jnp.dot(active, w_out, preferred_element_type=jnp.float32)
    partial_out = result.reshape(block.shape[0], block.shape[1], width).astype(jnp.bfloat16)
    returned = lax.all_to_all(partial_out, "expert", split_axis=1, concat_axis=1, tiled=True)
    returned = returned.reshape(capacity, experts, 2, width).astype(jnp.float32)
    expert_out = jnp.sum(returned, axis=2).astype(jnp.bfloat16).reshape(slot_total, width)
    pair_out = expert_out[place].astype(jnp.float32) * route_weights[0].reshape(-1)[:, None]
    layer_out = jnp.sum(pair_out.reshape(tok_count, top_count, width), axis=1).astype(jnp.bfloat16)
    return passed_along(layer_out, "section", 1)[None]


RING = (0, 1, 3, 2)
LANES = 128
TOKEN_LANE = 64


def on_ring(place):
    return place ^ (place >> 1)


def chip_at(chip, steps, flip):
    return (on_ring((on_ring(chip >> 1) + steps) & 3) << 1) | ((chip & 1) ^ flip)


def iota(shape, axis):
    return lax.broadcasted_iota(jnp.int32, shape, axis)


def ones_where(condition):
    return jnp.where(condition, 1.0, 0.0).astype(jnp.bfloat16)


def across(left, right):
    return lax.dot_general(left, right, (((0,), (0,)), ((), ())), preferred_element_type=jnp.float32)


def local_call(kernel, name, out_shape, in_specs, operands, scratch=(), limit=12, flops=0, moved=0):
    vmem = pl.BlockSpec(memory_space=pltpu.VMEM)
    return pl.pallas_call(
        kernel,
        out_shape=out_shape,
        in_specs=[vmem if spec is None else pl.BlockSpec(memory_space=spec) for spec in in_specs],
        out_specs=jax.tree.map(lambda _: vmem, out_shape),
        scratch_shapes=list(scratch),
        compiler_params=pltpu.CompilerParams(vmem_limit_bytes=limit << 20),
        cost_estimate=pl.CostEstimate(flops=flops, bytes_accessed=moved, transcendentals=0),
        name=name,
    )(*operands)


def prepare_kernel(ids_in, weights_in, rows_in, block, ids, weights, sems):
    tok_count, width = rows_in.shape
    top_count = ids.shape[0]
    experts = 2 * len(RING)
    copies = [
        pltpu.make_async_copy(ids_in, ids, sems.at[0]),
        pltpu.make_async_copy(weights_in, weights, sems.at[1]),
        pltpu.make_async_copy(rows_in, block.at[:, pl.ds(0, width)], sems.at[2]),
    ]
    for copy in copies:
        copy.start()
    square = (tok_count, tok_count)
    earlier = ones_where(iota(square, 0) < iota(square, 1))
    expert = iota((experts, tok_count), 0)
    unit = ones_where(iota((4 * experts, LANES), 0) == iota((4 * experts, LANES), 1))
    token = ones_where(iota((tok_count, LANES), 0) + TOKEN_LANE == iota((tok_count, LANES), 1))
    copies[0].wait()
    copies[1].wait()
    named = jnp.zeros((experts, tok_count), jnp.float32)
    scale = jnp.zeros((experts, tok_count), jnp.float32)
    for k in range(top_count):
        hit = ids[k : k + 1, :] == expert
        named = named + jnp.where(hit, 1.0, 0.0)
        scale = scale + jnp.where(hit, weights[k : k + 1, :], 0.0)
    rank = jnp.dot(named.astype(jnp.bfloat16), earlier, preferred_element_type=jnp.float32)
    notes = [jnp.where(named > 0.5, rank + 1.0, 0.0)]
    for _ in range(3):
        piece = scale.astype(jnp.bfloat16).astype(jnp.float32)
        scale = scale - piece
        notes.append(piece)
    notes = across(jnp.concatenate(notes, axis=0).astype(jnp.bfloat16), unit)
    block[:, width:] = notes.astype(jnp.bfloat16) + token
    copies[2].wait()


def prepare(ids, weights, tokens):
    tok_count, width = tokens.shape
    return local_call(
        prepare_kernel,
        "prepare",
        pltpu.VMEM((tok_count, width + LANES), jnp.bfloat16),
        [pl.ANY] * 3,
        tuple(pltpu.with_memory_space_constraint(x, pltpu.HBM) for x in (ids, weights, tokens)),
        [
            pltpu.VMEM(ids.shape, ids.dtype),
            pltpu.VMEM(weights.shape, weights.dtype),
            pltpu.SemaphoreType.DMA((3,)),
        ],
        limit=8,
    )


def choose_kernel(places, capacity, block, *refs):
    chip = lax.axis_index("expert") >> 1
    tok_count = block.shape[0]
    notes = block[:, -LANES:].astype(jnp.float32)
    lane = iota(notes.shape, 1)
    slot = iota((tok_count, len(places) * capacity), 1)
    code = jnp.zeros(slot.shape, jnp.float32)
    order = jnp.zeros(slot.shape, jnp.int32)
    for at, (steps, flip) in enumerate(places):
        wanted = chip_at(chip, steps, flip)
        column = jnp.sum(jnp.where(lane == wanted, notes, 0.0), axis=1, keepdims=True)
        code = jnp.where(slot >= at * capacity, column, code)
        order = jnp.where(slot >= at * capacity, slot + 1 - at * capacity, order)
    rows = across(ones_where(code == order.astype(jnp.float32)), block[...]).astype(jnp.bfloat16)
    for at in range(len(places)):
        refs[at][...] = rows[at * capacity : (at + 1) * capacity]


def choose(block, capacity, places):
    return local_call(
        functools.partial(choose_kernel, places, capacity),
        "choose",
        [jax.ShapeDtypeStruct((capacity, block.shape[1]), jnp.bfloat16) for _ in places],
        [None],
        (block,),
    )


def load_kernel(source, target, sem):
    copy = pltpu.make_async_copy(source, target, sem)
    copy.start()
    copy.wait()


def loaded(weights):
    return local_call(
        load_kernel,
        "loaded",
        pltpu.VMEM(weights.shape, weights.dtype),
        [pl.ANY],
        (weights,),
        [pltpu.SemaphoreType.DMA],
        limit=9,
        moved=2 * weights.size * weights.dtype.itemsize,
    )


def gated(both):
    hidden = both.shape[1] // 2
    gate = both[:, :hidden]
    return (gate / (1.0 + jnp.exp(-gate)) * both[:, hidden:]).astype(jnp.bfloat16)


def near_kernel(*refs):
    pieces, (first, second, slots, total) = refs[:-4], refs[-4:]
    start = 0
    for piece in pieces:
        slots[start : start + piece.shape[0]] = piece[...]
        start += piece.shape[0]
    width = total.shape[1]
    both = jnp.dot(slots[:, :width], first[...], preferred_element_type=jnp.float32)
    total[...] = jnp.dot(gated(both), second[...], preferred_element_type=jnp.float32)


def near_pass(pieces, weights):
    count = sum(piece.shape[0] for piece in pieces)
    full = pieces[0].shape[1]
    return local_call(
        near_kernel,
        "near_pass",
        [
            jax.ShapeDtypeStruct((count, full), jnp.bfloat16),
            jax.ShapeDtypeStruct((count, full - LANES), jnp.float32),
        ],
        [None] * (len(pieces) + 2),
        (*pieces, *weights),
        moved=2 * sum(w.size for w in weights),
    )


def far_kernel(picks, slots, before, first, second, *refs):
    outs, total = refs[:-1], refs[-1]
    device = lax.axis_index("expert")
    chip, odd = device >> 1, device & 1
    width = total.shape[1]
    experts = 2 * len(RING)
    both = jnp.dot(slots[:, :width], first[...], preferred_element_type=jnp.float32)
    term = jnp.dot(gated(both), second[...], preferred_element_type=jnp.float32)
    notes = slots[:, width:].astype(jnp.float32)
    lane = iota(notes.shape, 1)
    mine = (lane >= experts) & (lane < 4 * experts) & ((lane & (experts - 1)) == chip)
    scale = jnp.sum(jnp.where(mine, notes, 0.0), axis=1, keepdims=True)
    total[...] = (before[...] + term) * scale
    for out, (even_at, odd_at) in zip(outs, picks):
        capacity = out.shape[0]
        at = (even_at + odd * (odd_at - even_at)) * capacity
        rows = pl.ds(pl.multiple_of(at, capacity), capacity)
        out[:, :width] = total[rows, :].astype(jnp.bfloat16)
        out[:, width:] = slots[rows, width:]


def far_pass(slots, total, weights, capacity, picks):
    full = slots.shape[1]
    return local_call(
        functools.partial(far_kernel, picks),
        "far_pass",
        [jax.ShapeDtypeStruct((capacity, full), jnp.bfloat16) for _ in picks],
        [None] * 4,
        (slots, total, *weights),
        [pltpu.VMEM(total.shape, jnp.float32)],
        limit=24,
        moved=2 * sum(w.size for w in weights),
    )


def combine_kernel(picks, count, *refs):
    blocks, more, (out, slots) = refs[:count], refs[count:-2], refs[-2:]
    tok_count, width = out.shape
    capacity = blocks[0].shape[0]
    odd = lax.axis_index("expert") & 1
    for side in range(2):

        @pl.when(odd == side)
        def _():
            for at, pick in enumerate(picks):
                slots[at * capacity : (at + 1) * capacity] = blocks[pick[side]][...]

    token = slots[:, width:]
    part = width // 7
    for at in range(7):
        place = slice(at * part, (at + 1) * part)
        mixed = across(token, slots[:, place])[TOKEN_LANE : TOKEN_LANE + tok_count]
        for other in more:
            mixed = mixed + other[:, place].astype(jnp.float32)
        out[:, place] = mixed.astype(out.dtype)


def combine(blocks, picks, tok_count, *more):
    capacity, full = blocks[0].shape
    return local_call(
        functools.partial(combine_kernel, picks, len(blocks)),
        "combine",
        jax.ShapeDtypeStruct((tok_count, full - LANES), jnp.bfloat16),
        [None] * (len(blocks) + len(more)),
        (*blocks, *more),
        [pltpu.VMEM((capacity * len(picks), full), jnp.bfloat16)],
    )


def sent_by_core(shard, sections, moves):
    planes = len(RING)
    pairs = []
    for s in range(sections):
        for z in range(planes):
            for y in range(2):
                for core, (section_step, ring_step, flip) in enumerate(moves):
                    plane = RING[(RING.index(z) + ring_step) % planes]
                    target = (((s + section_step) % sections) * planes + plane) * 2 + (y ^ flip)
                    pairs.append((((s * planes + z) * 2 + y) * 2 + core, target * 2 + core))
    return lax.ppermute(shard, ("section", "expert"), pairs)


def sent(shard, sections, section_step, ring_step, flip):
    return sent_by_core(shard, sections, [(section_step, ring_step, flip)] * 2)


def after(value, other):
    return lax.optimization_barrier((value, other))[0]


def by_ring(rows, route_ids, route_weights, w_gate_up, w_down):
    sections = lax.axis_size("section")
    devices = lax.axis_size("expert")
    experts = devices // 2
    tokens = rows[0]
    tok_count = tokens.shape[0]
    top_count = route_ids.shape[2]
    capacity = max(2, 2 * tok_count * top_count // experts)
    swap = [(i, i ^ 1) for i in range(devices)]
    w_in, w_out = w_gate_up[0], w_down[0]
    far_out = lax.ppermute(w_out, "expert", swap)
    far_in = lax.ppermute(w_in, "expert", swap)
    block = prepare(route_ids[0].T, route_weights[0].T, tokens)
    block1 = sent(block, sections, 0, 1, 0)
    own0, other, back0, back1 = choose(block, capacity, ((0, 0), (0, 1), (3, 0), (3, 1)))
    other0 = sent(other, sections, 0, 0, 1)
    near = (loaded(after(w_in, own0)), loaded(after(w_out, own0)))
    block1 = after(block1, (near, other0))
    own1, other, on0, on1 = choose(block1, capacity, ((0, 0), (0, 1), (1, 0), (1, 1)))
    other1 = sent(other, sections, 0, 0, 1)
    own2 = sent(on0, sections, 0, 1, 0)
    other2 = sent(on1, sections, 0, 1, 1)
    back1, back0 = after((back1, back0), other1)
    other3 = sent(back1, sections, 0, 3, 1)
    own3 = sent(back0, sections, 0, 3, 0)
    pieces = (own0, other0, own1, own2, other2, other1, other3, own3)
    places = ((0, 0), (0, 1), (1, 0), (2, 0), (2, 1), (1, 1), (3, 1), (3, 0))
    slots, total = near_pass(pieces, near)
    moves = {(2, 1): (0, 1, 1), (3, 1): (0, 0, 1), (2, 0): (0, 1, 0), (0, 0): (1, 0, 0), (0, 1): (1, 0, 1)}
    even = ((2, 1), (3, 1), (2, 0), (0, 0), (0, 1))
    odd = ((0, 0), (0, 1), (2, 1), (3, 1), (2, 0))
    picks = [(places.index(a), places.index(b)) for a, b in zip(even, odd)]
    picks += [(places.index(at),) * 2 for at in ((3, 0), (1, 0), (1, 1))]
    *pieces, stays, near1, other1 = far_pass(slots, total, (far_in, far_out), capacity, picks)
    stage = [
        sent_by_core(piece, sections, (moves[a], moves[b])) for piece, a, b in zip(pieces, even, odd)
    ]
    stage = lax.optimization_barrier(stage)
    merged = combine([stays, *stage], ((0, 0), (1, 3), (2, 4), (3, 5)), tok_count)
    merged = sent(merged, sections, 1, 1, 0)
    last = [sent(near1, sections, 1, -1, 0), sent(other1, sections, 1, -1, 1)]
    picks = ((0, 0), (1, 1), (5, 2), (6, 3))
    return combine([*last, *stage], picks, tok_count, merged)[None]


def per_device(rows, route_ids, route_weights, w_gate_up, w_down):
    experts = lax.axis_size("expert") // 2
    fits = experts == 2 * len(RING) and rows.shape[1] <= LANES - TOKEN_LANE
    plan = by_ring if fits else by_slots
    return plan(rows, route_ids, route_weights, w_gate_up, w_down)


def solution(mesh):
    in_specs = (
        P("section", "expert", None),
        P("section", "expert", None),
        P("section", "expert", None),
        P("section", None, "expert"),
        P("section", "expert", None),
    )
    out_specs = P("section", "expert", None)
    return jax.shard_map(
        per_device, mesh=mesh, in_specs=in_specs, out_specs=out_specs, check_vma=False
    )
```

```python
import functools

import jax
import jax.numpy as jnp
from jax import lax
from jax.experimental import pallas as pl
from jax.experimental.pallas import tpu as pltpu
from jax.sharding import PartitionSpec as P


def passed_along(shard, axis, by):
    length = lax.axis_size(axis)
    return lax.ppermute(shard, axis, [(i, (i + by) % length) for i in range(length)])


def by_slots(rows, route_ids, route_weights, w_gate_up, w_down):
    devices = lax.axis_size("expert")
    experts = devices // 2
    tokens = rows[0]
    tok_count, width = tokens.shape
    top_count = route_ids.shape[2]
    choices_flat = route_ids[0].reshape(-1)
    capacity = max(2, 2 * tok_count * top_count // experts)
    onehot = (choices_flat[:, None] == jnp.arange(experts, dtype=jnp.int32)[None, :]).astype(
        jnp.int32
    )
    before = jnp.cumsum(onehot, axis=0) - onehot
    slot = jnp.sum(before * onehot, axis=1)
    place = slot * experts + choices_flat
    slot_total = experts * capacity
    picker = (place[None, :] == jnp.arange(slot_total, dtype=jnp.int32)[:, None]).astype(
        jnp.bfloat16
    )
    token_pairs = jnp.repeat(tokens, top_count, axis=0)
    packed = jnp.dot(picker, token_pairs, preferred_element_type=jnp.float32).astype(jnp.bfloat16)
    w_in = w_gate_up[0]
    w_out = w_down[0]
    hidden = w_out.shape[0]
    outgoing = jnp.broadcast_to(
        packed.reshape(capacity, experts, 1, width), (capacity, experts, 2, width)
    )
    outgoing = outgoing.reshape(capacity, devices, width)
    block = lax.all_to_all(outgoing, "expert", split_axis=1, concat_axis=1, tiled=True)
    flat = block.reshape(-1, width)
    both = jnp.dot(flat, w_in, preferred_element_type=jnp.float32)
    active = (jax.nn.silu(both[:, :hidden]) * both[:, hidden:]).astype(jnp.bfloat16)
    result = jnp.dot(active, w_out, preferred_element_type=jnp.float32)
    partial_out = result.reshape(block.shape[0], block.shape[1], width).astype(jnp.bfloat16)
    returned = lax.all_to_all(partial_out, "expert", split_axis=1, concat_axis=1, tiled=True)
    returned = returned.reshape(capacity, experts, 2, width).astype(jnp.float32)
    expert_out = jnp.sum(returned, axis=2).astype(jnp.bfloat16).reshape(slot_total, width)
    pair_out = expert_out[place].astype(jnp.float32) * route_weights[0].reshape(-1)[:, None]
    layer_out = jnp.sum(pair_out.reshape(tok_count, top_count, width), axis=1).astype(jnp.bfloat16)
    return passed_along(layer_out, "section", 1)[None]


RING = (0, 1, 3, 2)
LANES = 128
TOKEN_LANE = 64


def on_ring(place):
    return place ^ (place >> 1)


def chip_at(chip, steps, flip):
    return (on_ring((on_ring(chip >> 1) + steps) & 3) << 1) | ((chip & 1) ^ flip)


def iota(shape, axis):
    return lax.broadcasted_iota(jnp.int32, shape, axis)


def ones_where(condition):
    return jnp.where(condition, 1.0, 0.0).astype(jnp.bfloat16)


def across(left, right):
    return lax.dot_general(left, right, (((0,), (0,)), ((), ())), preferred_element_type=jnp.float32)


def local_call(kernel, name, out_shape, in_specs, operands, scratch=(), limit=12, flops=0, moved=0):
    vmem = pl.BlockSpec(memory_space=pltpu.VMEM)
    return pl.pallas_call(
        kernel,
        out_shape=out_shape,
        in_specs=[vmem if spec is None else pl.BlockSpec(memory_space=spec) for spec in in_specs],
        out_specs=jax.tree.map(lambda _: vmem, out_shape),
        scratch_shapes=list(scratch),
        compiler_params=pltpu.CompilerParams(vmem_limit_bytes=limit << 20),
        cost_estimate=pl.CostEstimate(flops=flops, bytes_accessed=moved, transcendentals=0),
        name=name,
    )(*operands)


def prepare_kernel(ids_in, weights_in, rows_in, block, ids, weights, sems):
    tok_count, width = rows_in.shape
    top_count = ids.shape[0]
    experts = 2 * len(RING)
    copies = [
        pltpu.make_async_copy(ids_in, ids, sems.at[0]),
        pltpu.make_async_copy(weights_in, weights, sems.at[1]),
        pltpu.make_async_copy(rows_in, block.at[:, pl.ds(0, width)], sems.at[2]),
    ]
    for copy in copies:
        copy.start()
    square = (tok_count, tok_count)
    earlier = ones_where(iota(square, 0) < iota(square, 1))
    expert = iota((experts, tok_count), 0)
    unit = ones_where(iota((4 * experts, LANES), 0) == iota((4 * experts, LANES), 1))
    token = ones_where(iota((tok_count, LANES), 0) + TOKEN_LANE == iota((tok_count, LANES), 1))
    copies[0].wait()
    copies[1].wait()
    named = jnp.zeros((experts, tok_count), jnp.float32)
    scale = jnp.zeros((experts, tok_count), jnp.float32)
    for k in range(top_count):
        hit = ids[k : k + 1, :] == expert
        named = named + jnp.where(hit, 1.0, 0.0)
        scale = scale + jnp.where(hit, weights[k : k + 1, :], 0.0)
    rank = jnp.dot(named.astype(jnp.bfloat16), earlier, preferred_element_type=jnp.float32)
    notes = [jnp.where(named > 0.5, rank + 1.0, 0.0)]
    for _ in range(3):
        piece = scale.astype(jnp.bfloat16).astype(jnp.float32)
        scale = scale - piece
        notes.append(piece)
    notes = across(jnp.concatenate(notes, axis=0).astype(jnp.bfloat16), unit)
    block[:, width:] = notes.astype(jnp.bfloat16) + token
    copies[2].wait()


def prepare(ids, weights, tokens):
    tok_count, width = tokens.shape
    return local_call(
        prepare_kernel,
        "prepare",
        pltpu.VMEM((tok_count, width + LANES), jnp.bfloat16),
        [pl.ANY] * 3,
        tuple(pltpu.with_memory_space_constraint(x, pltpu.HBM) for x in (ids, weights, tokens)),
        [
            pltpu.VMEM(ids.shape, ids.dtype),
            pltpu.VMEM(weights.shape, weights.dtype),
            pltpu.SemaphoreType.DMA((3,)),
        ],
        limit=8,
    )


def choose_kernel(places, capacity, block, *refs):
    chip = lax.axis_index("expert") >> 1
    tok_count = block.shape[0]
    notes = block[:, -LANES:].astype(jnp.float32)
    lane = iota(notes.shape, 1)
    slot = iota((tok_count, len(places) * capacity), 1)
    code = jnp.zeros(slot.shape, jnp.float32)
    order = jnp.zeros(slot.shape, jnp.int32)
    for at, (steps, flip) in enumerate(places):
        wanted = chip_at(chip, steps, flip)
        column = jnp.sum(jnp.where(lane == wanted, notes, 0.0), axis=1, keepdims=True)
        code = jnp.where(slot >= at * capacity, column, code)
        order = jnp.where(slot >= at * capacity, slot + 1 - at * capacity, order)
    rows = across(ones_where(code == order.astype(jnp.float32)), block[...]).astype(jnp.bfloat16)
    for at in range(len(places)):
        refs[at][...] = rows[at * capacity : (at + 1) * capacity]


def choose(block, capacity, places):
    return local_call(
        functools.partial(choose_kernel, places, capacity),
        "choose",
        [jax.ShapeDtypeStruct((capacity, block.shape[1]), jnp.bfloat16) for _ in places],
        [None],
        (block,),
    )


def load_kernel(source, target, sem):
    copy = pltpu.make_async_copy(source, target, sem)
    copy.start()
    copy.wait()


def loaded(weights):
    return local_call(
        load_kernel,
        "loaded",
        pltpu.VMEM(weights.shape, weights.dtype),
        [pl.ANY],
        (weights,),
        [pltpu.SemaphoreType.DMA],
        limit=9,
        moved=2 * weights.size * weights.dtype.itemsize,
    )


def gated(both):
    hidden = both.shape[1] // 2
    gate = both[:, :hidden]
    return (gate / (1.0 + jnp.exp(-gate)) * both[:, hidden:]).astype(jnp.bfloat16)


def write_pieces(slots, total, outs):
    chip = lax.axis_index("expert") >> 1
    width = total.shape[1]
    experts = 2 * len(RING)
    notes = slots[:, width:].astype(jnp.float32)
    lane = iota(notes.shape, 1)
    mine = (lane >= experts) & (lane < 4 * experts) & ((lane & (experts - 1)) == chip)
    scale = jnp.sum(jnp.where(mine, notes, 0.0), axis=1, keepdims=True)
    start = 0
    for out in outs:
        stop = start + out.shape[0]
        out[:, :width] = (total[start:stop] * scale[start:stop]).astype(jnp.bfloat16)
        out[:, width:] = slots[start:stop, width:]
        start = stop


def near_kernel(*refs):
    pieces, (first, second, slots, total) = refs[:-4], refs[-4:]
    start = 0
    for piece in pieces:
        slots[start : start + piece.shape[0]] = piece[...]
        start += piece.shape[0]
    width = total.shape[1]
    both = jnp.dot(slots[:, :width], first[...], preferred_element_type=jnp.float32)
    total[...] = jnp.dot(gated(both), second[...], preferred_element_type=jnp.float32)


def near_pass(pieces, weights):
    count = sum(piece.shape[0] for piece in pieces)
    full = pieces[0].shape[1]
    return local_call(
        near_kernel,
        "near_pass",
        [
            jax.ShapeDtypeStruct((count, full), jnp.bfloat16),
            jax.ShapeDtypeStruct((count, full - LANES), jnp.float32),
        ],
        [None] * (len(pieces) + 2),
        (*pieces, *weights),
        moved=2 * sum(w.size for w in weights),
    )


def far_kernel(slots, before, first, second, *refs):
    outs, total = refs[:-1], refs[-1]
    width = total.shape[1]
    both = jnp.dot(slots[:, :width], first[...], preferred_element_type=jnp.float32)
    term = jnp.dot(gated(both), second[...], preferred_element_type=jnp.float32)
    total[...] = before[...] + term
    write_pieces(slots, total, outs)


def far_pass(slots, total, weights, capacity):
    count, full = slots.shape
    return local_call(
        far_kernel,
        "far_pass",
        [jax.ShapeDtypeStruct((capacity, full), jnp.bfloat16)] * (count // capacity),
        [None] * 4,
        (slots, total, *weights),
        [pltpu.VMEM(total.shape, jnp.float32)],
        limit=24,
        moved=2 * sum(w.size for w in weights),
    )


def combine_kernel(count, *refs):
    blocks, more, (out, slots) = refs[:count], refs[count:-2], refs[-2:]
    tok_count, width = out.shape
    start = 0
    for block in blocks:
        slots[start : start + block.shape[0]] = block[...]
        start += block.shape[0]
    token = slots[:, width:]
    part = width // 7
    for at in range(7):
        place = slice(at * part, (at + 1) * part)
        mixed = across(token, slots[:, place])[TOKEN_LANE : TOKEN_LANE + tok_count]
        for other in more:
            mixed = mixed + other[:, place].astype(jnp.float32)
        out[:, place] = mixed.astype(out.dtype)


def combine(blocks, tok_count, *more):
    capacity, full = blocks[0].shape
    return local_call(
        functools.partial(combine_kernel, len(blocks)),
        "combine",
        jax.ShapeDtypeStruct((tok_count, full - LANES), jnp.bfloat16),
        [None] * (len(blocks) + len(more)),
        (*blocks, *more),
        [pltpu.VMEM((capacity * len(blocks), full), jnp.bfloat16)],
    )


def sent(shard, sections, section_step, ring_step, flip):
    planes = len(RING)
    pairs = []
    for s in range(sections):
        for z in range(planes):
            for y in range(2):
                for core in range(2):
                    plane = RING[(RING.index(z) + ring_step) % planes]
                    target = (((s + section_step) % sections) * planes + plane) * 2 + (y ^ flip)
                    pairs.append((((s * planes + z) * 2 + y) * 2 + core, target * 2 + core))
    return lax.ppermute(shard, ("section", "expert"), pairs)


def after(value, other):
    return lax.optimization_barrier((value, other))[0]


def by_ring(rows, route_ids, route_weights, w_gate_up, w_down):
    sections = lax.axis_size("section")
    devices = lax.axis_size("expert")
    experts = devices // 2
    tokens = rows[0]
    tok_count = tokens.shape[0]
    top_count = route_ids.shape[2]
    capacity = max(2, 2 * tok_count * top_count // experts)
    swap = [(i, i ^ 1) for i in range(devices)]
    w_in, w_out = w_gate_up[0], w_down[0]
    far_out = lax.ppermute(w_out, "expert", swap)
    far_in = lax.ppermute(w_in, "expert", swap)
    block = prepare(route_ids[0].T, route_weights[0].T, tokens)
    block1 = sent(block, sections, 0, 1, 0)
    own0, other, back0, back1 = choose(block, capacity, ((0, 0), (0, 1), (3, 0), (3, 1)))
    other0 = sent(other, sections, 0, 0, 1)
    near = (loaded(after(w_in, own0)), loaded(after(w_out, own0)))
    block1 = after(block1, (near, other0))
    own1, other, on0, on1 = choose(block1, capacity, ((0, 0), (0, 1), (1, 0), (1, 1)))
    other1 = sent(other, sections, 0, 0, 1)
    own2 = sent(on0, sections, 0, 1, 0)
    other2 = sent(on1, sections, 0, 1, 1)
    other3 = sent(after(back1, (near, other0)), sections, 0, 3, 1)
    own3 = sent(after(back0, (other1, other3)), sections, 0, 3, 0)
    pieces = (own0, other0, own1, own2, other2, other1, own3, other3)
    places = ((0, 0), (0, 1), (1, 0), (2, 0), (2, 1), (1, 1), (3, 0), (3, 1))
    slots, total = near_pass(pieces, near)
    pieces = far_pass(slots, total, (far_in, far_out), capacity)
    piece = dict(zip(places, pieces))
    merged = [
        piece[3, 0],
        sent(piece[2, 0], sections, 0, 1, 0),
        sent(piece[2, 1], sections, 0, 1, 1),
        sent(piece[3, 1], sections, 0, 0, 1),
    ]
    straight = [sent(piece[0, flip], sections, 1, 0, flip) for flip in range(2)]
    merged, straight = lax.optimization_barrier((merged, straight))
    straight += [sent(piece[1, flip], sections, 1, -1, flip) for flip in range(2)]
    merged = sent(combine(merged, tok_count), sections, 1, 1, 0)
    return combine(straight, tok_count, merged)[None]


def per_device(rows, route_ids, route_weights, w_gate_up, w_down):
    experts = lax.axis_size("expert") // 2
    fits = experts == 2 * len(RING) and rows.shape[1] <= LANES - TOKEN_LANE
    plan = by_ring if fits else by_slots
    return plan(rows, route_ids, route_weights, w_gate_up, w_down)


def solution(mesh):
    in_specs = (
        P("section", "expert", None),
        P("section", "expert", None),
        P("section", "expert", None),
        P("section", None, "expert"),
        P("section", "expert", None),
    )
    out_specs = P("section", "expert", None)
    return jax.shard_map(
        per_device, mesh=mesh, in_specs=in_specs, out_specs=out_specs, check_vma=False
    )
```

```python
import functools

import jax
import jax.numpy as jnp
from jax import lax
from jax.experimental import pallas as pl
from jax.experimental.pallas import tpu as pltpu
from jax.sharding import PartitionSpec as P


def passed_along(shard, axis, by):
    length = lax.axis_size(axis)
    return lax.ppermute(shard, axis, [(i, (i + by) % length) for i in range(length)])


def by_slots(rows, route_ids, route_weights, w_gate_up, w_down):
    devices = lax.axis_size("expert")
    experts = devices // 2
    tokens = rows[0]
    tok_count, width = tokens.shape
    top_count = route_ids.shape[2]
    choices_flat = route_ids[0].reshape(-1)
    capacity = max(2, 2 * tok_count * top_count // experts)
    onehot = (choices_flat[:, None] == jnp.arange(experts, dtype=jnp.int32)[None, :]).astype(
        jnp.int32
    )
    before = jnp.cumsum(onehot, axis=0) - onehot
    slot = jnp.sum(before * onehot, axis=1)
    place = slot * experts + choices_flat
    slot_total = experts * capacity
    picker = (place[None, :] == jnp.arange(slot_total, dtype=jnp.int32)[:, None]).astype(
        jnp.bfloat16
    )
    token_pairs = jnp.repeat(tokens, top_count, axis=0)
    packed = jnp.dot(picker, token_pairs, preferred_element_type=jnp.float32).astype(jnp.bfloat16)
    w_in = w_gate_up[0]
    w_out = w_down[0]
    hidden = w_out.shape[0]
    outgoing = jnp.broadcast_to(
        packed.reshape(capacity, experts, 1, width), (capacity, experts, 2, width)
    )
    outgoing = outgoing.reshape(capacity, devices, width)
    block = lax.all_to_all(outgoing, "expert", split_axis=1, concat_axis=1, tiled=True)
    flat = block.reshape(-1, width)
    both = jnp.dot(flat, w_in, preferred_element_type=jnp.float32)
    active = (jax.nn.silu(both[:, :hidden]) * both[:, hidden:]).astype(jnp.bfloat16)
    result = jnp.dot(active, w_out, preferred_element_type=jnp.float32)
    partial_out = result.reshape(block.shape[0], block.shape[1], width).astype(jnp.bfloat16)
    returned = lax.all_to_all(partial_out, "expert", split_axis=1, concat_axis=1, tiled=True)
    returned = returned.reshape(capacity, experts, 2, width).astype(jnp.float32)
    expert_out = jnp.sum(returned, axis=2).astype(jnp.bfloat16).reshape(slot_total, width)
    pair_out = expert_out[place].astype(jnp.float32) * route_weights[0].reshape(-1)[:, None]
    layer_out = jnp.sum(pair_out.reshape(tok_count, top_count, width), axis=1).astype(jnp.bfloat16)
    return passed_along(layer_out, "section", 1)[None]


RING = (0, 1, 3, 2)
LANES = 128
TOKEN_LANE = 64


def on_ring(place):
    return place ^ (place >> 1)


def chip_at(chip, steps, flip):
    return (on_ring((on_ring(chip >> 1) + steps) & 3) << 1) | ((chip & 1) ^ flip)


def iota(shape, axis):
    return lax.broadcasted_iota(jnp.int32, shape, axis)


def ones_where(condition):
    return jnp.where(condition, 1.0, 0.0).astype(jnp.bfloat16)


def across(left, right):
    return lax.dot_general(left, right, (((0,), (0,)), ((), ())), preferred_element_type=jnp.float32)


def local_call(kernel, name, out_shape, in_specs, operands, scratch=(), limit=12, flops=0, moved=0):
    vmem = pl.BlockSpec(memory_space=pltpu.VMEM)
    return pl.pallas_call(
        kernel,
        out_shape=out_shape,
        in_specs=[vmem if spec is None else pl.BlockSpec(memory_space=spec) for spec in in_specs],
        out_specs=jax.tree.map(lambda _: vmem, out_shape),
        scratch_shapes=list(scratch),
        compiler_params=pltpu.CompilerParams(vmem_limit_bytes=limit << 20),
        cost_estimate=pl.CostEstimate(flops=flops, bytes_accessed=moved, transcendentals=0),
        name=name,
    )(*operands)


def prepare_kernel(ids_in, weights_in, rows_in, block, ids, weights, sems):
    tok_count, width = rows_in.shape
    top_count = ids.shape[0]
    experts = 2 * len(RING)
    copies = [
        pltpu.make_async_copy(ids_in, ids, sems.at[0]),
        pltpu.make_async_copy(weights_in, weights, sems.at[1]),
        pltpu.make_async_copy(rows_in, block.at[:, pl.ds(0, width)], sems.at[2]),
    ]
    for copy in copies:
        copy.start()
    square = (tok_count, tok_count)
    earlier = ones_where(iota(square, 0) < iota(square, 1))
    expert = iota((experts, tok_count), 0)
    unit = ones_where(iota((4 * experts, LANES), 0) == iota((4 * experts, LANES), 1))
    token = ones_where(iota((tok_count, LANES), 0) + TOKEN_LANE == iota((tok_count, LANES), 1))
    copies[0].wait()
    copies[1].wait()
    named = jnp.zeros((experts, tok_count), jnp.float32)
    scale = jnp.zeros((experts, tok_count), jnp.float32)
    for k in range(top_count):
        hit = ids[k : k + 1, :] == expert
        named = named + jnp.where(hit, 1.0, 0.0)
        scale = scale + jnp.where(hit, weights[k : k + 1, :], 0.0)
    rank = jnp.dot(named.astype(jnp.bfloat16), earlier, preferred_element_type=jnp.float32)
    notes = [jnp.where(named > 0.5, rank + 1.0, 0.0)]
    for _ in range(3):
        piece = scale.astype(jnp.bfloat16).astype(jnp.float32)
        scale = scale - piece
        notes.append(piece)
    notes = across(jnp.concatenate(notes, axis=0).astype(jnp.bfloat16), unit)
    block[:, width:] = notes.astype(jnp.bfloat16) + token
    copies[2].wait()


def prepare(ids, weights, tokens):
    tok_count, width = tokens.shape
    return local_call(
        prepare_kernel,
        "prepare",
        pltpu.VMEM((tok_count, width + LANES), jnp.bfloat16),
        [pl.ANY] * 3,
        tuple(pltpu.with_memory_space_constraint(x, pltpu.HBM) for x in (ids, weights, tokens)),
        [
            pltpu.VMEM(ids.shape, ids.dtype),
            pltpu.VMEM(weights.shape, weights.dtype),
            pltpu.SemaphoreType.DMA((3,)),
        ],
        limit=8,
    )


def choose_kernel(places, capacity, block, *refs):
    chip = lax.axis_index("expert") >> 1
    tok_count = block.shape[0]
    notes = block[:, -LANES:].astype(jnp.float32)
    lane = iota(notes.shape, 1)
    slot = iota((tok_count, len(places) * capacity), 1)
    code = jnp.zeros(slot.shape, jnp.float32)
    order = jnp.zeros(slot.shape, jnp.int32)
    for at, (steps, flip) in enumerate(places):
        wanted = chip_at(chip, steps, flip)
        column = jnp.sum(jnp.where(lane == wanted, notes, 0.0), axis=1, keepdims=True)
        code = jnp.where(slot >= at * capacity, column, code)
        order = jnp.where(slot >= at * capacity, slot + 1 - at * capacity, order)
    rows = across(ones_where(code == order.astype(jnp.float32)), block[...]).astype(jnp.bfloat16)
    for at in range(len(places)):
        refs[at][...] = rows[at * capacity : (at + 1) * capacity]


def choose(block, capacity, places):
    return local_call(
        functools.partial(choose_kernel, places, capacity),
        "choose",
        [jax.ShapeDtypeStruct((capacity, block.shape[1]), jnp.bfloat16) for _ in places],
        [None],
        (block,),
    )


def load_kernel(source, target, sem):
    copy = pltpu.make_async_copy(source, target, sem)
    copy.start()
    copy.wait()


def loaded(weights):
    return local_call(
        load_kernel,
        "loaded",
        pltpu.VMEM(weights.shape, weights.dtype),
        [pl.ANY],
        (weights,),
        [pltpu.SemaphoreType.DMA],
        limit=9,
        moved=2 * weights.size * weights.dtype.itemsize,
    )


def gated(both):
    hidden = both.shape[1] // 2
    gate = both[:, :hidden]
    return (gate / (1.0 + jnp.exp(-gate)) * both[:, hidden:]).astype(jnp.bfloat16)


def write_pieces(slots, total, outs):
    chip = lax.axis_index("expert") >> 1
    width = total.shape[1]
    experts = 2 * len(RING)
    notes = slots[:, width:].astype(jnp.float32)
    lane = iota(notes.shape, 1)
    mine = (lane >= experts) & (lane < 4 * experts) & ((lane & (experts - 1)) == chip)
    scale = jnp.sum(jnp.where(mine, notes, 0.0), axis=1, keepdims=True)
    start = 0
    for out in outs:
        stop = start + out.shape[0]
        out[:, :width] = (total[start:stop] * scale[start:stop]).astype(jnp.bfloat16)
        out[:, width:] = slots[start:stop, width:]
        start = stop


def near_kernel(*refs):
    pieces, (first, second, slots, total) = refs[:-4], refs[-4:]
    start = 0
    for piece in pieces:
        slots[start : start + piece.shape[0]] = piece[...]
        start += piece.shape[0]
    width = total.shape[1]
    both = jnp.dot(slots[:, :width], first[...], preferred_element_type=jnp.float32)
    total[...] = jnp.dot(gated(both), second[...], preferred_element_type=jnp.float32)


def near_pass(pieces, weights):
    count = sum(piece.shape[0] for piece in pieces)
    full = pieces[0].shape[1]
    return local_call(
        near_kernel,
        "near_pass",
        [
            jax.ShapeDtypeStruct((count, full), jnp.bfloat16),
            jax.ShapeDtypeStruct((count, full - LANES), jnp.float32),
        ],
        [None] * (len(pieces) + 2),
        (*pieces, *weights),
        moved=2 * sum(w.size for w in weights),
    )


def far_kernel(slots, before, first, second, *refs):
    outs, total = refs[:-1], refs[-1]
    width = total.shape[1]
    both = jnp.dot(slots[:, :width], first[...], preferred_element_type=jnp.float32)
    term = jnp.dot(gated(both), second[...], preferred_element_type=jnp.float32)
    total[...] = before[...] + term
    write_pieces(slots, total, outs)


def far_pass(slots, total, weights, capacity):
    count, full = slots.shape
    return local_call(
        far_kernel,
        "far_pass",
        [jax.ShapeDtypeStruct((capacity, full), jnp.bfloat16)] * (count // capacity),
        [None] * 4,
        (slots, total, *weights),
        [pltpu.VMEM(total.shape, jnp.float32)],
        limit=24,
        moved=2 * sum(w.size for w in weights),
    )


def combine_kernel(count, *refs):
    blocks, more, (out, slots) = refs[:count], refs[count:-2], refs[-2:]
    tok_count, width = out.shape
    start = 0
    for block in blocks:
        slots[start : start + block.shape[0]] = block[...]
        start += block.shape[0]
    token = slots[:, width:]
    part = width // 7
    for at in range(7):
        place = slice(at * part, (at + 1) * part)
        mixed = across(token, slots[:, place])[TOKEN_LANE : TOKEN_LANE + tok_count]
        for other in more:
            mixed = mixed + other[:, place].astype(jnp.float32)
        out[:, place] = mixed.astype(out.dtype)


def combine(blocks, tok_count, *more):
    capacity, full = blocks[0].shape
    return local_call(
        functools.partial(combine_kernel, len(blocks)),
        "combine",
        jax.ShapeDtypeStruct((tok_count, full - LANES), jnp.bfloat16),
        [None] * (len(blocks) + len(more)),
        (*blocks, *more),
        [pltpu.VMEM((capacity * len(blocks), full), jnp.bfloat16)],
    )


def sent(shard, sections, section_step, ring_step, flip):
    planes = len(RING)
    pairs = []
    for s in range(sections):
        for z in range(planes):
            for y in range(2):
                for core in range(2):
                    plane = RING[(RING.index(z) + ring_step) % planes]
                    target = (((s + section_step) % sections) * planes + plane) * 2 + (y ^ flip)
                    pairs.append((((s * planes + z) * 2 + y) * 2 + core, target * 2 + core))
    return lax.ppermute(shard, ("section", "expert"), pairs)


def after(value, other):
    return lax.optimization_barrier((value, other))[0]


def by_ring(rows, route_ids, route_weights, w_gate_up, w_down):
    sections = lax.axis_size("section")
    devices = lax.axis_size("expert")
    experts = devices // 2
    tokens = rows[0]
    tok_count = tokens.shape[0]
    top_count = route_ids.shape[2]
    capacity = max(2, 2 * tok_count * top_count // experts)
    swap = [(i, i ^ 1) for i in range(devices)]
    w_in, w_out = w_gate_up[0], w_down[0]
    far_out = lax.ppermute(w_out, "expert", swap)
    far_in = lax.ppermute(w_in, "expert", swap)
    block = prepare(route_ids[0].T, route_weights[0].T, tokens)
    block1 = sent(block, sections, 0, 1, 0)
    own0, other, back0, back1 = choose(block, capacity, ((0, 0), (0, 1), (3, 0), (3, 1)))
    other0 = sent(other, sections, 0, 0, 1)
    near = (loaded(after(w_in, own0)), loaded(after(w_out, own0)))
    block1 = after(block1, (near, other0))
    own1, other, on0, on1 = choose(block1, capacity, ((0, 0), (0, 1), (1, 0), (1, 1)))
    own2 = sent(on0, sections, 0, 1, 0)
    other2 = sent(on1, sections, 0, 1, 1)
    other3 = sent(after(back1, (near, other0)), sections, 0, 3, 1)
    other1 = sent(after(other, (other3, own2)), sections, 0, 0, 1)
    own3 = sent(after(back0, (other3, own2)), sections, 0, 3, 0)
    pieces = (own0, other0, own1, own2, other2, other1, own3, other3)
    places = ((0, 0), (0, 1), (1, 0), (2, 0), (2, 1), (1, 1), (3, 0), (3, 1))
    slots, total = near_pass(pieces, near)
    pieces = far_pass(slots, total, (far_in, far_out), capacity)
    piece = dict(zip(places, pieces))
    merged = [
        piece[3, 0],
        sent(piece[2, 0], sections, 0, 1, 0),
        sent(piece[2, 1], sections, 0, 1, 1),
        sent(piece[3, 1], sections, 0, 0, 1),
    ]
    straight = [sent(piece[0, flip], sections, 1, 0, flip) for flip in range(2)]
    merged, straight = lax.optimization_barrier((merged, straight))
    straight += [sent(piece[1, flip], sections, 1, -1, flip) for flip in range(2)]
    merged = sent(combine(merged, tok_count), sections, 1, 1, 0)
    return combine(straight, tok_count, merged)[None]


def per_device(rows, route_ids, route_weights, w_gate_up, w_down):
    experts = lax.axis_size("expert") // 2
    fits = experts == 2 * len(RING) and rows.shape[1] <= LANES - TOKEN_LANE
    plan = by_ring if fits else by_slots
    return plan(rows, route_ids, route_weights, w_gate_up, w_down)


def solution(mesh):
    in_specs = (
        P("section", "expert", None),
        P("section", "expert", None),
        P("section", "expert", None),
        P("section", None, "expert"),
        P("section", "expert", None),
    )
    out_specs = P("section", "expert", None)
    return jax.shard_map(
        per_device, mesh=mesh, in_specs=in_specs, out_specs=out_specs, check_vma=False
    )
```

```python
import functools

import jax
import jax.numpy as jnp
from jax import lax
from jax.experimental import pallas as pl
from jax.experimental.pallas import tpu as pltpu
from jax.sharding import PartitionSpec as P


def passed_along(shard, axis, by):
    length = lax.axis_size(axis)
    return lax.ppermute(shard, axis, [(i, (i + by) % length) for i in range(length)])


def by_slots(rows, route_ids, route_weights, w_gate_up, w_down):
    devices = lax.axis_size("expert")
    experts = devices // 2
    tokens = rows[0]
    tok_count, width = tokens.shape
    top_count = route_ids.shape[2]
    choices_flat = route_ids[0].reshape(-1)
    capacity = max(2, 2 * tok_count * top_count // experts)
    onehot = (choices_flat[:, None] == jnp.arange(experts, dtype=jnp.int32)[None, :]).astype(
        jnp.int32
    )
    before = jnp.cumsum(onehot, axis=0) - onehot
    slot = jnp.sum(before * onehot, axis=1)
    place = slot * experts + choices_flat
    slot_total = experts * capacity
    picker = (place[None, :] == jnp.arange(slot_total, dtype=jnp.int32)[:, None]).astype(
        jnp.bfloat16
    )
    token_pairs = jnp.repeat(tokens, top_count, axis=0)
    packed = jnp.dot(picker, token_pairs, preferred_element_type=jnp.float32).astype(jnp.bfloat16)
    w_in = w_gate_up[0]
    w_out = w_down[0]
    hidden = w_out.shape[0]
    outgoing = jnp.broadcast_to(
        packed.reshape(capacity, experts, 1, width), (capacity, experts, 2, width)
    )
    outgoing = outgoing.reshape(capacity, devices, width)
    block = lax.all_to_all(outgoing, "expert", split_axis=1, concat_axis=1, tiled=True)
    flat = block.reshape(-1, width)
    both = jnp.dot(flat, w_in, preferred_element_type=jnp.float32)
    active = (jax.nn.silu(both[:, :hidden]) * both[:, hidden:]).astype(jnp.bfloat16)
    result = jnp.dot(active, w_out, preferred_element_type=jnp.float32)
    partial_out = result.reshape(block.shape[0], block.shape[1], width).astype(jnp.bfloat16)
    returned = lax.all_to_all(partial_out, "expert", split_axis=1, concat_axis=1, tiled=True)
    returned = returned.reshape(capacity, experts, 2, width).astype(jnp.float32)
    expert_out = jnp.sum(returned, axis=2).astype(jnp.bfloat16).reshape(slot_total, width)
    pair_out = expert_out[place].astype(jnp.float32) * route_weights[0].reshape(-1)[:, None]
    layer_out = jnp.sum(pair_out.reshape(tok_count, top_count, width), axis=1).astype(jnp.bfloat16)
    return passed_along(layer_out, "section", 1)[None]


RING = (0, 1, 3, 2)
LANES = 128
TOKEN_LANE = 64


def on_ring(place):
    return place ^ (place >> 1)


def chip_at(chip, steps, flip):
    return (on_ring((on_ring(chip >> 1) + steps) & 3) << 1) | ((chip & 1) ^ flip)


def iota(shape, axis):
    return lax.broadcasted_iota(jnp.int32, shape, axis)


def ones_where(condition):
    return jnp.where(condition, 1.0, 0.0).astype(jnp.bfloat16)


def across(left, right):
    return lax.dot_general(left, right, (((0,), (0,)), ((), ())), preferred_element_type=jnp.float32)


def local_call(kernel, name, out_shape, in_specs, operands, scratch=(), limit=12, flops=0, moved=0):
    vmem = pl.BlockSpec(memory_space=pltpu.VMEM)
    return pl.pallas_call(
        kernel,
        out_shape=out_shape,
        in_specs=[vmem if spec is None else pl.BlockSpec(memory_space=spec) for spec in in_specs],
        out_specs=jax.tree.map(lambda _: vmem, out_shape),
        scratch_shapes=list(scratch),
        compiler_params=pltpu.CompilerParams(vmem_limit_bytes=limit << 20),
        cost_estimate=pl.CostEstimate(flops=flops, bytes_accessed=moved, transcendentals=0),
        name=name,
    )(*operands)


def prepare_kernel(ids_in, weights_in, rows_in, block, ids, weights, sems):
    tok_count, width = rows_in.shape
    top_count = ids.shape[0]
    experts = 2 * len(RING)
    copies = [
        pltpu.make_async_copy(ids_in, ids, sems.at[0]),
        pltpu.make_async_copy(weights_in, weights, sems.at[1]),
        pltpu.make_async_copy(rows_in, block.at[:, pl.ds(0, width)], sems.at[2]),
    ]
    for copy in copies:
        copy.start()
    square = (tok_count, tok_count)
    earlier = ones_where(iota(square, 0) < iota(square, 1))
    expert = iota((experts, tok_count), 0)
    unit = ones_where(iota((4 * experts, LANES), 0) == iota((4 * experts, LANES), 1))
    token = ones_where(iota((tok_count, LANES), 0) + TOKEN_LANE == iota((tok_count, LANES), 1))
    copies[0].wait()
    copies[1].wait()
    named = jnp.zeros((experts, tok_count), jnp.float32)
    scale = jnp.zeros((experts, tok_count), jnp.float32)
    for k in range(top_count):
        hit = ids[k : k + 1, :] == expert
        named = named + jnp.where(hit, 1.0, 0.0)
        scale = scale + jnp.where(hit, weights[k : k + 1, :], 0.0)
    rank = jnp.dot(named.astype(jnp.bfloat16), earlier, preferred_element_type=jnp.float32)
    notes = [jnp.where(named > 0.5, rank + 1.0, 0.0)]
    for _ in range(3):
        piece = scale.astype(jnp.bfloat16).astype(jnp.float32)
        scale = scale - piece
        notes.append(piece)
    notes = across(jnp.concatenate(notes, axis=0).astype(jnp.bfloat16), unit)
    block[:, width:] = notes.astype(jnp.bfloat16) + token
    copies[2].wait()


def prepare(ids, weights, tokens):
    tok_count, width = tokens.shape
    return local_call(
        prepare_kernel,
        "prepare",
        pltpu.VMEM((tok_count, width + LANES), jnp.bfloat16),
        [pl.ANY] * 3,
        tuple(pltpu.with_memory_space_constraint(x, pltpu.HBM) for x in (ids, weights, tokens)),
        [
            pltpu.VMEM(ids.shape, ids.dtype),
            pltpu.VMEM(weights.shape, weights.dtype),
            pltpu.SemaphoreType.DMA((3,)),
        ],
        limit=8,
    )


def choose_kernel(places, capacity, block, *refs):
    chip = lax.axis_index("expert") >> 1
    tok_count = block.shape[0]
    notes = block[:, -LANES:].astype(jnp.float32)
    lane = iota(notes.shape, 1)
    slot = iota((tok_count, len(places) * capacity), 1)
    code = jnp.zeros(slot.shape, jnp.float32)
    order = jnp.zeros(slot.shape, jnp.int32)
    for at, (steps, flip) in enumerate(places):
        wanted = chip_at(chip, steps, flip)
        column = jnp.sum(jnp.where(lane == wanted, notes, 0.0), axis=1, keepdims=True)
        code = jnp.where(slot >= at * capacity, column, code)
        order = jnp.where(slot >= at * capacity, slot + 1 - at * capacity, order)
    rows = across(ones_where(code == order.astype(jnp.float32)), block[...]).astype(jnp.bfloat16)
    for at in range(len(places)):
        refs[at][...] = rows[at * capacity : (at + 1) * capacity]


def choose(block, capacity, places):
    return local_call(
        functools.partial(choose_kernel, places, capacity),
        "choose",
        [jax.ShapeDtypeStruct((capacity, block.shape[1]), jnp.bfloat16) for _ in places],
        [None],
        (block,),
    )


def load_kernel(source, target, sem):
    copy = pltpu.make_async_copy(source, target, sem)
    copy.start()
    copy.wait()


def loaded(weights):
    return local_call(
        load_kernel,
        "loaded",
        pltpu.VMEM(weights.shape, weights.dtype),
        [pl.ANY],
        (weights,),
        [pltpu.SemaphoreType.DMA],
        limit=9,
        moved=2 * weights.size * weights.dtype.itemsize,
    )


def gated(both):
    hidden = both.shape[1] // 2
    gate = both[:, :hidden]
    return (gate / (1.0 + jnp.exp(-gate)) * both[:, hidden:]).astype(jnp.bfloat16)


def write_pieces(slots, total, outs):
    chip = lax.axis_index("expert") >> 1
    width = total.shape[1]
    experts = 2 * len(RING)
    notes = slots[:, width:].astype(jnp.float32)
    lane = iota(notes.shape, 1)
    mine = (lane >= experts) & (lane < 4 * experts) & ((lane & (experts - 1)) == chip)
    scale = jnp.sum(jnp.where(mine, notes, 0.0), axis=1, keepdims=True)
    start = 0
    for out in outs:
        stop = start + out.shape[0]
        out[:, :width] = (total[start:stop] * scale[start:stop]).astype(jnp.bfloat16)
        out[:, width:] = slots[start:stop, width:]
        start = stop


def near_kernel(*refs):
    pieces, (first, second, slots, total) = refs[:-4], refs[-4:]
    start = 0
    for piece in pieces:
        slots[start : start + piece.shape[0]] = piece[...]
        start += piece.shape[0]
    width = total.shape[1]
    both = jnp.dot(slots[:, :width], first[...], preferred_element_type=jnp.float32)
    total[...] = jnp.dot(gated(both), second[...], preferred_element_type=jnp.float32)


def near_pass(pieces, weights):
    count = sum(piece.shape[0] for piece in pieces)
    full = pieces[0].shape[1]
    return local_call(
        near_kernel,
        "near_pass",
        [
            jax.ShapeDtypeStruct((count, full), jnp.bfloat16),
            jax.ShapeDtypeStruct((count, full - LANES), jnp.float32),
        ],
        [None] * (len(pieces) + 2),
        (*pieces, *weights),
        moved=2 * sum(w.size for w in weights),
    )


def far_kernel(slots, before, first, second, *refs):
    outs, total = refs[:-1], refs[-1]
    width = total.shape[1]
    both = jnp.dot(slots[:, :width], first[...], preferred_element_type=jnp.float32)
    term = jnp.dot(gated(both), second[...], preferred_element_type=jnp.float32)
    total[...] = before[...] + term
    write_pieces(slots, total, outs)


def far_pass(slots, total, weights, capacity):
    count, full = slots.shape
    return local_call(
        far_kernel,
        "far_pass",
        [jax.ShapeDtypeStruct((capacity, full), jnp.bfloat16)] * (count // capacity),
        [None] * 4,
        (slots, total, *weights),
        [pltpu.VMEM(total.shape, jnp.float32)],
        limit=24,
        moved=2 * sum(w.size for w in weights),
    )


def combine_kernel(count, *refs):
    blocks, more, (out, slots) = refs[:count], refs[count:-2], refs[-2:]
    tok_count, width = out.shape
    start = 0
    for block in blocks:
        slots[start : start + block.shape[0]] = block[...]
        start += block.shape[0]
    token = slots[:, width:]
    part = width // 7
    for at in range(7):
        place = slice(at * part, (at + 1) * part)
        mixed = across(token, slots[:, place])[TOKEN_LANE : TOKEN_LANE + tok_count]
        for other in more:
            mixed = mixed + other[:, place].astype(jnp.float32)
        out[:, place] = mixed.astype(out.dtype)


def combine(blocks, tok_count, *more):
    capacity, full = blocks[0].shape
    return local_call(
        functools.partial(combine_kernel, len(blocks)),
        "combine",
        jax.ShapeDtypeStruct((tok_count, full - LANES), jnp.bfloat16),
        [None] * (len(blocks) + len(more)),
        (*blocks, *more),
        [pltpu.VMEM((capacity * len(blocks), full), jnp.bfloat16)],
    )


def sent(shard, sections, section_step, ring_step, flip):
    planes = len(RING)
    pairs = []
    for s in range(sections):
        for z in range(planes):
            for y in range(2):
                for core in range(2):
                    plane = RING[(RING.index(z) + ring_step) % planes]
                    target = (((s + section_step) % sections) * planes + plane) * 2 + (y ^ flip)
                    pairs.append((((s * planes + z) * 2 + y) * 2 + core, target * 2 + core))
    return lax.ppermute(shard, ("section", "expert"), pairs)


def after(value, other):
    return lax.optimization_barrier((value, other))[0]


def by_ring(rows, route_ids, route_weights, w_gate_up, w_down):
    sections = lax.axis_size("section")
    devices = lax.axis_size("expert")
    experts = devices // 2
    tokens = rows[0]
    tok_count = tokens.shape[0]
    top_count = route_ids.shape[2]
    capacity = max(2, 2 * tok_count * top_count // experts)
    swap = [(i, i ^ 1) for i in range(devices)]
    w_in, w_out = w_gate_up[0], w_down[0]
    far_out = lax.ppermute(w_out, "expert", swap)
    far_in = lax.ppermute(w_in, "expert", swap)
    block = prepare(route_ids[0].T, route_weights[0].T, tokens)
    block1 = sent(block, sections, 0, 1, 0)
    own0, other, back0, back1 = choose(block, capacity, ((0, 0), (0, 1), (3, 0), (3, 1)))
    other0 = sent(other, sections, 0, 0, 1)
    near = (loaded(after(w_in, own0)), loaded(after(w_out, own0)))
    block1 = after(block1, (near, other0))
    own1, other, on0, on1 = choose(block1, capacity, ((0, 0), (0, 1), (1, 0), (1, 1)))
    other1 = sent(other, sections, 0, 0, 1)
    own2 = sent(on0, sections, 0, 1, 0)
    other2 = sent(on1, sections, 0, 1, 1)
    other3 = sent(after(back1, (near, other0)), sections, 0, 3, 1)
    own3 = sent(after(back0, (other1, other3)), sections, 0, 3, 0)
    pieces = (own0, other0, own1, own2, other2, other1, own3, other3)
    places = ((0, 0), (0, 1), (1, 0), (2, 0), (2, 1), (1, 1), (3, 0), (3, 1))
    slots, total = near_pass(pieces, near)
    pieces = far_pass(slots, total, (far_in, far_out), capacity)
    piece = dict(zip(places, pieces))
    merged = [
        piece[3, 0],
        sent(piece[2, 0], sections, 0, 1, 0),
        sent(piece[2, 1], sections, 0, 1, 1),
        sent(piece[3, 1], sections, 0, 0, 1),
    ]
    straight = [sent(piece[0, flip], sections, 1, 0, flip) for flip in range(2)]
    merged, straight = lax.optimization_barrier((merged, straight))
    straight.append(sent(piece[1, 0], sections, 1, -1, 0))
    straight.append(sent(after(piece[1, 1], straight[-1]), sections, 1, -1, 1))
    merged = sent(combine(merged, tok_count), sections, 1, 1, 0)
    return combine(straight, tok_count, merged)[None]


def per_device(rows, route_ids, route_weights, w_gate_up, w_down):
    experts = lax.axis_size("expert") // 2
    fits = experts == 2 * len(RING) and rows.shape[1] <= LANES - TOKEN_LANE
    plan = by_ring if fits else by_slots
    return plan(rows, route_ids, route_weights, w_gate_up, w_down)


def solution(mesh):
    in_specs = (
        P("section", "expert", None),
        P("section", "expert", None),
        P("section", "expert", None),
        P("section", None, "expert"),
        P("section", "expert", None),
    )
    out_specs = P("section", "expert", None)
    return jax.shard_map(
        per_device, mesh=mesh, in_specs=in_specs, out_specs=out_specs, check_vma=False
    )
```

```python
import functools

import jax
import jax.numpy as jnp
from jax import lax
from jax.experimental import pallas as pl
from jax.experimental.pallas import tpu as pltpu
from jax.sharding import PartitionSpec as P


def passed_along(shard, axis, by):
    length = lax.axis_size(axis)
    return lax.ppermute(shard, axis, [(i, (i + by) % length) for i in range(length)])


def by_slots(rows, route_ids, route_weights, w_gate_up, w_down):
    devices = lax.axis_size("expert")
    experts = devices // 2
    tokens = rows[0]
    tok_count, width = tokens.shape
    top_count = route_ids.shape[2]
    choices_flat = route_ids[0].reshape(-1)
    capacity = max(2, 2 * tok_count * top_count // experts)
    onehot = (choices_flat[:, None] == jnp.arange(experts, dtype=jnp.int32)[None, :]).astype(
        jnp.int32
    )
    before = jnp.cumsum(onehot, axis=0) - onehot
    slot = jnp.sum(before * onehot, axis=1)
    place = slot * experts + choices_flat
    slot_total = experts * capacity
    picker = (place[None, :] == jnp.arange(slot_total, dtype=jnp.int32)[:, None]).astype(
        jnp.bfloat16
    )
    token_pairs = jnp.repeat(tokens, top_count, axis=0)
    packed = jnp.dot(picker, token_pairs, preferred_element_type=jnp.float32).astype(jnp.bfloat16)
    w_in = w_gate_up[0]
    w_out = w_down[0]
    hidden = w_out.shape[0]
    outgoing = jnp.broadcast_to(
        packed.reshape(capacity, experts, 1, width), (capacity, experts, 2, width)
    )
    outgoing = outgoing.reshape(capacity, devices, width)
    block = lax.all_to_all(outgoing, "expert", split_axis=1, concat_axis=1, tiled=True)
    flat = block.reshape(-1, width)
    both = jnp.dot(flat, w_in, preferred_element_type=jnp.float32)
    active = (jax.nn.silu(both[:, :hidden]) * both[:, hidden:]).astype(jnp.bfloat16)
    result = jnp.dot(active, w_out, preferred_element_type=jnp.float32)
    partial_out = result.reshape(block.shape[0], block.shape[1], width).astype(jnp.bfloat16)
    returned = lax.all_to_all(partial_out, "expert", split_axis=1, concat_axis=1, tiled=True)
    returned = returned.reshape(capacity, experts, 2, width).astype(jnp.float32)
    expert_out = jnp.sum(returned, axis=2).astype(jnp.bfloat16).reshape(slot_total, width)
    pair_out = expert_out[place].astype(jnp.float32) * route_weights[0].reshape(-1)[:, None]
    layer_out = jnp.sum(pair_out.reshape(tok_count, top_count, width), axis=1).astype(jnp.bfloat16)
    return passed_along(layer_out, "section", 1)[None]


RING = (0, 1, 3, 2)
LANES = 128
TOKEN_LANE = 64


def on_ring(place):
    return place ^ (place >> 1)


def chip_at(chip, steps, flip):
    return (on_ring((on_ring(chip >> 1) + steps) & 3) << 1) | ((chip & 1) ^ flip)


def iota(shape, axis):
    return lax.broadcasted_iota(jnp.int32, shape, axis)


def ones_where(condition):
    return jnp.where(condition, 1.0, 0.0).astype(jnp.bfloat16)


def across(left, right):
    return lax.dot_general(left, right, (((0,), (0,)), ((), ())), preferred_element_type=jnp.float32)


def local_call(kernel, name, out_shape, in_specs, operands, scratch=(), limit=12, flops=0, moved=0):
    vmem = pl.BlockSpec(memory_space=pltpu.VMEM)
    return pl.pallas_call(
        kernel,
        out_shape=out_shape,
        in_specs=[vmem if spec is None else pl.BlockSpec(memory_space=spec) for spec in in_specs],
        out_specs=jax.tree.map(lambda _: vmem, out_shape),
        scratch_shapes=list(scratch),
        compiler_params=pltpu.CompilerParams(vmem_limit_bytes=limit << 20),
        cost_estimate=pl.CostEstimate(flops=flops, bytes_accessed=moved, transcendentals=0),
        name=name,
    )(*operands)


def prepare_kernel(ids_in, weights_in, rows_in, block, ids, weights, sems):
    tok_count, width = rows_in.shape
    top_count = ids.shape[0]
    experts = 2 * len(RING)
    copies = [
        pltpu.make_async_copy(ids_in, ids, sems.at[0]),
        pltpu.make_async_copy(weights_in, weights, sems.at[1]),
        pltpu.make_async_copy(rows_in, block.at[:, pl.ds(0, width)], sems.at[2]),
    ]
    for copy in copies:
        copy.start()
    square = (tok_count, tok_count)
    earlier = ones_where(iota(square, 0) < iota(square, 1))
    expert = iota((experts, tok_count), 0)
    unit = ones_where(iota((4 * experts, LANES), 0) == iota((4 * experts, LANES), 1))
    token = ones_where(iota((tok_count, LANES), 0) + TOKEN_LANE == iota((tok_count, LANES), 1))
    copies[0].wait()
    copies[1].wait()
    named = jnp.zeros((experts, tok_count), jnp.float32)
    scale = jnp.zeros((experts, tok_count), jnp.float32)
    for k in range(top_count):
        hit = ids[k : k + 1, :] == expert
        named = named + jnp.where(hit, 1.0, 0.0)
        scale = scale + jnp.where(hit, weights[k : k + 1, :], 0.0)
    rank = jnp.dot(named.astype(jnp.bfloat16), earlier, preferred_element_type=jnp.float32)
    notes = [jnp.where(named > 0.5, rank + 1.0, 0.0)]
    for _ in range(3):
        piece = scale.astype(jnp.bfloat16).astype(jnp.float32)
        scale = scale - piece
        notes.append(piece)
    notes = across(jnp.concatenate(notes, axis=0).astype(jnp.bfloat16), unit)
    block[:, width:] = notes.astype(jnp.bfloat16) + token
    copies[2].wait()


def prepare(ids, weights, tokens):
    tok_count, width = tokens.shape
    return local_call(
        prepare_kernel,
        "prepare",
        pltpu.VMEM((tok_count, width + LANES), jnp.bfloat16),
        [pl.ANY] * 3,
        tuple(pltpu.with_memory_space_constraint(x, pltpu.HBM) for x in (ids, weights, tokens)),
        [
            pltpu.VMEM(ids.shape, ids.dtype),
            pltpu.VMEM(weights.shape, weights.dtype),
            pltpu.SemaphoreType.DMA((3,)),
        ],
        limit=8,
    )


def choose_kernel(places, capacity, block, *refs):
    chip = lax.axis_index("expert") >> 1
    tok_count = block.shape[0]
    notes = block[:, -LANES:].astype(jnp.float32)
    lane = iota(notes.shape, 1)
    slot = iota((tok_count, len(places) * capacity), 1)
    code = jnp.zeros(slot.shape, jnp.float32)
    order = jnp.zeros(slot.shape, jnp.int32)
    for at, (steps, flip) in enumerate(places):
        wanted = chip_at(chip, steps, flip)
        column = jnp.sum(jnp.where(lane == wanted, notes, 0.0), axis=1, keepdims=True)
        code = jnp.where(slot >= at * capacity, column, code)
        order = jnp.where(slot >= at * capacity, slot + 1 - at * capacity, order)
    rows = across(ones_where(code == order.astype(jnp.float32)), block[...]).astype(jnp.bfloat16)
    for at in range(len(places)):
        refs[at][...] = rows[at * capacity : (at + 1) * capacity]


def choose(block, capacity, places):
    return local_call(
        functools.partial(choose_kernel, places, capacity),
        "choose",
        [jax.ShapeDtypeStruct((capacity, block.shape[1]), jnp.bfloat16) for _ in places],
        [None],
        (block,),
    )


def load_kernel(source, target, sem):
    copy = pltpu.make_async_copy(source, target, sem)
    copy.start()
    copy.wait()


def loaded(weights):
    return local_call(
        load_kernel,
        "loaded",
        pltpu.VMEM(weights.shape, weights.dtype),
        [pl.ANY],
        (weights,),
        [pltpu.SemaphoreType.DMA],
        limit=9,
        moved=2 * weights.size * weights.dtype.itemsize,
    )


def gated(both):
    hidden = both.shape[1] // 2
    gate = both[:, :hidden]
    return (gate / (1.0 + jnp.exp(-gate)) * both[:, hidden:]).astype(jnp.bfloat16)


def write_pieces(slots, total, outs):
    chip = lax.axis_index("expert") >> 1
    width = total.shape[1]
    experts = 2 * len(RING)
    notes = slots[:, width:].astype(jnp.float32)
    lane = iota(notes.shape, 1)
    mine = (lane >= experts) & (lane < 4 * experts) & ((lane & (experts - 1)) == chip)
    scale = jnp.sum(jnp.where(mine, notes, 0.0), axis=1, keepdims=True)
    start = 0
    for out in outs:
        stop = start + out.shape[0]
        out[:, :width] = (total[start:stop] * scale[start:stop]).astype(jnp.bfloat16)
        out[:, width:] = slots[start:stop, width:]
        start = stop


def near_kernel(*refs):
    pieces, (first, second, slots, total) = refs[:-4], refs[-4:]
    start = 0
    for piece in pieces:
        slots[start : start + piece.shape[0]] = piece[...]
        start += piece.shape[0]
    width = total.shape[1]
    both = jnp.dot(slots[:, :width], first[...], preferred_element_type=jnp.float32)
    total[...] = jnp.dot(gated(both), second[...], preferred_element_type=jnp.float32)


def near_pass(pieces, weights):
    count = sum(piece.shape[0] for piece in pieces)
    full = pieces[0].shape[1]
    return local_call(
        near_kernel,
        "near_pass",
        [
            jax.ShapeDtypeStruct((count, full), jnp.bfloat16),
            jax.ShapeDtypeStruct((count, full - LANES), jnp.float32),
        ],
        [None] * (len(pieces) + 2),
        (*pieces, *weights),
        moved=2 * sum(w.size for w in weights),
    )


def far_kernel(slots, before, first, second, *refs):
    outs, total = refs[:-1], refs[-1]
    width = total.shape[1]
    both = jnp.dot(slots[:, :width], first[...], preferred_element_type=jnp.float32)
    term = jnp.dot(gated(both), second[...], preferred_element_type=jnp.float32)
    total[...] = before[...] + term
    write_pieces(slots, total, outs)


def far_pass(slots, total, weights, capacity):
    count, full = slots.shape
    return local_call(
        far_kernel,
        "far_pass",
        [jax.ShapeDtypeStruct((capacity, full), jnp.bfloat16)] * (count // capacity),
        [None] * 4,
        (slots, total, *weights),
        [pltpu.VMEM(total.shape, jnp.float32)],
        limit=24,
        moved=2 * sum(w.size for w in weights),
    )


def combine_kernel(count, *refs):
    blocks, more, (out, slots) = refs[:count], refs[count:-2], refs[-2:]
    tok_count, width = out.shape
    start = 0
    for block in blocks:
        slots[start : start + block.shape[0]] = block[...]
        start += block.shape[0]
    token = slots[:, width:]
    part = width // 7
    for at in range(7):
        place = slice(at * part, (at + 1) * part)
        mixed = across(token, slots[:, place])[TOKEN_LANE : TOKEN_LANE + tok_count]
        for other in more:
            mixed = mixed + other[:, place].astype(jnp.float32)
        out[:, place] = mixed.astype(out.dtype)


def combine(blocks, tok_count, *more):
    capacity, full = blocks[0].shape
    return local_call(
        functools.partial(combine_kernel, len(blocks)),
        "combine",
        jax.ShapeDtypeStruct((tok_count, full - LANES), jnp.bfloat16),
        [None] * (len(blocks) + len(more)),
        (*blocks, *more),
        [pltpu.VMEM((capacity * len(blocks), full), jnp.bfloat16)],
    )


def sent(shard, sections, section_step, ring_step, flip):
    planes = len(RING)
    pairs = []
    for s in range(sections):
        for z in range(planes):
            for y in range(2):
                for core in range(2):
                    plane = RING[(RING.index(z) + ring_step) % planes]
                    target = (((s + section_step) % sections) * planes + plane) * 2 + (y ^ flip)
                    pairs.append((((s * planes + z) * 2 + y) * 2 + core, target * 2 + core))
    return lax.ppermute(shard, ("section", "expert"), pairs)


def after(value, other):
    return lax.optimization_barrier((value, other))[0]


def by_ring(rows, route_ids, route_weights, w_gate_up, w_down):
    sections = lax.axis_size("section")
    devices = lax.axis_size("expert")
    experts = devices // 2
    tokens = rows[0]
    tok_count = tokens.shape[0]
    top_count = route_ids.shape[2]
    capacity = max(2, 2 * tok_count * top_count // experts)
    swap = [(i, i ^ 1) for i in range(devices)]
    w_in, w_out = w_gate_up[0], w_down[0]
    far_out = lax.ppermute(w_out, "expert", swap)
    far_in = lax.ppermute(w_in, "expert", swap)
    block = prepare(route_ids[0].T, route_weights[0].T, tokens)
    block1 = sent(block, sections, 0, 1, 0)
    own0, other, back0, back1 = choose(block, capacity, ((0, 0), (0, 1), (3, 0), (3, 1)))
    other0 = sent(other, sections, 0, 0, 1)
    near = (loaded(after(w_in, own0)), loaded(after(w_out, own0)))
    block1 = after(block1, (near, other0))
    own1, other, on0, on1 = choose(block1, capacity, ((0, 0), (0, 1), (1, 0), (1, 1)))
    other1 = sent(other, sections, 0, 0, 1)
    own2 = sent(on0, sections, 0, 1, 0)
    other2 = sent(on1, sections, 0, 1, 1)
    other3 = sent(after(back1, (near, other0)), sections, 0, 3, 1)
    own3 = sent(after(back0, (other1, other3)), sections, 0, 3, 0)
    pieces = (own0, other0, own1, own2, other2, other1, own3, other3)
    places = ((0, 0), (0, 1), (1, 0), (2, 0), (2, 1), (1, 1), (3, 0), (3, 1))
    slots, total = near_pass(pieces, near)
    pieces = far_pass(slots, total, (far_in, far_out), capacity)
    piece = dict(zip(places, pieces))
    straight = [
        sent(piece[0, 0], sections, 1, 0, 0),
        sent(piece[0, 1], sections, 1, 0, 1),
        sent(piece[1, 0], sections, 1, -1, 0),
    ]
    merged = [
        piece[3, 0],
        sent(piece[2, 1], sections, 0, 1, 1),
        sent(piece[3, 1], sections, 0, 0, 1),
        sent(piece[2, 0], sections, 0, 1, 0),
    ]
    straight.append(sent(after(piece[1, 1], straight), sections, 1, -1, 1))
    merged = sent(combine(merged, tok_count), sections, 1, 1, 0)
    return combine(straight, tok_count, merged)[None]


def per_device(rows, route_ids, route_weights, w_gate_up, w_down):
    experts = lax.axis_size("expert") // 2
    fits = experts == 2 * len(RING) and rows.shape[1] <= LANES - TOKEN_LANE
    plan = by_ring if fits else by_slots
    return plan(rows, route_ids, route_weights, w_gate_up, w_down)


def solution(mesh):
    in_specs = (
        P("section", "expert", None),
        P("section", "expert", None),
        P("section", "expert", None),
        P("section", None, "expert"),
        P("section", "expert", None),
    )
    out_specs = P("section", "expert", None)
    return jax.shard_map(
        per_device, mesh=mesh, in_specs=in_specs, out_specs=out_specs, check_vma=False
    )
```

```python
import functools

import jax
import jax.numpy as jnp
from jax import lax
from jax.experimental import pallas as pl
from jax.experimental.pallas import tpu as pltpu
from jax.sharding import PartitionSpec as P


def passed_along(shard, axis, by):
    length = lax.axis_size(axis)
    return lax.ppermute(shard, axis, [(i, (i + by) % length) for i in range(length)])


def by_slots(rows, route_ids, route_weights, w_gate_up, w_down):
    devices = lax.axis_size("expert")
    experts = devices // 2
    tokens = rows[0]
    tok_count, width = tokens.shape
    top_count = route_ids.shape[2]
    choices_flat = route_ids[0].reshape(-1)
    capacity = max(2, 2 * tok_count * top_count // experts)
    onehot = (choices_flat[:, None] == jnp.arange(experts, dtype=jnp.int32)[None, :]).astype(
        jnp.int32
    )
    before = jnp.cumsum(onehot, axis=0) - onehot
    slot = jnp.sum(before * onehot, axis=1)
    place = slot * experts + choices_flat
    slot_total = experts * capacity
    picker = (place[None, :] == jnp.arange(slot_total, dtype=jnp.int32)[:, None]).astype(
        jnp.bfloat16
    )
    token_pairs = jnp.repeat(tokens, top_count, axis=0)
    packed = jnp.dot(picker, token_pairs, preferred_element_type=jnp.float32).astype(jnp.bfloat16)
    w_in = w_gate_up[0]
    w_out = w_down[0]
    hidden = w_out.shape[0]
    outgoing = jnp.broadcast_to(
        packed.reshape(capacity, experts, 1, width), (capacity, experts, 2, width)
    )
    outgoing = outgoing.reshape(capacity, devices, width)
    block = lax.all_to_all(outgoing, "expert", split_axis=1, concat_axis=1, tiled=True)
    flat = block.reshape(-1, width)
    both = jnp.dot(flat, w_in, preferred_element_type=jnp.float32)
    active = (jax.nn.silu(both[:, :hidden]) * both[:, hidden:]).astype(jnp.bfloat16)
    result = jnp.dot(active, w_out, preferred_element_type=jnp.float32)
    partial_out = result.reshape(block.shape[0], block.shape[1], width).astype(jnp.bfloat16)
    returned = lax.all_to_all(partial_out, "expert", split_axis=1, concat_axis=1, tiled=True)
    returned = returned.reshape(capacity, experts, 2, width).astype(jnp.float32)
    expert_out = jnp.sum(returned, axis=2).astype(jnp.bfloat16).reshape(slot_total, width)
    pair_out = expert_out[place].astype(jnp.float32) * route_weights[0].reshape(-1)[:, None]
    layer_out = jnp.sum(pair_out.reshape(tok_count, top_count, width), axis=1).astype(jnp.bfloat16)
    return passed_along(layer_out, "section", 1)[None]


RING = (0, 1, 3, 2)
LANES = 128
TOKEN_LANE = 64


def on_ring(place):
    return place ^ (place >> 1)


def chip_at(chip, steps, flip):
    return (on_ring((on_ring(chip >> 1) + steps) & 3) << 1) | ((chip & 1) ^ flip)


def iota(shape, axis):
    return lax.broadcasted_iota(jnp.int32, shape, axis)


def ones_where(condition):
    return jnp.where(condition, 1.0, 0.0).astype(jnp.bfloat16)


def across(left, right):
    return lax.dot_general(left, right, (((0,), (0,)), ((), ())), preferred_element_type=jnp.float32)


def local_call(kernel, name, out_shape, in_specs, operands, scratch=(), limit=12, flops=0, moved=0):
    vmem = pl.BlockSpec(memory_space=pltpu.VMEM)
    return pl.pallas_call(
        kernel,
        out_shape=out_shape,
        in_specs=[vmem if spec is None else pl.BlockSpec(memory_space=spec) for spec in in_specs],
        out_specs=jax.tree.map(lambda _: vmem, out_shape),
        scratch_shapes=list(scratch),
        compiler_params=pltpu.CompilerParams(vmem_limit_bytes=limit << 20),
        cost_estimate=pl.CostEstimate(flops=flops, bytes_accessed=moved, transcendentals=0),
        name=name,
    )(*operands)


def prepare_kernel(ids_in, weights_in, rows_in, block, ids, weights, sems):
    tok_count, width = rows_in.shape
    top_count = ids.shape[0]
    experts = 2 * len(RING)
    copies = [
        pltpu.make_async_copy(ids_in, ids, sems.at[0]),
        pltpu.make_async_copy(weights_in, weights, sems.at[1]),
        pltpu.make_async_copy(rows_in, block.at[:, pl.ds(0, width)], sems.at[2]),
    ]
    for copy in copies:
        copy.start()
    square = (tok_count, tok_count)
    earlier = ones_where(iota(square, 0) < iota(square, 1))
    expert = iota((experts, tok_count), 0)
    unit = ones_where(iota((4 * experts, LANES), 0) == iota((4 * experts, LANES), 1))
    token = ones_where(iota((tok_count, LANES), 0) + TOKEN_LANE == iota((tok_count, LANES), 1))
    copies[0].wait()
    copies[1].wait()
    named = jnp.zeros((experts, tok_count), jnp.float32)
    scale = jnp.zeros((experts, tok_count), jnp.float32)
    for k in range(top_count):
        hit = ids[k : k + 1, :] == expert
        named = named + jnp.where(hit, 1.0, 0.0)
        scale = scale + jnp.where(hit, weights[k : k + 1, :], 0.0)
    rank = jnp.dot(named.astype(jnp.bfloat16), earlier, preferred_element_type=jnp.float32)
    notes = [jnp.where(named > 0.5, rank + 1.0, 0.0)]
    for _ in range(3):
        piece = scale.astype(jnp.bfloat16).astype(jnp.float32)
        scale = scale - piece
        notes.append(piece)
    notes = across(jnp.concatenate(notes, axis=0).astype(jnp.bfloat16), unit)
    block[:, width:] = notes.astype(jnp.bfloat16) + token
    copies[2].wait()


def prepare(ids, weights, tokens):
    tok_count, width = tokens.shape
    return local_call(
        prepare_kernel,
        "prepare",
        pltpu.VMEM((tok_count, width + LANES), jnp.bfloat16),
        [pl.ANY] * 3,
        tuple(pltpu.with_memory_space_constraint(x, pltpu.HBM) for x in (ids, weights, tokens)),
        [
            pltpu.VMEM(ids.shape, ids.dtype),
            pltpu.VMEM(weights.shape, weights.dtype),
            pltpu.SemaphoreType.DMA((3,)),
        ],
        limit=8,
    )


def choose_kernel(places, capacity, block, *refs):
    chip = lax.axis_index("expert") >> 1
    tok_count = block.shape[0]
    notes = block[:, -LANES:].astype(jnp.float32)
    lane = iota(notes.shape, 1)
    slot = iota((tok_count, len(places) * capacity), 1)
    code = jnp.zeros(slot.shape, jnp.float32)
    order = jnp.zeros(slot.shape, jnp.int32)
    for at, (steps, flip) in enumerate(places):
        wanted = chip_at(chip, steps, flip)
        column = jnp.sum(jnp.where(lane == wanted, notes, 0.0), axis=1, keepdims=True)
        code = jnp.where(slot >= at * capacity, column, code)
        order = jnp.where(slot >= at * capacity, slot + 1 - at * capacity, order)
    rows = across(ones_where(code == order.astype(jnp.float32)), block[...]).astype(jnp.bfloat16)
    for at in range(len(places)):
        refs[at][...] = rows[at * capacity : (at + 1) * capacity]


def choose(block, capacity, places):
    return local_call(
        functools.partial(choose_kernel, places, capacity),
        "choose",
        [jax.ShapeDtypeStruct((capacity, block.shape[1]), jnp.bfloat16) for _ in places],
        [None],
        (block,),
    )


def load_kernel(source, target, sem):
    copy = pltpu.make_async_copy(source, target, sem)
    copy.start()
    copy.wait()


def loaded(weights):
    return local_call(
        load_kernel,
        "loaded",
        pltpu.VMEM(weights.shape, weights.dtype),
        [pl.ANY],
        (weights,),
        [pltpu.SemaphoreType.DMA],
        limit=9,
        moved=2 * weights.size * weights.dtype.itemsize,
    )


def gated(both):
    hidden = both.shape[1] // 2
    gate = both[:, :hidden]
    return (gate / (1.0 + jnp.exp(-gate)) * both[:, hidden:]).astype(jnp.bfloat16)


def write_pieces(slots, total, outs):
    chip = lax.axis_index("expert") >> 1
    width = total.shape[1]
    experts = 2 * len(RING)
    notes = slots[:, width:].astype(jnp.float32)
    lane = iota(notes.shape, 1)
    mine = (lane >= experts) & (lane < 4 * experts) & ((lane & (experts - 1)) == chip)
    scale = jnp.sum(jnp.where(mine, notes, 0.0), axis=1, keepdims=True)
    start = 0
    for out in outs:
        stop = start + out.shape[0]
        out[:, :width] = (total[start:stop] * scale[start:stop]).astype(jnp.bfloat16)
        out[:, width:] = slots[start:stop, width:]
        start = stop


def near_kernel(*refs):
    pieces, (first, second, slots, total) = refs[:-4], refs[-4:]
    start = 0
    for piece in pieces:
        slots[start : start + piece.shape[0]] = piece[...]
        start += piece.shape[0]
    width = total.shape[1]
    both = jnp.dot(slots[:, :width], first[...], preferred_element_type=jnp.float32)
    total[...] = jnp.dot(gated(both), second[...], preferred_element_type=jnp.float32)


def near_pass(pieces, weights):
    count = sum(piece.shape[0] for piece in pieces)
    full = pieces[0].shape[1]
    return local_call(
        near_kernel,
        "near_pass",
        [
            jax.ShapeDtypeStruct((count, full), jnp.bfloat16),
            jax.ShapeDtypeStruct((count, full - LANES), jnp.float32),
        ],
        [None] * (len(pieces) + 2),
        (*pieces, *weights),
        moved=2 * sum(w.size for w in weights),
    )


def far_kernel(slots, before, first, second, *refs):
    outs, total = refs[:-1], refs[-1]
    width = total.shape[1]
    both = jnp.dot(slots[:, :width], first[...], preferred_element_type=jnp.float32)
    term = jnp.dot(gated(both), second[...], preferred_element_type=jnp.float32)
    total[...] = before[...] + term
    write_pieces(slots, total, outs)


def far_pass(slots, total, weights, capacity):
    count, full = slots.shape
    return local_call(
        far_kernel,
        "far_pass",
        [jax.ShapeDtypeStruct((capacity, full), jnp.bfloat16)] * (count // capacity),
        [None] * 4,
        (slots, total, *weights),
        [pltpu.VMEM(total.shape, jnp.float32)],
        limit=24,
        moved=2 * sum(w.size for w in weights),
    )


def combine_kernel(count, *refs):
    blocks, more, (out, slots) = refs[:count], refs[count:-2], refs[-2:]
    tok_count, width = out.shape
    start = 0
    for block in blocks:
        slots[start : start + block.shape[0]] = block[...]
        start += block.shape[0]
    token = slots[:, width:]
    part = width // 7
    for at in range(7):
        place = slice(at * part, (at + 1) * part)
        mixed = across(token, slots[:, place])[TOKEN_LANE : TOKEN_LANE + tok_count]
        for other in more:
            mixed = mixed + other[:, place].astype(jnp.float32)
        out[:, place] = mixed.astype(out.dtype)


def combine(blocks, tok_count, *more):
    capacity, full = blocks[0].shape
    return local_call(
        functools.partial(combine_kernel, len(blocks)),
        "combine",
        jax.ShapeDtypeStruct((tok_count, full - LANES), jnp.bfloat16),
        [None] * (len(blocks) + len(more)),
        (*blocks, *more),
        [pltpu.VMEM((capacity * len(blocks), full), jnp.bfloat16)],
    )


def sent(shard, sections, section_step, ring_step, flip):
    planes = len(RING)
    pairs = []
    for s in range(sections):
        for z in range(planes):
            for y in range(2):
                for core in range(2):
                    plane = RING[(RING.index(z) + ring_step) % planes]
                    target = (((s + section_step) % sections) * planes + plane) * 2 + (y ^ flip)
                    pairs.append((((s * planes + z) * 2 + y) * 2 + core, target * 2 + core))
    return lax.ppermute(shard, ("section", "expert"), pairs)


def after(value, other):
    return lax.optimization_barrier((value, other))[0]


def by_ring(rows, route_ids, route_weights, w_gate_up, w_down):
    sections = lax.axis_size("section")
    devices = lax.axis_size("expert")
    experts = devices // 2
    tokens = rows[0]
    tok_count = tokens.shape[0]
    top_count = route_ids.shape[2]
    capacity = max(2, 2 * tok_count * top_count // experts)
    swap = [(i, i ^ 1) for i in range(devices)]
    w_in, w_out = w_gate_up[0], w_down[0]
    far_out = lax.ppermute(w_out, "expert", swap)
    far_in = lax.ppermute(w_in, "expert", swap)
    block = prepare(route_ids[0].T, route_weights[0].T, tokens)
    block1 = sent(block, sections, 0, 1, 0)
    own0, other, back0, back1 = choose(block, capacity, ((0, 0), (0, 1), (3, 0), (3, 1)))
    other0 = sent(other, sections, 0, 0, 1)
    near = (loaded(after(w_in, own0)), loaded(after(w_out, own0)))
    block1 = after(block1, (near, other0))
    own1, other, on0, on1 = choose(block1, capacity, ((0, 0), (0, 1), (1, 0), (1, 1)))
    other1 = sent(other, sections, 0, 0, 1)
    own2 = sent(on0, sections, 0, 1, 0)
    other2 = sent(on1, sections, 0, 1, 1)
    other3 = sent(after(back1, (near, other0)), sections, 0, 3, 1)
    own3 = sent(after(back0, (other1, other3)), sections, 0, 3, 0)
    pieces = (own0, other0, own1, own2, other2, other1, own3, other3)
    places = ((0, 0), (0, 1), (1, 0), (2, 0), (2, 1), (1, 1), (3, 0), (3, 1))
    slots, total = near_pass(pieces, near)
    pieces = far_pass(slots, total, (far_in, far_out), capacity)
    piece = dict(zip(places, pieces))
    first = [
        sent(piece[2, 0], sections, 0, 1, 0),
        sent(piece[2, 1], sections, 0, 1, 1),
        sent(piece[3, 1], sections, 0, 0, 1),
        sent(piece[0, 1], sections, 1, 0, 1),
        sent(piece[1, 0], sections, 1, -1, 0),
    ]
    *merged, zero, one = lax.optimization_barrier(first)
    merged.append(piece[3, 0])
    straight = [zero, one, sent(piece[1, 1], sections, 1, -1, 1), sent(piece[0, 0], sections, 1, 0, 0)]
    merged = sent(combine(merged, tok_count), sections, 1, 1, 0)
    return combine(straight, tok_count, merged)[None]


def per_device(rows, route_ids, route_weights, w_gate_up, w_down):
    experts = lax.axis_size("expert") // 2
    fits = experts == 2 * len(RING) and rows.shape[1] <= LANES - TOKEN_LANE
    plan = by_ring if fits else by_slots
    return plan(rows, route_ids, route_weights, w_gate_up, w_down)


def solution(mesh):
    in_specs = (
        P("section", "expert", None),
        P("section", "expert", None),
        P("section", "expert", None),
        P("section", None, "expert"),
        P("section", "expert", None),
    )
    out_specs = P("section", "expert", None)
    return jax.shard_map(
        per_device, mesh=mesh, in_specs=in_specs, out_specs=out_specs, check_vma=False
    )
```

```python
import functools

import jax
import jax.numpy as jnp
from jax import lax
from jax.experimental import pallas as pl
from jax.experimental.pallas import tpu as pltpu
from jax.sharding import PartitionSpec as P


def passed_along(shard, axis, by):
    length = lax.axis_size(axis)
    return lax.ppermute(shard, axis, [(i, (i + by) % length) for i in range(length)])


def by_slots(rows, route_ids, route_weights, w_gate_up, w_down):
    devices = lax.axis_size("expert")
    experts = devices // 2
    tokens = rows[0]
    tok_count, width = tokens.shape
    top_count = route_ids.shape[2]
    choices_flat = route_ids[0].reshape(-1)
    capacity = max(2, 2 * tok_count * top_count // experts)
    onehot = (choices_flat[:, None] == jnp.arange(experts, dtype=jnp.int32)[None, :]).astype(
        jnp.int32
    )
    before = jnp.cumsum(onehot, axis=0) - onehot
    slot = jnp.sum(before * onehot, axis=1)
    place = slot * experts + choices_flat
    slot_total = experts * capacity
    picker = (place[None, :] == jnp.arange(slot_total, dtype=jnp.int32)[:, None]).astype(
        jnp.bfloat16
    )
    token_pairs = jnp.repeat(tokens, top_count, axis=0)
    packed = jnp.dot(picker, token_pairs, preferred_element_type=jnp.float32).astype(jnp.bfloat16)
    w_in = w_gate_up[0]
    w_out = w_down[0]
    hidden = w_out.shape[0]
    outgoing = jnp.broadcast_to(
        packed.reshape(capacity, experts, 1, width), (capacity, experts, 2, width)
    )
    outgoing = outgoing.reshape(capacity, devices, width)
    block = lax.all_to_all(outgoing, "expert", split_axis=1, concat_axis=1, tiled=True)
    flat = block.reshape(-1, width)
    both = jnp.dot(flat, w_in, preferred_element_type=jnp.float32)
    active = (jax.nn.silu(both[:, :hidden]) * both[:, hidden:]).astype(jnp.bfloat16)
    result = jnp.dot(active, w_out, preferred_element_type=jnp.float32)
    partial_out = result.reshape(block.shape[0], block.shape[1], width).astype(jnp.bfloat16)
    returned = lax.all_to_all(partial_out, "expert", split_axis=1, concat_axis=1, tiled=True)
    returned = returned.reshape(capacity, experts, 2, width).astype(jnp.float32)
    expert_out = jnp.sum(returned, axis=2).astype(jnp.bfloat16).reshape(slot_total, width)
    pair_out = expert_out[place].astype(jnp.float32) * route_weights[0].reshape(-1)[:, None]
    layer_out = jnp.sum(pair_out.reshape(tok_count, top_count, width), axis=1).astype(jnp.bfloat16)
    return passed_along(layer_out, "section", 1)[None]


RING = (0, 1, 3, 2)
LANES = 128
TOKEN_LANE = 64


def on_ring(place):
    return place ^ (place >> 1)


def chip_at(chip, steps, flip):
    return (on_ring((on_ring(chip >> 1) + steps) & 3) << 1) | ((chip & 1) ^ flip)


def iota(shape, axis):
    return lax.broadcasted_iota(jnp.int32, shape, axis)


def ones_where(condition):
    return jnp.where(condition, 1.0, 0.0).astype(jnp.bfloat16)


def across(left, right):
    return lax.dot_general(left, right, (((0,), (0,)), ((), ())), preferred_element_type=jnp.float32)


def local_call(kernel, name, out_shape, in_specs, operands, scratch=(), limit=12, flops=0, moved=0):
    vmem = pl.BlockSpec(memory_space=pltpu.VMEM)
    return pl.pallas_call(
        kernel,
        out_shape=out_shape,
        in_specs=[vmem if spec is None else pl.BlockSpec(memory_space=spec) for spec in in_specs],
        out_specs=jax.tree.map(lambda _: vmem, out_shape),
        scratch_shapes=list(scratch),
        compiler_params=pltpu.CompilerParams(vmem_limit_bytes=limit << 20),
        cost_estimate=pl.CostEstimate(flops=flops, bytes_accessed=moved, transcendentals=0),
        name=name,
    )(*operands)


def prepare_kernel(ids_in, weights_in, rows_in, block, ids, weights, sems):
    tok_count, width = rows_in.shape
    top_count = ids.shape[0]
    experts = 2 * len(RING)
    copies = [
        pltpu.make_async_copy(ids_in, ids, sems.at[0]),
        pltpu.make_async_copy(weights_in, weights, sems.at[1]),
        pltpu.make_async_copy(rows_in, block.at[:, pl.ds(0, width)], sems.at[2]),
    ]
    for copy in copies:
        copy.start()
    square = (tok_count, tok_count)
    earlier = ones_where(iota(square, 0) < iota(square, 1))
    expert = iota((experts, tok_count), 0)
    unit = ones_where(iota((4 * experts, LANES), 0) == iota((4 * experts, LANES), 1))
    token = ones_where(iota((tok_count, LANES), 0) + TOKEN_LANE == iota((tok_count, LANES), 1))
    copies[0].wait()
    copies[1].wait()
    named = jnp.zeros((experts, tok_count), jnp.float32)
    scale = jnp.zeros((experts, tok_count), jnp.float32)
    for k in range(top_count):
        hit = ids[k : k + 1, :] == expert
        named = named + jnp.where(hit, 1.0, 0.0)
        scale = scale + jnp.where(hit, weights[k : k + 1, :], 0.0)
    rank = jnp.dot(named.astype(jnp.bfloat16), earlier, preferred_element_type=jnp.float32)
    notes = [jnp.where(named > 0.5, rank + 1.0, 0.0)]
    for _ in range(3):
        piece = scale.astype(jnp.bfloat16).astype(jnp.float32)
        scale = scale - piece
        notes.append(piece)
    notes = across(jnp.concatenate(notes, axis=0).astype(jnp.bfloat16), unit)
    block[:, width:] = notes.astype(jnp.bfloat16) + token
    copies[2].wait()


def prepare(ids, weights, tokens):
    tok_count, width = tokens.shape
    return local_call(
        prepare_kernel,
        "prepare",
        pltpu.VMEM((tok_count, width + LANES), jnp.bfloat16),
        [pl.ANY] * 3,
        tuple(pltpu.with_memory_space_constraint(x, pltpu.HBM) for x in (ids, weights, tokens)),
        [
            pltpu.VMEM(ids.shape, ids.dtype),
            pltpu.VMEM(weights.shape, weights.dtype),
            pltpu.SemaphoreType.DMA((3,)),
        ],
        limit=8,
    )


def choose_kernel(places, capacity, block, *refs):
    chip = lax.axis_index("expert") >> 1
    tok_count = block.shape[0]
    notes = block[:, -LANES:].astype(jnp.float32)
    lane = iota(notes.shape, 1)
    slot = iota((tok_count, len(places) * capacity), 1)
    code = jnp.zeros(slot.shape, jnp.float32)
    order = jnp.zeros(slot.shape, jnp.int32)
    for at, (steps, flip) in enumerate(places):
        wanted = chip_at(chip, steps, flip)
        column = jnp.sum(jnp.where(lane == wanted, notes, 0.0), axis=1, keepdims=True)
        code = jnp.where(slot >= at * capacity, column, code)
        order = jnp.where(slot >= at * capacity, slot + 1 - at * capacity, order)
    rows = across(ones_where(code == order.astype(jnp.float32)), block[...]).astype(jnp.bfloat16)
    for at in range(len(places)):
        refs[at][...] = rows[at * capacity : (at + 1) * capacity]


def choose(block, capacity, places):
    return local_call(
        functools.partial(choose_kernel, places, capacity),
        "choose",
        [jax.ShapeDtypeStruct((capacity, block.shape[1]), jnp.bfloat16) for _ in places],
        [None],
        (block,),
    )


def load_kernel(source, target, sem):
    copy = pltpu.make_async_copy(source, target, sem)
    copy.start()
    copy.wait()


def loaded(weights):
    return local_call(
        load_kernel,
        "loaded",
        pltpu.VMEM(weights.shape, weights.dtype),
        [pl.ANY],
        (weights,),
        [pltpu.SemaphoreType.DMA],
        limit=9,
        moved=2 * weights.size * weights.dtype.itemsize,
    )


def gated(both):
    hidden = both.shape[1] // 2
    gate = both[:, :hidden]
    return (gate / (1.0 + jnp.exp(-gate)) * both[:, hidden:]).astype(jnp.bfloat16)


def write_pieces(slots, total, outs):
    chip = lax.axis_index("expert") >> 1
    width = total.shape[1]
    experts = 2 * len(RING)
    notes = slots[:, width:].astype(jnp.float32)
    lane = iota(notes.shape, 1)
    mine = (lane >= experts) & (lane < 4 * experts) & ((lane & (experts - 1)) == chip)
    scale = jnp.sum(jnp.where(mine, notes, 0.0), axis=1, keepdims=True)
    start = 0
    for out in outs:
        stop = start + out.shape[0]
        out[:, :width] = (total[start:stop] * scale[start:stop]).astype(jnp.bfloat16)
        out[:, width:] = slots[start:stop, width:]
        start = stop


def near_kernel(*refs):
    pieces, (first, second, slots, total) = refs[:-4], refs[-4:]
    start = 0
    for piece in pieces:
        slots[start : start + piece.shape[0]] = piece[...]
        start += piece.shape[0]
    width = total.shape[1]
    both = jnp.dot(slots[:, :width], first[...], preferred_element_type=jnp.float32)
    total[...] = jnp.dot(gated(both), second[...], preferred_element_type=jnp.float32)


def near_pass(pieces, weights):
    count = sum(piece.shape[0] for piece in pieces)
    full = pieces[0].shape[1]
    return local_call(
        near_kernel,
        "near_pass",
        [
            jax.ShapeDtypeStruct((count, full), jnp.bfloat16),
            jax.ShapeDtypeStruct((count, full - LANES), jnp.float32),
        ],
        [None] * (len(pieces) + 2),
        (*pieces, *weights),
        moved=2 * sum(w.size for w in weights),
    )


def far_kernel(slots, before, first, second, *refs):
    outs, total = refs[:-1], refs[-1]
    width = total.shape[1]
    both = jnp.dot(slots[:, :width], first[...], preferred_element_type=jnp.float32)
    term = jnp.dot(gated(both), second[...], preferred_element_type=jnp.float32)
    total[...] = before[...] + term
    write_pieces(slots, total, outs)


def far_pass(slots, total, weights, capacity):
    count, full = slots.shape
    return local_call(
        far_kernel,
        "far_pass",
        [jax.ShapeDtypeStruct((capacity, full), jnp.bfloat16)] * (count // capacity),
        [None] * 4,
        (slots, total, *weights),
        [pltpu.VMEM(total.shape, jnp.float32)],
        limit=24,
        moved=2 * sum(w.size for w in weights),
    )


def combine_kernel(count, *refs):
    blocks, more, (out, slots) = refs[:count], refs[count:-2], refs[-2:]
    tok_count, width = out.shape
    start = 0
    for block in blocks:
        slots[start : start + block.shape[0]] = block[...]
        start += block.shape[0]
    token = slots[:, width:]
    part = width // 7
    for at in range(7):
        place = slice(at * part, (at + 1) * part)
        mixed = across(token, slots[:, place])[TOKEN_LANE : TOKEN_LANE + tok_count]
        for other in more:
            mixed = mixed + other[:, place].astype(jnp.float32)
        out[:, place] = mixed.astype(out.dtype)


def combine(blocks, tok_count, *more):
    capacity, full = blocks[0].shape
    return local_call(
        functools.partial(combine_kernel, len(blocks)),
        "combine",
        jax.ShapeDtypeStruct((tok_count, full - LANES), jnp.bfloat16),
        [None] * (len(blocks) + len(more)),
        (*blocks, *more),
        [pltpu.VMEM((capacity * len(blocks), full), jnp.bfloat16)],
    )


def sent(shard, sections, section_step, ring_step, flip):
    planes = len(RING)
    pairs = []
    for s in range(sections):
        for z in range(planes):
            for y in range(2):
                for core in range(2):
                    plane = RING[(RING.index(z) + ring_step) % planes]
                    target = (((s + section_step) % sections) * planes + plane) * 2 + (y ^ flip)
                    pairs.append((((s * planes + z) * 2 + y) * 2 + core, target * 2 + core))
    return lax.ppermute(shard, ("section", "expert"), pairs)


def after(value, other):
    return lax.optimization_barrier((value, other))[0]


def by_ring(rows, route_ids, route_weights, w_gate_up, w_down):
    sections = lax.axis_size("section")
    devices = lax.axis_size("expert")
    experts = devices // 2
    tokens = rows[0]
    tok_count = tokens.shape[0]
    top_count = route_ids.shape[2]
    capacity = max(2, 2 * tok_count * top_count // experts)
    swap = [(i, i ^ 1) for i in range(devices)]
    w_in, w_out = w_gate_up[0], w_down[0]
    far_out = lax.ppermute(w_out, "expert", swap)
    far_in = lax.ppermute(w_in, "expert", swap)
    block = prepare(route_ids[0].T, route_weights[0].T, tokens)
    block1 = sent(block, sections, 0, 1, 0)
    own0, other, back0, back1 = choose(block, capacity, ((0, 0), (0, 1), (3, 0), (3, 1)))
    other0 = sent(other, sections, 0, 0, 1)
    near = (loaded(after(w_in, own0)), loaded(after(w_out, own0)))
    block1 = after(block1, (near, other0))
    own1, other, on1, on0 = choose(block1, capacity, ((0, 0), (0, 1), (1, 1), (1, 0)))
    other1 = sent(other, sections, 0, 0, 1)
    other2 = sent(on1, sections, 0, 1, 1)
    own2 = sent(on0, sections, 0, 1, 0)
    other3 = sent(after(back1, (near, other0)), sections, 0, 3, 1)
    own3 = sent(after(back0, (other1, other3)), sections, 0, 3, 0)
    pieces = (own0, other0, own1, other2, own2, other1, own3, other3)
    places = ((0, 0), (0, 1), (1, 0), (2, 1), (2, 0), (1, 1), (3, 0), (3, 1))
    slots, total = near_pass(pieces, near)
    pieces = far_pass(slots, total, (far_in, far_out), capacity)
    piece = dict(zip(places, pieces))
    merged = [
        piece[3, 0],
        sent(piece[2, 0], sections, 0, 1, 0),
        sent(piece[2, 1], sections, 0, 1, 1),
        sent(piece[3, 1], sections, 0, 0, 1),
    ]
    straight = [sent(piece[0, flip], sections, 1, 0, flip) for flip in range(2)]
    merged, straight = lax.optimization_barrier((merged, straight))
    straight += [sent(piece[1, flip], sections, 1, -1, flip) for flip in range(2)]
    merged = sent(combine(merged, tok_count), sections, 1, 1, 0)
    return combine(straight, tok_count, merged)[None]


def per_device(rows, route_ids, route_weights, w_gate_up, w_down):
    experts = lax.axis_size("expert") // 2
    fits = experts == 2 * len(RING) and rows.shape[1] <= LANES - TOKEN_LANE
    plan = by_ring if fits else by_slots
    return plan(rows, route_ids, route_weights, w_gate_up, w_down)


def solution(mesh):
    in_specs = (
        P("section", "expert", None),
        P("section", "expert", None),
        P("section", "expert", None),
        P("section", None, "expert"),
        P("section", "expert", None),
    )
    out_specs = P("section", "expert", None)
    return jax.shard_map(
        per_device, mesh=mesh, in_specs=in_specs, out_specs=out_specs, check_vma=False
    )
```

```python
import functools

import jax
import jax.numpy as jnp
from jax import lax
from jax.experimental import pallas as pl
from jax.experimental.pallas import tpu as pltpu
from jax.sharding import PartitionSpec as P


def passed_along(shard, axis, by):
    length = lax.axis_size(axis)
    return lax.ppermute(shard, axis, [(i, (i + by) % length) for i in range(length)])


def by_slots(rows, route_ids, route_weights, w_gate_up, w_down):
    devices = lax.axis_size("expert")
    experts = devices // 2
    tokens = rows[0]
    tok_count, width = tokens.shape
    top_count = route_ids.shape[2]
    choices_flat = route_ids[0].reshape(-1)
    capacity = max(2, 2 * tok_count * top_count // experts)
    onehot = (choices_flat[:, None] == jnp.arange(experts, dtype=jnp.int32)[None, :]).astype(
        jnp.int32
    )
    before = jnp.cumsum(onehot, axis=0) - onehot
    slot = jnp.sum(before * onehot, axis=1)
    place = slot * experts + choices_flat
    slot_total = experts * capacity
    picker = (place[None, :] == jnp.arange(slot_total, dtype=jnp.int32)[:, None]).astype(
        jnp.bfloat16
    )
    token_pairs = jnp.repeat(tokens, top_count, axis=0)
    packed = jnp.dot(picker, token_pairs, preferred_element_type=jnp.float32).astype(jnp.bfloat16)
    w_in = w_gate_up[0]
    w_out = w_down[0]
    hidden = w_out.shape[0]
    outgoing = jnp.broadcast_to(
        packed.reshape(capacity, experts, 1, width), (capacity, experts, 2, width)
    )
    outgoing = outgoing.reshape(capacity, devices, width)
    block = lax.all_to_all(outgoing, "expert", split_axis=1, concat_axis=1, tiled=True)
    flat = block.reshape(-1, width)
    both = jnp.dot(flat, w_in, preferred_element_type=jnp.float32)
    active = (jax.nn.silu(both[:, :hidden]) * both[:, hidden:]).astype(jnp.bfloat16)
    result = jnp.dot(active, w_out, preferred_element_type=jnp.float32)
    partial_out = result.reshape(block.shape[0], block.shape[1], width).astype(jnp.bfloat16)
    returned = lax.all_to_all(partial_out, "expert", split_axis=1, concat_axis=1, tiled=True)
    returned = returned.reshape(capacity, experts, 2, width).astype(jnp.float32)
    expert_out = jnp.sum(returned, axis=2).astype(jnp.bfloat16).reshape(slot_total, width)
    pair_out = expert_out[place].astype(jnp.float32) * route_weights[0].reshape(-1)[:, None]
    layer_out = jnp.sum(pair_out.reshape(tok_count, top_count, width), axis=1).astype(jnp.bfloat16)
    return passed_along(layer_out, "section", 1)[None]


RING = (0, 1, 3, 2)
LANES = 128
TOKEN_LANE = 64


def on_ring(place):
    return place ^ (place >> 1)


def chip_at(chip, steps, flip):
    return (on_ring((on_ring(chip >> 1) + steps) & 3) << 1) | ((chip & 1) ^ flip)


def iota(shape, axis):
    return lax.broadcasted_iota(jnp.int32, shape, axis)


def ones_where(condition):
    return jnp.where(condition, 1.0, 0.0).astype(jnp.bfloat16)


def across(left, right):
    return lax.dot_general(left, right, (((0,), (0,)), ((), ())), preferred_element_type=jnp.float32)


def local_call(kernel, name, out_shape, in_specs, operands, scratch=(), limit=12, flops=0, moved=0):
    vmem = pl.BlockSpec(memory_space=pltpu.VMEM)
    return pl.pallas_call(
        kernel,
        out_shape=out_shape,
        in_specs=[vmem if spec is None else pl.BlockSpec(memory_space=spec) for spec in in_specs],
        out_specs=jax.tree.map(lambda _: vmem, out_shape),
        scratch_shapes=list(scratch),
        compiler_params=pltpu.CompilerParams(vmem_limit_bytes=limit << 20),
        cost_estimate=pl.CostEstimate(flops=flops, bytes_accessed=moved, transcendentals=0),
        name=name,
    )(*operands)


def prepare_kernel(ids_in, weights_in, out, ids, weights, sems):
    tok_count = out.shape[0]
    top_count = ids.shape[0]
    experts = 2 * len(RING)
    copies = [
        pltpu.make_async_copy(ids_in, ids, sems.at[0]),
        pltpu.make_async_copy(weights_in, weights, sems.at[1]),
    ]
    for copy in copies:
        copy.start()
    square = (tok_count, tok_count)
    earlier = ones_where(iota(square, 0) < iota(square, 1))
    expert = iota((experts, tok_count), 0)
    unit = ones_where(iota((4 * experts, LANES), 0) == iota((4 * experts, LANES), 1))
    token = ones_where(iota((tok_count, LANES), 0) + TOKEN_LANE == iota((tok_count, LANES), 1))
    copies[0].wait()
    copies[1].wait()
    named = jnp.zeros((experts, tok_count), jnp.float32)
    scale = jnp.zeros((experts, tok_count), jnp.float32)
    for k in range(top_count):
        hit = ids[k : k + 1, :] == expert
        named = named + jnp.where(hit, 1.0, 0.0)
        scale = scale + jnp.where(hit, weights[k : k + 1, :], 0.0)
    rank = jnp.dot(named.astype(jnp.bfloat16), earlier, preferred_element_type=jnp.float32)
    notes = [jnp.where(named > 0.5, rank + 1.0, 0.0)]
    for _ in range(3):
        piece = scale.astype(jnp.bfloat16).astype(jnp.float32)
        scale = scale - piece
        notes.append(piece)
    notes = across(jnp.concatenate(notes, axis=0).astype(jnp.bfloat16), unit)
    out[...] = notes.astype(jnp.bfloat16) + token


def prepare(ids, weights):
    tok_count = ids.shape[1]
    return local_call(
        prepare_kernel,
        "prepare",
        pltpu.VMEM((tok_count, LANES), jnp.bfloat16),
        [pl.ANY] * 2,
        tuple(pltpu.with_memory_space_constraint(x, pltpu.HBM) for x in (ids, weights)),
        [
            pltpu.VMEM(ids.shape, ids.dtype),
            pltpu.VMEM(weights.shape, weights.dtype),
            pltpu.SemaphoreType.DMA((2,)),
        ],
        limit=8,
    )


def choose_kernel(places, capacity, block, marks, *refs):
    chip = lax.axis_index("expert") >> 1
    tok_count = block.shape[0]
    notes = marks[...].astype(jnp.float32)
    width = block.shape[1]
    lane = iota(notes.shape, 1)
    slot = iota((tok_count, len(places) * capacity), 1)
    code = jnp.zeros(slot.shape, jnp.float32)
    order = jnp.zeros(slot.shape, jnp.int32)
    for at, (steps, flip) in enumerate(places):
        wanted = chip_at(chip, steps, flip)
        column = jnp.sum(jnp.where(lane == wanted, notes, 0.0), axis=1, keepdims=True)
        code = jnp.where(slot >= at * capacity, column, code)
        order = jnp.where(slot >= at * capacity, slot + 1 - at * capacity, order)
    pick = ones_where(code == order.astype(jnp.float32))
    rows = across(pick, block[...]).astype(jnp.bfloat16)
    marked = across(pick, marks[...]).astype(jnp.bfloat16)
    for at in range(len(places)):
        place = slice(at * capacity, (at + 1) * capacity)
        refs[at][:, :width] = rows[place]
        refs[at][:, width:] = marked[place]


def choose(block, marks, capacity, places):
    return local_call(
        functools.partial(choose_kernel, places, capacity),
        "choose",
        [jax.ShapeDtypeStruct((capacity, block.shape[1] + LANES), jnp.bfloat16) for _ in places],
        [None] * 2,
        (block, marks),
    )


def load_kernel(source, target, sem):
    copy = pltpu.make_async_copy(source, target, sem)
    copy.start()
    copy.wait()


def loaded(weights):
    return local_call(
        load_kernel,
        "loaded",
        pltpu.VMEM(weights.shape, weights.dtype),
        [pl.ANY],
        (weights,),
        [pltpu.SemaphoreType.DMA],
        limit=9,
        moved=2 * weights.size * weights.dtype.itemsize,
    )


def gated(both):
    hidden = both.shape[1] // 2
    gate = both[:, :hidden]
    return (gate / (1.0 + jnp.exp(-gate)) * both[:, hidden:]).astype(jnp.bfloat16)


def write_pieces(slots, total, outs):
    chip = lax.axis_index("expert") >> 1
    width = total.shape[1]
    experts = 2 * len(RING)
    notes = slots[:, width:].astype(jnp.float32)
    lane = iota(notes.shape, 1)
    mine = (lane >= experts) & (lane < 4 * experts) & ((lane & (experts - 1)) == chip)
    scale = jnp.sum(jnp.where(mine, notes, 0.0), axis=1, keepdims=True)
    start = 0
    for out in outs:
        stop = start + out.shape[0]
        out[:, :width] = (total[start:stop] * scale[start:stop]).astype(jnp.bfloat16)
        out[:, width:] = slots[start:stop, width:]
        start = stop


def near_kernel(*refs):
    pieces, (first, second, slots, total) = refs[:-4], refs[-4:]
    start = 0
    for piece in pieces:
        slots[start : start + piece.shape[0]] = piece[...]
        start += piece.shape[0]
    width = total.shape[1]
    both = jnp.dot(slots[:, :width], first[...], preferred_element_type=jnp.float32)
    total[...] = jnp.dot(gated(both), second[...], preferred_element_type=jnp.float32)


def near_pass(pieces, weights):
    count = sum(piece.shape[0] for piece in pieces)
    full = pieces[0].shape[1]
    return local_call(
        near_kernel,
        "near_pass",
        [
            jax.ShapeDtypeStruct((count, full), jnp.bfloat16),
            jax.ShapeDtypeStruct((count, full - LANES), jnp.float32),
        ],
        [None] * (len(pieces) + 2),
        (*pieces, *weights),
        moved=2 * sum(w.size for w in weights),
    )


def far_kernel(slots, before, first, second, *refs):
    outs, total = refs[:-1], refs[-1]
    width = total.shape[1]
    both = jnp.dot(slots[:, :width], first[...], preferred_element_type=jnp.float32)
    term = jnp.dot(gated(both), second[...], preferred_element_type=jnp.float32)
    total[...] = before[...] + term
    write_pieces(slots, total, outs)


def far_pass(slots, total, weights, capacity):
    count, full = slots.shape
    return local_call(
        far_kernel,
        "far_pass",
        [jax.ShapeDtypeStruct((capacity, full), jnp.bfloat16)] * (count // capacity),
        [None] * 4,
        (slots, total, *weights),
        [pltpu.VMEM(total.shape, jnp.float32)],
        limit=24,
        moved=2 * sum(w.size for w in weights),
    )


def combine_kernel(count, *refs):
    blocks, more, (out, slots) = refs[:count], refs[count:-2], refs[-2:]
    tok_count, width = out.shape
    start = 0
    for block in blocks:
        slots[start : start + block.shape[0]] = block[...]
        start += block.shape[0]
    token = slots[:, width:]
    part = width // 7
    for at in range(7):
        place = slice(at * part, (at + 1) * part)
        mixed = across(token, slots[:, place])[TOKEN_LANE : TOKEN_LANE + tok_count]
        for other in more:
            mixed = mixed + other[:, place].astype(jnp.float32)
        out[:, place] = mixed.astype(out.dtype)


def combine(blocks, tok_count, *more):
    capacity, full = blocks[0].shape
    return local_call(
        functools.partial(combine_kernel, len(blocks)),
        "combine",
        jax.ShapeDtypeStruct((tok_count, full - LANES), jnp.bfloat16),
        [None] * (len(blocks) + len(more)),
        (*blocks, *more),
        [pltpu.VMEM((capacity * len(blocks), full), jnp.bfloat16)],
    )


def sent(shard, sections, section_step, ring_step, flip):
    planes = len(RING)
    pairs = []
    for s in range(sections):
        for z in range(planes):
            for y in range(2):
                for core in range(2):
                    plane = RING[(RING.index(z) + ring_step) % planes]
                    target = (((s + section_step) % sections) * planes + plane) * 2 + (y ^ flip)
                    pairs.append((((s * planes + z) * 2 + y) * 2 + core, target * 2 + core))
    return lax.ppermute(shard, ("section", "expert"), pairs)


def after(value, other):
    return lax.optimization_barrier((value, other))[0]


def by_ring(rows, route_ids, route_weights, w_gate_up, w_down):
    sections = lax.axis_size("section")
    devices = lax.axis_size("expert")
    experts = devices // 2
    tokens = rows[0]
    tok_count = tokens.shape[0]
    top_count = route_ids.shape[2]
    capacity = max(2, 2 * tok_count * top_count // experts)
    swap = [(i, i ^ 1) for i in range(devices)]
    w_in, w_out = w_gate_up[0], w_down[0]
    far_out = lax.ppermute(w_out, "expert", swap)
    far_in = lax.ppermute(w_in, "expert", swap)
    block1 = sent(tokens, sections, 0, 1, 0)
    marks = prepare(route_ids[0].T, route_weights[0].T)
    marks1 = sent(marks, sections, 0, 1, 0)
    own0, other, back0, back1 = choose(tokens, marks, capacity, ((0, 0), (0, 1), (3, 0), (3, 1)))
    other0 = sent(other, sections, 0, 0, 1)
    near = (loaded(after(w_in, own0)), loaded(after(w_out, own0)))
    block1 = after(block1, (near, other0))
    own1, other, on0, on1 = choose(block1, marks1, capacity, ((0, 0), (0, 1), (1, 0), (1, 1)))
    other1 = sent(other, sections, 0, 0, 1)
    own2 = sent(on0, sections, 0, 1, 0)
    other2 = sent(on1, sections, 0, 1, 1)
    other3 = sent(after(back1, (near, other0)), sections, 0, 3, 1)
    own3 = sent(after(back0, (other1, other3)), sections, 0, 3, 0)
    pieces = (own0, other0, own1, own2, other2, other1, own3, other3)
    places = ((0, 0), (0, 1), (1, 0), (2, 0), (2, 1), (1, 1), (3, 0), (3, 1))
    slots, total = near_pass(pieces, near)
    pieces = far_pass(slots, total, (far_in, far_out), capacity)
    piece = dict(zip(places, pieces))
    first = [
        sent(piece[2, 1], sections, 0, 1, 1),
        sent(piece[3, 1], sections, 0, 0, 1),
        sent(piece[0, 0], sections, 1, 0, 0),
        sent(piece[0, 1], sections, 1, 0, 1),
        sent(piece[2, 0], sections, 0, 1, 0),
    ]
    two, three, *straight, four = lax.optimization_barrier(first)
    merged = [piece[3, 0], two, three, four]
    straight += [sent(piece[1, flip], sections, 1, -1, flip) for flip in range(2)]
    merged = sent(combine(merged, tok_count), sections, 1, 1, 0)
    return combine(straight, tok_count, merged)[None]


def per_device(rows, route_ids, route_weights, w_gate_up, w_down):
    experts = lax.axis_size("expert") // 2
    fits = experts == 2 * len(RING) and rows.shape[1] <= LANES - TOKEN_LANE
    plan = by_ring if fits else by_slots
    return plan(rows, route_ids, route_weights, w_gate_up, w_down)


def solution(mesh):
    in_specs = (
        P("section", "expert", None),
        P("section", "expert", None),
        P("section", "expert", None),
        P("section", None, "expert"),
        P("section", "expert", None),
    )
    out_specs = P("section", "expert", None)
    return jax.shard_map(
        per_device, mesh=mesh, in_specs=in_specs, out_specs=out_specs, check_vma=False
    )
```

```python
import functools

import jax
import jax.numpy as jnp
from jax import lax
from jax.experimental import pallas as pl
from jax.experimental.pallas import tpu as pltpu
from jax.sharding import PartitionSpec as P


def passed_along(shard, axis, by):
    length = lax.axis_size(axis)
    return lax.ppermute(shard, axis, [(i, (i + by) % length) for i in range(length)])


def by_slots(rows, route_ids, route_weights, w_gate_up, w_down):
    devices = lax.axis_size("expert")
    experts = devices // 2
    tokens = rows[0]
    tok_count, width = tokens.shape
    top_count = route_ids.shape[2]
    choices_flat = route_ids[0].reshape(-1)
    capacity = max(2, 2 * tok_count * top_count // experts)
    onehot = (choices_flat[:, None] == jnp.arange(experts, dtype=jnp.int32)[None, :]).astype(
        jnp.int32
    )
    before = jnp.cumsum(onehot, axis=0) - onehot
    slot = jnp.sum(before * onehot, axis=1)
    place = slot * experts + choices_flat
    slot_total = experts * capacity
    picker = (place[None, :] == jnp.arange(slot_total, dtype=jnp.int32)[:, None]).astype(
        jnp.bfloat16
    )
    token_pairs = jnp.repeat(tokens, top_count, axis=0)
    packed = jnp.dot(picker, token_pairs, preferred_element_type=jnp.float32).astype(jnp.bfloat16)
    w_in = w_gate_up[0]
    w_out = w_down[0]
    hidden = w_out.shape[0]
    outgoing = jnp.broadcast_to(
        packed.reshape(capacity, experts, 1, width), (capacity, experts, 2, width)
    )
    outgoing = outgoing.reshape(capacity, devices, width)
    block = lax.all_to_all(outgoing, "expert", split_axis=1, concat_axis=1, tiled=True)
    flat = block.reshape(-1, width)
    both = jnp.dot(flat, w_in, preferred_element_type=jnp.float32)
    active = (jax.nn.silu(both[:, :hidden]) * both[:, hidden:]).astype(jnp.bfloat16)
    result = jnp.dot(active, w_out, preferred_element_type=jnp.float32)
    partial_out = result.reshape(block.shape[0], block.shape[1], width).astype(jnp.bfloat16)
    returned = lax.all_to_all(partial_out, "expert", split_axis=1, concat_axis=1, tiled=True)
    returned = returned.reshape(capacity, experts, 2, width).astype(jnp.float32)
    expert_out = jnp.sum(returned, axis=2).astype(jnp.bfloat16).reshape(slot_total, width)
    pair_out = expert_out[place].astype(jnp.float32) * route_weights[0].reshape(-1)[:, None]
    layer_out = jnp.sum(pair_out.reshape(tok_count, top_count, width), axis=1).astype(jnp.bfloat16)
    return passed_along(layer_out, "section", 1)[None]


RING = (0, 1, 3, 2)
LANES = 128
TOKEN_LANE = 64


def on_ring(place):
    return place ^ (place >> 1)


def chip_at(chip, steps, flip):
    return (on_ring((on_ring(chip >> 1) + steps) & 3) << 1) | ((chip & 1) ^ flip)


def iota(shape, axis):
    return lax.broadcasted_iota(jnp.int32, shape, axis)


def ones_where(condition):
    return jnp.where(condition, 1.0, 0.0).astype(jnp.bfloat16)


def across(left, right):
    return lax.dot_general(left, right, (((0,), (0,)), ((), ())), preferred_element_type=jnp.float32)


def local_call(kernel, name, out_shape, in_specs, operands, scratch=(), limit=12, flops=0, moved=0):
    vmem = pl.BlockSpec(memory_space=pltpu.VMEM)
    return pl.pallas_call(
        kernel,
        out_shape=out_shape,
        in_specs=[vmem if spec is None else pl.BlockSpec(memory_space=spec) for spec in in_specs],
        out_specs=jax.tree.map(lambda _: vmem, out_shape),
        scratch_shapes=list(scratch),
        compiler_params=pltpu.CompilerParams(vmem_limit_bytes=limit << 20),
        cost_estimate=pl.CostEstimate(flops=flops, bytes_accessed=moved, transcendentals=0),
        name=name,
    )(*operands)


def prepare_kernel(ids_in, weights_in, out, ids, weights, sems):
    tok_count = out.shape[0]
    top_count = ids.shape[0]
    experts = 2 * len(RING)
    copies = [
        pltpu.make_async_copy(ids_in, ids, sems.at[0]),
        pltpu.make_async_copy(weights_in, weights, sems.at[1]),
    ]
    for copy in copies:
        copy.start()
    square = (tok_count, tok_count)
    earlier = ones_where(iota(square, 0) < iota(square, 1))
    expert = iota((experts, tok_count), 0)
    unit = ones_where(iota((4 * experts, LANES), 0) == iota((4 * experts, LANES), 1))
    token = ones_where(iota((tok_count, LANES), 0) + TOKEN_LANE == iota((tok_count, LANES), 1))
    copies[0].wait()
    copies[1].wait()
    named = jnp.zeros((experts, tok_count), jnp.float32)
    scale = jnp.zeros((experts, tok_count), jnp.float32)
    for k in range(top_count):
        hit = ids[k : k + 1, :] == expert
        named = named + jnp.where(hit, 1.0, 0.0)
        scale = scale + jnp.where(hit, weights[k : k + 1, :], 0.0)
    rank = jnp.dot(named.astype(jnp.bfloat16), earlier, preferred_element_type=jnp.float32)
    notes = [jnp.where(named > 0.5, rank + 1.0, 0.0)]
    for _ in range(3):
        piece = scale.astype(jnp.bfloat16).astype(jnp.float32)
        scale = scale - piece
        notes.append(piece)
    notes = across(jnp.concatenate(notes, axis=0).astype(jnp.bfloat16), unit)
    out[...] = notes.astype(jnp.bfloat16) + token


def prepare(ids, weights):
    tok_count = ids.shape[1]
    return local_call(
        prepare_kernel,
        "prepare",
        pltpu.VMEM((tok_count, LANES), jnp.bfloat16),
        [pl.ANY] * 2,
        tuple(pltpu.with_memory_space_constraint(x, pltpu.HBM) for x in (ids, weights)),
        [
            pltpu.VMEM(ids.shape, ids.dtype),
            pltpu.VMEM(weights.shape, weights.dtype),
            pltpu.SemaphoreType.DMA((2,)),
        ],
        limit=8,
    )


def choose_kernel(places, capacity, block, marks, *refs):
    chip = lax.axis_index("expert") >> 1
    tok_count = block.shape[0]
    notes = marks[...].astype(jnp.float32)
    width = block.shape[1]
    lane = iota(notes.shape, 1)
    slot = iota((tok_count, len(places) * capacity), 1)
    code = jnp.zeros(slot.shape, jnp.float32)
    order = jnp.zeros(slot.shape, jnp.int32)
    for at, (steps, flip) in enumerate(places):
        wanted = chip_at(chip, steps, flip)
        column = jnp.sum(jnp.where(lane == wanted, notes, 0.0), axis=1, keepdims=True)
        code = jnp.where(slot >= at * capacity, column, code)
        order = jnp.where(slot >= at * capacity, slot + 1 - at * capacity, order)
    pick = ones_where(code == order.astype(jnp.float32))
    rows = across(pick, block[...]).astype(jnp.bfloat16)
    marked = across(pick, marks[...]).astype(jnp.bfloat16)
    for at in range(len(places)):
        place = slice(at * capacity, (at + 1) * capacity)
        refs[at][:, :width] = rows[place]
        refs[at][:, width:] = marked[place]


def choose(block, marks, capacity, places):
    return local_call(
        functools.partial(choose_kernel, places, capacity),
        "choose",
        [jax.ShapeDtypeStruct((capacity, block.shape[1] + LANES), jnp.bfloat16) for _ in places],
        [None] * 2,
        (block, marks),
    )


def load_kernel(source, target, sem):
    copy = pltpu.make_async_copy(source, target, sem)
    copy.start()
    copy.wait()


def loaded(weights):
    return local_call(
        load_kernel,
        "loaded",
        pltpu.VMEM(weights.shape, weights.dtype),
        [pl.ANY],
        (weights,),
        [pltpu.SemaphoreType.DMA],
        limit=9,
        moved=2 * weights.size * weights.dtype.itemsize,
    )


def gated(both):
    hidden = both.shape[1] // 2
    gate = both[:, :hidden]
    return (gate / (1.0 + jnp.exp(-gate)) * both[:, hidden:]).astype(jnp.bfloat16)


def write_pieces(slots, total, outs):
    chip = lax.axis_index("expert") >> 1
    width = total.shape[1]
    experts = 2 * len(RING)
    notes = slots[:, width:].astype(jnp.float32)
    lane = iota(notes.shape, 1)
    mine = (lane >= experts) & (lane < 4 * experts) & ((lane & (experts - 1)) == chip)
    scale = jnp.sum(jnp.where(mine, notes, 0.0), axis=1, keepdims=True)
    start = 0
    for out in outs:
        stop = start + out.shape[0]
        out[:, :width] = (total[start:stop] * scale[start:stop]).astype(jnp.bfloat16)
        out[:, width:] = slots[start:stop, width:]
        start = stop


def near_kernel(*refs):
    pieces, (first, second, slots, total) = refs[:-4], refs[-4:]
    start = 0
    for piece in pieces:
        slots[start : start + piece.shape[0]] = piece[...]
        start += piece.shape[0]
    width = total.shape[1]
    both = jnp.dot(slots[:, :width], first[...], preferred_element_type=jnp.float32)
    total[...] = jnp.dot(gated(both), second[...], preferred_element_type=jnp.float32)


def near_pass(pieces, weights):
    count = sum(piece.shape[0] for piece in pieces)
    full = pieces[0].shape[1]
    return local_call(
        near_kernel,
        "near_pass",
        [
            jax.ShapeDtypeStruct((count, full), jnp.bfloat16),
            jax.ShapeDtypeStruct((count, full - LANES), jnp.float32),
        ],
        [None] * (len(pieces) + 2),
        (*pieces, *weights),
        moved=2 * sum(w.size for w in weights),
    )


def far_kernel(slots, before, first, second, *refs):
    outs, total = refs[:-1], refs[-1]
    width = total.shape[1]
    both = jnp.dot(slots[:, :width], first[...], preferred_element_type=jnp.float32)
    term = jnp.dot(gated(both), second[...], preferred_element_type=jnp.float32)
    total[...] = before[...] + term
    write_pieces(slots, total, outs)


def far_pass(slots, total, weights, capacity):
    count, full = slots.shape
    return local_call(
        far_kernel,
        "far_pass",
        [jax.ShapeDtypeStruct((capacity, full), jnp.bfloat16)] * (count // capacity),
        [None] * 4,
        (slots, total, *weights),
        [pltpu.VMEM(total.shape, jnp.float32)],
        limit=24,
        moved=2 * sum(w.size for w in weights),
    )


def combine_kernel(count, *refs):
    blocks, more, (out, slots) = refs[:count], refs[count:-2], refs[-2:]
    tok_count, width = out.shape
    start = 0
    for block in blocks:
        slots[start : start + block.shape[0]] = block[...]
        start += block.shape[0]
    token = slots[:, width:]
    part = width // 7
    for at in range(7):
        place = slice(at * part, (at + 1) * part)
        mixed = across(token, slots[:, place])[TOKEN_LANE : TOKEN_LANE + tok_count]
        for other in more:
            mixed = mixed + other[:, place].astype(jnp.float32)
        out[:, place] = mixed.astype(out.dtype)


def combine(blocks, tok_count, *more):
    capacity, full = blocks[0].shape
    return local_call(
        functools.partial(combine_kernel, len(blocks)),
        "combine",
        jax.ShapeDtypeStruct((tok_count, full - LANES), jnp.bfloat16),
        [None] * (len(blocks) + len(more)),
        (*blocks, *more),
        [pltpu.VMEM((capacity * len(blocks), full), jnp.bfloat16)],
    )


def sent(shard, sections, section_step, ring_step, flip):
    planes = len(RING)
    pairs = []
    for s in range(sections):
        for z in range(planes):
            for y in range(2):
                for core in range(2):
                    plane = RING[(RING.index(z) + ring_step) % planes]
                    target = (((s + section_step) % sections) * planes + plane) * 2 + (y ^ flip)
                    pairs.append((((s * planes + z) * 2 + y) * 2 + core, target * 2 + core))
    return lax.ppermute(shard, ("section", "expert"), pairs)


def after(value, other):
    return lax.optimization_barrier((value, other))[0]


def by_ring(rows, route_ids, route_weights, w_gate_up, w_down):
    sections = lax.axis_size("section")
    devices = lax.axis_size("expert")
    experts = devices // 2
    tokens = rows[0]
    tok_count = tokens.shape[0]
    top_count = route_ids.shape[2]
    capacity = max(2, 2 * tok_count * top_count // experts)
    swap = [(i, i ^ 1) for i in range(devices)]
    w_in, w_out = w_gate_up[0], w_down[0]
    far_out = lax.ppermute(w_out, "expert", swap)
    far_in = lax.ppermute(w_in, "expert", swap)
    block1 = sent(tokens, sections, 0, 1, 0)
    marks = prepare(route_ids[0].T, route_weights[0].T)
    marks1 = sent(marks, sections, 0, 1, 0)
    own0, other, back0, back1 = choose(tokens, marks, capacity, ((0, 0), (0, 1), (3, 0), (3, 1)))
    other0 = sent(other, sections, 0, 0, 1)
    block1 = after(block1, other0)
    own1, other, on0, on1 = choose(block1, marks1, capacity, ((0, 0), (0, 1), (1, 0), (1, 1)))
    other1 = sent(other, sections, 0, 0, 1)
    own2 = sent(on0, sections, 0, 1, 0)
    other2 = sent(on1, sections, 0, 1, 1)
    other3 = sent(after(back1, other0), sections, 0, 3, 1)
    back0 = after(back0, (other1, other3))
    own3 = sent(back0, sections, 0, 3, 0)
    near = (loaded(after(w_in, back0)), loaded(after(w_out, back0)))
    pieces = (own0, other0, own1, own2, other2, other1, own3, other3)
    places = ((0, 0), (0, 1), (1, 0), (2, 0), (2, 1), (1, 1), (3, 0), (3, 1))
    slots, total = near_pass(pieces, near)
    pieces = far_pass(slots, total, (far_in, far_out), capacity)
    piece = dict(zip(places, pieces))
    first = [
        sent(piece[2, 1], sections, 0, 1, 1),
        sent(piece[3, 1], sections, 0, 0, 1),
        sent(piece[0, 0], sections, 1, 0, 0),
        sent(piece[0, 1], sections, 1, 0, 1),
        sent(piece[2, 0], sections, 0, 1, 0),
    ]
    two, three, *straight, four = lax.optimization_barrier(first)
    merged = [piece[3, 0], two, three, four]
    straight += [sent(piece[1, flip], sections, 1, -1, flip) for flip in range(2)]
    merged = sent(combine(merged, tok_count), sections, 1, 1, 0)
    return combine(straight, tok_count, merged)[None]


def per_device(rows, route_ids, route_weights, w_gate_up, w_down):
    experts = lax.axis_size("expert") // 2
    fits = experts == 2 * len(RING) and rows.shape[1] <= LANES - TOKEN_LANE
    plan = by_ring if fits else by_slots
    return plan(rows, route_ids, route_weights, w_gate_up, w_down)


def solution(mesh):
    in_specs = (
        P("section", "expert", None),
        P("section", "expert", None),
        P("section", "expert", None),
        P("section", None, "expert"),
        P("section", "expert", None),
    )
    out_specs = P("section", "expert", None)
    return jax.shard_map(
        per_device, mesh=mesh, in_specs=in_specs, out_specs=out_specs, check_vma=False
    )
```

```python
import functools

import jax
import jax.numpy as jnp
from jax import lax
from jax.experimental import pallas as pl
from jax.experimental.pallas import tpu as pltpu
from jax.sharding import PartitionSpec as P


def passed_along(shard, axis, by):
    length = lax.axis_size(axis)
    return lax.ppermute(shard, axis, [(i, (i + by) % length) for i in range(length)])


def by_slots(rows, route_ids, route_weights, w_gate_up, w_down):
    devices = lax.axis_size("expert")
    experts = devices // 2
    tokens = rows[0]
    tok_count, width = tokens.shape
    top_count = route_ids.shape[2]
    choices_flat = route_ids[0].reshape(-1)
    capacity = max(2, 2 * tok_count * top_count // experts)
    onehot = (choices_flat[:, None] == jnp.arange(experts, dtype=jnp.int32)[None, :]).astype(
        jnp.int32
    )
    before = jnp.cumsum(onehot, axis=0) - onehot
    slot = jnp.sum(before * onehot, axis=1)
    place = slot * experts + choices_flat
    slot_total = experts * capacity
    picker = (place[None, :] == jnp.arange(slot_total, dtype=jnp.int32)[:, None]).astype(
        jnp.bfloat16
    )
    token_pairs = jnp.repeat(tokens, top_count, axis=0)
    packed = jnp.dot(picker, token_pairs, preferred_element_type=jnp.float32).astype(jnp.bfloat16)
    w_in = w_gate_up[0]
    w_out = w_down[0]
    hidden = w_out.shape[0]
    outgoing = jnp.broadcast_to(
        packed.reshape(capacity, experts, 1, width), (capacity, experts, 2, width)
    )
    outgoing = outgoing.reshape(capacity, devices, width)
    block = lax.all_to_all(outgoing, "expert", split_axis=1, concat_axis=1, tiled=True)
    flat = block.reshape(-1, width)
    both = jnp.dot(flat, w_in, preferred_element_type=jnp.float32)
    active = (jax.nn.silu(both[:, :hidden]) * both[:, hidden:]).astype(jnp.bfloat16)
    result = jnp.dot(active, w_out, preferred_element_type=jnp.float32)
    partial_out = result.reshape(block.shape[0], block.shape[1], width).astype(jnp.bfloat16)
    returned = lax.all_to_all(partial_out, "expert", split_axis=1, concat_axis=1, tiled=True)
    returned = returned.reshape(capacity, experts, 2, width).astype(jnp.float32)
    expert_out = jnp.sum(returned, axis=2).astype(jnp.bfloat16).reshape(slot_total, width)
    pair_out = expert_out[place].astype(jnp.float32) * route_weights[0].reshape(-1)[:, None]
    layer_out = jnp.sum(pair_out.reshape(tok_count, top_count, width), axis=1).astype(jnp.bfloat16)
    return passed_along(layer_out, "section", 1)[None]


RING = (0, 1, 3, 2)
LANES = 128
TOKEN_LANE = 64


def on_ring(place):
    return place ^ (place >> 1)


def chip_at(chip, steps, flip):
    return (on_ring((on_ring(chip >> 1) + steps) & 3) << 1) | ((chip & 1) ^ flip)


def iota(shape, axis):
    return lax.broadcasted_iota(jnp.int32, shape, axis)


def ones_where(condition):
    return jnp.where(condition, 1.0, 0.0).astype(jnp.bfloat16)


def across(left, right):
    return lax.dot_general(left, right, (((0,), (0,)), ((), ())), preferred_element_type=jnp.float32)


def local_call(kernel, name, out_shape, in_specs, operands, scratch=(), limit=12, flops=0, moved=0):
    vmem = pl.BlockSpec(memory_space=pltpu.VMEM)
    return pl.pallas_call(
        kernel,
        out_shape=out_shape,
        in_specs=[vmem if spec is None else pl.BlockSpec(memory_space=spec) for spec in in_specs],
        out_specs=jax.tree.map(lambda _: vmem, out_shape),
        scratch_shapes=list(scratch),
        compiler_params=pltpu.CompilerParams(vmem_limit_bytes=limit << 20),
        cost_estimate=pl.CostEstimate(flops=flops, bytes_accessed=moved, transcendentals=0),
        name=name,
    )(*operands)


def prepare_kernel(ids_in, weights_in, out, ids, weights, sems):
    tok_count = out.shape[0]
    top_count = ids.shape[0]
    experts = 2 * len(RING)
    copies = [
        pltpu.make_async_copy(ids_in, ids, sems.at[0]),
        pltpu.make_async_copy(weights_in, weights, sems.at[1]),
    ]
    for copy in copies:
        copy.start()
    square = (tok_count, tok_count)
    earlier = ones_where(iota(square, 0) < iota(square, 1))
    expert = iota((experts, tok_count), 0)
    unit = ones_where(iota((4 * experts, LANES), 0) == iota((4 * experts, LANES), 1))
    token = ones_where(iota((tok_count, LANES), 0) + TOKEN_LANE == iota((tok_count, LANES), 1))
    copies[0].wait()
    copies[1].wait()
    named = jnp.zeros((experts, tok_count), jnp.float32)
    scale = jnp.zeros((experts, tok_count), jnp.float32)
    for k in range(top_count):
        hit = ids[k : k + 1, :] == expert
        named = named + jnp.where(hit, 1.0, 0.0)
        scale = scale + jnp.where(hit, weights[k : k + 1, :], 0.0)
    rank = jnp.dot(named.astype(jnp.bfloat16), earlier, preferred_element_type=jnp.float32)
    notes = [jnp.where(named > 0.5, rank + 1.0, 0.0)]
    for _ in range(3):
        piece = scale.astype(jnp.bfloat16).astype(jnp.float32)
        scale = scale - piece
        notes.append(piece)
    notes = across(jnp.concatenate(notes, axis=0).astype(jnp.bfloat16), unit)
    out[...] = notes.astype(jnp.bfloat16) + token


def prepare(ids, weights):
    tok_count = ids.shape[1]
    return local_call(
        prepare_kernel,
        "prepare",
        pltpu.VMEM((tok_count, LANES), jnp.bfloat16),
        [pl.ANY] * 2,
        tuple(pltpu.with_memory_space_constraint(x, pltpu.HBM) for x in (ids, weights)),
        [
            pltpu.VMEM(ids.shape, ids.dtype),
            pltpu.VMEM(weights.shape, weights.dtype),
            pltpu.SemaphoreType.DMA((2,)),
        ],
        limit=8,
    )


def choose_kernel(places, capacity, block, marks, *refs):
    chip = lax.axis_index("expert") >> 1
    tok_count = block.shape[0]
    notes = marks[...].astype(jnp.float32)
    width = block.shape[1]
    lane = iota(notes.shape, 1)
    slot = iota((tok_count, len(places) * capacity), 1)
    code = jnp.zeros(slot.shape, jnp.float32)
    order = jnp.zeros(slot.shape, jnp.int32)
    for at, (steps, flip) in enumerate(places):
        wanted = chip_at(chip, steps, flip)
        column = jnp.sum(jnp.where(lane == wanted, notes, 0.0), axis=1, keepdims=True)
        code = jnp.where(slot >= at * capacity, column, code)
        order = jnp.where(slot >= at * capacity, slot + 1 - at * capacity, order)
    pick = ones_where(code == order.astype(jnp.float32))
    rows = across(pick, block[...]).astype(jnp.bfloat16)
    marked = across(pick, marks[...]).astype(jnp.bfloat16)
    for at in range(len(places)):
        place = slice(at * capacity, (at + 1) * capacity)
        refs[at][:, :width] = rows[place]
        refs[at][:, width:] = marked[place]


def choose(block, marks, capacity, places):
    return local_call(
        functools.partial(choose_kernel, places, capacity),
        "choose",
        [jax.ShapeDtypeStruct((capacity, block.shape[1] + LANES), jnp.bfloat16) for _ in places],
        [None] * 2,
        (block, marks),
    )


def load_kernel(source, target, sem):
    copy = pltpu.make_async_copy(source, target, sem)
    copy.start()
    copy.wait()


def loaded(weights):
    return local_call(
        load_kernel,
        "loaded",
        pltpu.VMEM(weights.shape, weights.dtype),
        [pl.ANY],
        (weights,),
        [pltpu.SemaphoreType.DMA],
        limit=9,
        moved=2 * weights.size * weights.dtype.itemsize,
    )


def gated(both):
    hidden = both.shape[1] // 2
    gate = both[:, :hidden]
    return (gate / (1.0 + jnp.exp(-gate)) * both[:, hidden:]).astype(jnp.bfloat16)


def write_pieces(slots, total, outs):
    chip = lax.axis_index("expert") >> 1
    width = total.shape[1]
    experts = 2 * len(RING)
    notes = slots[:, width:].astype(jnp.float32)
    lane = iota(notes.shape, 1)
    mine = (lane >= experts) & (lane < 4 * experts) & ((lane & (experts - 1)) == chip)
    scale = jnp.sum(jnp.where(mine, notes, 0.0), axis=1, keepdims=True)
    start = 0
    for out in outs:
        stop = start + out.shape[0]
        out[:, :width] = (total[start:stop] * scale[start:stop]).astype(jnp.bfloat16)
        out[:, width:] = slots[start:stop, width:]
        start = stop


def near_kernel(*refs):
    pieces, (first, second, slots, total) = refs[:-4], refs[-4:]
    start = 0
    for piece in pieces:
        slots[start : start + piece.shape[0]] = piece[...]
        start += piece.shape[0]
    width = total.shape[1]
    both = jnp.dot(slots[:, :width], first[...], preferred_element_type=jnp.float32)
    total[...] = jnp.dot(gated(both), second[...], preferred_element_type=jnp.float32)


def near_pass(pieces, weights):
    count = sum(piece.shape[0] for piece in pieces)
    full = pieces[0].shape[1]
    return local_call(
        near_kernel,
        "near_pass",
        [
            jax.ShapeDtypeStruct((count, full), jnp.bfloat16),
            jax.ShapeDtypeStruct((count, full - LANES), jnp.float32),
        ],
        [None] * (len(pieces) + 2),
        (*pieces, *weights),
        moved=2 * sum(w.size for w in weights),
    )


def far_kernel(slots, before, first, second, *refs):
    outs, total = refs[:-1], refs[-1]
    width = total.shape[1]
    both = jnp.dot(slots[:, :width], first[...], preferred_element_type=jnp.float32)
    term = jnp.dot(gated(both), second[...], preferred_element_type=jnp.float32)
    total[...] = before[...] + term
    write_pieces(slots, total, outs)


def far_pass(slots, total, weights, capacity):
    count, full = slots.shape
    return local_call(
        far_kernel,
        "far_pass",
        [jax.ShapeDtypeStruct((capacity, full), jnp.bfloat16)] * (count // capacity),
        [None] * 4,
        (slots, total, *weights),
        [pltpu.VMEM(total.shape, jnp.float32)],
        limit=24,
        moved=2 * sum(w.size for w in weights),
    )


def combine_kernel(count, *refs):
    blocks, more, (out, slots) = refs[:count], refs[count:-2], refs[-2:]
    tok_count, width = out.shape
    start = 0
    for block in blocks:
        slots[start : start + block.shape[0]] = block[...]
        start += block.shape[0]
    token = slots[:, width:]
    part = width // 7
    for at in range(7):
        place = slice(at * part, (at + 1) * part)
        mixed = across(token, slots[:, place])[TOKEN_LANE : TOKEN_LANE + tok_count]
        for other in more:
            mixed = mixed + other[:, place].astype(jnp.float32)
        out[:, place] = mixed.astype(out.dtype)


def combine(blocks, tok_count, *more):
    capacity, full = blocks[0].shape
    return local_call(
        functools.partial(combine_kernel, len(blocks)),
        "combine",
        jax.ShapeDtypeStruct((tok_count, full - LANES), jnp.bfloat16),
        [None] * (len(blocks) + len(more)),
        (*blocks, *more),
        [pltpu.VMEM((capacity * len(blocks), full), jnp.bfloat16)],
    )


def sent(shard, sections, section_step, ring_step, flip):
    planes = len(RING)
    pairs = []
    for s in range(sections):
        for z in range(planes):
            for y in range(2):
                for core in range(2):
                    plane = RING[(RING.index(z) + ring_step) % planes]
                    target = (((s + section_step) % sections) * planes + plane) * 2 + (y ^ flip)
                    pairs.append((((s * planes + z) * 2 + y) * 2 + core, target * 2 + core))
    return lax.ppermute(shard, ("section", "expert"), pairs)


def after(value, other):
    return lax.optimization_barrier((value, other))[0]


def by_ring(rows, route_ids, route_weights, w_gate_up, w_down):
    sections = lax.axis_size("section")
    devices = lax.axis_size("expert")
    experts = devices // 2
    tokens = rows[0]
    tok_count = tokens.shape[0]
    top_count = route_ids.shape[2]
    capacity = max(2, 2 * tok_count * top_count // experts)
    swap = [(i, i ^ 1) for i in range(devices)]
    w_in, w_out = w_gate_up[0], w_down[0]
    far_out = lax.ppermute(w_out, "expert", swap)
    far_in = lax.ppermute(w_in, "expert", swap)
    block1 = sent(tokens, sections, 0, 1, 0)
    marks = prepare(route_ids[0].T, route_weights[0].T)
    marks1 = sent(marks, sections, 0, 1, 0)
    own0, other, back0, back1 = choose(tokens, marks, capacity, ((0, 0), (0, 1), (3, 0), (3, 1)))
    other0 = sent(other, sections, 0, 0, 1)
    near_in = loaded(after(w_in, own0))
    block1 = after(block1, (near_in, other0))
    own1, other, on0, on1 = choose(block1, marks1, capacity, ((0, 0), (0, 1), (1, 0), (1, 1)))
    other1 = sent(other, sections, 0, 0, 1)
    own2 = sent(on0, sections, 0, 1, 0)
    other2 = sent(on1, sections, 0, 1, 1)
    other3 = sent(after(back1, other0), sections, 0, 3, 1)
    back0 = after(back0, (other1, other3))
    own3 = sent(back0, sections, 0, 3, 0)
    near = (near_in, loaded(after(w_out, back0)))
    pieces = (own0, other0, own1, own2, other2, other1, own3, other3)
    places = ((0, 0), (0, 1), (1, 0), (2, 0), (2, 1), (1, 1), (3, 0), (3, 1))
    slots, total = near_pass(pieces, near)
    pieces = far_pass(slots, total, (far_in, far_out), capacity)
    piece = dict(zip(places, pieces))
    first = [
        sent(piece[2, 1], sections, 0, 1, 1),
        sent(piece[3, 1], sections, 0, 0, 1),
        sent(piece[0, 0], sections, 1, 0, 0),
        sent(piece[0, 1], sections, 1, 0, 1),
        sent(piece[2, 0], sections, 0, 1, 0),
    ]
    two, three, *straight, four = lax.optimization_barrier(first)
    merged = [piece[3, 0], two, three, four]
    straight += [sent(piece[1, flip], sections, 1, -1, flip) for flip in range(2)]
    merged = sent(combine(merged, tok_count), sections, 1, 1, 0)
    return combine(straight, tok_count, merged)[None]


def per_device(rows, route_ids, route_weights, w_gate_up, w_down):
    experts = lax.axis_size("expert") // 2
    fits = experts == 2 * len(RING) and rows.shape[1] <= LANES - TOKEN_LANE
    plan = by_ring if fits else by_slots
    return plan(rows, route_ids, route_weights, w_gate_up, w_down)


def solution(mesh):
    in_specs = (
        P("section", "expert", None),
        P("section", "expert", None),
        P("section", "expert", None),
        P("section", None, "expert"),
        P("section", "expert", None),
    )
    out_specs = P("section", "expert", None)
    return jax.shard_map(
        per_device, mesh=mesh, in_specs=in_specs, out_specs=out_specs, check_vma=False
    )
```

```python
import functools

import jax
import jax.numpy as jnp
from jax import lax
from jax.experimental import pallas as pl
from jax.experimental.pallas import tpu as pltpu
from jax.sharding import PartitionSpec as P


def passed_along(shard, axis, by):
    length = lax.axis_size(axis)
    return lax.ppermute(shard, axis, [(i, (i + by) % length) for i in range(length)])


def by_slots(rows, route_ids, route_weights, w_gate_up, w_down):
    devices = lax.axis_size("expert")
    experts = devices // 2
    tokens = rows[0]
    tok_count, width = tokens.shape
    top_count = route_ids.shape[2]
    choices_flat = route_ids[0].reshape(-1)
    capacity = max(2, 2 * tok_count * top_count // experts)
    onehot = (choices_flat[:, None] == jnp.arange(experts, dtype=jnp.int32)[None, :]).astype(
        jnp.int32
    )
    before = jnp.cumsum(onehot, axis=0) - onehot
    slot = jnp.sum(before * onehot, axis=1)
    place = slot * experts + choices_flat
    slot_total = experts * capacity
    picker = (place[None, :] == jnp.arange(slot_total, dtype=jnp.int32)[:, None]).astype(
        jnp.bfloat16
    )
    token_pairs = jnp.repeat(tokens, top_count, axis=0)
    packed = jnp.dot(picker, token_pairs, preferred_element_type=jnp.float32).astype(jnp.bfloat16)
    w_in = w_gate_up[0]
    w_out = w_down[0]
    hidden = w_out.shape[0]
    outgoing = jnp.broadcast_to(
        packed.reshape(capacity, experts, 1, width), (capacity, experts, 2, width)
    )
    outgoing = outgoing.reshape(capacity, devices, width)
    block = lax.all_to_all(outgoing, "expert", split_axis=1, concat_axis=1, tiled=True)
    flat = block.reshape(-1, width)
    both = jnp.dot(flat, w_in, preferred_element_type=jnp.float32)
    active = (jax.nn.silu(both[:, :hidden]) * both[:, hidden:]).astype(jnp.bfloat16)
    result = jnp.dot(active, w_out, preferred_element_type=jnp.float32)
    partial_out = result.reshape(block.shape[0], block.shape[1], width).astype(jnp.bfloat16)
    returned = lax.all_to_all(partial_out, "expert", split_axis=1, concat_axis=1, tiled=True)
    returned = returned.reshape(capacity, experts, 2, width).astype(jnp.float32)
    expert_out = jnp.sum(returned, axis=2).astype(jnp.bfloat16).reshape(slot_total, width)
    pair_out = expert_out[place].astype(jnp.float32) * route_weights[0].reshape(-1)[:, None]
    layer_out = jnp.sum(pair_out.reshape(tok_count, top_count, width), axis=1).astype(jnp.bfloat16)
    return passed_along(layer_out, "section", 1)[None]


RING = (0, 1, 3, 2)
LANES = 128
TOKEN_LANE = 64


def on_ring(place):
    return place ^ (place >> 1)


def chip_at(chip, steps, flip):
    return (on_ring((on_ring(chip >> 1) + steps) & 3) << 1) | ((chip & 1) ^ flip)


def iota(shape, axis):
    return lax.broadcasted_iota(jnp.int32, shape, axis)


def ones_where(condition):
    return jnp.where(condition, 1.0, 0.0).astype(jnp.bfloat16)


def across(left, right):
    return lax.dot_general(left, right, (((0,), (0,)), ((), ())), preferred_element_type=jnp.float32)


def local_call(kernel, name, out_shape, in_specs, operands, scratch=(), limit=12, flops=0, moved=0):
    vmem = pl.BlockSpec(memory_space=pltpu.VMEM)
    return pl.pallas_call(
        kernel,
        out_shape=out_shape,
        in_specs=[vmem if spec is None else pl.BlockSpec(memory_space=spec) for spec in in_specs],
        out_specs=jax.tree.map(lambda _: vmem, out_shape),
        scratch_shapes=list(scratch),
        compiler_params=pltpu.CompilerParams(vmem_limit_bytes=limit << 20),
        cost_estimate=pl.CostEstimate(flops=flops, bytes_accessed=moved, transcendentals=0),
        name=name,
    )(*operands)


def prepare_kernel(ids_in, weights_in, out, ids, weights, sems):
    tok_count = out.shape[0]
    top_count = ids.shape[0]
    experts = 2 * len(RING)
    copies = [
        pltpu.make_async_copy(ids_in, ids, sems.at[0]),
        pltpu.make_async_copy(weights_in, weights, sems.at[1]),
    ]
    for copy in copies:
        copy.start()
    square = (tok_count, tok_count)
    earlier = ones_where(iota(square, 0) < iota(square, 1))
    expert = iota((experts, tok_count), 0)
    unit = ones_where(iota((4 * experts, LANES), 0) == iota((4 * experts, LANES), 1))
    token = ones_where(iota((tok_count, LANES), 0) + TOKEN_LANE == iota((tok_count, LANES), 1))
    copies[0].wait()
    copies[1].wait()
    named = jnp.zeros((experts, tok_count), jnp.float32)
    scale = jnp.zeros((experts, tok_count), jnp.float32)
    for k in range(top_count):
        hit = ids[k : k + 1, :] == expert
        named = named + jnp.where(hit, 1.0, 0.0)
        scale = scale + jnp.where(hit, weights[k : k + 1, :], 0.0)
    rank = jnp.dot(named.astype(jnp.bfloat16), earlier, preferred_element_type=jnp.float32)
    notes = [jnp.where(named > 0.5, rank + 1.0, 0.0)]
    for _ in range(3):
        piece = scale.astype(jnp.bfloat16).astype(jnp.float32)
        scale = scale - piece
        notes.append(piece)
    notes = across(jnp.concatenate(notes, axis=0).astype(jnp.bfloat16), unit)
    out[...] = notes.astype(jnp.bfloat16) + token


def prepare(ids, weights):
    tok_count = ids.shape[1]
    return local_call(
        prepare_kernel,
        "prepare",
        pltpu.VMEM((tok_count, LANES), jnp.bfloat16),
        [pl.ANY] * 2,
        tuple(pltpu.with_memory_space_constraint(x, pltpu.HBM) for x in (ids, weights)),
        [
            pltpu.VMEM(ids.shape, ids.dtype),
            pltpu.VMEM(weights.shape, weights.dtype),
            pltpu.SemaphoreType.DMA((2,)),
        ],
        limit=8,
    )


def choose_kernel(places, capacity, block, marks, *refs):
    chip = lax.axis_index("expert") >> 1
    tok_count = block.shape[0]
    notes = marks[...].astype(jnp.float32)
    width = block.shape[1]
    lane = iota(notes.shape, 1)
    slot = iota((tok_count, len(places) * capacity), 1)
    code = jnp.zeros(slot.shape, jnp.float32)
    order = jnp.zeros(slot.shape, jnp.int32)
    for at, (steps, flip) in enumerate(places):
        wanted = chip_at(chip, steps, flip)
        column = jnp.sum(jnp.where(lane == wanted, notes, 0.0), axis=1, keepdims=True)
        code = jnp.where(slot >= at * capacity, column, code)
        order = jnp.where(slot >= at * capacity, slot + 1 - at * capacity, order)
    pick = ones_where(code == order.astype(jnp.float32))
    rows = across(pick, block[...]).astype(jnp.bfloat16)
    marked = across(pick, marks[...]).astype(jnp.bfloat16)
    for at in range(len(places)):
        place = slice(at * capacity, (at + 1) * capacity)
        refs[at][:, :width] = rows[place]
        refs[at][:, width:] = marked[place]


def choose(block, marks, capacity, places):
    return local_call(
        functools.partial(choose_kernel, places, capacity),
        "choose",
        [jax.ShapeDtypeStruct((capacity, block.shape[1] + LANES), jnp.bfloat16) for _ in places],
        [None] * 2,
        (block, marks),
    )


def load_kernel(source, target, sem):
    copy = pltpu.make_async_copy(source, target, sem)
    copy.start()
    copy.wait()


def loaded(weights):
    return local_call(
        load_kernel,
        "loaded",
        pltpu.VMEM(weights.shape, weights.dtype),
        [pl.ANY],
        (weights,),
        [pltpu.SemaphoreType.DMA],
        limit=9,
        moved=2 * weights.size * weights.dtype.itemsize,
    )


def gated(both):
    hidden = both.shape[1] // 2
    gate = both[:, :hidden]
    return (gate / (1.0 + jnp.exp(-gate)) * both[:, hidden:]).astype(jnp.bfloat16)


def write_pieces(slots, total, outs):
    chip = lax.axis_index("expert") >> 1
    width = total.shape[1]
    experts = 2 * len(RING)
    notes = slots[:, width:].astype(jnp.float32)
    lane = iota(notes.shape, 1)
    mine = (lane >= experts) & (lane < 4 * experts) & ((lane & (experts - 1)) == chip)
    scale = jnp.sum(jnp.where(mine, notes, 0.0), axis=1, keepdims=True)
    start = 0
    for out in outs:
        stop = start + out.shape[0]
        out[:, :width] = (total[start:stop] * scale[start:stop]).astype(jnp.bfloat16)
        out[:, width:] = slots[start:stop, width:]
        start = stop


def near_kernel(*refs):
    pieces, (first, second, slots, total) = refs[:-4], refs[-4:]
    start = 0
    for piece in pieces:
        slots[start : start + piece.shape[0]] = piece[...]
        start += piece.shape[0]
    width = total.shape[1]
    both = jnp.dot(slots[:, :width], first[...], preferred_element_type=jnp.float32)
    total[...] = jnp.dot(gated(both), second[...], preferred_element_type=jnp.float32)


def near_pass(pieces, weights):
    count = sum(piece.shape[0] for piece in pieces)
    full = pieces[0].shape[1]
    return local_call(
        near_kernel,
        "near_pass",
        [
            jax.ShapeDtypeStruct((count, full), jnp.bfloat16),
            jax.ShapeDtypeStruct((count, full - LANES), jnp.float32),
        ],
        [None] * (len(pieces) + 2),
        (*pieces, *weights),
        moved=2 * sum(w.size for w in weights),
    )


def far_kernel(slots, before, first, second, *refs):
    outs, total = refs[:-1], refs[-1]
    width = total.shape[1]
    both = jnp.dot(slots[:, :width], first[...], preferred_element_type=jnp.float32)
    term = jnp.dot(gated(both), second[...], preferred_element_type=jnp.float32)
    total[...] = before[...] + term
    write_pieces(slots, total, outs)


def far_pass(slots, total, weights, capacity):
    count, full = slots.shape
    return local_call(
        far_kernel,
        "far_pass",
        [jax.ShapeDtypeStruct((capacity, full), jnp.bfloat16)] * (count // capacity),
        [None] * 4,
        (slots, total, *weights),
        [pltpu.VMEM(total.shape, jnp.float32)],
        limit=24,
        moved=2 * sum(w.size for w in weights),
    )


def combine_kernel(count, *refs):
    blocks, more, (out, slots) = refs[:count], refs[count:-2], refs[-2:]
    tok_count, width = out.shape
    start = 0
    for block in blocks:
        slots[start : start + block.shape[0]] = block[...]
        start += block.shape[0]
    token = slots[:, width:]
    part = width // 7
    for at in range(7):
        place = slice(at * part, (at + 1) * part)
        mixed = across(token, slots[:, place])[TOKEN_LANE : TOKEN_LANE + tok_count]
        for other in more:
            mixed = mixed + other[:, place].astype(jnp.float32)
        out[:, place] = mixed.astype(out.dtype)


def combine(blocks, tok_count, *more):
    capacity, full = blocks[0].shape
    return local_call(
        functools.partial(combine_kernel, len(blocks)),
        "combine",
        jax.ShapeDtypeStruct((tok_count, full - LANES), jnp.bfloat16),
        [None] * (len(blocks) + len(more)),
        (*blocks, *more),
        [pltpu.VMEM((capacity * len(blocks), full), jnp.bfloat16)],
    )


def sent(shard, sections, section_step, ring_step, flip):
    planes = len(RING)
    pairs = []
    for s in range(sections):
        for z in range(planes):
            for y in range(2):
                for core in range(2):
                    plane = RING[(RING.index(z) + ring_step) % planes]
                    target = (((s + section_step) % sections) * planes + plane) * 2 + (y ^ flip)
                    pairs.append((((s * planes + z) * 2 + y) * 2 + core, target * 2 + core))
    return lax.ppermute(shard, ("section", "expert"), pairs)


def after(value, other):
    return lax.optimization_barrier((value, other))[0]


def by_ring(rows, route_ids, route_weights, w_gate_up, w_down):
    sections = lax.axis_size("section")
    devices = lax.axis_size("expert")
    experts = devices // 2
    tokens = rows[0]
    tok_count = tokens.shape[0]
    top_count = route_ids.shape[2]
    capacity = max(2, 2 * tok_count * top_count // experts)
    swap = [(i, i ^ 1) for i in range(devices)]
    w_in, w_out = w_gate_up[0], w_down[0]
    far_out = lax.ppermute(w_out, "expert", swap)
    far_in = lax.ppermute(w_in, "expert", swap)
    block1 = sent(tokens, sections, 0, 1, 0)
    marks = prepare(route_ids[0].T, route_weights[0].T)
    marks1 = sent(marks, sections, 0, 1, 0)
    own0, other, back0, back1 = choose(tokens, marks, capacity, ((0, 0), (0, 1), (3, 0), (3, 1)))
    other0 = sent(other, sections, 0, 0, 1)
    near_out = loaded(after(w_out, own0))
    block1 = after(block1, (near_out, other0))
    own1, other, on0, on1 = choose(block1, marks1, capacity, ((0, 0), (0, 1), (1, 0), (1, 1)))
    other1 = sent(other, sections, 0, 0, 1)
    own2 = sent(on0, sections, 0, 1, 0)
    other2 = sent(on1, sections, 0, 1, 1)
    other3 = sent(after(back1, other0), sections, 0, 3, 1)
    back0 = after(back0, (other1, other3))
    own3 = sent(back0, sections, 0, 3, 0)
    near = (loaded(after(w_in, back0)), near_out)
    pieces = (own0, other0, own1, own2, other2, other1, own3, other3)
    places = ((0, 0), (0, 1), (1, 0), (2, 0), (2, 1), (1, 1), (3, 0), (3, 1))
    slots, total = near_pass(pieces, near)
    pieces = far_pass(slots, total, (far_in, far_out), capacity)
    piece = dict(zip(places, pieces))
    first = [
        sent(piece[2, 1], sections, 0, 1, 1),
        sent(piece[3, 1], sections, 0, 0, 1),
        sent(piece[0, 0], sections, 1, 0, 0),
        sent(piece[0, 1], sections, 1, 0, 1),
        sent(piece[2, 0], sections, 0, 1, 0),
    ]
    two, three, *straight, four = lax.optimization_barrier(first)
    merged = [piece[3, 0], two, three, four]
    straight += [sent(piece[1, flip], sections, 1, -1, flip) for flip in range(2)]
    merged = sent(combine(merged, tok_count), sections, 1, 1, 0)
    return combine(straight, tok_count, merged)[None]


def per_device(rows, route_ids, route_weights, w_gate_up, w_down):
    experts = lax.axis_size("expert") // 2
    fits = experts == 2 * len(RING) and rows.shape[1] <= LANES - TOKEN_LANE
    plan = by_ring if fits else by_slots
    return plan(rows, route_ids, route_weights, w_gate_up, w_down)


def solution(mesh):
    in_specs = (
        P("section", "expert", None),
        P("section", "expert", None),
        P("section", "expert", None),
        P("section", None, "expert"),
        P("section", "expert", None),
    )
    out_specs = P("section", "expert", None)
    return jax.shard_map(
        per_device, mesh=mesh, in_specs=in_specs, out_specs=out_specs, check_vma=False
    )
```

```python
import functools

import jax
import jax.numpy as jnp
from jax import lax
from jax.experimental import pallas as pl
from jax.experimental.pallas import tpu as pltpu
from jax.sharding import PartitionSpec as P


def passed_along(shard, axis, by):
    length = lax.axis_size(axis)
    return lax.ppermute(shard, axis, [(i, (i + by) % length) for i in range(length)])


def by_slots(rows, route_ids, route_weights, w_gate_up, w_down):
    devices = lax.axis_size("expert")
    experts = devices // 2
    tokens = rows[0]
    tok_count, width = tokens.shape
    top_count = route_ids.shape[2]
    choices_flat = route_ids[0].reshape(-1)
    capacity = max(2, 2 * tok_count * top_count // experts)
    onehot = (choices_flat[:, None] == jnp.arange(experts, dtype=jnp.int32)[None, :]).astype(
        jnp.int32
    )
    before = jnp.cumsum(onehot, axis=0) - onehot
    slot = jnp.sum(before * onehot, axis=1)
    place = slot * experts + choices_flat
    slot_total = experts * capacity
    picker = (place[None, :] == jnp.arange(slot_total, dtype=jnp.int32)[:, None]).astype(
        jnp.bfloat16
    )
    token_pairs = jnp.repeat(tokens, top_count, axis=0)
    packed = jnp.dot(picker, token_pairs, preferred_element_type=jnp.float32).astype(jnp.bfloat16)
    w_in = w_gate_up[0]
    w_out = w_down[0]
    hidden = w_out.shape[0]
    outgoing = jnp.broadcast_to(
        packed.reshape(capacity, experts, 1, width), (capacity, experts, 2, width)
    )
    outgoing = outgoing.reshape(capacity, devices, width)
    block = lax.all_to_all(outgoing, "expert", split_axis=1, concat_axis=1, tiled=True)
    flat = block.reshape(-1, width)
    both = jnp.dot(flat, w_in, preferred_element_type=jnp.float32)
    active = (jax.nn.silu(both[:, :hidden]) * both[:, hidden:]).astype(jnp.bfloat16)
    result = jnp.dot(active, w_out, preferred_element_type=jnp.float32)
    partial_out = result.reshape(block.shape[0], block.shape[1], width).astype(jnp.bfloat16)
    returned = lax.all_to_all(partial_out, "expert", split_axis=1, concat_axis=1, tiled=True)
    returned = returned.reshape(capacity, experts, 2, width).astype(jnp.float32)
    expert_out = jnp.sum(returned, axis=2).astype(jnp.bfloat16).reshape(slot_total, width)
    pair_out = expert_out[place].astype(jnp.float32) * route_weights[0].reshape(-1)[:, None]
    layer_out = jnp.sum(pair_out.reshape(tok_count, top_count, width), axis=1).astype(jnp.bfloat16)
    return passed_along(layer_out, "section", 1)[None]


RING = (0, 1, 3, 2)
LANES = 128
TOKEN_LANE = 64


def on_ring(place):
    return place ^ (place >> 1)


def chip_at(chip, steps, flip):
    return (on_ring((on_ring(chip >> 1) + steps) & 3) << 1) | ((chip & 1) ^ flip)


def iota(shape, axis):
    return lax.broadcasted_iota(jnp.int32, shape, axis)


def ones_where(condition):
    return jnp.where(condition, 1.0, 0.0).astype(jnp.bfloat16)


def across(left, right):
    return lax.dot_general(left, right, (((0,), (0,)), ((), ())), preferred_element_type=jnp.float32)


def local_call(kernel, name, out_shape, in_specs, operands, scratch=(), limit=12, flops=0, moved=0):
    vmem = pl.BlockSpec(memory_space=pltpu.VMEM)
    return pl.pallas_call(
        kernel,
        out_shape=out_shape,
        in_specs=[vmem if spec is None else pl.BlockSpec(memory_space=spec) for spec in in_specs],
        out_specs=jax.tree.map(lambda _: vmem, out_shape),
        scratch_shapes=list(scratch),
        compiler_params=pltpu.CompilerParams(vmem_limit_bytes=limit << 20),
        cost_estimate=pl.CostEstimate(flops=flops, bytes_accessed=moved, transcendentals=0),
        name=name,
    )(*operands)


def prepare_kernel(ids_in, weights_in, out, ids, weights, sems):
    tok_count = out.shape[0]
    top_count = ids.shape[0]
    experts = 2 * len(RING)
    copies = [
        pltpu.make_async_copy(ids_in, ids, sems.at[0]),
        pltpu.make_async_copy(weights_in, weights, sems.at[1]),
    ]
    for copy in copies:
        copy.start()
    square = (tok_count, tok_count)
    earlier = ones_where(iota(square, 0) < iota(square, 1))
    expert = iota((experts, tok_count), 0)
    unit = ones_where(iota((4 * experts, LANES), 0) == iota((4 * experts, LANES), 1))
    token = ones_where(iota((tok_count, LANES), 0) + TOKEN_LANE == iota((tok_count, LANES), 1))
    copies[0].wait()
    copies[1].wait()
    named = jnp.zeros((experts, tok_count), jnp.float32)
    scale = jnp.zeros((experts, tok_count), jnp.float32)
    for k in range(top_count):
        hit = ids[k : k + 1, :] == expert
        named = named + jnp.where(hit, 1.0, 0.0)
        scale = scale + jnp.where(hit, weights[k : k + 1, :], 0.0)
    rank = jnp.dot(named.astype(jnp.bfloat16), earlier, preferred_element_type=jnp.float32)
    notes = [jnp.where(named > 0.5, rank + 1.0, 0.0)]
    for _ in range(3):
        piece = scale.astype(jnp.bfloat16).astype(jnp.float32)
        scale = scale - piece
        notes.append(piece)
    notes = across(jnp.concatenate(notes, axis=0).astype(jnp.bfloat16), unit)
    out[...] = notes.astype(jnp.bfloat16) + token


def prepare(ids, weights):
    tok_count = ids.shape[1]
    return local_call(
        prepare_kernel,
        "prepare",
        pltpu.VMEM((tok_count, LANES), jnp.bfloat16),
        [pl.ANY] * 2,
        tuple(pltpu.with_memory_space_constraint(x, pltpu.HBM) for x in (ids, weights)),
        [
            pltpu.VMEM(ids.shape, ids.dtype),
            pltpu.VMEM(weights.shape, weights.dtype),
            pltpu.SemaphoreType.DMA((2,)),
        ],
        limit=8,
    )


def choose_kernel(places, capacity, block, marks, *refs):
    chip = lax.axis_index("expert") >> 1
    tok_count = block.shape[0]
    notes = marks[...].astype(jnp.float32)
    width = block.shape[1]
    lane = iota(notes.shape, 1)
    slot = iota((tok_count, len(places) * capacity), 1)
    code = jnp.zeros(slot.shape, jnp.float32)
    order = jnp.zeros(slot.shape, jnp.int32)
    for at, (steps, flip) in enumerate(places):
        wanted = chip_at(chip, steps, flip)
        column = jnp.sum(jnp.where(lane == wanted, notes, 0.0), axis=1, keepdims=True)
        code = jnp.where(slot >= at * capacity, column, code)
        order = jnp.where(slot >= at * capacity, slot + 1 - at * capacity, order)
    pick = ones_where(code == order.astype(jnp.float32))
    rows = across(pick, block[...]).astype(jnp.bfloat16)
    marked = across(pick, marks[...]).astype(jnp.bfloat16)
    for at in range(len(places)):
        place = slice(at * capacity, (at + 1) * capacity)
        refs[at][:, :width] = rows[place]
        refs[at][:, width:] = marked[place]


def choose(block, marks, capacity, places):
    return local_call(
        functools.partial(choose_kernel, places, capacity),
        "choose",
        [jax.ShapeDtypeStruct((capacity, block.shape[1] + LANES), jnp.bfloat16) for _ in places],
        [None] * 2,
        (block, marks),
    )


def load_kernel(source, target, sem):
    copy = pltpu.make_async_copy(source, target, sem)
    copy.start()
    copy.wait()


def loaded(weights):
    return local_call(
        load_kernel,
        "loaded",
        pltpu.VMEM(weights.shape, weights.dtype),
        [pl.ANY],
        (weights,),
        [pltpu.SemaphoreType.DMA],
        limit=9,
        moved=2 * weights.size * weights.dtype.itemsize,
    )


def gated(both):
    hidden = both.shape[1] // 2
    gate = both[:, :hidden]
    return (gate / (1.0 + jnp.exp(-gate)) * both[:, hidden:]).astype(jnp.bfloat16)


def write_pieces(slots, total, outs):
    chip = lax.axis_index("expert") >> 1
    width = total.shape[1]
    experts = 2 * len(RING)
    notes = slots[:, width:].astype(jnp.float32)
    lane = iota(notes.shape, 1)
    mine = (lane >= experts) & (lane < 4 * experts) & ((lane & (experts - 1)) == chip)
    scale = jnp.sum(jnp.where(mine, notes, 0.0), axis=1, keepdims=True)
    start = 0
    for out in outs:
        stop = start + out.shape[0]
        out[:, :width] = (total[start:stop] * scale[start:stop]).astype(jnp.bfloat16)
        out[:, width:] = slots[start:stop, width:]
        start = stop


def near_kernel(*refs):
    pieces, (first, second, slots, total) = refs[:-4], refs[-4:]
    start = 0
    for piece in pieces:
        slots[start : start + piece.shape[0]] = piece[...]
        start += piece.shape[0]
    width = total.shape[1]
    both = jnp.dot(slots[:, :width], first[...], preferred_element_type=jnp.float32)
    total[...] = jnp.dot(gated(both), second[...], preferred_element_type=jnp.float32)


def near_pass(pieces, weights):
    count = sum(piece.shape[0] for piece in pieces)
    full = pieces[0].shape[1]
    return local_call(
        near_kernel,
        "near_pass",
        [
            jax.ShapeDtypeStruct((count, full), jnp.bfloat16),
            jax.ShapeDtypeStruct((count, full - LANES), jnp.float32),
        ],
        [None] * (len(pieces) + 2),
        (*pieces, *weights),
        moved=2 * sum(w.size for w in weights),
    )


def far_kernel(slots, before, first, second, *refs):
    outs, total = refs[:-1], refs[-1]
    width = total.shape[1]
    both = jnp.dot(slots[:, :width], first[...], preferred_element_type=jnp.float32)
    term = jnp.dot(gated(both), second[...], preferred_element_type=jnp.float32)
    total[...] = before[...] + term
    write_pieces(slots, total, outs)


def far_pass(slots, total, weights, capacity):
    count, full = slots.shape
    return local_call(
        far_kernel,
        "far_pass",
        [jax.ShapeDtypeStruct((capacity, full), jnp.bfloat16)] * (count // capacity),
        [None] * 4,
        (slots, total, *weights),
        [pltpu.VMEM(total.shape, jnp.float32)],
        limit=24,
        moved=2 * sum(w.size for w in weights),
    )


def combine_kernel(count, *refs):
    blocks, more, (out, slots) = refs[:count], refs[count:-2], refs[-2:]
    tok_count, width = out.shape
    start = 0
    for block in blocks:
        slots[start : start + block.shape[0]] = block[...]
        start += block.shape[0]
    token = slots[:, width:]
    part = width // 7
    for at in range(7):
        place = slice(at * part, (at + 1) * part)
        mixed = across(token, slots[:, place])[TOKEN_LANE : TOKEN_LANE + tok_count]
        for other in more:
            mixed = mixed + other[:, place].astype(jnp.float32)
        out[:, place] = mixed.astype(out.dtype)


def combine(blocks, tok_count, dtype=jnp.bfloat16):
    capacity, full = blocks[0].shape
    return local_call(
        functools.partial(combine_kernel, len(blocks)),
        "combine",
        jax.ShapeDtypeStruct((tok_count, full - LANES), dtype),
        [None] * len(blocks),
        tuple(blocks),
        [pltpu.VMEM((capacity * len(blocks), full), jnp.bfloat16)],
    )


def add_kernel(left, right, out):
    out[...] = (left[...] + right[...].astype(jnp.float32)).astype(out.dtype)


def added(left, right):
    out_shape = jax.ShapeDtypeStruct(right.shape, right.dtype)
    return local_call(add_kernel, "added", out_shape, [None] * 2, (left, right))


def sent(shard, sections, section_step, ring_step, flip):
    planes = len(RING)
    pairs = []
    for s in range(sections):
        for z in range(planes):
            for y in range(2):
                for core in range(2):
                    plane = RING[(RING.index(z) + ring_step) % planes]
                    target = (((s + section_step) % sections) * planes + plane) * 2 + (y ^ flip)
                    pairs.append((((s * planes + z) * 2 + y) * 2 + core, target * 2 + core))
    return lax.ppermute(shard, ("section", "expert"), pairs)


def after(value, other):
    return lax.optimization_barrier((value, other))[0]


def by_ring(rows, route_ids, route_weights, w_gate_up, w_down):
    sections = lax.axis_size("section")
    devices = lax.axis_size("expert")
    experts = devices // 2
    tokens = rows[0]
    tok_count = tokens.shape[0]
    top_count = route_ids.shape[2]
    capacity = max(2, 2 * tok_count * top_count // experts)
    swap = [(i, i ^ 1) for i in range(devices)]
    w_in, w_out = w_gate_up[0], w_down[0]
    far_out = lax.ppermute(w_out, "expert", swap)
    far_in = lax.ppermute(w_in, "expert", swap)
    block1 = sent(tokens, sections, 0, 1, 0)
    marks = prepare(route_ids[0].T, route_weights[0].T)
    marks1 = sent(marks, sections, 0, 1, 0)
    own0, other, back0, back1 = choose(tokens, marks, capacity, ((0, 0), (0, 1), (3, 0), (3, 1)))
    other0 = sent(other, sections, 0, 0, 1)
    near_out = loaded(after(w_out, own0))
    block1 = after(block1, (near_out, other0))
    own1, other, on0, on1 = choose(block1, marks1, capacity, ((0, 0), (0, 1), (1, 0), (1, 1)))
    other1 = sent(other, sections, 0, 0, 1)
    own2 = sent(on0, sections, 0, 1, 0)
    other2 = sent(on1, sections, 0, 1, 1)
    other3 = sent(after(back1, other0), sections, 0, 3, 1)
    back0 = after(back0, (other1, other3))
    own3 = sent(back0, sections, 0, 3, 0)
    near = (loaded(after(w_in, back0)), near_out)
    pieces = (own0, other0, own1, own2, other2, other1, own3, other3)
    places = ((0, 0), (0, 1), (1, 0), (2, 0), (2, 1), (1, 1), (3, 0), (3, 1))
    slots, total = near_pass(pieces, near)
    pieces = far_pass(slots, total, (far_in, far_out), capacity)
    piece = dict(zip(places, pieces))
    first = [
        sent(piece[2, 1], sections, 0, 1, 1),
        sent(piece[3, 1], sections, 0, 0, 1),
        sent(piece[0, 0], sections, 1, 0, 0),
        sent(piece[0, 1], sections, 1, 0, 1),
        sent(piece[2, 0], sections, 0, 1, 0),
    ]
    two, three, *straight, four = lax.optimization_barrier(first)
    merged = [piece[3, 0], two, three, four]
    straight += [sent(piece[1, flip], sections, 1, -1, flip) for flip in range(2)]
    merged = sent(combine(merged, tok_count), sections, 1, 1, 0)
    return added(combine(straight, tok_count, jnp.float32), merged)[None]


def per_device(rows, route_ids, route_weights, w_gate_up, w_down):
    experts = lax.axis_size("expert") // 2
    fits = experts == 2 * len(RING) and rows.shape[1] <= LANES - TOKEN_LANE
    plan = by_ring if fits else by_slots
    return plan(rows, route_ids, route_weights, w_gate_up, w_down)


def solution(mesh):
    in_specs = (
        P("section", "expert", None),
        P("section", "expert", None),
        P("section", "expert", None),
        P("section", None, "expert"),
        P("section", "expert", None),
    )
    out_specs = P("section", "expert", None)
    return jax.shard_map(
        per_device, mesh=mesh, in_specs=in_specs, out_specs=out_specs, check_vma=False
    )
```

```python
import functools

import jax
import jax.numpy as jnp
from jax import lax
from jax.experimental import pallas as pl
from jax.experimental.pallas import tpu as pltpu
from jax.sharding import PartitionSpec as P


def passed_along(shard, axis, by):
    length = lax.axis_size(axis)
    return lax.ppermute(shard, axis, [(i, (i + by) % length) for i in range(length)])


def by_slots(rows, route_ids, route_weights, w_gate_up, w_down):
    devices = lax.axis_size("expert")
    experts = devices // 2
    tokens = rows[0]
    tok_count, width = tokens.shape
    top_count = route_ids.shape[2]
    choices_flat = route_ids[0].reshape(-1)
    capacity = max(2, 2 * tok_count * top_count // experts)
    onehot = (choices_flat[:, None] == jnp.arange(experts, dtype=jnp.int32)[None, :]).astype(
        jnp.int32
    )
    before = jnp.cumsum(onehot, axis=0) - onehot
    slot = jnp.sum(before * onehot, axis=1)
    place = slot * experts + choices_flat
    slot_total = experts * capacity
    picker = (place[None, :] == jnp.arange(slot_total, dtype=jnp.int32)[:, None]).astype(
        jnp.bfloat16
    )
    token_pairs = jnp.repeat(tokens, top_count, axis=0)
    packed = jnp.dot(picker, token_pairs, preferred_element_type=jnp.float32).astype(jnp.bfloat16)
    w_in = w_gate_up[0]
    w_out = w_down[0]
    hidden = w_out.shape[0]
    outgoing = jnp.broadcast_to(
        packed.reshape(capacity, experts, 1, width), (capacity, experts, 2, width)
    )
    outgoing = outgoing.reshape(capacity, devices, width)
    block = lax.all_to_all(outgoing, "expert", split_axis=1, concat_axis=1, tiled=True)
    flat = block.reshape(-1, width)
    both = jnp.dot(flat, w_in, preferred_element_type=jnp.float32)
    active = (jax.nn.silu(both[:, :hidden]) * both[:, hidden:]).astype(jnp.bfloat16)
    result = jnp.dot(active, w_out, preferred_element_type=jnp.float32)
    partial_out = result.reshape(block.shape[0], block.shape[1], width).astype(jnp.bfloat16)
    returned = lax.all_to_all(partial_out, "expert", split_axis=1, concat_axis=1, tiled=True)
    returned = returned.reshape(capacity, experts, 2, width).astype(jnp.float32)
    expert_out = jnp.sum(returned, axis=2).astype(jnp.bfloat16).reshape(slot_total, width)
    pair_out = expert_out[place].astype(jnp.float32) * route_weights[0].reshape(-1)[:, None]
    layer_out = jnp.sum(pair_out.reshape(tok_count, top_count, width), axis=1).astype(jnp.bfloat16)
    return passed_along(layer_out, "section", 1)[None]


RING = (0, 1, 3, 2)
LANES = 128
TOKEN_LANE = 64


def on_ring(place):
    return place ^ (place >> 1)


def chip_at(chip, steps, flip):
    return (on_ring((on_ring(chip >> 1) + steps) & 3) << 1) | ((chip & 1) ^ flip)


def iota(shape, axis):
    return lax.broadcasted_iota(jnp.int32, shape, axis)


def ones_where(condition):
    return jnp.where(condition, 1.0, 0.0).astype(jnp.bfloat16)


def across(left, right):
    return lax.dot_general(left, right, (((0,), (0,)), ((), ())), preferred_element_type=jnp.float32)


def local_call(kernel, name, out_shape, in_specs, operands, scratch=(), limit=12, flops=0, moved=0):
    vmem = pl.BlockSpec(memory_space=pltpu.VMEM)
    return pl.pallas_call(
        kernel,
        out_shape=out_shape,
        in_specs=[vmem if spec is None else pl.BlockSpec(memory_space=spec) for spec in in_specs],
        out_specs=jax.tree.map(lambda _: vmem, out_shape),
        scratch_shapes=list(scratch),
        compiler_params=pltpu.CompilerParams(vmem_limit_bytes=limit << 20),
        cost_estimate=pl.CostEstimate(flops=flops, bytes_accessed=moved, transcendentals=0),
        name=name,
    )(*operands)


def prepare_kernel(ids_in, weights_in, out, ids, weights, sems):
    tok_count = out.shape[0]
    top_count = ids.shape[0]
    experts = 2 * len(RING)
    copies = [
        pltpu.make_async_copy(ids_in, ids, sems.at[0]),
        pltpu.make_async_copy(weights_in, weights, sems.at[1]),
    ]
    for copy in copies:
        copy.start()
    square = (tok_count, tok_count)
    earlier = ones_where(iota(square, 0) < iota(square, 1))
    expert = iota((experts, tok_count), 0)
    unit = ones_where(iota((4 * experts, LANES), 0) == iota((4 * experts, LANES), 1))
    token = ones_where(iota((tok_count, LANES), 0) + TOKEN_LANE == iota((tok_count, LANES), 1))
    copies[0].wait()
    copies[1].wait()
    named = jnp.zeros((experts, tok_count), jnp.float32)
    scale = jnp.zeros((experts, tok_count), jnp.float32)
    for k in range(top_count):
        hit = ids[k : k + 1, :] == expert
        named = named + jnp.where(hit, 1.0, 0.0)
        scale = scale + jnp.where(hit, weights[k : k + 1, :], 0.0)
    rank = jnp.dot(named.astype(jnp.bfloat16), earlier, preferred_element_type=jnp.float32)
    notes = [jnp.where(named > 0.5, rank + 1.0, 0.0)]
    for _ in range(3):
        piece = scale.astype(jnp.bfloat16).astype(jnp.float32)
        scale = scale - piece
        notes.append(piece)
    notes = across(jnp.concatenate(notes, axis=0).astype(jnp.bfloat16), unit)
    out[...] = notes.astype(jnp.bfloat16) + token


def prepare(ids, weights):
    tok_count = ids.shape[1]
    return local_call(
        prepare_kernel,
        "prepare",
        pltpu.VMEM((tok_count, LANES), jnp.bfloat16),
        [pl.ANY] * 2,
        tuple(pltpu.with_memory_space_constraint(x, pltpu.HBM) for x in (ids, weights)),
        [
            pltpu.VMEM(ids.shape, ids.dtype),
            pltpu.VMEM(weights.shape, weights.dtype),
            pltpu.SemaphoreType.DMA((2,)),
        ],
        limit=8,
    )


def choose_kernel(places, capacity, block, marks, *refs):
    chip = lax.axis_index("expert") >> 1
    tok_count = block.shape[0]
    notes = marks[...].astype(jnp.float32)
    width = block.shape[1]
    lane = iota(notes.shape, 1)
    slot = iota((tok_count, len(places) * capacity), 1)
    code = jnp.zeros(slot.shape, jnp.float32)
    order = jnp.zeros(slot.shape, jnp.int32)
    for at, (steps, flip) in enumerate(places):
        wanted = chip_at(chip, steps, flip)
        column = jnp.sum(jnp.where(lane == wanted, notes, 0.0), axis=1, keepdims=True)
        code = jnp.where(slot >= at * capacity, column, code)
        order = jnp.where(slot >= at * capacity, slot + 1 - at * capacity, order)
    pick = ones_where(code == order.astype(jnp.float32))
    rows = across(pick, block[...]).astype(jnp.bfloat16)
    marked = across(pick, marks[...]).astype(jnp.bfloat16)
    for at in range(len(places)):
        place = slice(at * capacity, (at + 1) * capacity)
        refs[at][:, :width] = rows[place]
        refs[at][:, width:] = marked[place]


def choose(block, marks, capacity, places):
    return local_call(
        functools.partial(choose_kernel, places, capacity),
        "choose",
        [jax.ShapeDtypeStruct((capacity, block.shape[1] + LANES), jnp.bfloat16) for _ in places],
        [None] * 2,
        (block, marks),
    )


def load_kernel(source, target, sem):
    copy = pltpu.make_async_copy(source, target, sem)
    copy.start()
    copy.wait()


def loaded(weights):
    return local_call(
        load_kernel,
        "loaded",
        pltpu.VMEM(weights.shape, weights.dtype),
        [pl.ANY],
        (weights,),
        [pltpu.SemaphoreType.DMA],
        limit=9,
        moved=2 * weights.size * weights.dtype.itemsize,
    )


def gated(both):
    hidden = both.shape[1] // 2
    gate = both[:, :hidden]
    return (gate / (1.0 + jnp.exp(-gate)) * both[:, hidden:]).astype(jnp.bfloat16)


def write_pieces(slots, total, outs):
    chip = lax.axis_index("expert") >> 1
    width = total.shape[1]
    experts = 2 * len(RING)
    notes = slots[:, width:].astype(jnp.float32)
    lane = iota(notes.shape, 1)
    mine = (lane >= experts) & (lane < 4 * experts) & ((lane & (experts - 1)) == chip)
    scale = jnp.sum(jnp.where(mine, notes, 0.0), axis=1, keepdims=True)
    start = 0
    for out in outs:
        stop = start + out.shape[0]
        out[:, :width] = (total[start:stop] * scale[start:stop]).astype(jnp.bfloat16)
        out[:, width:] = slots[start:stop, width:]
        start = stop


def near_kernel(*refs):
    pieces, (first, second, slots, total) = refs[:-4], refs[-4:]
    start = 0
    for piece in pieces:
        slots[start : start + piece.shape[0]] = piece[...]
        start += piece.shape[0]
    width = total.shape[1]
    both = jnp.dot(slots[:, :width], first[...], preferred_element_type=jnp.float32)
    total[...] = jnp.dot(gated(both), second[...], preferred_element_type=jnp.float32)


def near_pass(pieces, weights):
    count = sum(piece.shape[0] for piece in pieces)
    full = pieces[0].shape[1]
    return local_call(
        near_kernel,
        "near_pass",
        [
            jax.ShapeDtypeStruct((count, full), jnp.bfloat16),
            jax.ShapeDtypeStruct((count, full - LANES), jnp.float32),
        ],
        [None] * (len(pieces) + 2),
        (*pieces, *weights),
        moved=2 * sum(w.size for w in weights),
    )


def far_kernel(slots, before, first, second, *refs):
    outs, total = refs[:-1], refs[-1]
    width = total.shape[1]
    both = jnp.dot(slots[:, :width], first[...], preferred_element_type=jnp.float32)
    term = jnp.dot(gated(both), second[...], preferred_element_type=jnp.float32)
    total[...] = before[...] + term
    write_pieces(slots, total, outs)


def far_pass(slots, total, weights, capacity):
    count, full = slots.shape
    return local_call(
        far_kernel,
        "far_pass",
        [jax.ShapeDtypeStruct((capacity, full), jnp.bfloat16)] * (count // capacity),
        [None] * 4,
        (slots, total, *weights),
        [pltpu.VMEM(total.shape, jnp.float32)],
        limit=24,
        moved=2 * sum(w.size for w in weights),
    )


def combine_kernel(count, *refs):
    blocks, more, (out, slots) = refs[:count], refs[count:-2], refs[-2:]
    tok_count, width = out.shape
    start = 0
    for block in blocks:
        slots[start : start + block.shape[0]] = block[...]
        start += block.shape[0]
    token = slots[:, width:]
    part = width // 7
    for at in range(7):
        place = slice(at * part, (at + 1) * part)
        mixed = across(token, slots[:, place])[TOKEN_LANE : TOKEN_LANE + tok_count]
        for other in more:
            mixed = mixed + other[:, place].astype(jnp.float32)
        out[:, place] = mixed.astype(out.dtype)


def combine(blocks, tok_count, *more):
    capacity, full = blocks[0].shape
    return local_call(
        functools.partial(combine_kernel, len(blocks)),
        "combine",
        jax.ShapeDtypeStruct((tok_count, full - LANES), jnp.bfloat16),
        [None] * (len(blocks) + len(more)),
        (*blocks, *more),
        [pltpu.VMEM((capacity * len(blocks), full), jnp.bfloat16)],
    )


def sent(shard, sections, section_step, ring_step, flip):
    planes = len(RING)
    pairs = []
    for s in range(sections):
        for z in range(planes):
            for y in range(2):
                for core in range(2):
                    plane = RING[(RING.index(z) + ring_step) % planes]
                    target = (((s + section_step) % sections) * planes + plane) * 2 + (y ^ flip)
                    pairs.append((((s * planes + z) * 2 + y) * 2 + core, target * 2 + core))
    return lax.ppermute(shard, ("section", "expert"), pairs)


def after(value, other):
    return lax.optimization_barrier((value, other))[0]


def by_ring(rows, route_ids, route_weights, w_gate_up, w_down):
    sections = lax.axis_size("section")
    devices = lax.axis_size("expert")
    experts = devices // 2
    tokens = rows[0]
    tok_count = tokens.shape[0]
    top_count = route_ids.shape[2]
    capacity = max(2, 2 * tok_count * top_count // experts)
    swap = [(i, i ^ 1) for i in range(devices)]
    w_in, w_out = w_gate_up[0], w_down[0]
    far_out = lax.ppermute(w_out, "expert", swap)
    far_in = lax.ppermute(w_in, "expert", swap)
    block1 = sent(tokens, sections, 0, 1, 0)
    marks = prepare(route_ids[0].T, route_weights[0].T)
    marks1 = sent(marks, sections, 0, 1, 0)
    own0, other, back0, back1 = choose(tokens, marks, capacity, ((0, 0), (0, 1), (3, 0), (3, 1)))
    other0 = sent(other, sections, 0, 0, 1)
    near_out = loaded(after(w_out, own0))
    block1 = after(block1, (near_out, other0))
    own1, other, on0, on1 = choose(block1, marks1, capacity, ((0, 0), (0, 1), (1, 0), (1, 1)))
    other1 = sent(other, sections, 0, 0, 1)
    own2 = sent(on0, sections, 0, 1, 0)
    other2 = sent(on1, sections, 0, 1, 1)
    other3 = sent(after(back1, other0), sections, 0, 3, 1)
    back0 = after(back0, (other1, other3))
    own3 = sent(back0, sections, 0, 3, 0)
    near = (loaded(after(w_in, back0)), near_out)
    pieces = (own0, other0, own1, own2, other2, other1, own3, other3)
    places = ((0, 0), (0, 1), (1, 0), (2, 0), (2, 1), (1, 1), (3, 0), (3, 1))
    slots, total = near_pass(pieces, near)
    pieces = far_pass(slots, total, (far_in, far_out), capacity)
    piece = dict(zip(places, pieces))
    first = [
        sent(piece[2, 1], sections, 0, 1, 1),
        sent(piece[3, 1], sections, 0, 0, 1),
        sent(piece[0, 0], sections, 1, 0, 0),
        sent(piece[0, 1], sections, 1, 0, 1),
        sent(piece[2, 0], sections, 0, 1, 0),
    ]
    two, three, *straight, four = lax.optimization_barrier(first)
    merged = [piece[3, 0], two, three, four]
    straight.append(sent(piece[1, 0], sections, 1, -1, 0))
    straight.append(sent(after(piece[1, 1], straight[-1]), sections, 1, -1, 1))
    merged = sent(combine(merged, tok_count), sections, 1, 1, 0)
    return combine(straight, tok_count, merged)[None]


def per_device(rows, route_ids, route_weights, w_gate_up, w_down):
    experts = lax.axis_size("expert") // 2
    fits = experts == 2 * len(RING) and rows.shape[1] <= LANES - TOKEN_LANE
    plan = by_ring if fits else by_slots
    return plan(rows, route_ids, route_weights, w_gate_up, w_down)


def solution(mesh):
    in_specs = (
        P("section", "expert", None),
        P("section", "expert", None),
        P("section", "expert", None),
        P("section", None, "expert"),
        P("section", "expert", None),
    )
    out_specs = P("section", "expert", None)
    return jax.shard_map(
        per_device, mesh=mesh, in_specs=in_specs, out_specs=out_specs, check_vma=False
    )
```
